32 devices in a mesh: seq: 8 (over z, y), exp: 4 (over x, core).
Axes of the slice: x: 2, y: 2, z: 4, core: 2. Of those that a mesh axis runs over, the one named last changes fastest.
Arguments:
- hidden_in: bfloat16 [4, 3072, 768], P('exp', 'seq'), may hold values from -6 to 6
- memory: bfloat16 [4, 1024, 768], P('exp', 'seq'), may hold values from -6 to 6
- proj_in: bfloat16 [6, 768, 768], replicated, may hold values from -0.21875 to 0.21875
- proj_out: bfloat16 [2, 768, 768], replicated, may hold values from -0.625 to 0.625
- norm_gains: bfloat16 [3, 768], replicated, may hold values from 0.5 to 1.5
- rel_bias: float32 [32, 12], replicated, may hold values from -4 to 4
- router: bfloat16 [768, 8], replicated, may hold values from -0.109375 to 0.109375
- expert_choice: int32 [4, 3072, 1], P('exp', 'seq'), may hold values from 0 to 7
- expert_in: bfloat16 [8, 768, 3072], P('exp', None, 'seq'), may hold values from -0.21875 to 0.21875
- expert_out: bfloat16 [8, 768, 3072], P('exp', None, 'seq'), may hold values from -1.5 to 1.5
- cotangent: bfloat16 [4, 3072, 768], P('exp', 'seq'), may hold values from -6 to 6
Outputs:
- output: bfloat16 [4, 3072, 768], P('exp', 'seq')
- grad_in: bfloat16 [4, 3072, 768], P('exp', 'seq')
- grad_memory: bfloat16 [4, 1024, 768], P('exp', 'seq')
- grad_proj_in: float32 [6, 768, 768], replicated
- grad_proj_out: float32 [2, 768, 768], replicated
- grad_gains: float32 [3, 768], replicated
- grad_rel_bias: float32 [32, 12], replicated
- grad_router: float32 [768, 8], replicated
- grad_expert_in: float32 [8, 768, 3072], P('exp', None, 'seq')
- grad_expert_out: float32 [8, 768, 3072], P('exp', None, 'seq')
- expert_tally: int32 [4, 8, 2, 8], P('exp', 'seq')
The draws below stay inside these ranges and needn't reach their ends.
Inputs may be any that keep to these rules, and one draw needn't show every extreme that they name: `expert_choice`: each token names one expert; every expert is named by some token.
All inputs are finite; a program needn't handle non-finite values.
Results may differ from the reference program's by a relative error of at most 0.03.
Values may be sent and summed in bfloat16 or wider, within the bound.
A program may use at most 320 MiB of HBM per device.

```python
import jax
import jax.numpy as jnp
from jax import lax

D = 768
HEADS = 12
HEAD_DIM = 64
FF = 3072
NBUCKET = 32
MAXDIST = 128
TOK_DEV = 384
LEN = 3072
MEM = 1024
SEQUENCES = 4
EXPERTS = 8
CAP = 60
N_SEQ = 8
N_EXP = 4


def block_levels(own_key, dims, shards, least, high):
    gain, own = 1.0, jax.random.fold_in(own_key, 6)
    for axis_at, shards_of in shards:
        draws = jnp.exp(jax.random.uniform(jax.random.fold_in(own, axis_at), (shards_of,), jnp.float32, least / len(shards), high / len(shards)))
        gain = gain * jnp.repeat(draws, dims[axis_at] // shards_of).reshape([-1 if axis == axis_at else 1 for axis in range(len(dims))])
    return gain


def picks_of(stream_key, rows, amount, top, lift):
    sequence = jax.random.permutation(jax.random.fold_in(stream_key, 1), amount)
    pull = sequence
    for power in range(3):
        pull = pull * pull // amount
    pull = pull * lift // amount
    chance = jax.random.randint(jax.random.fold_in(stream_key, 2), (rows, amount), 0, 4096) + pull
    sure = jax.random.permutation(jax.random.fold_in(stream_key, 3), rows)[jnp.arange(amount) % rows]
    chance = jnp.where(jnp.arange(rows)[:, None] == sure[None, :], 1 << 14, chance)
    priority = chance * amount + jnp.arange(amount)
    return lax.top_k(priority.astype(jnp.int32), top)[1].astype(jnp.int32)


def bell_draw(stream_key, extent, spread, reach, cuts=(), kind=jnp.bfloat16):
    factor_of = block_levels(stream_key, extent, cuts, -0.22, 0.18) if cuts else 1.0
    drawn = jax.random.normal(stream_key, extent, jnp.float32) * spread * factor_of
    return jnp.minimum(jnp.maximum(drawn, -reach), reach).astype(kind)


def setup_inputs(seed: int = 0) -> dict:
    streams_of = jax.random.split(jax.random.key(seed), 12)
    hidden_in = bell_draw(streams_of[0], (SEQUENCES, LEN, D), 1.0, 6.0, ((0, 4), (1, 8)))
    memory = bell_draw(streams_of[1], (SEQUENCES, MEM, D), 1.0, 6.0, ((0, 4), (1, 8)))
    proj_in = bell_draw(streams_of[2], (6, D, D), D ** -0.5, 0.21875)
    proj_out = bell_draw(streams_of[3], (2, D, D), (D // 8) ** -0.5, 0.625)
    norm_gains = jnp.clip(1.0 + 0.1 * jax.random.normal(streams_of[4], (3, D), jnp.float32), 0.5, 1.5).astype(jnp.bfloat16)
    rel_bias = bell_draw(streams_of[5], (NBUCKET, HEADS), 1.0, 4.0, (), jnp.float32)
    router = bell_draw(streams_of[6], (D, EXPERTS), (4 * D) ** -0.5, 0.109375)
    expert_choice = picks_of(streams_of[7], SEQUENCES * LEN, EXPERTS, 1, 1024).reshape((SEQUENCES, LEN, 1))
    expert_in = bell_draw(streams_of[8], (EXPERTS, D, FF), D ** -0.5, 0.21875, ((0, 4), (2, 8)))
    expert_out = bell_draw(streams_of[9], (EXPERTS, D, FF), (max(1, FF // (3 * EXPERTS * EXPERTS))) ** -0.5, 1.5, ((0, 4), (2, 8)))
    cotangent = bell_draw(streams_of[10], (SEQUENCES, LEN, D), 1.0, 6.0, ((0, 4), (1, 8)))
    return {"hidden_in": hidden_in, "memory": memory, "proj_in": proj_in, "proj_out": proj_out, "norm_gains": norm_gains, "rel_bias": rel_bias, "router": router, "expert_choice": expert_choice, "expert_in": expert_in, "expert_out": expert_out, "cotangent": cotangent}


norm_eps = 1e-06
masked_score = -1e+30
highest = lax.Precision.HIGHEST

@jax.custom_vjp
def low(v):
    return lax.optimization_barrier(v.astype(jnp.bfloat16)).astype(jnp.float32)

@jax.custom_vjp
def low_back(v):
    return v

def low_keep(v):
    return (low(v), None)

def low_pass(kept, grad):
    return (grad,)

def back_keep(v):
    return (v, None)

def back_low(kept, grad):
    return (low(grad),)
low.defvjp(low_keep, low_pass)
low_back.defvjp(back_keep, back_low)

def bucket_edges():
    half_count = NBUCKET // 2
    thresholds = []
    for bucket_number in range(1, NBUCKET):
        if bucket_number < half_count:
            thresholds.append(bucket_number)
        else:
            thresholds.append(int(half_count * (MAXDIST / half_count) ** ((bucket_number - half_count) / half_count)))
    return thresholds

def rms_apply(values, gain_row):
    return values * lax.rsqrt(lax.optimization_barrier(jnp.mean(values * values, axis=-1, keepdims=True)) + norm_eps) * gain_row

def heads_of(matrix):
    return matrix.reshape(matrix.shape[0], HEADS, HEAD_DIM)

def attend(queries, key_rows, value_rows, bias_table, causal):
    length = queries.shape[0]
    block_size = 512 if length % 512 == 0 else length
    block_count = length // block_size
    query_blocks = queries.reshape(block_count, block_size, HEADS, HEAD_DIM)
    block_starts = jnp.arange(block_count, dtype=jnp.int32) * block_size
    scale_factor = HEAD_DIM ** (-0.5)

    def one_block(inputs):
        query_block, block_start = inputs
        scores = jnp.einsum('qhd,khd->hqk', query_block, key_rows, precision=highest) * scale_factor
        if causal:
            distance = block_start + jnp.arange(block_size, dtype=jnp.int32)[:, None] - jnp.arange(key_rows.shape[0], dtype=jnp.int32)[None, :]
            bucket_ids = jnp.zeros(distance.shape, jnp.int32)
            for threshold in bucket_edges():
                bucket_ids = bucket_ids + (distance >= threshold).astype(jnp.int32)
            scores = scores + jnp.take(bias_table, bucket_ids, axis=0).transpose(2, 0, 1)
        scores = low_back(scores)
        if causal:
            scores = jnp.where(distance[None] >= 0, scores, masked_score)
        weights = low(jax.nn.softmax(scores, axis=-1))
        return jnp.einsum('hqk,khd->qhd', weights, value_rows, precision=highest)
    attended = lax.map(jax.checkpoint(one_block), (query_blocks, block_starts))
    return attended.reshape(length, HEADS * HEAD_DIM)

def project(source, matrix):
    return low(low_back(jnp.dot(source, matrix, precision=highest)))

def decoder_layer(tokens, memory_rows, chosen, weights_in, weights_out, gain_rows, bias_table, router_map, up_maps, down_maps):
    normed = low(rms_apply(tokens, gain_rows[0]))
    queries = project(normed, weights_in[0])
    key_rows = project(normed, weights_in[1])
    value_rows = project(normed, weights_in[2])
    attended = low(low_back(attend(heads_of(queries), heads_of(key_rows), heads_of(value_rows), bias_table, True)))
    after_self = tokens + low_back(jnp.dot(attended, weights_out[0], precision=highest))
    normed_cross = low(rms_apply(after_self, gain_rows[1]))
    cross_queries = project(normed_cross, weights_in[3])
    memory_keys = project(memory_rows, weights_in[4])
    memory_values = project(memory_rows, weights_in[5])
    cross_out = low(low_back(attend(heads_of(cross_queries), heads_of(memory_keys), heads_of(memory_values), bias_table, False)))
    after_cross = after_self + low_back(jnp.dot(cross_out, weights_out[1], precision=highest))
    mixed = low(rms_apply(after_cross, gain_rows[2]))
    expert_total = router_map.shape[1]
    softmax_probs = jax.nn.softmax(jnp.dot(mixed, router_map, precision=highest), axis=-1)
    onehot = (chosen[:, None] == jnp.arange(expert_total, dtype=jnp.int32)[None, :]).astype(jnp.float32)
    gate_prob = lax.optimization_barrier(jnp.sum(softmax_probs * onehot, axis=-1))
    per_device = onehot.reshape(N_SEQ, TOK_DEV, expert_total)
    slot_index = lax.optimization_barrier(jnp.sum(jnp.cumsum(per_device, axis=1) * per_device, axis=-1)) - 1.0
    is_kept = (slot_index < CAP).astype(jnp.float32)
    slot_onehot = (slot_index[..., None] == jnp.arange(CAP, dtype=jnp.float32)).astype(jnp.float32) * is_kept[..., None]
    dispatch = per_device[..., :, None] * slot_onehot[..., None, :]
    routed = low_back(mixed).reshape(N_SEQ, TOK_DEV, D)
    buffers = jnp.einsum('stec,std->secd', dispatch, routed, precision=highest)
    pre_act = low_back(jnp.einsum('secd,edf->secf', buffers, up_maps, precision=highest))
    activated = low(jax.nn.gelu(pre_act))
    expert_result = low(low_back(jnp.einsum('secf,edf->secd', activated, down_maps, precision=highest)))
    returned = jnp.einsum('stec,secd->std', dispatch, expert_result, precision=highest).reshape(LEN, D)
    return after_cross + gate_prob[:, None] * returned

def reference(hidden_in, memory, proj_in, proj_out, norm_gains, rel_bias, router, expert_choice, expert_in, expert_out, cotangent):
    chosen = expert_choice[..., 0].astype(jnp.int32)

    def forward(tokens, memory_rows, weights_in, weights_out, gain_rows, bias_table, router_map, up_maps, down_maps):

        def per_sequence(inputs):
            seq_tokens, seq_memory, seq_chosen = inputs
            return decoder_layer(seq_tokens, seq_memory, seq_chosen, weights_in, weights_out, gain_rows, bias_table, router_map, up_maps, down_maps)
        return lax.map(per_sequence, (tokens, memory_rows, chosen))
    result, pullback = jax.vjp(forward, hidden_in.astype(jnp.float32), memory.astype(jnp.float32), proj_in.astype(jnp.float32), proj_out.astype(jnp.float32), norm_gains.astype(jnp.float32), rel_bias.astype(jnp.float32), router.astype(jnp.float32), expert_in.astype(jnp.float32), expert_out.astype(jnp.float32))
    gradients = pullback(cotangent.astype(jnp.float32))
    by_device = chosen.reshape(N_EXP, N_SEQ, TOK_DEV)
    onehot_int = (by_device[..., None] == jnp.arange(EXPERTS, dtype=jnp.int32)).astype(jnp.int32)
    slot_int = lax.optimization_barrier(jnp.sum(jnp.cumsum(onehot_int, axis=2) * onehot_int, axis=-1)) - 1
    kept_int = (slot_int < CAP).astype(jnp.int32)
    dispatched = lax.optimization_barrier(jnp.sum(onehot_int * kept_int[..., None], axis=2))
    dropped = lax.optimization_barrier(jnp.sum(onehot_int, axis=2)) - dispatched
    tally_counts = jnp.stack([dispatched, dropped], axis=2).astype(jnp.int32)
    return (result.astype(jnp.bfloat16), gradients[0].astype(jnp.bfloat16), gradients[1].astype(jnp.bfloat16), gradients[2], gradients[3], gradients[4], gradients[5], gradients[6], gradients[7], gradients[8], tally_counts)
```

```python
import functools
import math

import jax
import jax.numpy as jnp
from jax import lax
from jax.experimental import pallas as pl
from jax.experimental.pallas import tpu as pltpu
from jax.sharding import PartitionSpec as P

D = 768
HEADS = 12
HEAD_DIM = 64
NBUCKET = 32
MAXDIST = 128
TILE = 128
PAIRS = HEADS * HEAD_DIM // TILE

MESH = pl.DeviceIdType.MESH
ANY = pl.BlockSpec(memory_space=pl.ANY)
SMEM = pl.BlockSpec(memory_space=pltpu.SMEM)

norm_eps = 1e-06
masked_score = -1e30
highest = lax.Precision.HIGHEST
log2e = 1.0 / math.log(2.0)
scale_factor = HEAD_DIM ** (-0.5)


def bucket_edges():
    half_count = NBUCKET // 2
    thresholds = []
    for bucket_number in range(1, NBUCKET):
        if bucket_number < half_count:
            thresholds.append(bucket_number)
        else:
            thresholds.append(
                int(
                    half_count
                    * (MAXDIST / half_count) ** ((bucket_number - half_count) / half_count)
                )
            )
    return thresholds


def rms_apply(values, gain_row):
    return (
        values * lax.rsqrt(jnp.mean(values * values, axis=-1, keepdims=True) + norm_eps) * gain_row
    )


def rms_backward(values, gain_row, upstream):
    _, pullback = jax.vjp(rms_apply, values, gain_row)
    return pullback(upstream)


def seq_cycle(n):
    cols = n // 4
    if n % 4 or cols < 2:
        return list(range(n))
    order = [0]
    for row in range(4):
        span = range(1, cols) if row % 2 == 0 else range(cols - 1, 0, -1)
        order += [row * cols + col for col in span]
    return order + [3 * cols, 2 * cols, cols]


def chip_cycle(n, chips):
    order = seq_cycle(n)
    if chips == 1:
        return [(place, 0) for place in order]
    cycle = [(order[0], 0)]
    for row in range(n):
        span = range(1, chips) if row % 2 == 0 else range(chips - 1, 0, -1)
        cycle += [(order[row], chip) for chip in span]
    return cycle + [(order[row], 0) for row in range(n - 1, 0, -1)]


def look_up(index, table):
    value = jnp.int32(table[0])
    for number, entry in enumerate(table[1:], 1):
        value = jnp.where(index == number, jnp.int32(entry), value)
    return value


def greet(others):
    barrier = pltpu.get_barrier_semaphore()
    for other in others:
        pl.semaphore_signal(barrier, inc=1, device_id=other, device_id_type=MESH)
    pl.semaphore_wait(barrier, len(others))


def seq_ring(n):
    order = seq_cycle(n)
    pos = look_up(lax.axis_index("seq"), [order.index(i) for i in range(n)])

    def at(place):
        return look_up(lax.rem(place + 4 * n, n), order)

    return pos, at, ({"seq": at(pos + 1)}, {"seq": at(pos - 1)})


def gather_kernel(n, parts, count, *refs):
    sources, outs = refs[:count], refs[count : 2 * count]
    own_sem, send_sem, recv_sem = refs[2 * count :]
    pos, at, sides = seq_ring(n)
    me = at(pos)
    greet(sides)
    own = [
        pltpu.make_async_copy(sources[a], outs[a].at[me], own_sem.at[a]) for a in range(count)
    ]
    for copy in own:
        copy.start()
    started, latest = [], {}
    for step in range(n - 1):
        for a in range(count):
            rows = sources[a].shape[0] // 2 // parts
            for part in range(parts):
                for way in range(2):
                    if step:
                        latest[a, way, part].wait_recv()
                    block = at(pos - step) if way == 0 else at(pos + step)
                    span = pl.ds((way * parts + part) * rows, rows)
                    copy = pltpu.make_async_remote_copy(
                        src_ref=outs[a].at[block, span] if step else sources[a].at[span],
                        dst_ref=outs[a].at[block, span],
                        send_sem=send_sem.at[a, way, step, part],
                        recv_sem=recv_sem.at[a, way, step, part],
                        device_id=sides[way],
                        device_id_type=MESH,
                    )
                    copy.start()
                    started.append(copy)
                    latest[a, way, part] = copy
    for copy in latest.values():
        copy.wait_recv()
    for copy in started:
        copy.wait_send()
    for copy in own:
        copy.wait()


def ring_gather(arrays, n, number, parts=2):
    count = len(arrays)
    copies = (count, 2, n - 1, parts)
    return pl.pallas_call(
        functools.partial(gather_kernel, n, parts, count),
        out_shape=[jax.ShapeDtypeStruct((n,) + a.shape, a.dtype) for a in arrays],
        in_specs=[ANY] * count,
        out_specs=[ANY] * count,
        scratch_shapes=[
            pltpu.SemaphoreType.DMA((count,)),
            pltpu.SemaphoreType.DMA(copies),
            pltpu.SemaphoreType.DMA(copies),
        ],
        compiler_params=pltpu.CompilerParams(collective_id=number, has_side_effects=True),
        name="ring_gather",
    )(*arrays)


def scatter_kernel(n, parts, count, *refs):
    sources, outs = refs[:count], refs[count : 2 * count]
    own_bufs, got_bufs = refs[2 * count : 3 * count], refs[3 * count : 4 * count]
    own_sem, send_sem, recv_sem = refs[4 * count :]
    pos, at, sides = seq_ring(n)
    greet(sides)
    lanes = [(a, part, way) for a in range(count) for part in range(parts) for way in range(2)]

    def span(a, part, way):
        rows = sources[a].shape[1] // 2 // parts
        return pl.ds((way * parts + part) * rows, rows)

    def block(way, step):
        return at(pos - 1 - step) if way == 0 else at(pos + 1 + step)

    def send(lane, step, source):
        a, part, way = lane
        copy = pltpu.make_async_remote_copy(
            src_ref=source,
            dst_ref=got_bufs[a].at[way, step, part],
            send_sem=send_sem.at[a, way, step, part],
            recv_sem=recv_sem.at[a, way, step, part],
            device_id=sides[way],
            device_id_type=MESH,
        )
        copy.start()
        return copy

    latest, started, own = {}, [], {}
    for lane in lanes:
        a, part, way = lane
        latest[lane] = send(lane, 0, sources[a].at[block(way, 0), span(a, part, way)])
        started.append(latest[lane])
    for step in range(1, n):
        for lane in lanes:
            a, part, way = lane
            own[lane, step] = pltpu.make_async_copy(
                sources[a].at[block(way, step), span(a, part, way)],
                own_bufs[a].at[way, step - 1, part],
                own_sem.at[a, way, step - 1, part],
            )
            own[lane, step].start()
    for step in range(1, n):
        for lane in lanes:
            a, part, way = lane
            own[lane, step].wait()
            latest[lane].wait_recv()
            total = got_bufs[a][way, step - 1, part].astype(jnp.float32) + own_bufs[a][
                way, step - 1, part
            ].astype(jnp.float32)
            if step == n - 1:
                outs[a][span(a, part, way)] = total.astype(outs[a].dtype)
            else:
                got_bufs[a][way, step - 1, part] = total.astype(got_bufs[a].dtype)
                latest[lane] = send(lane, step, got_bufs[a].at[way, step - 1, part])
                started.append(latest[lane])
    for copy in started:
        copy.wait_send()


def ring_scatter(arrays, n, number, out_dtype, parts=2):
    count = len(arrays)
    copies = (count, 2, n - 1, parts)
    bufs = [
        pltpu.VMEM((2, n - 1, parts, a.shape[1] // 2 // parts, a.shape[2]), a.dtype)
        for a in arrays
    ]
    return pl.pallas_call(
        functools.partial(scatter_kernel, n, parts, count),
        out_shape=[jax.ShapeDtypeStruct(a.shape[1:], out_dtype) for a in arrays],
        in_specs=[ANY] * count,
        out_specs=[pl.BlockSpec(memory_space=pltpu.VMEM)] * count,
        scratch_shapes=bufs + bufs + [pltpu.SemaphoreType.DMA(copies)] * 3,
        compiler_params=pltpu.CompilerParams(
            collective_id=number, has_side_effects=True, vmem_limit_bytes=58 << 20
        ),
        name="ring_scatter",
    )(*arrays)


def total_kernel(n, chips, x_ref, out_ref, mine, twin, got, own_sem, twin_sem, ring_sem, back_sem):
    cycle = chip_cycle(n, chips)
    length = len(cycle)
    seq, exp = lax.axis_index("seq"), lax.axis_index("exp")
    core = lax.rem(exp, 2)
    places = [cycle.index((i // chips, i % chips)) for i in range(length)]
    pos = look_up(seq * chips + exp // 2, places)

    def device(place):
        place = lax.rem(place + length, length)
        return {
            "seq": look_up(place, [c[0] for c in cycle]),
            "exp": look_up(place, [c[1] for c in cycle]) * 2 + core,
        }

    def block(way, step):
        place = pos - 1 - step if way == 0 else pos + 1 + step
        return lax.rem(place + 2 * length, length)

    peer = {"exp": exp + 1 - 2 * core}
    sides = (device(pos + 1), device(pos - 1))
    greet((peer,) + sides)
    rows = x_ref.shape[2] // 2
    spans = (pl.ds(0, rows), pl.ds(rows, rows))
    started = []

    def push(source, target, sems, index, to):
        copy = pltpu.make_async_remote_copy(
            src_ref=source,
            dst_ref=target,
            send_sem=sems.at[(0,) + index],
            recv_sem=sems.at[(1,) + index],
            device_id=to,
            device_id_type=MESH,
        )
        copy.start()
        started.append(copy)
        return copy

    pairs, own = {}, {}
    for step in range(length):
        for way in range(2):
            where = block(way, step)
            pairs[way, step] = push(
                x_ref.at[1 - core, where, spans[way]], twin.at[way, step], twin_sem, (way, step), peer
            )
            own[way, step] = pltpu.make_async_copy(
                x_ref.at[core, where, spans[way]], mine.at[way, step], own_sem.at[way, step]
            )
            own[way, step].start()
    latest = {}
    for step in range(length):
        for way in range(2):
            own[way, step].wait()
            pairs[way, step].wait_recv()
            total = mine[way, step].astype(jnp.float32) + twin[way, step].astype(jnp.float32)
            if step:
                latest[way].wait_recv()
                total = total + got[way, step - 1].astype(jnp.float32)
            mine[way, step] = total.astype(mine.dtype)
            if step < length - 1:
                latest[way] = push(
                    mine.at[way, step], got.at[way, step], ring_sem, (0, way, step), sides[way]
                )
    keep = []
    for step in range(length):
        for way in range(2):
            if step:
                latest[way].wait_recv()
            where = lax.rem(pos - step + length, length) if way == 0 else lax.rem(pos + step, length)
            target = out_ref.at[core, where, spans[way]]
            source = target if step else mine.at[way, length - 1]
            if step < length - 1:
                latest[way] = push(source, target, ring_sem, (1, way, step), sides[way])
            pairs[way, step] = push(source, target, back_sem, (way, step), peer)
            if step == 0:
                copy = pltpu.make_async_copy(source, target, own_sem.at[way, 0])
                copy.start()
                keep.append(copy)
    for copy in keep:
        copy.wait()
    for copy in pairs.values():
        copy.wait_recv()
    for copy in started:
        copy.wait_send()


def total_everywhere(rows_in, n, m, number):
    chips = m // 2
    length = n * chips
    rows, cols = rows_in.shape
    each = rows // (2 * length)
    if m % 2 or rows % (2 * length * 32):
        return lax.psum(rows_in, ("seq", "exp"))
    x = rows_in.reshape(2, length, each, cols)
    buf = pltpu.VMEM((2, length, each // 2, cols), x.dtype)
    return pl.pallas_call(
        functools.partial(total_kernel, n, chips),
        out_shape=jax.ShapeDtypeStruct(x.shape, x.dtype),
        in_specs=[ANY],
        out_specs=ANY,
        scratch_shapes=[
            buf,
            buf,
            buf,
            pltpu.SemaphoreType.DMA((2, length)),
            pltpu.SemaphoreType.DMA((2, 2, length)),
            pltpu.SemaphoreType.DMA((2, 2, 2, length)),
            pltpu.SemaphoreType.DMA((2, 2, length)),
        ],
        compiler_params=pltpu.CompilerParams(
            collective_id=number, has_side_effects=True, vmem_limit_bytes=58 << 20
        ),
        name="total_everywhere",
    )(x).reshape(rows, cols)


def dot_last(a, b):
    return lax.dot_general(a, b, (((1,), (1,)), ((), ())), preferred_element_type=jnp.float32)


def dot_first(a, b):
    return lax.dot_general(a, b, (((0,), (0,)), ((), ())), preferred_element_type=jnp.float32)


def dot_plain(a, b):
    return jnp.dot(a, b, preferred_element_type=jnp.float32)


def head_masks(dtype):
    low = lax.broadcasted_iota(jnp.int32, (1, TILE), 1) < HEAD_DIM
    first = jnp.where(low, 1.0, 0.0).astype(jnp.float32)
    return first.astype(dtype), (1.0 - first).astype(dtype)


def split_heads(pair):
    return jnp.concatenate([pair * mask for mask in head_masks(pair.dtype)], axis=0)


def own_bias(tiles, count):
    rows = []
    for r in range(count):
        row = []
        for c in range(count):
            if c == r:
                row.append(tiles[:, TILE:])
            elif c == r - 1:
                row.append(tiles[:, :TILE])
            else:
                row.append(jnp.full((TILE, TILE), 0.0 if c < r else masked_score, jnp.float32))
        rows.append(jnp.concatenate(row, axis=1))
    return jnp.concatenate(rows, axis=0)


def attend_kernel(causal, block, s_ref, q_ref, k_ref, v_ref, *refs):
    if causal:
        tile_ref, low_ref, wide_ref, lse_ref, acc_ref, top_ref = refs
    else:
        low_ref, wide_ref, lse_ref, acc_ref, top_ref = refs
    rows = q_ref.shape[0]
    both = split_heads(q_ref[...])
    masks = head_masks(v_ref.dtype)

    def visit(start, bias, first):
        keys = k_ref[pl.ds(start, block), :]
        values = v_ref[pl.ds(start, block), :]
        t = dot_last(both, keys) * (scale_factor * log2e)
        if bias is not None:
            t = t + bias
        top = jnp.max(t, axis=1, keepdims=True)
        if not first:
            before = top_ref[...]
            top = jnp.maximum(before, top)
            fade = jnp.exp2(before - top)
        top_ref[...] = top
        p = jnp.exp2(t - top).astype(values.dtype)
        for h in range(2):
            part = dot_plain(p[h * rows : (h + 1) * rows], values * masks[h] + masks[1 - h])
            if first:
                acc_ref[h] = part
            else:
                acc_ref[h] = acc_ref[h] * fade[h * rows : (h + 1) * rows] + part

    if causal:
        s = s_ref[0]
        count = rows // TILE
        visit(
            pl.multiple_of(s * block, block),
            jnp.concatenate([own_bias(tile_ref[h], count) for h in range(2)], axis=0),
            True,
        )

        @pl.when(s > 0)
        def _():
            edge = []
            for h in range(2):
                top_row = jnp.concatenate(
                    [jnp.zeros((TILE, rows - TILE), jnp.float32), tile_ref[h][:, :TILE]], axis=1
                )
                edge += [top_row, jnp.zeros((rows - TILE, rows), jnp.float32)]
            visit(pl.multiple_of((s - 1) * block, block), jnp.concatenate(edge, axis=0), False)

        def far(j, carry):
            visit(pl.multiple_of(j * block, block), None, False)
            return carry

        lax.fori_loop(0, s - 1, far, 0)
    else:
        for j in range(k_ref.shape[0] // block):
            visit(j * block, None, j == 0)
    low = lax.broadcasted_iota(jnp.int32, (rows, TILE), 1) < HEAD_DIM
    acc0, acc1 = acc_ref[0], acc_ref[1]
    wide = jnp.where(
        low,
        acc0 / pltpu.roll(acc0, HEAD_DIM, 1),
        acc1 / pltpu.roll(acc1, HEAD_DIM, 1),
    )
    wide_ref[...] = wide
    low_ref[...] = wide.astype(low_ref.dtype)
    lse0 = top_ref[:rows] + jnp.log2(acc0[:, HEAD_DIM : HEAD_DIM + 1])
    lse1 = top_ref[rows:] + jnp.log2(acc1[:, :1])
    turned = jnp.where(low, lse0, lse1).T
    lse_ref[0] = jnp.concatenate([turned[:1], turned[HEAD_DIM : HEAD_DIM + 1]], axis=0)


def attend(seq_at, queries, keys, values, tiles):
    rows, total = queries.shape[0], keys.shape[0]
    causal = tiles is not None
    block = rows if causal else math.gcd(total, 512)
    pair = pl.BlockSpec((rows, TILE), lambda g: (0, g))
    long = pl.BlockSpec((total, TILE), lambda g: (0, g))
    extra, specs = [], []
    if causal:
        extra, specs = [tiles], [pl.BlockSpec((2,) + tiles.shape[1:], lambda g: (g, 0, 0))]
    return pl.pallas_call(
        functools.partial(attend_kernel, causal, block),
        grid=(PAIRS,),
        out_shape=[
            jax.ShapeDtypeStruct((rows, D), jnp.bfloat16),
            jax.ShapeDtypeStruct((rows, D), jnp.float32),
            jax.ShapeDtypeStruct((PAIRS, 2, rows), jnp.float32),
        ],
        in_specs=[SMEM, pair, long, long] + specs,
        out_specs=[pair, pair, pl.BlockSpec((1, 2, rows), lambda g: (g, 0, 0))],
        scratch_shapes=[
            pltpu.VMEM((2, rows, TILE), jnp.float32),
            pltpu.VMEM((2 * rows, 1), jnp.float32),
        ],
        compiler_params=pltpu.CompilerParams(vmem_limit_bytes=48 << 20),
        name="attend_self" if causal else "attend_cross",
    )(seq_at, queries, keys, values, *extra)


def attend_back_kernel(causal, block, s_ref, q_ref, k_ref, v_ref, up_ref, wide_ref, lse_ref, *refs):
    if causal:
        tile_ref, dq_ref, dk_ref, dv_ref, near_ref, sum_ref, acc_ref = refs
    else:
        dq_ref, dk_ref, dv_ref, acc_ref = refs
    rows = q_ref.shape[0]
    both = split_heads(q_ref[...])
    up = up_ref[...]
    up_both = split_heads(up)
    turned = (up.astype(jnp.float32) * wide_ref[...]).T
    delta = jnp.concatenate(
        [
            jnp.sum(turned[:HEAD_DIM], axis=0, keepdims=True),
            jnp.sum(turned[HEAD_DIM:], axis=0, keepdims=True),
        ],
        axis=1,
    )
    lse = jnp.concatenate([lse_ref[0, :1], lse_ref[0, 1:]], axis=1)
    ones = jnp.ones((16, block), k_ref.dtype)

    def visit(start, bias, first):
        keys = k_ref[pl.ds(start, block), :]
        values = v_ref[pl.ds(start, block), :]
        t = dot_last(keys, both) * (scale_factor * log2e)
        if bias is not None:
            t = t + bias
        p = jnp.exp2(t - lse)
        ds = (p * (dot_last(values, up_both) - delta)).astype(keys.dtype)
        dv_ref[pl.ds(start, block), :] = dot_plain(p.astype(keys.dtype), up_both).astype(
            dv_ref.dtype
        )
        dk_ref[pl.ds(start, block), :] = (dot_plain(ds, both) * scale_factor).astype(dk_ref.dtype)
        part = dot_plain(jnp.concatenate([keys.T, ones], axis=0), ds)
        if first:
            acc_ref[...] = part
        else:
            acc_ref[...] += part
        return ds

    if causal:
        s = s_ref[0]
        count = rows // TILE
        ds = visit(
            pl.multiple_of(s * block, block),
            jnp.concatenate([own_bias(tile_ref[h], count).T for h in range(2)], axis=1),
            True,
        )
        for h in range(2):
            same = before = jnp.zeros((TILE, TILE), jnp.float32)
            for r in range(count):
                columns = slice(h * rows + r * TILE, h * rows + (r + 1) * TILE)
                same = same + ds[r * TILE : (r + 1) * TILE, columns].astype(jnp.float32)
                if r:
                    before = before + ds[(r - 1) * TILE : r * TILE, columns].astype(jnp.float32)
            near_ref[h, :TILE] = before
            near_ref[h, TILE:] = same

        @pl.when(s > 0)
        def _():
            edge = []
            for h in range(2):
                first_rows = jnp.concatenate(
                    [jnp.zeros((rows - TILE, TILE), jnp.float32), tile_ref[h][:, :TILE].T], axis=0
                )
                edge += [first_rows, jnp.zeros((rows, rows - TILE), jnp.float32)]
            ds = visit(pl.multiple_of((s - 1) * block, block), jnp.concatenate(edge, axis=1), False)
            for h in range(2):
                near_ref[h, :TILE] += ds[rows - TILE :, h * rows : h * rows + TILE].astype(
                    jnp.float32
                )

        def far(j, carry):
            visit(pl.multiple_of(j * block, block), None, False)
            return carry

        lax.fori_loop(0, s - 1, far, 0)

        def beyond(j, carry):
            start = pl.multiple_of(j * block, block)
            dk_ref[pl.ds(start, block), :] = jnp.zeros((block, TILE), dk_ref.dtype)
            dv_ref[pl.ds(start, block), :] = jnp.zeros((block, TILE), dv_ref.dtype)
            return carry

        lax.fori_loop(s + 1, k_ref.shape[0] // block, beyond, 0)
        sum_ref[0] = jnp.concatenate(
            [acc_ref[TILE : TILE + 1, :rows], acc_ref[TILE : TILE + 1, rows:]], axis=0
        )
    else:
        for j in range(k_ref.shape[0] // block):
            visit(j * block, None, j == 0)
    dq = jnp.concatenate([acc_ref[:HEAD_DIM, :rows], acc_ref[HEAD_DIM:TILE, rows:]], axis=0)
    dq_ref[...] = (dq.T * scale_factor).astype(dq_ref.dtype)


def attend_back(seq_at, queries, keys, values, upstream, wide, lse, tiles):
    rows, total = queries.shape[0], keys.shape[0]
    causal = tiles is not None
    block = rows if causal else math.gcd(total, 512)
    pair = pl.BlockSpec((rows, TILE), lambda g: (0, g))
    long = pl.BlockSpec((total, TILE), lambda g: (0, g))
    line = pl.BlockSpec((1, 2, rows), lambda g: (g, 0, 0))
    extra, specs, shapes, out_specs = [], [], [], []
    if causal:
        extra, specs = [tiles], [pl.BlockSpec((2,) + tiles.shape[1:], lambda g: (g, 0, 0))]
        shapes = [
            jax.ShapeDtypeStruct((HEADS, 2 * TILE, TILE), jnp.float32),
            jax.ShapeDtypeStruct((PAIRS, 2, rows), jnp.float32),
        ]
        out_specs = [pl.BlockSpec((2, 2 * TILE, TILE), lambda g: (g, 0, 0)), line]
    return pl.pallas_call(
        functools.partial(attend_back_kernel, causal, block),
        grid=(PAIRS,),
        out_shape=[
            jax.ShapeDtypeStruct((rows, D), jnp.bfloat16),
            jax.ShapeDtypeStruct((total, D), jnp.bfloat16),
            jax.ShapeDtypeStruct((total, D), jnp.bfloat16),
        ]
        + shapes,
        in_specs=[SMEM, pair, long, long, pair, pair, line] + specs,
        out_specs=[pair, long, long] + out_specs,
        scratch_shapes=[pltpu.VMEM((TILE + 16, 2 * rows), jnp.float32)],
        compiler_params=pltpu.CompilerParams(vmem_limit_bytes=48 << 20),
        name="attend_self_back" if causal else "attend_cross_back",
    )(seq_at, queries, keys, values, upstream, wide, lse, *extra)


def bias_tiles(bias_table):
    distance = (
        TILE
        + jnp.arange(TILE, dtype=jnp.int32)[:, None]
        - jnp.arange(2 * TILE, dtype=jnp.int32)[None, :]
    )
    table = (bias_table - bias_table[NBUCKET - 1 :]) * log2e
    terms = jnp.broadcast_to(table[0][:, None, None], (HEADS, TILE, 2 * TILE))
    for number, threshold in enumerate(bucket_edges()):
        terms = jnp.where((distance >= threshold)[None], table[number + 1][:, None, None], terms)
    return jnp.where((distance >= 0)[None], terms, masked_score)


def bias_gradient(near, sums):
    distance = (
        TILE
        + jnp.arange(TILE, dtype=jnp.int32)[None, :]
        - jnp.arange(2 * TILE, dtype=jnp.int32)[:, None]
    )
    bucket = jnp.zeros(distance.shape, jnp.int32)
    for threshold in bucket_edges():
        bucket = bucket + (distance >= threshold).astype(jnp.int32)
    onehot = (
        bucket.reshape(-1)[None, :] == jnp.arange(NBUCKET, dtype=jnp.int32)[:, None]
    ).astype(jnp.float32)
    flat = near.reshape(HEADS, -1)
    table = lax.dot_general(
        onehot, flat, (((1,), (1,)), ((), ())), precision=highest
    )
    far = jnp.sum(sums, axis=-1).reshape(HEADS) - jnp.sum(flat, axis=-1)
    last = jnp.arange(NBUCKET, dtype=jnp.int32)[:, None] == NBUCKET - 1
    return table + jnp.where(last, far[None, :], 0.0)


def expert_kernel(rows_ref, in_ref, out_ref, part_ref, gin_ref, gout_ref):
    tokens = rows_ref[0, :, :D]
    upstream = rows_ref[0, :, D:]
    up_map, down_map = in_ref[0], out_ref[0]
    u = dot_plain(tokens, up_map)
    square = u * u
    slope = math.sqrt(2.0 / math.pi)
    bend = jnp.tanh(slope * (u + 0.044715 * (square * u)))
    half = 0.5 * (1.0 + bend)
    act = (u * half).astype(tokens.dtype)
    rise = half + 0.5 * u * (1.0 - bend * bend) * (slope * (1.0 + 3 * 0.044715 * square))
    du = (dot_plain(upstream, down_map) * rise).astype(tokens.dtype)
    part_ref[0, :, :D] = dot_last(act, down_map).astype(part_ref.dtype)
    part_ref[0, :, D:] = dot_last(du, up_map).astype(part_ref.dtype)
    gin, gout = dot_first(tokens, du), dot_first(upstream, act)

    @pl.when(pl.program_id(1) == 0)
    def _():
        gin_ref[0] = gin
        gout_ref[0] = gout

    @pl.when(pl.program_id(1) > 0)
    def _():
        gin_ref[0] += gin
        gout_ref[0] += gout


def run_experts(gathered, expert_in, expert_out):
    n, rows, width = gathered.shape
    count, _, hidden = expert_in.shape
    each = rows // count
    block = pl.BlockSpec((1, each, width), lambda e, s: (s, e, 0))
    weight = pl.BlockSpec((1, D, hidden), lambda e, s: (e, 0, 0))
    grad = jax.ShapeDtypeStruct(expert_in.shape, jnp.float32)
    return pl.pallas_call(
        expert_kernel,
        grid=(count, n),
        out_shape=[jax.ShapeDtypeStruct(gathered.shape, gathered.dtype), grad, grad],
        in_specs=[block, weight, weight],
        out_specs=[block, weight, weight],
        compiler_params=pltpu.CompilerParams(vmem_limit_bytes=48 << 20),
        name="run_experts",
    )(gathered, expert_in, expert_out)


def project(source, matrix):
    return jnp.dot(source, matrix, preferred_element_type=jnp.float32).astype(jnp.bfloat16)


def weight_grad(source, upstream):
    return jnp.einsum("td,te->de", source, upstream, preferred_element_type=jnp.float32).astype(
        jnp.bfloat16
    )


def input_grad(upstream, matrix):
    return jnp.einsum("te,de->td", upstream, matrix, preferred_element_type=jnp.float32)


def body(
    n,
    m,
    hidden_in,
    memory,
    proj_in,
    proj_out,
    norm_gains,
    rel_bias,
    router,
    expert_choice,
    expert_in,
    expert_out,
    cotangent,
):
    tokens = hidden_in[0].astype(jnp.float32)
    memory_rows = memory[0]
    memory_count = memory_rows.shape[0]
    gain_rows = norm_gains.astype(jnp.float32)
    token_count = tokens.shape[0]
    seq_at = lax.axis_index("seq").astype(jnp.int32).reshape(1)
    normed_self = rms_apply(tokens, gain_rows[0]).astype(jnp.bfloat16)
    tiles = bias_tiles(rel_bias)

    normed_all, memory_all = ring_gather([normed_self, memory_rows], n, 1)
    normed_all = normed_all.reshape(n * token_count, D)
    memory_all = memory_all.reshape(n * memory_count, D)
    queries = project(normed_self, proj_in[0])
    key_all = project(normed_all, proj_in[1])
    value_all = project(normed_all, proj_in[2])
    memory_key_all = project(memory_all, proj_in[4])
    memory_value_all = project(memory_all, proj_in[5])
    attended_self_low, attended_self, lse_self = attend(
        seq_at, queries, key_all, value_all, tiles
    )
    after_self = tokens + jnp.dot(
        attended_self_low, proj_out[0], preferred_element_type=jnp.float32
    )

    normed_cross = rms_apply(after_self, gain_rows[1]).astype(jnp.bfloat16)
    cross_queries = project(normed_cross, proj_in[3])
    attended_cross_low, attended_cross, lse_cross = attend(
        seq_at, cross_queries, memory_key_all, memory_value_all, None
    )
    after_cross = after_self + jnp.dot(
        attended_cross_low, proj_out[1], preferred_element_type=jnp.float32
    )

    mixed_low = rms_apply(after_cross, gain_rows[2]).astype(jnp.bfloat16)
    softmax_probs = jax.nn.softmax(
        jnp.dot(mixed_low, router, preferred_element_type=jnp.float32), axis=-1
    )
    expert_count = router.shape[1]
    local_experts = expert_in.shape[0]
    capacity = max(2, 5 * token_count // (4 * expert_count))
    chosen = expert_choice[0, :, 0]
    onehot_int = (chosen[:, None] == jnp.arange(expert_count, dtype=jnp.int32)[None, :]).astype(
        jnp.int32
    )
    onehot = onehot_int.astype(jnp.float32)
    gate_prob = jnp.sum(softmax_probs * onehot, axis=-1)
    slot_index = jnp.sum(jnp.cumsum(onehot_int, axis=0) * onehot_int, axis=-1) - 1
    is_kept = slot_index < capacity
    place = jnp.where(is_kept, chosen * capacity + slot_index, -1)
    dispatch = (
        place[:, None] == jnp.arange(expert_count * capacity, dtype=jnp.int32)[None, :]
    ).astype(jnp.bfloat16)
    dispatched = jnp.sum(onehot_int * is_kept[:, None].astype(jnp.int32), axis=0)
    tally_counts = jnp.stack(
        [dispatched, jnp.sum(onehot_int, axis=0) - dispatched], axis=0
    ).reshape(1, 1, 2, expert_count)

    grad_top = cotangent[0].astype(jnp.float32)
    scaled = (gate_prob[:, None] * grad_top).astype(jnp.bfloat16)
    sent_rows = (
        jnp.einsum(
            "tx,td->xd",
            dispatch,
            jnp.concatenate([mixed_low, scaled], axis=1),
            preferred_element_type=jnp.float32,
        )
        .astype(jnp.bfloat16)
        .reshape(expert_count, capacity, 2 * D)
    )
    received = lax.all_to_all(sent_rows, "exp", split_axis=0, concat_axis=1, tiled=True)
    (gathered,) = ring_gather([received.reshape(local_experts * m * capacity, 2 * D)], n, 2)
    parts, grad_expert_in, grad_expert_out = run_experts(gathered, expert_in, expert_out)
    (summed,) = ring_scatter([parts], n, 3, jnp.bfloat16)
    returned = lax.all_to_all(
        summed.reshape(local_experts, m * capacity, 2 * D),
        "exp",
        split_axis=1,
        concat_axis=0,
        tiled=True,
    ).reshape(expert_count * capacity, 2 * D)
    routed = jnp.dot(dispatch, returned, preferred_element_type=jnp.float32)
    combined, grad_mixed = routed[:, :D], routed[:, D:]
    output = (after_cross + gate_prob[:, None] * combined).astype(jnp.bfloat16)

    grad_gate = jnp.sum(grad_top * combined, axis=-1)
    grad_logits = softmax_probs * (onehot - gate_prob[:, None]) * grad_gate[:, None]
    grad_router = jnp.einsum(
        "td,te->de", mixed_low.astype(jnp.float32), grad_logits, precision=highest
    )
    grad_mixed = grad_mixed + jnp.einsum(
        "te,de->td", grad_logits, router.astype(jnp.float32), precision=highest
    )
    grad_cross_part, grad_gain_mix = rms_backward(after_cross, gain_rows[2], grad_mixed)
    grad_after_cross = grad_top + grad_cross_part

    grad_cross_low = grad_after_cross.astype(jnp.bfloat16)
    grad_out_cross = weight_grad(attended_cross_low, grad_cross_low)
    grad_attended_cross = input_grad(grad_cross_low, proj_out[1]).astype(jnp.bfloat16)
    grad_cross_query, grad_memory_keys, grad_memory_values = attend_back(
        seq_at,
        cross_queries,
        memory_key_all,
        memory_value_all,
        grad_attended_cross,
        attended_cross,
        lse_cross,
        None,
    )
    grad_query_cross = weight_grad(normed_cross, grad_cross_query)
    grad_self_part, grad_gain_cross = rms_backward(
        after_self, gain_rows[1], input_grad(grad_cross_query, proj_in[3])
    )
    grad_after_self = grad_after_cross + grad_self_part
    grad_memory_part = (
        input_grad(grad_memory_keys, proj_in[4]) + input_grad(grad_memory_values, proj_in[5])
    ).astype(jnp.bfloat16)

    grad_self_low = grad_after_self.astype(jnp.bfloat16)
    grad_out_self = weight_grad(attended_self_low, grad_self_low)
    grad_attended_self = input_grad(grad_self_low, proj_out[0]).astype(jnp.bfloat16)
    grad_self_query, grad_keys, grad_values, near, sums = attend_back(
        seq_at,
        queries,
        key_all,
        value_all,
        grad_attended_self,
        attended_self,
        lse_self,
        tiles,
    )
    grad_table = bias_gradient(near, sums)
    grad_normed_part = (
        input_grad(grad_keys, proj_in[1]) + input_grad(grad_values, proj_in[2])
    ).astype(jnp.bfloat16)
    grad_normed_own, grad_memory = ring_scatter(
        [
            grad_normed_part.reshape(n, token_count, D),
            grad_memory_part.reshape(n, memory_count, D),
        ],
        n,
        4,
        jnp.float32,
    )
    grad_normed_self = input_grad(grad_self_query, proj_in[0]) + grad_normed_own
    grad_token_part, grad_gain_self = rms_backward(tokens, gain_rows[0], grad_normed_self)
    grad_in = (grad_after_self + grad_token_part).astype(jnp.bfloat16)

    grads = jnp.stack(
        [
            weight_grad(normed_self, grad_self_query),
            weight_grad(normed_all, grad_keys),
            weight_grad(normed_all, grad_values),
            grad_query_cross,
            weight_grad(memory_all, grad_memory_keys),
            weight_grad(memory_all, grad_memory_values),
            grad_out_self,
            grad_out_cross,
        ]
    )
    grads = total_everywhere(grads.reshape(-1, D), n, m, 5).reshape(-1, D, D).astype(jnp.float32)
    grad_gains = jnp.stack([grad_gain_self, grad_gain_cross, grad_gain_mix])
    small = lax.psum(
        jnp.concatenate([grad_gains.reshape(-1), grad_table.reshape(-1), grad_router.reshape(-1)]),
        ("seq", "exp"),
    )
    ends = (grad_gains.size, grad_gains.size + grad_table.size)
    return (
        output.reshape(1, token_count, D),
        grad_in.reshape(1, token_count, D),
        grad_memory.astype(jnp.bfloat16).reshape(1, memory_count, D),
        grads[:6],
        grads[6:],
        small[: ends[0]].reshape(grad_gains.shape),
        small[ends[0] : ends[1]].reshape(grad_table.shape),
        small[ends[1] :].reshape(grad_router.shape),
        grad_expert_in,
        grad_expert_out,
        tally_counts,
    )


def solution(mesh):
    rows = P("exp", "seq", None)
    hidden = P("exp", None, "seq")
    return jax.shard_map(
        functools.partial(body, mesh.shape["seq"], mesh.shape["exp"]),
        mesh=mesh,
        in_specs=(rows, rows, P(), P(), P(), P(), P(), rows, hidden, hidden, rows),
        out_specs=(
            rows,
            rows,
            rows,
            P(),
            P(),
            P(),
            P(),
            P(),
            hidden,
            hidden,
            P("exp", "seq", None, None),
        ),
        check_vma=False,
    )
```

```python
import functools
import math

import jax
import jax.numpy as jnp
from jax import lax
from jax.experimental import pallas as pl
from jax.experimental.pallas import tpu as pltpu
from jax.sharding import PartitionSpec as P

D = 768
HEADS = 12
HEAD_DIM = 64
NBUCKET = 32
MAXDIST = 128
TILE = 128
PAIRS = HEADS * HEAD_DIM // TILE

MESH = pl.DeviceIdType.MESH
ANY = pl.BlockSpec(memory_space=pl.ANY)
SMEM = pl.BlockSpec(memory_space=pltpu.SMEM)

norm_eps = 1e-06
masked_score = -1e30
highest = lax.Precision.HIGHEST
log2e = 1.0 / math.log(2.0)
scale_factor = HEAD_DIM ** (-0.5)


def bucket_edges():
    half_count = NBUCKET // 2
    thresholds = []
    for bucket_number in range(1, NBUCKET):
        if bucket_number < half_count:
            thresholds.append(bucket_number)
        else:
            thresholds.append(
                int(
                    half_count
                    * (MAXDIST / half_count) ** ((bucket_number - half_count) / half_count)
                )
            )
    return thresholds


def rms_apply(values, gain_row):
    return (
        values * lax.rsqrt(jnp.mean(values * values, axis=-1, keepdims=True) + norm_eps) * gain_row
    )


def rms_backward(values, gain_row, upstream):
    _, pullback = jax.vjp(rms_apply, values, gain_row)
    return pullback(upstream)


def seq_cycle(n):
    cols = n // 4
    if n % 4 or cols < 2:
        return list(range(n))
    order = [0]
    for row in range(4):
        span = range(1, cols) if row % 2 == 0 else range(cols - 1, 0, -1)
        order += [row * cols + col for col in span]
    return order + [3 * cols, 2 * cols, cols]


def chip_cycle(n, chips):
    order = seq_cycle(n)
    if chips == 1:
        return [(place, 0) for place in order]
    cycle = [(order[0], 0)]
    for row in range(n):
        span = range(1, chips) if row % 2 == 0 else range(chips - 1, 0, -1)
        cycle += [(order[row], chip) for chip in span]
    return cycle + [(order[row], 0) for row in range(n - 1, 0, -1)]


def look_up(index, table):
    value = jnp.int32(table[0])
    for number, entry in enumerate(table[1:], 1):
        value = jnp.where(index == number, jnp.int32(entry), value)
    return value


def greet(others):
    barrier = pltpu.get_barrier_semaphore()
    for other in others:
        pl.semaphore_signal(barrier, inc=1, device_id=other, device_id_type=MESH)
    pl.semaphore_wait(barrier, len(others))


def seq_ring(n):
    order = seq_cycle(n)
    pos = look_up(lax.axis_index("seq"), [order.index(i) for i in range(n)])

    def at(place):
        return look_up(lax.rem(place + 4 * n, n), order)

    return pos, at, ({"seq": at(pos + 1)}, {"seq": at(pos - 1)})


def gather_kernel(n, parts, count, *refs):
    sources, outs = refs[:count], refs[count : 2 * count]
    own_sem, send_sem, recv_sem = refs[2 * count :]
    pos, at, sides = seq_ring(n)
    me = at(pos)
    greet(sides)
    own = [
        pltpu.make_async_copy(sources[a], outs[a].at[me], own_sem.at[a]) for a in range(count)
    ]
    for copy in own:
        copy.start()
    started, latest = [], {}
    for step in range(n - 1):
        for a in range(count):
            rows = sources[a].shape[0] // 2 // parts
            for part in range(parts):
                for way in range(2):
                    if step:
                        latest[a, way, part].wait_recv()
                    block = at(pos - step) if way == 0 else at(pos + step)
                    span = pl.ds((way * parts + part) * rows, rows)
                    copy = pltpu.make_async_remote_copy(
                        src_ref=outs[a].at[block, span] if step else sources[a].at[span],
                        dst_ref=outs[a].at[block, span],
                        send_sem=send_sem.at[a, way, step, part],
                        recv_sem=recv_sem.at[a, way, step, part],
                        device_id=sides[way],
                        device_id_type=MESH,
                    )
                    copy.start()
                    started.append(copy)
                    latest[a, way, part] = copy
    for copy in latest.values():
        copy.wait_recv()
    for copy in started:
        copy.wait_send()
    for copy in own:
        copy.wait()


def ring_gather(arrays, n, number, parts=2):
    count = len(arrays)
    copies = (count, 2, n - 1, parts)
    return pl.pallas_call(
        functools.partial(gather_kernel, n, parts, count),
        out_shape=[jax.ShapeDtypeStruct((n,) + a.shape, a.dtype) for a in arrays],
        in_specs=[ANY] * count,
        out_specs=[ANY] * count,
        scratch_shapes=[
            pltpu.SemaphoreType.DMA((count,)),
            pltpu.SemaphoreType.DMA(copies),
            pltpu.SemaphoreType.DMA(copies),
        ],
        compiler_params=pltpu.CompilerParams(collective_id=number, has_side_effects=True),
        name="ring_gather",
    )(*arrays)


def scatter_kernel(n, parts, count, *refs):
    sources, outs = refs[:count], refs[count : 2 * count]
    own_bufs, got_bufs = refs[2 * count : 3 * count], refs[3 * count : 4 * count]
    own_sem, send_sem, recv_sem = refs[4 * count :]
    pos, at, sides = seq_ring(n)
    greet(sides)
    lanes = [(a, part, way) for a in range(count) for part in range(parts) for way in range(2)]

    def span(a, part, way):
        rows = sources[a].shape[1] // 2 // parts
        return pl.ds((way * parts + part) * rows, rows)

    def block(way, step):
        return at(pos - 1 - step) if way == 0 else at(pos + 1 + step)

    def send(lane, step, source):
        a, part, way = lane
        copy = pltpu.make_async_remote_copy(
            src_ref=source,
            dst_ref=got_bufs[a].at[way, step, part],
            send_sem=send_sem.at[a, way, step, part],
            recv_sem=recv_sem.at[a, way, step, part],
            device_id=sides[way],
            device_id_type=MESH,
        )
        copy.start()
        return copy

    latest, started, own = {}, [], {}
    for lane in lanes:
        a, part, way = lane
        latest[lane] = send(lane, 0, sources[a].at[block(way, 0), span(a, part, way)])
        started.append(latest[lane])
    for step in range(1, n):
        for lane in lanes:
            a, part, way = lane
            own[lane, step] = pltpu.make_async_copy(
                sources[a].at[block(way, step), span(a, part, way)],
                own_bufs[a].at[way, step - 1, part],
                own_sem.at[a, way, step - 1, part],
            )
            own[lane, step].start()
    for step in range(1, n):
        for lane in lanes:
            a, part, way = lane
            own[lane, step].wait()
            latest[lane].wait_recv()
            total = got_bufs[a][way, step - 1, part].astype(jnp.float32) + own_bufs[a][
                way, step - 1, part
            ].astype(jnp.float32)
            if step == n - 1:
                outs[a][span(a, part, way)] = total.astype(outs[a].dtype)
            else:
                got_bufs[a][way, step - 1, part] = total.astype(got_bufs[a].dtype)
                latest[lane] = send(lane, step, got_bufs[a].at[way, step - 1, part])
                started.append(latest[lane])
    for copy in started:
        copy.wait_send()


def ring_scatter(arrays, n, number, out_dtype, parts=2):
    count = len(arrays)
    copies = (count, 2, n - 1, parts)
    bufs = [
        pltpu.VMEM((2, n - 1, parts, a.shape[1] // 2 // parts, a.shape[2]), a.dtype)
        for a in arrays
    ]
    return pl.pallas_call(
        functools.partial(scatter_kernel, n, parts, count),
        out_shape=[jax.ShapeDtypeStruct(a.shape[1:], out_dtype) for a in arrays],
        in_specs=[ANY] * count,
        out_specs=[pl.BlockSpec(memory_space=pltpu.VMEM)] * count,
        scratch_shapes=bufs + bufs + [pltpu.SemaphoreType.DMA(copies)] * 3,
        compiler_params=pltpu.CompilerParams(
            collective_id=number, has_side_effects=True, vmem_limit_bytes=58 << 20
        ),
        name="ring_scatter",
    )(*arrays)


def total_kernel(n, chips, parts, *refs):
    count = len(parts)
    xs, outs = refs[:count], refs[count : 2 * count]
    mines, twins, gots = (refs[(2 + i) * count : (3 + i) * count] for i in range(3))
    own_sem, twin_sem, ring_sem, back_sem = refs[5 * count :]
    cycle = chip_cycle(n, chips)
    length = len(cycle)
    seq, exp = lax.axis_index("seq"), lax.axis_index("exp")
    core = lax.rem(exp, 2)
    places = [cycle.index((i // chips, i % chips)) for i in range(length)]
    pos = look_up(seq * chips + exp // 2, places)

    def device(place):
        place = lax.rem(place + length, length)
        return {
            "seq": look_up(place, [c[0] for c in cycle]),
            "exp": look_up(place, [c[1] for c in cycle]) * 2 + core,
        }

    def block(way, step):
        place = pos - 1 - step if way == 0 else pos + 1 + step
        return lax.rem(place + 2 * length, length)

    peer = {"exp": exp + 1 - 2 * core}
    sides = (device(pos + 1), device(pos - 1))
    greet((peer,) + sides)
    lanes = [(a, part, way) for a in range(count) for part in range(parts[a]) for way in range(2)]
    started = []

    def push(source, target, sems, index, to):
        copy = pltpu.make_async_remote_copy(
            src_ref=source,
            dst_ref=target,
            send_sem=sems.at[(0,) + index],
            recv_sem=sems.at[(1,) + index],
            device_id=to,
            device_id_type=MESH,
        )
        copy.start()
        started.append(copy)
        return copy

    def spans(lane):
        a, part, way = lane
        half = xs[a].shape[2] // 2
        rows = half // parts[a]
        return pl.ds(part * rows, rows), pl.ds(way * half + part * rows, rows)

    pairs, own, latest = {}, {}, {}
    for step in range(length):
        for lane in lanes:
            a, part, way = lane
            near, wide = spans(lane)
            where = block(way, step)
            pairs[lane, step] = push(
                xs[a].at[1 - core, where, wide],
                twins[a].at[way, step, near],
                twin_sem,
                lane + (step,),
                peer,
            )
            own[lane, step] = pltpu.make_async_copy(
                xs[a].at[core, where, wide], mines[a].at[way, step, near], own_sem.at[lane + (step,)]
            )
            own[lane, step].start()
    for step in range(length):
        for lane in lanes:
            a, part, way = lane
            near, wide = spans(lane)
            own[lane, step].wait()
            pairs[lane, step].wait_recv()
            total = mines[a][way, step, near].astype(jnp.float32) + twins[a][
                way, step, near
            ].astype(jnp.float32)
            if step:
                latest[lane].wait_recv()
                total = total + gots[a][way, step - 1, near].astype(jnp.float32)
            mines[a][way, step, near] = total.astype(mines[a].dtype)
            if step < length - 1:
                latest[lane] = push(
                    mines[a].at[way, step, near],
                    gots[a].at[way, step, near],
                    ring_sem,
                    (0,) + lane + (step,),
                    sides[way],
                )
    keep = []
    for step in range(length):
        for lane in lanes:
            a, part, way = lane
            near, wide = spans(lane)
            if step:
                latest[lane].wait_recv()
            where = lax.rem(pos - step + length if way == 0 else pos + step, length)
            target = outs[a].at[core, where, wide]
            source = target if step else mines[a].at[way, length - 1, near]
            if step < length - 1:
                latest[lane] = push(source, target, ring_sem, (1,) + lane + (step,), sides[way])
            pairs[lane, step] = push(source, target, back_sem, lane + (step,), peer)
            if step == 0:
                copy = pltpu.make_async_copy(source, target, own_sem.at[lane + (0,)])
                copy.start()
                keep.append(copy)
    for copy in keep:
        copy.wait()
    for copy in pairs.values():
        copy.wait_recv()
    for copy in started:
        copy.wait_send()


def total_everywhere(rows_in, small, n, m, number):
    chips = m // 2
    length = n * chips
    rows, cols = rows_in.shape
    lanes_of = TILE * 8
    parts = (3, 1)
    if m % 2 or rows % (4 * length * parts[0] * 16) or small.size > 4 * length * lanes_of:
        return lax.psum((rows_in, small), ("seq", "exp"))
    padded = jnp.pad(small, (0, 4 * length * lanes_of - small.size))
    arrays = [
        rows_in.reshape(2, length, rows // (2 * length), cols),
        padded.reshape(2, length, 16, TILE),
    ]
    bufs = [pltpu.VMEM((2, length, x.shape[2] // 2, x.shape[3]), x.dtype) for x in arrays]
    sems = (len(arrays), max(parts), 2, length)
    big, little = pl.pallas_call(
        functools.partial(total_kernel, n, chips, parts),
        out_shape=[jax.ShapeDtypeStruct(x.shape, x.dtype) for x in arrays],
        in_specs=[ANY] * 2,
        out_specs=[ANY] * 2,
        scratch_shapes=bufs * 3
        + [
            pltpu.SemaphoreType.DMA(sems),
            pltpu.SemaphoreType.DMA((2,) + sems),
            pltpu.SemaphoreType.DMA((2, 2) + sems),
            pltpu.SemaphoreType.DMA((2,) + sems),
        ],
        compiler_params=pltpu.CompilerParams(
            collective_id=number, has_side_effects=True, vmem_limit_bytes=58 << 20
        ),
        name="total_everywhere",
    )(*arrays)
    return big.reshape(rows, cols), little.reshape(-1)[: small.size]


QUAD = 4


def quad_moves(n):
    ring = (0, 1, 3, 2)
    step = lambda i, by: i - i % QUAD + ring[(ring.index(i % QUAD) + by) % QUAD]
    return [(i, step(i, 1)) for i in range(n)], [(i, step(i, -1)) for i in range(n)]


def spread_kernel(n, m, back, x_ref, out_ref, own_sem, send_sem, recv_sem):
    seq, exp = lax.axis_index("seq"), lax.axis_index("exp")
    groups = n // QUAD
    moves = [(g, k) for g in reversed(range(groups)) for k in range(m) if g or k]

    def target(g, k):
        shift = n - g * QUAD if back else g * QUAD
        return lax.rem(seq + shift, n), lax.rem(exp + k, m)

    greet([dict(zip(("seq", "exp"), target(g, k))) for g, k in moves])
    started = []
    for g, k in moves:
        to_seq, to_exp = target(g, k)
        copy = pltpu.make_async_remote_copy(
            src_ref=x_ref.at[g, to_exp] if back else x_ref.at[to_exp],
            dst_ref=out_ref.at[g, exp],
            send_sem=send_sem.at[g, k],
            recv_sem=recv_sem.at[g, k],
            device_id={"seq": to_seq, "exp": to_exp},
            device_id_type=MESH,
        )
        copy.start()
        started.append(copy)
    own = pltpu.make_async_copy(
        x_ref.at[0, exp] if back else x_ref.at[exp], out_ref.at[0, exp], own_sem
    )
    own.start()
    for copy in started:
        copy.wait_recv()
    for copy in started:
        copy.wait_send()
    own.wait()


def spread(x, n, m, back, number):
    groups = n // QUAD
    return pl.pallas_call(
        functools.partial(spread_kernel, n, m, back),
        out_shape=jax.ShapeDtypeStruct((groups,) + x.shape[-3:], x.dtype),
        in_specs=[ANY],
        out_specs=ANY,
        scratch_shapes=[
            pltpu.SemaphoreType.DMA,
            pltpu.SemaphoreType.DMA((groups, m)),
            pltpu.SemaphoreType.DMA((groups, m)),
        ],
        compiler_params=pltpu.CompilerParams(collective_id=number, has_side_effects=True),
        name="spread_back" if back else "spread",
    )(x)


def dot_last(a, b):
    return lax.dot_general(a, b, (((1,), (1,)), ((), ())), preferred_element_type=jnp.float32)


def dot_first(a, b):
    return lax.dot_general(a, b, (((0,), (0,)), ((), ())), preferred_element_type=jnp.float32)


def dot_plain(a, b):
    return jnp.dot(a, b, preferred_element_type=jnp.float32)


def head_masks(dtype):
    low = lax.broadcasted_iota(jnp.int32, (1, TILE), 1) < HEAD_DIM
    first = jnp.where(low, 1.0, 0.0).astype(jnp.float32)
    return first.astype(dtype), (1.0 - first).astype(dtype)


def split_heads(pair):
    return jnp.concatenate([pair * mask for mask in head_masks(pair.dtype)], axis=0)


def own_bias(tiles, count):
    rows = []
    for r in range(count):
        row = []
        for c in range(count):
            if c == r:
                row.append(tiles[:, TILE:])
            elif c == r - 1:
                row.append(tiles[:, :TILE])
            else:
                row.append(jnp.full((TILE, TILE), 0.0 if c < r else masked_score, jnp.float32))
        rows.append(jnp.concatenate(row, axis=1))
    return jnp.concatenate(rows, axis=0)


def edge_bias(tile_ref, rows):
    edge = []
    for h in range(2):
        first = jnp.concatenate(
            [jnp.zeros((rows - TILE, TILE), jnp.float32), tile_ref[h][:, :TILE].T], axis=0
        )
        edge += [first, jnp.zeros((rows, rows - TILE), jnp.float32)]
    return jnp.concatenate(edge, axis=1)


def attend_kernel(causal, block, s_ref, q_ref, k_ref, v_ref, *refs):
    if causal:
        tile_ref, low_ref, wide_ref, lse_ref, acc_ref, top_ref = refs
    else:
        low_ref, wide_ref, lse_ref, acc_ref, top_ref = refs
    rows = q_ref.shape[0]
    both = split_heads(q_ref[...])
    ones = jnp.ones((16, block), v_ref.dtype)

    def visit(start, bias, first):
        keys = k_ref[pl.ds(start, block), :]
        values = v_ref[pl.ds(start, block), :]
        t = dot_last(keys, both) * (scale_factor * log2e)
        if bias is not None:
            t = t + bias
        top = jnp.max(t, axis=0, keepdims=True)
        if not first:
            before = top_ref[...]
            top = jnp.maximum(before, top)
            fade = jnp.exp2(before - top)
        top_ref[...] = top
        p = jnp.exp2(t - top).astype(values.dtype)
        part = dot_plain(jnp.concatenate([values.T, ones], axis=0), p)
        if first:
            acc_ref[...] = part
        else:
            acc_ref[...] = acc_ref[...] * fade + part

    if causal:
        s = s_ref[0]
        count = rows // TILE
        visit(
            pl.multiple_of(s * block, block),
            jnp.concatenate([own_bias(tile_ref[h], count).T for h in range(2)], axis=1),
            True,
        )

        @pl.when(s > 0)
        def _():
            visit(pl.multiple_of((s - 1) * block, block), edge_bias(tile_ref, rows), False)

        def far(j, carry):
            visit(pl.multiple_of(j * block, block), None, False)
            return carry

        lax.fori_loop(0, s - 1, far, 0)
    else:
        for j in range(k_ref.shape[0] // block):
            visit(j * block, None, j == 0)
    sums = acc_ref[TILE : TILE + 1, :]
    wide = jnp.concatenate(
        [
            acc_ref[:HEAD_DIM, :rows] / sums[:, :rows],
            acc_ref[HEAD_DIM:TILE, rows:] / sums[:, rows:],
        ],
        axis=0,
    ).T
    wide_ref[...] = wide
    low_ref[...] = wide.astype(low_ref.dtype)
    lse = top_ref[...] + jnp.log2(sums)
    lse_ref[0] = jnp.concatenate([lse[:, :rows], lse[:, rows:]], axis=0)


def attend(seq_at, queries, keys, values, tiles):
    rows, total = queries.shape[0], keys.shape[0]
    causal = tiles is not None
    block = rows if causal else math.gcd(total, 512)
    pair = pl.BlockSpec((rows, TILE), lambda g: (0, g))
    long = pl.BlockSpec((total, TILE), lambda g: (0, g))
    extra, specs = [], []
    if causal:
        extra, specs = [tiles], [pl.BlockSpec((2,) + tiles.shape[1:], lambda g: (g, 0, 0))]
    return pl.pallas_call(
        functools.partial(attend_kernel, causal, block),
        grid=(PAIRS,),
        out_shape=[
            jax.ShapeDtypeStruct((rows, D), jnp.bfloat16),
            jax.ShapeDtypeStruct((rows, D), jnp.float32),
            jax.ShapeDtypeStruct((PAIRS, 2, rows), jnp.float32),
        ],
        in_specs=[SMEM, pair, long, long] + specs,
        out_specs=[pair, pair, pl.BlockSpec((1, 2, rows), lambda g: (g, 0, 0))],
        scratch_shapes=[
            pltpu.VMEM((TILE + 16, 2 * rows), jnp.float32),
            pltpu.VMEM((1, 2 * rows), jnp.float32),
        ],
        compiler_params=pltpu.CompilerParams(vmem_limit_bytes=48 << 20),
        name="attend_self" if causal else "attend_cross",
    )(seq_at, queries, keys, values, *extra)


def attend_back_kernel(causal, block, s_ref, q_ref, k_ref, v_ref, up_ref, wide_ref, lse_ref, *refs):
    if causal:
        tile_ref, dq_ref, dk_ref, dv_ref, near_ref, sum_ref, acc_ref = refs
    else:
        dq_ref, dk_ref, dv_ref, acc_ref = refs
    rows = q_ref.shape[0]
    both = split_heads(q_ref[...])
    up = up_ref[...]
    up_both = split_heads(up)
    turned = (up.astype(jnp.float32) * wide_ref[...]).T
    delta = jnp.concatenate(
        [
            jnp.sum(turned[:HEAD_DIM], axis=0, keepdims=True),
            jnp.sum(turned[HEAD_DIM:], axis=0, keepdims=True),
        ],
        axis=1,
    )
    lse = jnp.concatenate([lse_ref[0, :1], lse_ref[0, 1:]], axis=1)
    ones = jnp.ones((16, block), k_ref.dtype)

    def visit(start, bias, first):
        keys = k_ref[pl.ds(start, block), :]
        values = v_ref[pl.ds(start, block), :]
        t = dot_last(keys, both) * (scale_factor * log2e)
        if bias is not None:
            t = t + bias
        p = jnp.exp2(t - lse)
        ds = (p * (dot_last(values, up_both) - delta)).astype(keys.dtype)
        dv_ref[pl.ds(start, block), :] = dot_plain(p.astype(keys.dtype), up_both).astype(
            dv_ref.dtype
        )
        dk_ref[pl.ds(start, block), :] = (dot_plain(ds, both) * scale_factor).astype(dk_ref.dtype)
        part = dot_plain(jnp.concatenate([keys.T, ones], axis=0), ds)
        if first:
            acc_ref[...] = part
        else:
            acc_ref[...] += part
        return ds

    if causal:
        s = s_ref[0]
        count = rows // TILE
        ds = visit(
            pl.multiple_of(s * block, block),
            jnp.concatenate([own_bias(tile_ref[h], count).T for h in range(2)], axis=1),
            True,
        )
        for h in range(2):
            same = before = jnp.zeros((TILE, TILE), jnp.float32)
            for r in range(count):
                columns = slice(h * rows + r * TILE, h * rows + (r + 1) * TILE)
                same = same + ds[r * TILE : (r + 1) * TILE, columns].astype(jnp.float32)
                if r:
                    before = before + ds[(r - 1) * TILE : r * TILE, columns].astype(jnp.float32)
            near_ref[h, :TILE] = before
            near_ref[h, TILE:] = same

        @pl.when(s > 0)
        def _():
            ds = visit(pl.multiple_of((s - 1) * block, block), edge_bias(tile_ref, rows), False)
            for h in range(2):
                near_ref[h, :TILE] += ds[rows - TILE :, h * rows : h * rows + TILE].astype(
                    jnp.float32
                )

        def far(j, carry):
            visit(pl.multiple_of(j * block, block), None, False)
            return carry

        lax.fori_loop(0, s - 1, far, 0)

        def beyond(j, carry):
            start = pl.multiple_of(j * block, block)
            dk_ref[pl.ds(start, block), :] = jnp.zeros((block, TILE), dk_ref.dtype)
            dv_ref[pl.ds(start, block), :] = jnp.zeros((block, TILE), dv_ref.dtype)
            return carry

        lax.fori_loop(s + 1, k_ref.shape[0] // block, beyond, 0)
        sum_ref[0] = jnp.concatenate(
            [acc_ref[TILE : TILE + 1, :rows], acc_ref[TILE : TILE + 1, rows:]], axis=0
        )
    else:
        for j in range(k_ref.shape[0] // block):
            visit(j * block, None, j == 0)
    dq = jnp.concatenate([acc_ref[:HEAD_DIM, :rows], acc_ref[HEAD_DIM:TILE, rows:]], axis=0)
    dq_ref[...] = (dq.T * scale_factor).astype(dq_ref.dtype)


def attend_back(seq_at, queries, keys, values, upstream, wide, lse, tiles):
    rows, total = queries.shape[0], keys.shape[0]
    causal = tiles is not None
    block = rows if causal else math.gcd(total, 512)
    pair = pl.BlockSpec((rows, TILE), lambda g: (0, g))
    long = pl.BlockSpec((total, TILE), lambda g: (0, g))
    line = pl.BlockSpec((1, 2, rows), lambda g: (g, 0, 0))
    extra, specs, shapes, out_specs = [], [], [], []
    if causal:
        extra, specs = [tiles], [pl.BlockSpec((2,) + tiles.shape[1:], lambda g: (g, 0, 0))]
        shapes = [
            jax.ShapeDtypeStruct((HEADS, 2 * TILE, TILE), jnp.float32),
            jax.ShapeDtypeStruct((PAIRS, 2, rows), jnp.float32),
        ]
        out_specs = [pl.BlockSpec((2, 2 * TILE, TILE), lambda g: (g, 0, 0)), line]
    return pl.pallas_call(
        functools.partial(attend_back_kernel, causal, block),
        grid=(PAIRS,),
        out_shape=[
            jax.ShapeDtypeStruct((rows, D), jnp.bfloat16),
            jax.ShapeDtypeStruct((total, D), jnp.bfloat16),
            jax.ShapeDtypeStruct((total, D), jnp.bfloat16),
        ]
        + shapes,
        in_specs=[SMEM, pair, long, long, pair, pair, line] + specs,
        out_specs=[pair, long, long] + out_specs,
        scratch_shapes=[pltpu.VMEM((TILE + 16, 2 * rows), jnp.float32)],
        compiler_params=pltpu.CompilerParams(vmem_limit_bytes=48 << 20),
        name="attend_self_back" if causal else "attend_cross_back",
    )(seq_at, queries, keys, values, upstream, wide, lse, *extra)


def bias_tiles(bias_table):
    distance = (
        TILE
        + jnp.arange(TILE, dtype=jnp.int32)[:, None]
        - jnp.arange(2 * TILE, dtype=jnp.int32)[None, :]
    )
    table = (bias_table - bias_table[NBUCKET - 1 :]) * log2e
    terms = jnp.broadcast_to(table[0][:, None, None], (HEADS, TILE, 2 * TILE))
    for number, threshold in enumerate(bucket_edges()):
        terms = jnp.where((distance >= threshold)[None], table[number + 1][:, None, None], terms)
    return jnp.where((distance >= 0)[None], terms, masked_score)


def bias_gradient(near, sums):
    distance = (
        TILE
        + jnp.arange(TILE, dtype=jnp.int32)[None, :]
        - jnp.arange(2 * TILE, dtype=jnp.int32)[:, None]
    )
    bucket = jnp.zeros(distance.shape, jnp.int32)
    for threshold in bucket_edges():
        bucket = bucket + (distance >= threshold).astype(jnp.int32)
    onehot = (
        bucket.reshape(-1)[None, :] == jnp.arange(NBUCKET, dtype=jnp.int32)[:, None]
    ).astype(jnp.float32)
    flat = near.reshape(HEADS, -1)
    table = lax.dot_general(
        onehot, flat, (((1,), (1,)), ((), ())), precision=highest
    )
    far = jnp.sum(sums, axis=-1).reshape(HEADS) - jnp.sum(flat, axis=-1)
    last = jnp.arange(NBUCKET, dtype=jnp.int32)[:, None] == NBUCKET - 1
    return table + jnp.where(last, far[None, :], 0.0)


def expert_kernel(*refs):
    rows_ref, maps = refs[0], refs[1 : 1 + 2 * QUAD]
    part_ref, grads = refs[1 + 2 * QUAD], refs[2 + 2 * QUAD :]
    shape = rows_ref.shape
    rows = rows_ref[...].reshape(shape[0] * shape[1] * shape[2], shape[3])
    tokens, upstream = rows[:, :D], rows[:, D:]
    slope = math.sqrt(2.0 / math.pi)
    result = back = None
    for j in range(QUAD):
        up_map, down_map = maps[2 * j][0], maps[2 * j + 1][0]
        u = dot_plain(tokens, up_map)
        square = u * u
        bend = jnp.tanh(slope * (u + 0.044715 * (square * u)))
        half = 0.5 * (1.0 + bend)
        act = (u * half).astype(tokens.dtype)
        rise = half + 0.5 * u * (1.0 - bend * bend) * (slope * (1.0 + 3 * 0.044715 * square))
        du = (dot_plain(upstream, down_map) * rise).astype(tokens.dtype)
        y, dn = dot_last(act, down_map), dot_last(du, up_map)
        result = y if result is None else result + y
        back = dn if back is None else back + dn
        for ref, left, right in ((grads[2 * j], tokens, du), (grads[2 * j + 1], upstream, act)):
            ref[0] = dot_first(left, right).astype(ref.dtype)
    part_ref[...] = (
        jnp.concatenate([result, back], axis=1).astype(part_ref.dtype).reshape(part_ref.shape)
    )


def run_experts(rows, maps):
    groups, m, slots, width = rows.shape
    count, _, hidden = maps[0].shape
    block = pl.BlockSpec((groups, m, slots // count, width), lambda e: (0, 0, e, 0))
    weight = pl.BlockSpec((1, D, hidden), lambda e: (e, 0, 0))
    return pl.pallas_call(
        expert_kernel,
        grid=(count,),
        out_shape=[jax.ShapeDtypeStruct(rows.shape, rows.dtype)]
        + [
            jax.ShapeDtypeStruct(w.shape, jnp.float32 if i < 2 else jnp.bfloat16)
            for i, w in enumerate(maps)
        ],
        in_specs=[block] + [weight] * len(maps),
        out_specs=[block] + [weight] * len(maps),
        compiler_params=pltpu.CompilerParams(vmem_limit_bytes=58 << 20),
        name="run_experts",
    )(rows, *maps)


def project(source, matrix):
    return jnp.dot(source, matrix, preferred_element_type=jnp.float32).astype(jnp.bfloat16)


def weight_grad(source, upstream):
    return jnp.einsum("td,te->de", source, upstream, preferred_element_type=jnp.float32).astype(
        jnp.bfloat16
    )


def input_grad(upstream, matrix):
    return jnp.einsum("te,de->td", upstream, matrix, preferred_element_type=jnp.float32)


def body(
    n,
    m,
    hidden_in,
    memory,
    proj_in,
    proj_out,
    norm_gains,
    rel_bias,
    router,
    expert_choice,
    expert_in,
    expert_out,
    cotangent,
):
    tokens = hidden_in[0].astype(jnp.float32)
    memory_rows = memory[0]
    memory_count = memory_rows.shape[0]
    gain_rows = norm_gains.astype(jnp.float32)
    token_count = tokens.shape[0]
    seq_at = lax.axis_index("seq").astype(jnp.int32).reshape(1)
    normed_self = rms_apply(tokens, gain_rows[0]).astype(jnp.bfloat16)
    tiles = bias_tiles(rel_bias)

    normed_all, memory_all = ring_gather([normed_self, memory_rows], n, 1)
    to_next, to_last = quad_moves(n)
    in_own, out_own, normed_all = lax.optimization_barrier((expert_in, expert_out, normed_all))
    in_last, out_last = (lax.ppermute(w, "seq", to_next) for w in (in_own, out_own))
    in_next, out_next = (lax.ppermute(w, "seq", to_last) for w in (in_own, out_own))
    in_far = lax.ppermute(in_last, "seq", to_next)
    out_far = lax.ppermute(out_next, "seq", to_last)
    maps = [in_own, out_own, in_last, out_last, in_next, out_next, in_far, out_far]
    normed_all = normed_all.reshape(n * token_count, D)
    memory_all = memory_all.reshape(n * memory_count, D)
    queries = project(normed_self, proj_in[0])
    key_all = project(normed_all, proj_in[1])
    value_all = project(normed_all, proj_in[2])
    memory_key_all = project(memory_all, proj_in[4])
    memory_value_all = project(memory_all, proj_in[5])
    attended_self_low, attended_self, lse_self = attend(
        seq_at, queries, key_all, value_all, tiles
    )
    after_self = tokens + jnp.dot(
        attended_self_low, proj_out[0], preferred_element_type=jnp.float32
    )

    normed_cross = rms_apply(after_self, gain_rows[1]).astype(jnp.bfloat16)
    cross_queries = project(normed_cross, proj_in[3])
    attended_cross_low, attended_cross, lse_cross = attend(
        seq_at, cross_queries, memory_key_all, memory_value_all, None
    )
    after_cross = after_self + jnp.dot(
        attended_cross_low, proj_out[1], preferred_element_type=jnp.float32
    )

    mixed_low = rms_apply(after_cross, gain_rows[2]).astype(jnp.bfloat16)
    softmax_probs = jax.nn.softmax(
        jnp.dot(mixed_low, router, preferred_element_type=jnp.float32), axis=-1
    )
    expert_count = router.shape[1]
    local_experts = expert_in.shape[0]
    capacity = max(2, 5 * token_count // (4 * expert_count))
    chosen = expert_choice[0, :, 0]
    onehot_int = (chosen[:, None] == jnp.arange(expert_count, dtype=jnp.int32)[None, :]).astype(
        jnp.int32
    )
    onehot = onehot_int.astype(jnp.float32)
    gate_prob = jnp.sum(softmax_probs * onehot, axis=-1)
    slot_index = jnp.sum(jnp.cumsum(onehot_int, axis=0) * onehot_int, axis=-1) - 1
    is_kept = slot_index < capacity
    slots = -(-capacity // 16) * 16
    place = jnp.where(is_kept, chosen * slots + slot_index, -1)
    dispatch = (
        place[:, None] == jnp.arange(expert_count * slots, dtype=jnp.int32)[None, :]
    ).astype(jnp.bfloat16)
    dispatched = jnp.sum(onehot_int * is_kept[:, None].astype(jnp.int32), axis=0)
    tally_counts = jnp.stack(
        [dispatched, jnp.sum(onehot_int, axis=0) - dispatched], axis=0
    ).reshape(1, 1, 2, expert_count)

    grad_top = cotangent[0].astype(jnp.float32)
    scaled = (gate_prob[:, None] * grad_top).astype(jnp.bfloat16)
    sent_rows = (
        jnp.einsum(
            "tx,td->xd",
            dispatch,
            jnp.concatenate([mixed_low, scaled], axis=1),
            preferred_element_type=jnp.float32,
        )
        .astype(jnp.bfloat16)
        .reshape(m, local_experts * slots, 2 * D)
    )
    received = spread(sent_rows, n, m, False, 2)
    parts, *terms = run_experts(received, maps)
    returned = spread(parts, n, m, True, 3)
    returned = jnp.sum(returned.astype(jnp.float32), axis=0).astype(jnp.bfloat16)
    returned = returned.reshape(expert_count * slots, 2 * D)
    gin_own, gout_own, gin_last, gout_last, gin_next, gout_next, gin_far, gout_far = terms
    gin_next = gin_next + lax.ppermute(gin_far, "seq", to_next)
    gout_last = gout_last + lax.ppermute(gout_far, "seq", to_last)
    gin_next, gout_next = (lax.ppermute(w, "seq", to_next) for w in (gin_next, gout_next))
    gin_last, gout_last = (lax.ppermute(w, "seq", to_last) for w in (gin_last, gout_last))
    grad_expert_in = gin_own + gin_last.astype(jnp.float32) + gin_next.astype(jnp.float32)
    grad_expert_out = gout_own + gout_last.astype(jnp.float32) + gout_next.astype(jnp.float32)
    routed = jnp.dot(dispatch, returned, preferred_element_type=jnp.float32)
    combined, grad_mixed = routed[:, :D], routed[:, D:]
    output = (after_cross + gate_prob[:, None] * combined).astype(jnp.bfloat16)

    grad_gate = jnp.sum(grad_top * combined, axis=-1)
    grad_logits = softmax_probs * (onehot - gate_prob[:, None]) * grad_gate[:, None]
    grad_router = jnp.einsum(
        "td,te->de", mixed_low.astype(jnp.float32), grad_logits, precision=highest
    )
    grad_mixed = grad_mixed + jnp.einsum(
        "te,de->td", grad_logits, router.astype(jnp.float32), precision=highest
    )
    grad_cross_part, grad_gain_mix = rms_backward(after_cross, gain_rows[2], grad_mixed)
    grad_after_cross = grad_top + grad_cross_part

    grad_cross_low = grad_after_cross.astype(jnp.bfloat16)
    grad_out_cross = weight_grad(attended_cross_low, grad_cross_low)
    grad_attended_cross = input_grad(grad_cross_low, proj_out[1]).astype(jnp.bfloat16)
    grad_cross_query, grad_memory_keys, grad_memory_values = attend_back(
        seq_at,
        cross_queries,
        memory_key_all,
        memory_value_all,
        grad_attended_cross,
        attended_cross,
        lse_cross,
        None,
    )
    grad_query_cross = weight_grad(normed_cross, grad_cross_query)
    grad_self_part, grad_gain_cross = rms_backward(
        after_self, gain_rows[1], input_grad(grad_cross_query, proj_in[3])
    )
    grad_after_self = grad_after_cross + grad_self_part
    grad_memory_part = (
        input_grad(grad_memory_keys, proj_in[4]) + input_grad(grad_memory_values, proj_in[5])
    ).astype(jnp.bfloat16)

    grad_self_low = grad_after_self.astype(jnp.bfloat16)
    grad_out_self = weight_grad(attended_self_low, grad_self_low)
    grad_attended_self = input_grad(grad_self_low, proj_out[0]).astype(jnp.bfloat16)
    grad_self_query, grad_keys, grad_values, near, sums = attend_back(
        seq_at,
        queries,
        key_all,
        value_all,
        grad_attended_self,
        attended_self,
        lse_self,
        tiles,
    )
    grad_table = bias_gradient(near, sums)
    grad_normed_part = (
        input_grad(grad_keys, proj_in[1]) + input_grad(grad_values, proj_in[2])
    ).astype(jnp.bfloat16)
    grad_normed_own, grad_memory = ring_scatter(
        [
            grad_normed_part.reshape(n, token_count, D),
            grad_memory_part.reshape(n, memory_count, D),
        ],
        n,
        4,
        jnp.float32,
    )
    grad_normed_self = input_grad(grad_self_query, proj_in[0]) + grad_normed_own
    grad_token_part, grad_gain_self = rms_backward(tokens, gain_rows[0], grad_normed_self)
    grad_in = (grad_after_self + grad_token_part).astype(jnp.bfloat16)

    grads = jnp.stack(
        [
            weight_grad(normed_self, grad_self_query),
            weight_grad(normed_all, grad_keys),
            weight_grad(normed_all, grad_values),
            grad_query_cross,
            weight_grad(memory_all, grad_memory_keys),
            weight_grad(memory_all, grad_memory_values),
            grad_out_self,
            grad_out_cross,
        ]
    )
    grad_gains = jnp.stack([grad_gain_self, grad_gain_cross, grad_gain_mix])
    grads, small = total_everywhere(
        grads.reshape(-1, D),
        jnp.concatenate([grad_gains.reshape(-1), grad_table.reshape(-1), grad_router.reshape(-1)]),
        n,
        m,
        5,
    )
    grads = grads.reshape(-1, D, D).astype(jnp.float32)
    ends = (grad_gains.size, grad_gains.size + grad_table.size)
    return (
        output.reshape(1, token_count, D),
        grad_in.reshape(1, token_count, D),
        grad_memory.astype(jnp.bfloat16).reshape(1, memory_count, D),
        grads[:6],
        grads[6:],
        small[: ends[0]].reshape(grad_gains.shape),
        small[ends[0] : ends[1]].reshape(grad_table.shape),
        small[ends[1] :].reshape(grad_router.shape),
        grad_expert_in,
        grad_expert_out,
        tally_counts,
    )


def solution(mesh):
    rows = P("exp", "seq", None)
    hidden = P("exp", None, "seq")
    return jax.shard_map(
        functools.partial(body, mesh.shape["seq"], mesh.shape["exp"]),
        mesh=mesh,
        in_specs=(rows, rows, P(), P(), P(), P(), P(), rows, hidden, hidden, rows),
        out_specs=(
            rows,
            rows,
            rows,
            P(),
            P(),
            P(),
            P(),
            P(),
            hidden,
            hidden,
            P("exp", "seq", None, None),
        ),
        check_vma=False,
    )
```

```python
import functools
import math

import jax
import jax.numpy as jnp
from jax import lax
from jax.experimental import pallas as pl
from jax.experimental.pallas import tpu as pltpu
from jax.sharding import PartitionSpec as P

D = 768
HEADS = 12
HEAD_DIM = 64
NBUCKET = 32
MAXDIST = 128
TILE = 128
PAIRS = HEADS * HEAD_DIM // TILE

MESH = pl.DeviceIdType.MESH
ANY = pl.BlockSpec(memory_space=pl.ANY)
SMEM = pl.BlockSpec(memory_space=pltpu.SMEM)

norm_eps = 1e-06
masked_score = -1e30
highest = lax.Precision.HIGHEST
log2e = 1.0 / math.log(2.0)
scale_factor = HEAD_DIM ** (-0.5)


def bucket_edges():
    half_count = NBUCKET // 2
    thresholds = []
    for bucket_number in range(1, NBUCKET):
        if bucket_number < half_count:
            thresholds.append(bucket_number)
        else:
            thresholds.append(
                int(
                    half_count
                    * (MAXDIST / half_count) ** ((bucket_number - half_count) / half_count)
                )
            )
    return thresholds


def rms_apply(values, gain_row):
    return (
        values * lax.rsqrt(jnp.mean(values * values, axis=-1, keepdims=True) + norm_eps) * gain_row
    )


def rms_backward(values, gain_row, upstream):
    _, pullback = jax.vjp(rms_apply, values, gain_row)
    return pullback(upstream)


def cost(us):
    return pl.CostEstimate(flops=us * 10**9, bytes_accessed=0, transcendentals=0)


def seq_cycle(n):
    cols = n // 4
    if n % 4 or cols < 2:
        return list(range(n))
    order = [0]
    for row in range(4):
        span = range(1, cols) if row % 2 == 0 else range(cols - 1, 0, -1)
        order += [row * cols + col for col in span]
    return order + [3 * cols, 2 * cols, cols]


def look_up(index, table):
    value = jnp.int32(table[0])
    for number, entry in enumerate(table[1:], 1):
        value = jnp.where(index == number, jnp.int32(entry), value)
    return value


def greet(others):
    barrier = pltpu.get_barrier_semaphore()
    for other in others:
        pl.semaphore_signal(barrier, inc=1, device_id=other, device_id_type=MESH)
    pl.semaphore_wait(barrier, len(others))


def seq_ring(n):
    order = seq_cycle(n)
    pos = look_up(lax.axis_index("seq"), [order.index(i) for i in range(n)])

    def at(place):
        return look_up(lax.rem(place + 4 * n, n), order)

    return pos, at, ({"seq": at(pos + 1)}, {"seq": at(pos - 1)})


def gather_kernel(n, parts, count, *refs):
    sources, outs = refs[:count], refs[count : 2 * count]
    own_sem, send_sem, recv_sem = refs[2 * count :]
    pos, at, sides = seq_ring(n)
    me = at(pos)
    greet(sides)
    own = [
        pltpu.make_async_copy(sources[a], outs[a].at[me], own_sem.at[a]) for a in range(count)
    ]
    for copy in own:
        copy.start()
    started, latest = [], {}
    for step in range(n - 1):
        for a in range(count):
            rows = sources[a].shape[0] // 2 // parts
            for part in range(parts):
                for way in range(2):
                    if step:
                        latest[a, way, part].wait_recv()
                    block = at(pos - step) if way == 0 else at(pos + step)
                    span = pl.ds((way * parts + part) * rows, rows)
                    copy = pltpu.make_async_remote_copy(
                        src_ref=outs[a].at[block, span] if step else sources[a].at[span],
                        dst_ref=outs[a].at[block, span],
                        send_sem=send_sem.at[a, way, step, part],
                        recv_sem=recv_sem.at[a, way, step, part],
                        device_id=sides[way],
                        device_id_type=MESH,
                    )
                    copy.start()
                    started.append(copy)
                    latest[a, way, part] = copy
    for copy in latest.values():
        copy.wait_recv()
    for copy in started:
        copy.wait_send()
    for copy in own:
        copy.wait()


def ring_gather(arrays, n, number, parts=2):
    count = len(arrays)
    copies = (count, 2, n - 1, parts)
    return pl.pallas_call(
        functools.partial(gather_kernel, n, parts, count),
        out_shape=[jax.ShapeDtypeStruct((n,) + a.shape, a.dtype) for a in arrays],
        in_specs=[ANY] * count,
        out_specs=[ANY] * count,
        scratch_shapes=[
            pltpu.SemaphoreType.DMA((count,)),
            pltpu.SemaphoreType.DMA(copies),
            pltpu.SemaphoreType.DMA(copies),
        ],
        compiler_params=pltpu.CompilerParams(collective_id=number, has_side_effects=True),
        cost_estimate=cost(60),
        name="ring_gather",
    )(*arrays)


def scatter_kernel(n, parts, count, *refs):
    sources, outs = refs[:count], refs[count : 2 * count]
    own_bufs, got_bufs = refs[2 * count : 3 * count], refs[3 * count : 4 * count]
    own_sem, send_sem, recv_sem = refs[4 * count :]
    pos, at, sides = seq_ring(n)
    greet(sides)
    lanes = [(a, part, way) for a in range(count) for part in range(parts) for way in range(2)]

    def span(a, part, way):
        rows = sources[a].shape[1] // 2 // parts
        return pl.ds((way * parts + part) * rows, rows)

    def block(way, step):
        return at(pos - 1 - step) if way == 0 else at(pos + 1 + step)

    def send(lane, step, source):
        a, part, way = lane
        copy = pltpu.make_async_remote_copy(
            src_ref=source,
            dst_ref=got_bufs[a].at[way, step, part],
            send_sem=send_sem.at[a, way, step, part],
            recv_sem=recv_sem.at[a, way, step, part],
            device_id=sides[way],
            device_id_type=MESH,
        )
        copy.start()
        return copy

    latest, started, own = {}, [], {}
    for lane in lanes:
        a, part, way = lane
        latest[lane] = send(lane, 0, sources[a].at[block(way, 0), span(a, part, way)])
        started.append(latest[lane])
    for step in range(1, n):
        for lane in lanes:
            a, part, way = lane
            own[lane, step] = pltpu.make_async_copy(
                sources[a].at[block(way, step), span(a, part, way)],
                own_bufs[a].at[way, step - 1, part],
                own_sem.at[a, way, step - 1, part],
            )
            own[lane, step].start()
    for step in range(1, n):
        for lane in lanes:
            a, part, way = lane
            own[lane, step].wait()
            latest[lane].wait_recv()
            total = got_bufs[a][way, step - 1, part].astype(jnp.float32) + own_bufs[a][
                way, step - 1, part
            ].astype(jnp.float32)
            if step == n - 1:
                outs[a][span(a, part, way)] = total.astype(outs[a].dtype)
            else:
                got_bufs[a][way, step - 1, part] = total.astype(got_bufs[a].dtype)
                latest[lane] = send(lane, step, got_bufs[a].at[way, step - 1, part])
                started.append(latest[lane])
    for copy in started:
        copy.wait_send()


def ring_scatter(arrays, n, number, out_dtype, parts=2):
    count = len(arrays)
    copies = (count, 2, n - 1, parts)
    bufs = [
        pltpu.VMEM((2, n - 1, parts, a.shape[1] // 2 // parts, a.shape[2]), a.dtype)
        for a in arrays
    ]
    return pl.pallas_call(
        functools.partial(scatter_kernel, n, parts, count),
        out_shape=[jax.ShapeDtypeStruct(a.shape[1:], out_dtype) for a in arrays],
        in_specs=[ANY] * count,
        out_specs=[pl.BlockSpec(memory_space=pltpu.VMEM)] * count,
        scratch_shapes=bufs + bufs + [pltpu.SemaphoreType.DMA(copies)] * 3,
        compiler_params=pltpu.CompilerParams(
            collective_id=number, has_side_effects=True, vmem_limit_bytes=58 << 20
        ),
        name="ring_scatter",
    )(*arrays)


def finish_kernel(n, counts, *refs):
    few, many = counts
    refs = list(refs)
    take = lambda count: [refs.pop(0) for _ in range(count)]
    blocks, xs, sums, outs = take(few), take(many), take(few), take(many)
    own_bufs, got_bufs = take(few), take(few)
    mines, twins, crosses, gots = take(many), take(many), take(many), take(many)
    near_sem, far_sem, own_sem, pair_sem, cross_sem, ring_sem = refs
    pos, at, sides = seq_ring(n)
    exp = lax.axis_index("exp")
    core, chip = lax.rem(exp, 2), exp // 2
    peer, over = {"exp": exp + 1 - 2 * core}, {"exp": core + 2 * (1 - chip)}
    greet(sides + (peer, over))
    started = []

    def push(source, target, sems, index, to):
        copy = pltpu.make_async_remote_copy(
            src_ref=source,
            dst_ref=target,
            send_sem=sems.at[(0,) + index],
            recv_sem=sems.at[(1,) + index],
            device_id=to,
            device_id_type=MESH,
        )
        copy.start()
        started.append(copy)
        return copy

    def block(way, step):
        return at(pos - 1 - step) if way == 0 else at(pos + 1 + step)

    def fetch(source, target, sem):
        copy = pltpu.make_async_copy(source, target, sem)
        copy.start()
        return copy

    add = lambda *terms: functools.reduce(lambda u, v: u + v, [t.astype(jnp.float32) for t in terms])
    ways = range(2)
    lanes = [(a, way) for a in range(many) for way in ways]
    rings = [(a, way) for a in range(few) for way in ways]

    def span(ref, way):
        half = ref.shape[-2] // 2
        return pl.ds(way * half, half)

    pairs, own, crossing, ring = {}, {}, {}, {}
    for side in range(2):
        for step in range(n):
            for lane in lanes:
                a, way = lane
                place = chip if side else 1 - chip
                where, rows = block(way, step), span(xs[a], way)
                pairs[side, lane, step] = push(
                    xs[a].at[1 - core, place, where, rows],
                    twins[a].at[side, way, step],
                    pair_sem,
                    (0, side) + lane + (step,),
                    peer,
                )
                own[side, lane, step] = fetch(
                    xs[a].at[core, place, where, rows],
                    mines[a].at[side, way, step],
                    own_sem.at[(side,) + lane + (step,)],
                )
        if side == 0:
            for lane in rings:
                a, way = lane
                ring[lane] = push(
                    blocks[a].at[block(way, 0), span(blocks[a], way)],
                    got_bufs[a].at[way, 0],
                    far_sem,
                    lane + (0,),
                    sides[way],
                )
            near = {
                (lane, step): fetch(
                    blocks[lane[0]].at[block(lane[1], step), span(blocks[lane[0]], lane[1])],
                    own_bufs[lane[0]].at[lane[1], step - 1],
                    near_sem.at[lane + (step - 1,)],
                )
                for step in range(1, n)
                for lane in rings
            }

    def scatter(step):
        for lane in rings:
            a, way = lane
            near[lane, step].wait()
            ring[lane].wait_recv()
            total = add(got_bufs[a][way, step - 1], own_bufs[a][way, step - 1])
            if step == n - 1:
                sums[a][span(sums[a], way)] = total.astype(sums[a].dtype)
            else:
                got_bufs[a][way, step - 1] = total.astype(got_bufs[a].dtype)
                ring[lane] = push(
                    got_bufs[a].at[way, step - 1],
                    got_bufs[a].at[way, step],
                    far_sem,
                    lane + (step,),
                    sides[way],
                )

    for step in range(n):
        for lane in lanes:
            a, way = lane
            own[0, lane, step].wait()
            pairs[0, lane, step].wait_recv()
            mines[a][0, way, step] = add(mines[a][0, way, step], twins[a][0, way, step]).astype(
                mines[a].dtype
            )
            crossing[lane, step] = push(
                mines[a].at[0, way, step],
                crosses[a].at[way, step],
                cross_sem,
                (0,) + lane + (step,),
                over,
            )
        if step == n // 2:
            scatter(1)
    latest = {}
    for step in range(n):
        for lane in lanes:
            a, way = lane
            own[1, lane, step].wait()
            pairs[1, lane, step].wait_recv()
            crossing[lane, step].wait_recv()
            terms = [mines[a][1, way, step], twins[a][1, way, step], crosses[a][way, step]]
            if step:
                latest[lane].wait_recv()
                terms.append(gots[a][way, step - 1])
            mines[a][1, way, step] = add(*terms).astype(mines[a].dtype)
            if step < n - 1:
                latest[lane] = push(
                    mines[a].at[1, way, step],
                    gots[a].at[way, step],
                    ring_sem,
                    (0,) + lane + (step,),
                    sides[way],
                )
        if 2 <= step + 2 < n:
            scatter(step + 2)
    keep, done = [], []

    def hand_on(step):
        for lane in lanes:
            a, way = lane
            crossing[lane, step].wait_recv()
            where = at(pos - step) if way == 0 else at(pos + step)
            place = outs[a].at[core, 1 - chip, where, span(outs[a], way)]
            done.append(push(place, place, pair_sem, (1, 1) + lane + (step,), peer))

    for step in range(n):
        for lane in lanes:
            a, way = lane
            if step:
                latest[lane].wait_recv()
            where = at(pos - step) if way == 0 else at(pos + step)
            target = outs[a].at[core, chip, where, span(outs[a], way)]
            source = target if step else mines[a].at[1, way, n - 1]
            if step < n - 1:
                latest[lane] = push(source, target, ring_sem, (1,) + lane + (step,), sides[way])
            crossing[lane, step] = push(source, target, cross_sem, (1,) + lane + (step,), over)
            done.append(push(source, target, pair_sem, (1, 0) + lane + (step,), peer))
            if step == 0:
                keep.append(fetch(source, target, own_sem.at[(0,) + lane + (0,)]))
        if step:
            hand_on(step - 1)
    hand_on(n - 1)
    for copy in keep:
        copy.wait()
    for copy in done:
        copy.wait_recv()
    for copy in started:
        copy.wait_send()


def finish(blocks, rows_in, small, n, m, number):
    rows, cols = rows_in.shape
    each = rows // (4 * n)
    if m != 4 or rows % (4 * n * 32) or small.size > 4 * n * 16 * TILE:
        return (
            ring_scatter(blocks, n, number, jnp.float32),
            *lax.psum((rows_in, small), ("seq", "exp")),
        )
    padded = jnp.pad(small, (0, 4 * n * 16 * TILE - small.size))
    arrays = [rows_in.reshape(2, 2, n, each, cols), padded.reshape(2, 2, n, 16, TILE)]
    few, many = len(blocks), len(arrays)
    halves = [(x.shape[-2] // 2, x.shape[-1], x.dtype) for x in blocks + arrays]
    ring_bufs = [pltpu.VMEM((2, n - 1, r, c), t) for r, c, t in halves[:few]]
    two = [pltpu.VMEM((2, 2, n, r, c), t) for r, c, t in halves[few:]]
    one = [pltpu.VMEM((2, n, r, c), t) for r, c, t in halves[few:]]
    dma = pltpu.SemaphoreType.DMA
    results = pl.pallas_call(
        functools.partial(finish_kernel, n, (few, many)),
        out_shape=[jax.ShapeDtypeStruct(x.shape[1:], jnp.float32) for x in blocks]
        + [jax.ShapeDtypeStruct(x.shape, x.dtype) for x in arrays],
        in_specs=[ANY] * (few + many),
        out_specs=[pl.BlockSpec(memory_space=pltpu.VMEM)] * few + [ANY] * many,
        scratch_shapes=ring_bufs * 2
        + two * 2
        + one * 2
        + [
            dma((few, 2, n)),
            dma((2, few, 2, n)),
            dma((2, many, 2, n)),
            dma((2, 2, 2, many, 2, n)),
            dma((2, 2, many, 2, n)),
            dma((2, 2, many, 2, n)),
        ],
        compiler_params=pltpu.CompilerParams(
            collective_id=number, has_side_effects=True, vmem_limit_bytes=58 << 20
        ),
        cost_estimate=cost(120),
        name="finish",
    )(*blocks, *arrays)
    return results[:few], results[few].reshape(rows, cols), results[-1].reshape(-1)[: small.size]


QUAD = 4


def quad_moves(n):
    ring = (0, 1, 3, 2)
    step = lambda i, by: i - i % QUAD + ring[(ring.index(i % QUAD) + by) % QUAD]
    return [(i, step(i, 1)) for i in range(n)], [(i, step(i, -1)) for i in range(n)]


def spread_kernel(n, m, back, x_ref, out_ref, own_sem, send_sem, recv_sem):
    seq, exp = lax.axis_index("seq"), lax.axis_index("exp")
    groups = n // QUAD
    moves = [(g, k) for g in reversed(range(groups)) for k in range(m) if g or k]

    def target(g, k):
        shift = n - g * QUAD if back else g * QUAD
        return lax.rem(seq + shift, n), lax.rem(exp + k, m)

    greet([dict(zip(("seq", "exp"), target(g, k))) for g, k in moves])
    started = []
    for g, k in moves:
        to_seq, to_exp = target(g, k)
        copy = pltpu.make_async_remote_copy(
            src_ref=x_ref.at[g, to_exp] if back else x_ref.at[to_exp],
            dst_ref=out_ref.at[g, exp],
            send_sem=send_sem.at[g, k],
            recv_sem=recv_sem.at[g, k],
            device_id={"seq": to_seq, "exp": to_exp},
            device_id_type=MESH,
        )
        copy.start()
        started.append(copy)
    own = pltpu.make_async_copy(
        x_ref.at[0, exp] if back else x_ref.at[exp], out_ref.at[0, exp], own_sem
    )
    own.start()
    for copy in started:
        copy.wait_recv()
    for copy in started:
        copy.wait_send()
    own.wait()


def spread(x, n, m, back, number):
    groups = n // QUAD
    return pl.pallas_call(
        functools.partial(spread_kernel, n, m, back),
        out_shape=jax.ShapeDtypeStruct((groups,) + x.shape[-3:], x.dtype),
        in_specs=[ANY],
        out_specs=ANY,
        scratch_shapes=[
            pltpu.SemaphoreType.DMA,
            pltpu.SemaphoreType.DMA((groups, m)),
            pltpu.SemaphoreType.DMA((groups, m)),
        ],
        compiler_params=pltpu.CompilerParams(collective_id=number, has_side_effects=True),
        cost_estimate=cost(70),
        name="spread_back" if back else "spread",
    )(x)


def dot_last(a, b):
    return lax.dot_general(a, b, (((1,), (1,)), ((), ())), preferred_element_type=jnp.float32)


def dot_first(a, b):
    return lax.dot_general(a, b, (((0,), (0,)), ((), ())), preferred_element_type=jnp.float32)


def dot_plain(a, b):
    return jnp.dot(a, b, preferred_element_type=jnp.float32)


def head_masks(dtype):
    low = lax.broadcasted_iota(jnp.int32, (1, TILE), 1) < HEAD_DIM
    first = jnp.where(low, 1.0, 0.0).astype(jnp.float32)
    return first.astype(dtype), (1.0 - first).astype(dtype)


def split_heads(pair):
    return jnp.concatenate([pair * mask for mask in head_masks(pair.dtype)], axis=0)


def own_bias(tiles, count):
    rows = []
    for r in range(count):
        row = []
        for c in range(count):
            if c == r:
                row.append(tiles[:, TILE:])
            elif c == r - 1:
                row.append(tiles[:, :TILE])
            else:
                row.append(jnp.full((TILE, TILE), 0.0 if c < r else masked_score, jnp.float32))
        rows.append(jnp.concatenate(row, axis=1))
    return jnp.concatenate(rows, axis=0)


def edge_bias(tile_ref, rows):
    edge = []
    for h in range(2):
        first = jnp.concatenate(
            [jnp.zeros((rows - TILE, TILE), jnp.float32), tile_ref[h][:, :TILE].T], axis=0
        )
        edge += [first, jnp.zeros((rows, rows - TILE), jnp.float32)]
    return jnp.concatenate(edge, axis=1)


def attend_kernel(causal, block, s_ref, q_ref, k_ref, v_ref, *refs):
    if causal:
        tile_ref, low_ref, wide_ref, lse_ref, acc_ref, top_ref = refs
    else:
        low_ref, wide_ref, lse_ref, acc_ref, top_ref = refs
    rows = q_ref.shape[0]
    both = split_heads(q_ref[...])
    ones = jnp.ones((16, block), v_ref.dtype)

    def visit(start, bias, first):
        keys = k_ref[pl.ds(start, block), :]
        values = v_ref[pl.ds(start, block), :]
        t = dot_last(keys, both) * (scale_factor * log2e)
        if bias is not None:
            t = t + bias
        top = jnp.max(t, axis=0, keepdims=True)
        if not first:
            before = top_ref[...]
            top = jnp.maximum(before, top)
            fade = jnp.exp2(before - top)
        top_ref[...] = top
        p = jnp.exp2(t - top).astype(values.dtype)
        part = dot_plain(jnp.concatenate([values.T, ones], axis=0), p)
        if first:
            acc_ref[...] = part
        else:
            acc_ref[...] = acc_ref[...] * fade + part

    if causal:
        s = s_ref[0]
        count = rows // TILE
        visit(
            pl.multiple_of(s * block, block),
            jnp.concatenate([own_bias(tile_ref[h], count).T for h in range(2)], axis=1),
            True,
        )

        @pl.when(s > 0)
        def _():
            visit(pl.multiple_of((s - 1) * block, block), edge_bias(tile_ref, rows), False)

        def far(j, carry):
            visit(pl.multiple_of(j * block, block), None, False)
            return carry

        lax.fori_loop(0, s - 1, far, 0)
    else:
        for j in range(k_ref.shape[0] // block):
            visit(j * block, None, j == 0)
    sums = acc_ref[TILE : TILE + 1, :]
    wide = jnp.concatenate(
        [
            acc_ref[:HEAD_DIM, :rows] / sums[:, :rows],
            acc_ref[HEAD_DIM:TILE, rows:] / sums[:, rows:],
        ],
        axis=0,
    ).T
    wide_ref[...] = wide
    low_ref[...] = wide.astype(low_ref.dtype)
    lse = top_ref[...] + jnp.log2(sums)
    lse_ref[0] = jnp.concatenate([lse[:, :rows], lse[:, rows:]], axis=0)


def attend(seq_at, queries, keys, values, tiles):
    rows, total = queries.shape[0], keys.shape[0]
    causal = tiles is not None
    block = rows if causal else math.gcd(total, 512)
    pair = pl.BlockSpec((rows, TILE), lambda g: (0, g))
    long = pl.BlockSpec((total, TILE), lambda g: (0, g))
    extra, specs = [], []
    if causal:
        extra, specs = [tiles], [pl.BlockSpec((2,) + tiles.shape[1:], lambda g: (g, 0, 0))]
    return pl.pallas_call(
        functools.partial(attend_kernel, causal, block),
        grid=(PAIRS,),
        out_shape=[
            jax.ShapeDtypeStruct((rows, D), jnp.bfloat16),
            jax.ShapeDtypeStruct((rows, D), jnp.float32),
            jax.ShapeDtypeStruct((PAIRS, 2, rows), jnp.float32),
        ],
        in_specs=[SMEM, pair, long, long] + specs,
        out_specs=[pair, pair, pl.BlockSpec((1, 2, rows), lambda g: (g, 0, 0))],
        scratch_shapes=[
            pltpu.VMEM((TILE + 16, 2 * rows), jnp.float32),
            pltpu.VMEM((1, 2 * rows), jnp.float32),
        ],
        compiler_params=pltpu.CompilerParams(vmem_limit_bytes=48 << 20),
        cost_estimate=cost(40 if causal else 10),
        name="attend_self" if causal else "attend_cross",
    )(seq_at, queries, keys, values, *extra)


def attend_back_kernel(causal, block, s_ref, q_ref, k_ref, v_ref, up_ref, wide_ref, lse_ref, *refs):
    if causal:
        tile_ref, dq_ref, dk_ref, dv_ref, near_ref, sum_ref, acc_ref = refs
    else:
        dq_ref, dk_ref, dv_ref, acc_ref = refs
    rows = q_ref.shape[0]
    both = split_heads(q_ref[...])
    up = up_ref[...]
    up_both = split_heads(up)
    turned = (up.astype(jnp.float32) * wide_ref[...]).T
    delta = jnp.concatenate(
        [
            jnp.sum(turned[:HEAD_DIM], axis=0, keepdims=True),
            jnp.sum(turned[HEAD_DIM:], axis=0, keepdims=True),
        ],
        axis=1,
    )
    lse = jnp.concatenate([lse_ref[0, :1], lse_ref[0, 1:]], axis=1)
    ones = jnp.ones((16, block), k_ref.dtype)

    def visit(start, bias, first):
        keys = k_ref[pl.ds(start, block), :]
        values = v_ref[pl.ds(start, block), :]
        t = dot_last(keys, both) * (scale_factor * log2e)
        if bias is not None:
            t = t + bias
        p = jnp.exp2(t - lse)
        ds = (p * (dot_last(values, up_both) - delta)).astype(keys.dtype)
        dv_ref[pl.ds(start, block), :] = dot_plain(p.astype(keys.dtype), up_both).astype(
            dv_ref.dtype
        )
        dk_ref[pl.ds(start, block), :] = (dot_plain(ds, both) * scale_factor).astype(dk_ref.dtype)
        part = dot_plain(jnp.concatenate([keys.T, ones], axis=0), ds)
        if first:
            acc_ref[...] = part
        else:
            acc_ref[...] += part
        return ds

    if causal:
        s = s_ref[0]
        count = rows // TILE
        ds = visit(
            pl.multiple_of(s * block, block),
            jnp.concatenate([own_bias(tile_ref[h], count).T for h in range(2)], axis=1),
            True,
        )
        for h in range(2):
            same = before = jnp.zeros((TILE, TILE), jnp.float32)
            for r in range(count):
                columns = slice(h * rows + r * TILE, h * rows + (r + 1) * TILE)
                same = same + ds[r * TILE : (r + 1) * TILE, columns].astype(jnp.float32)
                if r:
                    before = before + ds[(r - 1) * TILE : r * TILE, columns].astype(jnp.float32)
            near_ref[h, :TILE] = before
            near_ref[h, TILE:] = same

        @pl.when(s > 0)
        def _():
            ds = visit(pl.multiple_of((s - 1) * block, block), edge_bias(tile_ref, rows), False)
            for h in range(2):
                near_ref[h, :TILE] += ds[rows - TILE :, h * rows : h * rows + TILE].astype(
                    jnp.float32
                )

        def far(j, carry):
            visit(pl.multiple_of(j * block, block), None, False)
            return carry

        lax.fori_loop(0, s - 1, far, 0)

        def beyond(j, carry):
            start = pl.multiple_of(j * block, block)
            dk_ref[pl.ds(start, block), :] = jnp.zeros((block, TILE), dk_ref.dtype)
            dv_ref[pl.ds(start, block), :] = jnp.zeros((block, TILE), dv_ref.dtype)
            return carry

        lax.fori_loop(s + 1, k_ref.shape[0] // block, beyond, 0)
        sum_ref[0] = jnp.concatenate(
            [acc_ref[TILE : TILE + 1, :rows], acc_ref[TILE : TILE + 1, rows:]], axis=0
        )
    else:
        for j in range(k_ref.shape[0] // block):
            visit(j * block, None, j == 0)
    dq = jnp.concatenate([acc_ref[:HEAD_DIM, :rows], acc_ref[HEAD_DIM:TILE, rows:]], axis=0)
    dq_ref[...] = (dq.T * scale_factor).astype(dq_ref.dtype)


def attend_back(seq_at, queries, keys, values, upstream, wide, lse, tiles):
    rows, total = queries.shape[0], keys.shape[0]
    causal = tiles is not None
    block = rows if causal else math.gcd(total, 512)
    pair = pl.BlockSpec((rows, TILE), lambda g: (0, g))
    long = pl.BlockSpec((total, TILE), lambda g: (0, g))
    line = pl.BlockSpec((1, 2, rows), lambda g: (g, 0, 0))
    extra, specs, shapes, out_specs = [], [], [], []
    if causal:
        extra, specs = [tiles], [pl.BlockSpec((2,) + tiles.shape[1:], lambda g: (g, 0, 0))]
        shapes = [
            jax.ShapeDtypeStruct((HEADS, 2 * TILE, TILE), jnp.float32),
            jax.ShapeDtypeStruct((PAIRS, 2, rows), jnp.float32),
        ]
        out_specs = [pl.BlockSpec((2, 2 * TILE, TILE), lambda g: (g, 0, 0)), line]
    return pl.pallas_call(
        functools.partial(attend_back_kernel, causal, block),
        grid=(PAIRS,),
        out_shape=[
            jax.ShapeDtypeStruct((rows, D), jnp.bfloat16),
            jax.ShapeDtypeStruct((total, D), jnp.bfloat16),
            jax.ShapeDtypeStruct((total, D), jnp.bfloat16),
        ]
        + shapes,
        in_specs=[SMEM, pair, long, long, pair, pair, line] + specs,
        out_specs=[pair, long, long] + out_specs,
        scratch_shapes=[pltpu.VMEM((TILE + 16, 2 * rows), jnp.float32)],
        compiler_params=pltpu.CompilerParams(vmem_limit_bytes=48 << 20),
        cost_estimate=cost(48 if causal else 15),
        name="attend_self_back" if causal else "attend_cross_back",
    )(seq_at, queries, keys, values, upstream, wide, lse, *extra)


def bias_tiles(bias_table):
    distance = (
        TILE
        + jnp.arange(TILE, dtype=jnp.int32)[:, None]
        - jnp.arange(2 * TILE, dtype=jnp.int32)[None, :]
    )
    table = (bias_table - bias_table[NBUCKET - 1 :]) * log2e
    terms = jnp.broadcast_to(table[0][:, None, None], (HEADS, TILE, 2 * TILE))
    for number, threshold in enumerate(bucket_edges()):
        terms = jnp.where((distance >= threshold)[None], table[number + 1][:, None, None], terms)
    return jnp.where((distance >= 0)[None], terms, masked_score)


def bias_gradient(near, sums):
    distance = (
        TILE
        + jnp.arange(TILE, dtype=jnp.int32)[None, :]
        - jnp.arange(2 * TILE, dtype=jnp.int32)[:, None]
    )
    bucket = jnp.zeros(distance.shape, jnp.int32)
    for threshold in bucket_edges():
        bucket = bucket + (distance >= threshold).astype(jnp.int32)
    onehot = (
        bucket.reshape(-1)[None, :] == jnp.arange(NBUCKET, dtype=jnp.int32)[:, None]
    ).astype(jnp.float32)
    flat = near.reshape(HEADS, -1)
    table = lax.dot_general(
        onehot, flat, (((1,), (1,)), ((), ())), precision=highest
    )
    far = jnp.sum(sums, axis=-1).reshape(HEADS) - jnp.sum(flat, axis=-1)
    last = jnp.arange(NBUCKET, dtype=jnp.int32)[:, None] == NBUCKET - 1
    return table + jnp.where(last, far[None, :], 0.0)


def expert_kernel(*refs):
    rows_ref, maps = refs[0], refs[1 : 1 + 2 * QUAD]
    part_ref, grads = refs[1 + 2 * QUAD], refs[2 + 2 * QUAD :]
    shape = rows_ref.shape
    rows = rows_ref[...].reshape(shape[0] * shape[1] * shape[2], shape[3])
    tokens, upstream = rows[:, :D], rows[:, D:]
    slope = math.sqrt(2.0 / math.pi)
    result = back = None
    for j in range(QUAD):
        up_map, down_map = maps[2 * j][0], maps[2 * j + 1][0]
        u = dot_plain(tokens, up_map)
        square = u * u
        bend = jnp.tanh(slope * (u + 0.044715 * (square * u)))
        half = 0.5 * (1.0 + bend)
        act = (u * half).astype(tokens.dtype)
        rise = half + 0.5 * u * (1.0 - bend * bend) * (slope * (1.0 + 3 * 0.044715 * square))
        du = (dot_plain(upstream, down_map) * rise).astype(tokens.dtype)
        y, dn = dot_last(act, down_map), dot_last(du, up_map)
        result = y if result is None else result + y
        back = dn if back is None else back + dn
        for ref, left, right in ((grads[2 * j], tokens, du), (grads[2 * j + 1], upstream, act)):
            ref[0] = dot_first(left, right).astype(ref.dtype)
    part_ref[...] = (
        jnp.concatenate([result, back], axis=1).astype(part_ref.dtype).reshape(part_ref.shape)
    )


def run_experts(rows, maps):
    groups, m, slots, width = rows.shape
    count, _, hidden = maps[0].shape
    block = pl.BlockSpec((groups, m, slots // count, width), lambda e: (0, 0, e, 0))
    weight = pl.BlockSpec((1, D, hidden), lambda e: (e, 0, 0))
    return pl.pallas_call(
        expert_kernel,
        grid=(count,),
        out_shape=[jax.ShapeDtypeStruct(rows.shape, rows.dtype)]
        + [
            jax.ShapeDtypeStruct(w.shape, jnp.float32 if i < 2 else jnp.bfloat16)
            for i, w in enumerate(maps)
        ],
        in_specs=[block] + [weight] * len(maps),
        out_specs=[block] + [weight] * len(maps),
        compiler_params=pltpu.CompilerParams(vmem_limit_bytes=58 << 20),
        cost_estimate=cost(28),
        name="run_experts",
    )(rows, *maps)


def project(source, matrix):
    return jnp.dot(source, matrix, preferred_element_type=jnp.float32).astype(jnp.bfloat16)


def weight_grad(source, upstream):
    return jnp.einsum("td,te->de", source, upstream, preferred_element_type=jnp.float32).astype(
        jnp.bfloat16
    )


def input_grad(upstream, matrix):
    return jnp.einsum("te,de->td", upstream, matrix, preferred_element_type=jnp.float32)


def body(
    n,
    m,
    hidden_in,
    memory,
    proj_in,
    proj_out,
    norm_gains,
    rel_bias,
    router,
    expert_choice,
    expert_in,
    expert_out,
    cotangent,
):
    tokens = hidden_in[0].astype(jnp.float32)
    memory_rows = memory[0]
    memory_count = memory_rows.shape[0]
    gain_rows = norm_gains.astype(jnp.float32)
    token_count = tokens.shape[0]
    seq_at = lax.axis_index("seq").astype(jnp.int32).reshape(1)
    normed_self = rms_apply(tokens, gain_rows[0]).astype(jnp.bfloat16)
    tiles = bias_tiles(rel_bias)

    normed_all, memory_all = ring_gather([normed_self, memory_rows], n, 1)
    to_next, to_last = quad_moves(n)
    in_own, out_own, normed_all = lax.optimization_barrier((expert_in, expert_out, normed_all))
    in_last, out_last = (lax.ppermute(w, "seq", to_next) for w in (in_own, out_own))
    in_next, out_next = (lax.ppermute(w, "seq", to_last) for w in (in_own, out_own))
    normed_all = normed_all.reshape(n * token_count, D)
    memory_all = memory_all.reshape(n * memory_count, D)
    queries = project(normed_self, proj_in[0])
    key_all = project(normed_all, proj_in[1])
    value_all = project(normed_all, proj_in[2])
    memory_key_all = project(memory_all, proj_in[4])
    memory_value_all = project(memory_all, proj_in[5])
    attended_self_low, attended_self, lse_self = attend(
        seq_at, queries, key_all, value_all, tiles
    )
    attended_self_low, in_last, out_next = lax.optimization_barrier(
        (attended_self_low, in_last, out_next)
    )
    in_far = lax.ppermute(in_last, "seq", to_next)
    out_far = lax.ppermute(out_next, "seq", to_last)
    after_self = tokens + jnp.dot(
        attended_self_low, proj_out[0], preferred_element_type=jnp.float32
    )

    normed_cross = rms_apply(after_self, gain_rows[1]).astype(jnp.bfloat16)
    cross_queries = project(normed_cross, proj_in[3])
    attended_cross_low, attended_cross, lse_cross = attend(
        seq_at, cross_queries, memory_key_all, memory_value_all, None
    )
    after_cross = after_self + jnp.dot(
        attended_cross_low, proj_out[1], preferred_element_type=jnp.float32
    )

    mixed_low = rms_apply(after_cross, gain_rows[2]).astype(jnp.bfloat16)
    softmax_probs = jax.nn.softmax(
        jnp.dot(mixed_low, router, preferred_element_type=jnp.float32), axis=-1
    )
    expert_count = router.shape[1]
    local_experts = expert_in.shape[0]
    capacity = max(2, 5 * token_count // (4 * expert_count))
    chosen = expert_choice[0, :, 0]
    onehot_int = (chosen[:, None] == jnp.arange(expert_count, dtype=jnp.int32)[None, :]).astype(
        jnp.int32
    )
    onehot = onehot_int.astype(jnp.float32)
    gate_prob = jnp.sum(softmax_probs * onehot, axis=-1)
    slot_index = jnp.sum(jnp.cumsum(onehot_int, axis=0) * onehot_int, axis=-1) - 1
    is_kept = slot_index < capacity
    slots = -(-capacity // 16) * 16
    place = jnp.where(is_kept, chosen * slots + slot_index, -1)
    dispatch = (
        place[:, None] == jnp.arange(expert_count * slots, dtype=jnp.int32)[None, :]
    ).astype(jnp.bfloat16)
    dispatched = jnp.sum(onehot_int * is_kept[:, None].astype(jnp.int32), axis=0)
    tally_counts = jnp.stack(
        [dispatched, jnp.sum(onehot_int, axis=0) - dispatched], axis=0
    ).reshape(1, 1, 2, expert_count)

    grad_top = cotangent[0].astype(jnp.float32)
    scaled = (gate_prob[:, None] * grad_top).astype(jnp.bfloat16)
    sent_rows = (
        jnp.einsum(
            "tx,td->xd",
            dispatch,
            jnp.concatenate([mixed_low, scaled], axis=1),
            preferred_element_type=jnp.float32,
        )
        .astype(jnp.bfloat16)
        .reshape(m, local_experts * slots, 2 * D)
    )
    sent_rows, in_far, out_far = lax.optimization_barrier((sent_rows, in_far, out_far))
    maps = [in_own, out_own, in_last, out_last, in_next, out_next, in_far, out_far]
    received = spread(sent_rows, n, m, False, 2)
    parts, *terms = run_experts(received, maps)
    returned = spread(parts, n, m, True, 3)
    gin_own, gout_own, gin_last, gout_last, gin_next, gout_next, gin_far, gout_far = terms
    gin_far = lax.ppermute(gin_far, "seq", to_next)
    gout_far = lax.ppermute(gout_far, "seq", to_last)
    returned, gin_far, gout_far = lax.optimization_barrier((returned, gin_far, gout_far))
    gin_next, gout_last = gin_next + gin_far, gout_last + gout_far
    gin_next, gout_next = (lax.ppermute(w, "seq", to_next) for w in (gin_next, gout_next))
    gin_last, gout_last = (lax.ppermute(w, "seq", to_last) for w in (gin_last, gout_last))
    returned = jnp.sum(returned.astype(jnp.float32), axis=0).astype(jnp.bfloat16)
    returned = returned.reshape(expert_count * slots, 2 * D)
    routed = jnp.dot(dispatch, returned, preferred_element_type=jnp.float32)
    combined, grad_mixed = routed[:, :D], routed[:, D:]
    output = (after_cross + gate_prob[:, None] * combined).astype(jnp.bfloat16)

    grad_gate = jnp.sum(grad_top * combined, axis=-1)
    grad_logits = softmax_probs * (onehot - gate_prob[:, None]) * grad_gate[:, None]
    grad_router = jnp.einsum(
        "td,te->de", mixed_low.astype(jnp.float32), grad_logits, precision=highest
    )
    grad_mixed = grad_mixed + jnp.einsum(
        "te,de->td", grad_logits, router.astype(jnp.float32), precision=highest
    )
    grad_cross_part, grad_gain_mix = rms_backward(after_cross, gain_rows[2], grad_mixed)
    grad_after_cross = grad_top + grad_cross_part

    grad_cross_low = grad_after_cross.astype(jnp.bfloat16)
    grad_out_cross = weight_grad(attended_cross_low, grad_cross_low)
    grad_attended_cross = input_grad(grad_cross_low, proj_out[1]).astype(jnp.bfloat16)
    grad_cross_query, grad_memory_keys, grad_memory_values = attend_back(
        seq_at,
        cross_queries,
        memory_key_all,
        memory_value_all,
        grad_attended_cross,
        attended_cross,
        lse_cross,
        None,
    )
    grad_query_cross = weight_grad(normed_cross, grad_cross_query)
    grad_self_part, grad_gain_cross = rms_backward(
        after_self, gain_rows[1], input_grad(grad_cross_query, proj_in[3])
    )
    grad_after_self = grad_after_cross + grad_self_part
    grad_memory_part = (
        input_grad(grad_memory_keys, proj_in[4]) + input_grad(grad_memory_values, proj_in[5])
    ).astype(jnp.bfloat16)

    grad_self_low = grad_after_self.astype(jnp.bfloat16)
    grad_out_self = weight_grad(attended_self_low, grad_self_low)
    grad_attended_self = input_grad(grad_self_low, proj_out[0]).astype(jnp.bfloat16)
    grad_self_query, grad_keys, grad_values, near, sums = attend_back(
        seq_at,
        queries,
        key_all,
        value_all,
        grad_attended_self,
        attended_self,
        lse_self,
        tiles,
    )
    grad_keys, grad_values, gin_last, gout_last, gin_next, gout_next = lax.optimization_barrier(
        (grad_keys, grad_values, gin_last, gout_last, gin_next, gout_next)
    )
    grad_expert_in = gin_own + gin_last.astype(jnp.float32) + gin_next.astype(jnp.float32)
    grad_expert_out = gout_own + gout_last.astype(jnp.float32) + gout_next.astype(jnp.float32)
    grad_table = bias_gradient(near, sums)
    grad_normed_query = input_grad(grad_self_query, proj_in[0])
    grad_normed_part = input_grad(grad_keys, proj_in[1]) + input_grad(grad_values, proj_in[2])
    grad_gain_self = (
        jnp.sum(grad_normed_part * normed_all.astype(jnp.float32), axis=0)
        + jnp.sum(grad_normed_query * normed_self.astype(jnp.float32), axis=0)
    ) / gain_rows[0]

    grads = jnp.stack(
        [
            weight_grad(normed_self, grad_self_query),
            weight_grad(normed_all, grad_keys),
            weight_grad(normed_all, grad_values),
            grad_query_cross,
            weight_grad(memory_all, grad_memory_keys),
            weight_grad(memory_all, grad_memory_values),
            grad_out_self,
            grad_out_cross,
        ]
    )
    grad_gains = jnp.stack([grad_gain_self, grad_gain_cross, grad_gain_mix])
    (grad_normed_own, grad_memory), grads, small = finish(
        [
            grad_normed_part.astype(jnp.bfloat16).reshape(n, token_count, D),
            grad_memory_part.reshape(n, memory_count, D),
        ],
        grads.reshape(-1, D),
        jnp.concatenate([grad_gains.reshape(-1), grad_table.reshape(-1), grad_router.reshape(-1)]),
        n,
        m,
        4,
    )
    grad_token_part, _ = rms_backward(tokens, gain_rows[0], grad_normed_query + grad_normed_own)
    grad_in = (grad_after_self + grad_token_part).astype(jnp.bfloat16)
    grads = grads.reshape(-1, D, D).astype(jnp.float32)
    ends = (grad_gains.size, grad_gains.size + grad_table.size)
    return (
        output.reshape(1, token_count, D),
        grad_in.reshape(1, token_count, D),
        grad_memory.astype(jnp.bfloat16).reshape(1, memory_count, D),
        grads[:6],
        grads[6:],
        small[: ends[0]].reshape(grad_gains.shape),
        small[ends[0] : ends[1]].reshape(grad_table.shape),
        small[ends[1] :].reshape(grad_router.shape),
        grad_expert_in,
        grad_expert_out,
        tally_counts,
    )


def solution(mesh):
    rows = P("exp", "seq", None)
    hidden = P("exp", None, "seq")
    return jax.shard_map(
        functools.partial(body, mesh.shape["seq"], mesh.shape["exp"]),
        mesh=mesh,
        in_specs=(rows, rows, P(), P(), P(), P(), P(), rows, hidden, hidden, rows),
        out_specs=(
            rows,
            rows,
            rows,
            P(),
            P(),
            P(),
            P(),
            P(),
            hidden,
            hidden,
            P("exp", "seq", None, None),
        ),
        check_vma=False,
    )
```

```python
import functools
import math

import jax
import jax.numpy as jnp
from jax import lax
from jax.experimental import pallas as pl
from jax.experimental.pallas import tpu as pltpu
from jax.sharding import PartitionSpec as P

D = 768
HEADS = 12
HEAD_DIM = 64
NBUCKET = 32
MAXDIST = 128
TILE = 128
PAIRS = HEADS * HEAD_DIM // TILE

MESH = pl.DeviceIdType.MESH
ANY = pl.BlockSpec(memory_space=pl.ANY)
SMEM = pl.BlockSpec(memory_space=pltpu.SMEM)

norm_eps = 1e-06
masked_score = -1e30
highest = lax.Precision.HIGHEST
log2e = 1.0 / math.log(2.0)
scale_factor = HEAD_DIM ** (-0.5)


def bucket_edges():
    half_count = NBUCKET // 2
    thresholds = []
    for bucket_number in range(1, NBUCKET):
        if bucket_number < half_count:
            thresholds.append(bucket_number)
        else:
            thresholds.append(
                int(
                    half_count
                    * (MAXDIST / half_count) ** ((bucket_number - half_count) / half_count)
                )
            )
    return thresholds


def rms_apply(values, gain_row):
    return (
        values * lax.rsqrt(jnp.mean(values * values, axis=-1, keepdims=True) + norm_eps) * gain_row
    )


def rms_backward(values, gain_row, upstream):
    _, pullback = jax.vjp(rms_apply, values, gain_row)
    return pullback(upstream)


def cost(us):
    return pl.CostEstimate(flops=us * 10**9, bytes_accessed=0, transcendentals=0)


def seq_cycle(n):
    cols = n // 4
    if n % 4 or cols < 2:
        return list(range(n))
    order = [0]
    for row in range(4):
        span = range(1, cols) if row % 2 == 0 else range(cols - 1, 0, -1)
        order += [row * cols + col for col in span]
    return order + [3 * cols, 2 * cols, cols]


def look_up(index, table):
    value = jnp.int32(table[0])
    for number, entry in enumerate(table[1:], 1):
        value = jnp.where(index == number, jnp.int32(entry), value)
    return value


def greet(others):
    barrier = pltpu.get_barrier_semaphore()
    for other in others:
        pl.semaphore_signal(barrier, inc=1, device_id=other, device_id_type=MESH)
    pl.semaphore_wait(barrier, len(others))


def seq_ring(n):
    order = seq_cycle(n)
    pos = look_up(lax.axis_index("seq"), [order.index(i) for i in range(n)])

    def at(place):
        return look_up(lax.rem(place + 4 * n, n), order)

    return pos, at, ({"seq": at(pos + 1)}, {"seq": at(pos - 1)})


def gather_kernel(n, parts, *refs):
    sources, proj_ref, outs = refs[:2], refs[2], refs[3:10]
    lands, w_buf, bufs = refs[10:12], refs[12], refs[13:18]
    own_sem, w_sem, send_sem, recv_sem, store_sem = refs[18:]
    pos, at, sides = seq_ring(n)
    me = at(pos)
    greet(sides)
    own = [pltpu.make_async_copy(sources[a], lands[a].at[me], own_sem.at[a]) for a in range(2)]
    weights = [
        pltpu.make_async_copy(proj_ref.at[number], w_buf.at[i], w_sem.at[i])
        for i, number in enumerate((0, 1, 2, 4, 5))
    ]
    started, latest, stored = [], {}, []

    def pass_on(step):
        for part in range(parts):
            for a in range(2):
                rows = sources[a].shape[0] // 2 // parts
                for way in range(2):
                    if step:
                        latest[a, way, part].wait_recv()
                    if step == n - 1:
                        continue
                    block = at(pos - step) if way == 0 else at(pos + step)
                    span = pl.ds((way * parts + part) * rows, rows)
                    copy = pltpu.make_async_remote_copy(
                        src_ref=lands[a].at[block, span] if step else sources[a].at[span],
                        dst_ref=lands[a].at[block, span],
                        send_sem=send_sem.at[a, way, step, part],
                        recv_sem=recv_sem.at[a, way, step, part],
                        device_id=sides[way],
                        device_id_type=MESH,
                    )
                    copy.start()
                    started.append(copy)
                    latest[a, way, part] = copy

    def store(source, target, number, step, way):
        copy = pltpu.make_async_copy(source, target, store_sem.at[number, step, way])
        copy.start()
        stored.append(copy)

    def work(step):
        blocks = (at(pos - step), at(pos + step))
        for a in range(2):
            half = sources[a].shape[0] // 2
            spans = (pl.ds(0, half), pl.ds(half, half))
            rows = jnp.concatenate([lands[a][blocks[way], spans[way], :] for way in range(2)], axis=0)
            for i in range(2):
                buf = bufs[1 + 2 * a + i]
                made = dot_plain(rows, w_buf[1 + 2 * a + i]).astype(buf.dtype)
                for way in range(2):
                    buf[blocks[way], spans[way], :] = made[way * half : (way + 1) * half]
            for way in range(2):
                where = (blocks[way], spans[way])
                store(lands[a].at[where], outs[a].at[where], a, step, way)
                for i in range(2):
                    number = 1 + 2 * a + i
                    store(bufs[number].at[where], outs[2 + number].at[where], 2 + number, step, way)

    pass_on(0)
    for copy in own + weights:
        copy.start()
    for copy in own + weights:
        copy.wait()
    bufs[0][...] = dot_plain(lands[0][me], w_buf[0]).astype(bufs[0].dtype)
    store(bufs[0], outs[2], 2, 0, 0)
    work(0)
    for step in range(1, n):
        pass_on(step)
        work(step)
    for copy in started:
        copy.wait_send()
    for copy in stored:
        copy.wait()


def gather_projected(tokens, memory_rows, proj_in, n, number, parts=2):
    both = (tokens, memory_rows)
    copies = (2, 2, n - 1, parts)
    wide = [(n,) + x.shape for x in both]
    shapes = wide + [tokens.shape] + [wide[0]] * 2 + [wide[1]] * 2
    dma = pltpu.SemaphoreType.DMA
    return pl.pallas_call(
        functools.partial(gather_kernel, n, parts),
        out_shape=[jax.ShapeDtypeStruct(shape, tokens.dtype) for shape in shapes],
        in_specs=[ANY] * 3,
        out_specs=[ANY] * 7,
        scratch_shapes=[pltpu.VMEM(shape, tokens.dtype) for shape in wide]
        + [pltpu.VMEM((5,) + proj_in.shape[1:], tokens.dtype)]
        + [pltpu.VMEM(shape, tokens.dtype) for shape in shapes[2:]]
        + [dma((2,)), dma((5,)), dma(copies), dma(copies), dma((7, n, 2))],
        compiler_params=pltpu.CompilerParams(
            collective_id=number, has_side_effects=True, vmem_limit_bytes=58 << 20
        ),
        cost_estimate=cost(60),
        name="gather_projected",
    )(tokens, memory_rows, proj_in)


def scatter_kernel(n, parts, count, *refs):
    sources, outs = refs[:count], refs[count : 2 * count]
    own_bufs, got_bufs = refs[2 * count : 3 * count], refs[3 * count : 4 * count]
    own_sem, send_sem, recv_sem = refs[4 * count :]
    pos, at, sides = seq_ring(n)
    greet(sides)
    lanes = [(a, part, way) for a in range(count) for part in range(parts) for way in range(2)]

    def span(a, part, way):
        rows = sources[a].shape[1] // 2 // parts
        return pl.ds((way * parts + part) * rows, rows)

    def block(way, step):
        return at(pos - 1 - step) if way == 0 else at(pos + 1 + step)

    def send(lane, step, source):
        a, part, way = lane
        copy = pltpu.make_async_remote_copy(
            src_ref=source,
            dst_ref=got_bufs[a].at[way, step, part],
            send_sem=send_sem.at[a, way, step, part],
            recv_sem=recv_sem.at[a, way, step, part],
            device_id=sides[way],
            device_id_type=MESH,
        )
        copy.start()
        return copy

    latest, started, own = {}, [], {}
    for lane in lanes:
        a, part, way = lane
        latest[lane] = send(lane, 0, sources[a].at[block(way, 0), span(a, part, way)])
        started.append(latest[lane])
    for step in range(1, n):
        for lane in lanes:
            a, part, way = lane
            own[lane, step] = pltpu.make_async_copy(
                sources[a].at[block(way, step), span(a, part, way)],
                own_bufs[a].at[way, step - 1, part],
                own_sem.at[a, way, step - 1, part],
            )
            own[lane, step].start()
    for step in range(1, n):
        for lane in lanes:
            a, part, way = lane
            own[lane, step].wait()
            latest[lane].wait_recv()
            total = got_bufs[a][way, step - 1, part].astype(jnp.float32) + own_bufs[a][
                way, step - 1, part
            ].astype(jnp.float32)
            if step == n - 1:
                outs[a][span(a, part, way)] = total.astype(outs[a].dtype)
            else:
                got_bufs[a][way, step - 1, part] = total.astype(got_bufs[a].dtype)
                latest[lane] = send(lane, step, got_bufs[a].at[way, step - 1, part])
                started.append(latest[lane])
    for copy in started:
        copy.wait_send()


def ring_scatter(arrays, n, number, out_dtype, parts=2):
    count = len(arrays)
    copies = (count, 2, n - 1, parts)
    bufs = [
        pltpu.VMEM((2, n - 1, parts, a.shape[1] // 2 // parts, a.shape[2]), a.dtype)
        for a in arrays
    ]
    return pl.pallas_call(
        functools.partial(scatter_kernel, n, parts, count),
        out_shape=[jax.ShapeDtypeStruct(a.shape[1:], out_dtype) for a in arrays],
        in_specs=[ANY] * count,
        out_specs=[pl.BlockSpec(memory_space=pltpu.VMEM)] * count,
        scratch_shapes=bufs + bufs + [pltpu.SemaphoreType.DMA(copies)] * 3,
        compiler_params=pltpu.CompilerParams(
            collective_id=number, has_side_effects=True, vmem_limit_bytes=58 << 20
        ),
        name="ring_scatter",
    )(*arrays)


def finish_kernel(n, counts, *refs):
    few, many = counts
    refs = list(refs)
    take = lambda count: [refs.pop(0) for _ in range(count)]
    blocks, xs, sums, outs = take(few), take(many), take(few), take(many)
    own_bufs, got_bufs = take(few), take(few)
    mines, twins, crosses, gots = take(many), take(many), take(many), take(many)
    near_sem, far_sem, own_sem, pair_sem, cross_sem, ring_sem = refs
    pos, at, sides = seq_ring(n)
    exp = lax.axis_index("exp")
    core, chip = lax.rem(exp, 2), exp // 2
    peer, over = {"exp": exp + 1 - 2 * core}, {"exp": core + 2 * (1 - chip)}
    greet(sides + (peer, over))
    started = []

    def push(source, target, sems, index, to):
        copy = pltpu.make_async_remote_copy(
            src_ref=source,
            dst_ref=target,
            send_sem=sems.at[(0,) + index],
            recv_sem=sems.at[(1,) + index],
            device_id=to,
            device_id_type=MESH,
        )
        copy.start()
        started.append(copy)
        return copy

    def block(way, step):
        return at(pos - 1 - step) if way == 0 else at(pos + 1 + step)

    def fetch(source, target, sem):
        copy = pltpu.make_async_copy(source, target, sem)
        copy.start()
        return copy

    add = lambda *terms: functools.reduce(lambda u, v: u + v, [t.astype(jnp.float32) for t in terms])
    ways = range(2)
    lanes = [(a, way) for a in range(many) for way in ways]
    parts = 2
    rings = [(a, way, part) for part in range(parts) for a in range(few) for way in ways]

    def span(ref, way):
        half = ref.shape[-2] // 2
        return pl.ds(way * half, half)

    def piece(lane):
        a, way, part = lane
        rows = blocks[a].shape[-2] // 2 // parts
        return pl.ds(way * parts * rows + part * rows, rows), pl.ds(part * rows, rows)

    pairs, own, crossing, ring = {}, {}, {}, {}
    for side in range(2):
        for step in range(n):
            for lane in lanes:
                a, way = lane
                place = chip if side else 1 - chip
                where, rows = block(way, step), span(xs[a], way)
                pairs[side, lane, step] = push(
                    xs[a].at[1 - core, place, where, rows],
                    twins[a].at[side, way, step],
                    pair_sem,
                    (0, side) + lane + (0, step),
                    peer,
                )
                own[side, lane, step] = fetch(
                    xs[a].at[core, place, where, rows],
                    mines[a].at[side, way, step],
                    own_sem.at[(side,) + lane + (step,)],
                )
        if side == 0:
            for lane in rings:
                a, way, part = lane
                wide, thin = piece(lane)
                ring[lane] = push(
                    blocks[a].at[block(way, 0), wide],
                    got_bufs[a].at[way, 0, thin],
                    far_sem,
                    lane + (0,),
                    sides[way],
                )
            near = {}
            for step in range(1, n):
                for lane in rings:
                    a, way, part = lane
                    wide, thin = piece(lane)
                    near[lane, step] = fetch(
                        blocks[a].at[block(way, step), wide],
                        own_bufs[a].at[way, step - 1, thin],
                        near_sem.at[lane + (step - 1,)],
                    )

    def scatter(step, which):
        for lane in rings:
            a, way, part = lane
            if part != which:
                continue
            wide, thin = piece(lane)
            near[lane, step].wait()
            ring[lane].wait_recv()
            total = add(got_bufs[a][way, step - 1, thin], own_bufs[a][way, step - 1, thin])
            if step == n - 1:
                sums[a][wide] = total.astype(sums[a].dtype)
            else:
                got_bufs[a][way, step - 1, thin] = total.astype(got_bufs[a].dtype)
                ring[lane] = push(
                    got_bufs[a].at[way, step - 1, thin],
                    got_bufs[a].at[way, step, thin],
                    far_sem,
                    lane + (step,),
                    sides[way],
                )

    for step in range(n):
        for lane in lanes:
            a, way = lane
            own[0, lane, step].wait()
            pairs[0, lane, step].wait_recv()
            mines[a][0, way, step] = add(mines[a][0, way, step], twins[a][0, way, step]).astype(
                mines[a].dtype
            )
            crossing[lane, step] = push(
                mines[a].at[0, way, step],
                crosses[a].at[way, step],
                cross_sem,
                (0,) + lane + (0, step),
                over,
            )
        if step >= n - 2:
            scatter(1, step - n + 2)
    latest = {}
    for step in range(n):
        if step + 2 < n:
            scatter(step + 2, 0)
        for lane in lanes:
            a, way = lane
            own[1, lane, step].wait()
            pairs[1, lane, step].wait_recv()
            crossing[lane, step].wait_recv()
            terms = [mines[a][1, way, step], twins[a][1, way, step], crosses[a][way, step]]
            if step:
                latest[lane].wait_recv()
                terms.append(gots[a][way, step - 1])
            mines[a][1, way, step] = add(*terms).astype(mines[a].dtype)
            if step < n - 1:
                latest[lane] = push(
                    mines[a].at[1, way, step],
                    gots[a].at[way, step],
                    ring_sem,
                    (0,) + lane + (0, step),
                    sides[way],
                )
        if step + 2 < n:
            scatter(step + 2, 1)
    keep, done = [], []
    streams = []
    for a, way in lanes:
        half = xs[a].shape[-2] // 2
        if half % 48 == 0:
            some = half * 2 // 3
            streams += [
                (a, way, 0, way * half, some, False, True),
                (a, way, 1, way * half + some, half - some, False, False),
                (a, way, 2, way * half + some, half - some, True, False),
            ]
        else:
            streams.append((a, way, 0, way * half, half, False, True))
    latest, crossing = {}, {}

    def target_of(stream, step, other):
        a, way, number, first, size = stream[:5]
        where = at(pos - step) if way == 0 else at(pos + step)
        return outs[a].at[core, 1 - chip if other else chip, where, pl.ds(first, size)]

    def hand_on(stream, step):
        a, way, number = stream[:3]
        crossing[stream, step].wait_recv()
        target = target_of(stream, step, True)
        done.append(push(target, target, pair_sem, (1, 1, a, way, number, step), peer))

    for step in range(n):
        for stream in streams:
            a, way, number, first, size, other, always = stream
            if step:
                latest[stream].wait_recv()
            target = target_of(stream, step, other)
            if step or other:
                source = target
            else:
                source = mines[a].at[1, way, n - 1, pl.ds(first - way * (xs[a].shape[-2] // 2), size)]
            if step == 0 and other:
                crossing[streams[streams.index(stream) - 1], 0].wait_recv()
            if step < n - 1:
                latest[stream] = push(
                    source, target, ring_sem, (1, a, way, number, step), sides[way]
                )
            if not other and (always or step == 0):
                crossing[stream, step] = push(
                    source, target, cross_sem, (1, a, way, number, step), over
                )
            done.append(push(source, target, pair_sem, (1, 0, a, way, number, step), peer))
            if step == 0 and not other:
                keep.append(fetch(source, target, own_sem.at[0, a, way, number]))
        if step:
            for stream in streams:
                if stream[6]:
                    hand_on(stream, step - 1)
    for stream in streams:
        if stream[6]:
            hand_on(stream, n - 1)
    for copy in keep:
        copy.wait()
    for copy in done:
        copy.wait_recv()
    for copy in started:
        copy.wait_send()


def finish(blocks, rows_in, small, n, m, number):
    rows, cols = rows_in.shape
    each = rows // (4 * n)
    if m != 4 or rows % (4 * n * 32) or small.shape[0] > 4 * n * 16:
        return (
            ring_scatter(blocks, n, number, jnp.float32),
            *lax.psum((rows_in, small), ("seq", "exp")),
        )
    padded = jnp.pad(small, ((0, 4 * n * 16 - small.shape[0]), (0, 0)))
    arrays = [rows_in.reshape(2, 2, n, each, cols), padded.reshape(2, 2, n, 16, TILE)]
    few, many = len(blocks), len(arrays)
    halves = [(x.shape[-2] // 2, x.shape[-1], x.dtype) for x in blocks + arrays]
    ring_bufs = [pltpu.VMEM((2, n - 1, r, c), t) for r, c, t in halves[:few]]
    two = [pltpu.VMEM((2, 2, n, r, c), t) for r, c, t in halves[few:]]
    one = [pltpu.VMEM((2, n, r, c), t) for r, c, t in halves[few:]]
    dma = pltpu.SemaphoreType.DMA
    results = pl.pallas_call(
        functools.partial(finish_kernel, n, (few, many)),
        out_shape=[jax.ShapeDtypeStruct(x.shape[1:], jnp.float32) for x in blocks]
        + [jax.ShapeDtypeStruct(x.shape, x.dtype) for x in arrays],
        in_specs=[ANY] * (few + many),
        out_specs=[pl.BlockSpec(memory_space=pltpu.VMEM)] * few + [ANY] * many,
        scratch_shapes=ring_bufs * 2
        + two * 2
        + one * 2
        + [
            dma((few, 2, 2, n)),
            dma((2, few, 2, 2, n)),
            dma((2, many, 2, n)),
            dma((2, 2, 2, many, 2, 3, n)),
            dma((2, 2, many, 2, 3, n)),
            dma((2, 2, many, 2, 3, n)),
        ],
        compiler_params=pltpu.CompilerParams(
            collective_id=number, has_side_effects=True, vmem_limit_bytes=58 << 20
        ),
        cost_estimate=cost(120),
        name="finish",
    )(*blocks, *arrays)
    return results[:few], results[few].reshape(rows, cols), results[-1].reshape(-1, TILE)


def dot_last(a, b):
    return lax.dot_general(a, b, (((1,), (1,)), ((), ())), preferred_element_type=jnp.float32)


def dot_first(a, b):
    return lax.dot_general(a, b, (((0,), (0,)), ((), ())), preferred_element_type=jnp.float32)


def dot_plain(a, b):
    return jnp.dot(a, b, preferred_element_type=jnp.float32)


def head_masks(dtype):
    low = lax.broadcasted_iota(jnp.int32, (1, TILE), 1) < HEAD_DIM
    first = jnp.where(low, 1.0, 0.0).astype(jnp.float32)
    return first.astype(dtype), (1.0 - first).astype(dtype)


def split_heads(pair):
    return jnp.concatenate([pair * mask for mask in head_masks(pair.dtype)], axis=0)


def own_bias(tiles, count):
    rows = []
    for r in range(count):
        row = []
        for c in range(count):
            if c == r:
                row.append(tiles[:, TILE:])
            elif c == r - 1:
                row.append(tiles[:, :TILE])
            else:
                row.append(jnp.full((TILE, TILE), 0.0 if c < r else masked_score, jnp.float32))
        rows.append(jnp.concatenate(row, axis=1))
    return jnp.concatenate(rows, axis=0)


def edge_bias(tiles, rows):
    edge = []
    for h in range(2):
        first = jnp.concatenate(
            [jnp.zeros((rows - TILE, TILE), jnp.float32), tiles[h][:, :TILE].T], axis=0
        )
        edge += [first, jnp.zeros((rows, rows - TILE), jnp.float32)]
    return jnp.concatenate(edge, axis=1)


def attend_kernel(causal, block, s_ref, q_ref, k_ref, v_ref, *refs):
    if causal:
        line_ref, low_ref, wide_ref, lse_ref, acc_ref, top_ref = refs
    else:
        low_ref, wide_ref, lse_ref, acc_ref, top_ref = refs
    rows = q_ref.shape[0]
    both = split_heads(q_ref[...])
    ones = jnp.ones((16, block), v_ref.dtype)

    def visit(start, bias, first):
        keys = k_ref[pl.ds(start, block), :]
        values = v_ref[pl.ds(start, block), :]
        t = dot_last(keys, both) * (scale_factor * log2e)
        if bias is not None:
            t = t + bias
        top = jnp.max(t, axis=0, keepdims=True)
        if not first:
            before = top_ref[...]
            top = jnp.maximum(before, top)
            fade = jnp.exp2(before - top)
        top_ref[...] = top
        p = jnp.exp2(t - top).astype(values.dtype)
        part = dot_plain(jnp.concatenate([values.T, ones], axis=0), p)
        if first:
            acc_ref[...] = part
        else:
            acc_ref[...] = acc_ref[...] * fade + part

    if causal:
        s = s_ref[0]
        count = rows // TILE
        tiles = [bias_tile(line_ref, h) for h in range(2)]
        visit(
            pl.multiple_of(s * block, block),
            jnp.concatenate([own_bias(tiles[h], count).T for h in range(2)], axis=1),
            True,
        )

        @pl.when(s > 0)
        def _():
            visit(pl.multiple_of((s - 1) * block, block), edge_bias(tiles, rows), False)

        def far(j, carry):
            visit(pl.multiple_of(j * block, block), None, False)
            return carry

        lax.fori_loop(0, s - 1, far, 0)
    else:
        for j in range(k_ref.shape[0] // block):
            visit(j * block, None, j == 0)
    sums = acc_ref[TILE : TILE + 1, :]
    wide = jnp.concatenate(
        [
            acc_ref[:HEAD_DIM, :rows] / sums[:, :rows],
            acc_ref[HEAD_DIM:TILE, rows:] / sums[:, rows:],
        ],
        axis=0,
    ).T
    wide_ref[...] = wide
    low_ref[...] = wide.astype(low_ref.dtype)
    lse = top_ref[...] + jnp.log2(sums)
    lse_ref[0] = jnp.concatenate([lse[:, :rows], lse[:, rows:]], axis=0)


def attend(seq_at, queries, keys, values, lines):
    rows, total = queries.shape[0], keys.shape[0]
    causal = lines is not None
    block = rows if causal else math.gcd(total, 512)
    pair = pl.BlockSpec((rows, TILE), lambda g: (0, g))
    long = pl.BlockSpec((total, TILE), lambda g: (0, g))
    extra, specs = [], []
    if causal:
        extra, specs = [lines], [pl.BlockSpec((1,) + lines.shape[1:], lambda g: (g, 0, 0))]
    return pl.pallas_call(
        functools.partial(attend_kernel, causal, block),
        grid=(PAIRS,),
        out_shape=[
            jax.ShapeDtypeStruct((rows, D), jnp.bfloat16),
            jax.ShapeDtypeStruct((rows, D), jnp.float32),
            jax.ShapeDtypeStruct((PAIRS, 2, rows), jnp.float32),
        ],
        in_specs=[SMEM, pair, long, long] + specs,
        out_specs=[pair, pair, pl.BlockSpec((1, 2, rows), lambda g: (g, 0, 0))],
        scratch_shapes=[
            pltpu.VMEM((TILE + 16, 2 * rows), jnp.float32),
            pltpu.VMEM((1, 2 * rows), jnp.float32),
        ],
        compiler_params=pltpu.CompilerParams(vmem_limit_bytes=48 << 20),
        cost_estimate=cost(40 if causal else 10),
        name="attend_self" if causal else "attend_cross",
    )(seq_at, queries, keys, values, *extra)


def attend_back_kernel(causal, block, s_ref, q_ref, k_ref, v_ref, up_ref, wide_ref, lse_ref, *refs):
    if causal:
        line_ref, dq_ref, dk_ref, dv_ref, near_ref, sum_ref, acc_ref = refs
    else:
        dq_ref, dk_ref, dv_ref, acc_ref = refs
    rows = q_ref.shape[0]
    both = split_heads(q_ref[...])
    up = up_ref[...]
    up_both = split_heads(up)
    turned = (up.astype(jnp.float32) * wide_ref[...]).T
    delta = jnp.concatenate(
        [
            jnp.sum(turned[:HEAD_DIM], axis=0, keepdims=True),
            jnp.sum(turned[HEAD_DIM:], axis=0, keepdims=True),
        ],
        axis=1,
    )
    lse = jnp.concatenate([lse_ref[0, :1], lse_ref[0, 1:]], axis=1)
    ones = jnp.ones((16, block), k_ref.dtype)

    def visit(start, bias, first):
        keys = k_ref[pl.ds(start, block), :]
        values = v_ref[pl.ds(start, block), :]
        t = dot_last(keys, both) * (scale_factor * log2e)
        if bias is not None:
            t = t + bias
        p = jnp.exp2(t - lse)
        ds = (p * (dot_last(values, up_both) - delta)).astype(keys.dtype)
        dv_ref[pl.ds(start, block), :] = dot_plain(p.astype(keys.dtype), up_both).astype(
            dv_ref.dtype
        )
        dk_ref[pl.ds(start, block), :] = (dot_plain(ds, both) * scale_factor).astype(dk_ref.dtype)
        part = dot_plain(jnp.concatenate([keys.T, ones], axis=0), ds)
        if first:
            acc_ref[...] = part
        else:
            acc_ref[...] += part
        return ds

    if causal:
        s = s_ref[0]
        count = rows // TILE
        tiles = [bias_tile(line_ref, h) for h in range(2)]
        ds = visit(
            pl.multiple_of(s * block, block),
            jnp.concatenate([own_bias(tiles[h], count).T for h in range(2)], axis=1),
            True,
        )
        for h in range(2):
            same = before = jnp.zeros((TILE, TILE), jnp.float32)
            for r in range(count):
                columns = slice(h * rows + r * TILE, h * rows + (r + 1) * TILE)
                same = same + ds[r * TILE : (r + 1) * TILE, columns].astype(jnp.float32)
                if r:
                    before = before + ds[(r - 1) * TILE : r * TILE, columns].astype(jnp.float32)
            near_ref[h, :TILE] = before
            near_ref[h, TILE:] = same

        @pl.when(s > 0)
        def _():
            ds = visit(pl.multiple_of((s - 1) * block, block), edge_bias(tiles, rows), False)
            for h in range(2):
                near_ref[h, :TILE] += ds[rows - TILE :, h * rows : h * rows + TILE].astype(
                    jnp.float32
                )

        def far(j, carry):
            visit(pl.multiple_of(j * block, block), None, False)
            return carry

        lax.fori_loop(0, s - 1, far, 0)

        def beyond(j, carry):
            start = pl.multiple_of(j * block, block)
            dk_ref[pl.ds(start, block), :] = jnp.zeros((block, TILE), dk_ref.dtype)
            dv_ref[pl.ds(start, block), :] = jnp.zeros((block, TILE), dv_ref.dtype)
            return carry

        lax.fori_loop(s + 1, k_ref.shape[0] // block, beyond, 0)
        sum_ref[0] = jnp.concatenate(
            [acc_ref[TILE : TILE + 1, :rows], acc_ref[TILE : TILE + 1, rows:]], axis=0
        )
    else:
        for j in range(k_ref.shape[0] // block):
            visit(j * block, None, j == 0)
    dq = jnp.concatenate([acc_ref[:HEAD_DIM, :rows], acc_ref[HEAD_DIM:TILE, rows:]], axis=0)
    dq_ref[...] = (dq.T * scale_factor).astype(dq_ref.dtype)


def attend_back(seq_at, queries, keys, values, upstream, wide, lse, lines):
    rows, total = queries.shape[0], keys.shape[0]
    causal = lines is not None
    block = rows if causal else math.gcd(total, 512)
    pair = pl.BlockSpec((rows, TILE), lambda g: (0, g))
    long = pl.BlockSpec((total, TILE), lambda g: (0, g))
    line = pl.BlockSpec((1, 2, rows), lambda g: (g, 0, 0))
    extra, specs, shapes, out_specs = [], [], [], []
    if causal:
        extra, specs = [lines], [pl.BlockSpec((1,) + lines.shape[1:], lambda g: (g, 0, 0))]
        shapes = [
            jax.ShapeDtypeStruct((HEADS, 2 * TILE, TILE), jnp.float32),
            jax.ShapeDtypeStruct((PAIRS, 2, rows), jnp.float32),
        ]
        out_specs = [pl.BlockSpec((2, 2 * TILE, TILE), lambda g: (g, 0, 0)), line]
    return pl.pallas_call(
        functools.partial(attend_back_kernel, causal, block),
        grid=(PAIRS,),
        out_shape=[
            jax.ShapeDtypeStruct((rows, D), jnp.bfloat16),
            jax.ShapeDtypeStruct((total, D), jnp.bfloat16),
            jax.ShapeDtypeStruct((total, D), jnp.bfloat16),
        ]
        + shapes,
        in_specs=[SMEM, pair, long, long, pair, pair, line] + specs,
        out_specs=[pair, long, long] + out_specs,
        scratch_shapes=[pltpu.VMEM((TILE + 16, 2 * rows), jnp.float32)],
        compiler_params=pltpu.CompilerParams(vmem_limit_bytes=48 << 20),
        cost_estimate=cost(48 if causal else 15),
        name="attend_self_back" if causal else "attend_cross_back",
    )(seq_at, queries, keys, values, upstream, wide, lse, *extra)


def bias_lines(bias_table):
    at = jnp.arange(3 * TILE, dtype=jnp.int32)
    distance = jnp.where(at <= 2 * TILE, TILE - at, 4 * TILE - at)
    table = (bias_table - bias_table[NBUCKET - 1 :]) * log2e
    terms = jnp.broadcast_to(table[0][:, None], (HEADS, 3 * TILE))
    for number, threshold in enumerate(bucket_edges()):
        terms = jnp.where((distance >= threshold)[None], table[number + 1][:, None], terms)
    return jnp.where((distance >= 0)[None], terms, masked_score).reshape(PAIRS, 2, 3 * TILE)


def bias_tile(line_ref, h):
    line = jnp.broadcast_to(line_ref[0, h : h + 1, :], (TILE, 3 * TILE))
    return pltpu.roll(line, 0, 1, stride=1, stride_axis=0)[:, : 2 * TILE]


def bias_gradient(near, sums):
    distance = (
        TILE
        + jnp.arange(TILE, dtype=jnp.int32)[None, :]
        - jnp.arange(2 * TILE, dtype=jnp.int32)[:, None]
    )
    bucket = jnp.zeros(distance.shape, jnp.int32)
    for threshold in bucket_edges():
        bucket = bucket + (distance >= threshold).astype(jnp.int32)
    onehot = (
        bucket.reshape(-1)[None, :] == jnp.arange(NBUCKET, dtype=jnp.int32)[:, None]
    ).astype(jnp.float32)
    flat = near.reshape(HEADS, -1)
    table = lax.dot_general(
        onehot, flat, (((1,), (1,)), ((), ())), precision=highest
    )
    far = jnp.sum(sums, axis=-1).reshape(HEADS) - jnp.sum(flat, axis=-1)
    last = jnp.arange(NBUCKET, dtype=jnp.int32)[:, None] == NBUCKET - 1
    return table + jnp.where(last, far[None, :], 0.0)


def expert_kernel(n, m, slots, *refs):
    x_ref, maps, result_ref, grads = refs[0], refs[1:9], refs[9], refs[10:16]
    rows, parts, backs, up_all, down_all, act_all, du_all = refs[16:23]
    grad_bufs, far_bufs = refs[23:31], refs[31:33]
    map_sem, own_sem, grad_sem, go_sem, back_sem, term_sem = refs[33:]
    seq, exp = lax.axis_index("seq"), lax.axis_index("exp")
    groups, count = n // QUAD, x_ref.shape[1] // slots
    batch = max(1, 128 // slots)
    far = [(g, k) for g in range(1, groups) for k in range(m)]
    moves = far + [(0, k) for k in range(1, m)]
    source_of = lambda k: lax.rem(exp + m - k, m)

    def push(source, target, sems, g, k, to_seq, to_exp):
        copy = pltpu.make_async_remote_copy(
            src_ref=source,
            dst_ref=target,
            send_sem=sems.at[0, g, k],
            recv_sem=sems.at[1, g, k],
            device_id={"seq": to_seq, "exp": to_exp},
            device_id_type=MESH,
        )
        copy.start()
        return copy

    def place(g, k):
        return lax.rem(seq + g * QUAD, n), lax.rem(exp + k, m)

    to_next, to_last = quad_moves(n)
    side = {"next": look_up(seq, [b for _, b in to_next]), "last": look_up(seq, [b for _, b in to_last])}
    greet(
        [dict(zip(("seq", "exp"), place(g, k))) for g, k in moves]
        + [{"seq": side["next"], "exp": exp}, {"seq": side["last"], "exp": exp}]
    )
    going = {}
    for g, k in moves:
        to_seq, to_exp = place(g, k)
        going[g, k] = push(x_ref.at[to_exp], rows.at[g, exp], go_sem, g, k, to_seq, to_exp)
    own = pltpu.make_async_copy(x_ref.at[exp], rows.at[0, exp], own_sem.at[0])
    own.start()
    fetched = []
    for j in range(QUAD):
        for at, (source, target) in enumerate(((maps[2 * j], up_all), (maps[2 * j + 1], down_all))):
            copy = pltpu.make_async_copy(source, target.at[j], map_sem.at[at, j])
            copy.start()
            fetched.append(copy)
    for copy in fetched:
        copy.wait()
    own.wait()
    slope = math.sqrt(2.0 / math.pi)
    coming = {}

    def work(g, first, last):
        for k in range(first, last):
            if g or k:
                going[g, k].wait_recv()
        size = (last - first) * slots
        base = (g * m + first) * slots

        def one(e, carry):
            start = pl.multiple_of(e * slots, slots)
            piece = jnp.concatenate(
                [rows[g, source_of(k), pl.ds(start, slots), :] for k in range(first, last)], axis=0
            )
            tokens, upstream = piece[:, :D], piece[:, D:]
            result = back = None
            for j in range(QUAD):
                up_map, down_map = up_all[j, e], down_all[j, e]
                u = dot_plain(tokens, up_map)
                square = u * u
                bend = jnp.tanh(slope * (u + 0.044715 * (square * u)))
                half = 0.5 * (1.0 + bend)
                act = (u * half).astype(tokens.dtype)
                rise = half + 0.5 * u * (1.0 - bend * bend) * (
                    slope * (1.0 + 3 * 0.044715 * square)
                )
                du = (dot_plain(upstream, down_map) * rise).astype(tokens.dtype)
                act_all[e, j, base : base + size] = act
                du_all[e, j, base : base + size] = du
                y, dn = dot_last(act, down_map), dot_last(du, up_map)
                result = y if result is None else result + y
                back = dn if back is None else back + dn
            for i, k in enumerate(range(first, last)):
                span = slice(i * slots, (i + 1) * slots)
                where = (g, source_of(k), pl.ds(start, slots))
                parts[where + (slice(0, D),)] = result[span].astype(parts.dtype)
                parts[where + (slice(D, 2 * D),)] = back[span].astype(parts.dtype)
            return carry

        lax.fori_loop(0, count, one, 0)
        for k in range(first, last):
            if g or k:
                source = source_of(k)
                coming[g, k] = push(
                    parts.at[g, source],
                    backs.at[g, exp],
                    back_sem,
                    g,
                    k,
                    lax.rem(seq + n - g * QUAD, n),
                    source,
                )

    work(0, 0, m)
    for g in range(1, groups):
        for first in range(0, m, batch):
            work(g, first, min(m, first + batch))

    total = groups * m * slots

    def weigh(j):
        def one(e, carry):
            start = pl.multiple_of(e * slots, slots)
            piece = jnp.concatenate(
                [
                    rows[g, source_of(k), pl.ds(start, slots), :]
                    for g in range(groups)
                    for k in range(m)
                ],
                axis=0,
            )
            tokens, upstream = piece[:, :D], piece[:, D:]
            up_buf, down_buf = grad_bufs[2 * j], grad_bufs[2 * j + 1]
            up_buf[e] = dot_first(tokens, du_all[e, j, :total]).astype(up_buf.dtype)
            down_buf[e] = dot_first(upstream, act_all[e, j, :total]).astype(down_buf.dtype)
            return carry

        lax.fori_loop(0, count, one, 0)

    def term(source, target, number, to):
        return push(source, target, term_sem, 0, number, side[to], exp)

    def store(source, number):
        copy = pltpu.make_async_copy(source, grads[number], grad_sem.at[number])
        copy.start()
        return copy

    weigh(3)
    terms_out = [
        term(grad_bufs[6], far_bufs[0], 0, "next"),
        term(grad_bufs[7], far_bufs[1], 1, "last"),
    ]
    weigh(1)
    weigh(2)
    weigh(0)
    stored = [
        store(grad_bufs[i], number) for number, i in ((0, 0), (1, 1), (4, 2), (5, 5))
    ]
    for number, (buf, far_buf) in enumerate(((grad_bufs[4], far_bufs[0]), (grad_bufs[3], far_bufs[1]))):
        terms_out[number].wait_recv()
        buf[...] = (buf[...].astype(jnp.float32) + far_buf[...].astype(jnp.float32)).astype(buf.dtype)
        stored.append(store(buf, 2 + number))
    for k in range(m):
        where = source_of(k)
        terms = []
        for g in range(groups):
            back_k = (m - k) % m
            if g == 0 and k == 0:
                terms.append(parts[0, exp])
            else:
                coming[g, back_k].wait_recv()
                terms.append(backs[g, where])
        total_row = terms[0].astype(jnp.float32)
        for term in terms[1:]:
            total_row = total_row + term.astype(jnp.float32)
        result_ref[where] = total_row.astype(result_ref.dtype)
    for copy in stored:
        copy.wait()
    for copy in terms_out:
        copy.wait_send()
    for copies in (going, coming):
        for copy in copies.values():
            copy.wait_send()


def run_experts(x, maps, n, m, slots, number):
    groups = n // QUAD
    count, _, hidden = maps[0].shape
    total = groups * m * slots
    big = pltpu.VMEM((groups,) + x.shape, x.dtype)
    stack = pltpu.VMEM((QUAD,) + maps[0].shape, x.dtype)
    kept = pltpu.VMEM((count, QUAD, total, hidden), x.dtype)
    grads = [(w.shape, jnp.float32 if i < 2 else jnp.bfloat16) for i, w in enumerate(maps)]
    dma = pltpu.SemaphoreType.DMA
    return pl.pallas_call(
        functools.partial(expert_kernel, n, m, slots),
        out_shape=[jax.ShapeDtypeStruct(x.shape, x.dtype)]
        + [jax.ShapeDtypeStruct(shape, dtype) for shape, dtype in grads[:6]],
        in_specs=[ANY] * (1 + len(maps)),
        out_specs=[pl.BlockSpec(memory_space=pltpu.VMEM)] + [ANY] * 6,
        scratch_shapes=[big] * 3
        + [stack] * 2
        + [kept] * 2
        + [pltpu.VMEM(shape, dtype) for shape, dtype in grads + grads[6:]]
        + [
            dma((2, QUAD)),
            dma((1,)),
            dma((6,)),
            dma((2, groups, m)),
            dma((2, groups, m)),
            dma((2, 1, 2)),
        ],
        compiler_params=pltpu.CompilerParams(
            collective_id=number, has_side_effects=True, vmem_limit_bytes=60 << 20
        ),
        cost_estimate=cost(150),
        name="run_experts",
    )(x, *maps)


QUAD = 4


def quad_moves(n):
    ring = (0, 1, 3, 2)
    step = lambda i, by: i - i % QUAD + ring[(ring.index(i % QUAD) + by) % QUAD]
    return [(i, step(i, 1)) for i in range(n)], [(i, step(i, -1)) for i in range(n)]


def project(source, matrix):
    return jnp.dot(source, matrix, preferred_element_type=jnp.float32).astype(jnp.bfloat16)


def weight_grad(source, upstream):
    return jnp.einsum("td,te->de", source, upstream, preferred_element_type=jnp.float32).astype(
        jnp.bfloat16
    )


def input_grad(upstream, matrix):
    return jnp.einsum("te,de->td", upstream, matrix, preferred_element_type=jnp.float32)


def body(
    n,
    m,
    hidden_in,
    memory,
    proj_in,
    proj_out,
    norm_gains,
    rel_bias,
    router,
    expert_choice,
    expert_in,
    expert_out,
    cotangent,
):
    tokens = hidden_in[0].astype(jnp.float32)
    memory_rows = memory[0]
    memory_count = memory_rows.shape[0]
    gain_rows = norm_gains.astype(jnp.float32)
    token_count = tokens.shape[0]
    seq_at = lax.axis_index("seq").astype(jnp.int32).reshape(1)
    normed_self = rms_apply(tokens, gain_rows[0]).astype(jnp.bfloat16)
    lines = bias_lines(rel_bias)

    normed_all, memory_all, queries, key_all, value_all, memory_key_all, memory_value_all = (
        gather_projected(normed_self, memory_rows, proj_in, n, 1)
    )
    to_next, to_last = quad_moves(n)
    in_own, out_own, normed_all = lax.optimization_barrier((expert_in, expert_out, normed_all))
    in_last, out_last = (lax.ppermute(w, "seq", to_next) for w in (in_own, out_own))
    in_next, out_next = (lax.ppermute(w, "seq", to_last) for w in (in_own, out_own))
    normed_all = normed_all.reshape(n * token_count, D)
    memory_all = memory_all.reshape(n * memory_count, D)
    key_all, value_all = (x.reshape(n * token_count, D) for x in (key_all, value_all))
    memory_key_all, memory_value_all = (
        x.reshape(n * memory_count, D) for x in (memory_key_all, memory_value_all)
    )
    attended_self_low, attended_self, lse_self = attend(
        seq_at, queries, key_all, value_all, lines
    )
    attended_self_low, in_last, out_next = lax.optimization_barrier(
        (attended_self_low, in_last, out_next)
    )
    in_far = lax.ppermute(in_last, "seq", to_next)
    out_far = lax.ppermute(out_next, "seq", to_last)
    after_self = tokens + jnp.dot(
        attended_self_low, proj_out[0], preferred_element_type=jnp.float32
    )

    normed_cross = rms_apply(after_self, gain_rows[1]).astype(jnp.bfloat16)
    cross_queries = project(normed_cross, proj_in[3])
    attended_cross_low, attended_cross, lse_cross = attend(
        seq_at, cross_queries, memory_key_all, memory_value_all, None
    )
    after_cross = after_self + jnp.dot(
        attended_cross_low, proj_out[1], preferred_element_type=jnp.float32
    )

    mixed_low = rms_apply(after_cross, gain_rows[2]).astype(jnp.bfloat16)
    softmax_probs = jax.nn.softmax(
        jnp.dot(mixed_low, router, preferred_element_type=jnp.float32), axis=-1
    )
    expert_count = router.shape[1]
    local_experts = expert_in.shape[0]
    capacity = max(2, 5 * token_count // (4 * expert_count))
    chosen = expert_choice[0, :, 0]
    onehot_int = (chosen[:, None] == jnp.arange(expert_count, dtype=jnp.int32)[None, :]).astype(
        jnp.int32
    )
    onehot = onehot_int.astype(jnp.float32)
    gate_prob = jnp.sum(softmax_probs * onehot, axis=-1)
    slot_index = jnp.sum(jnp.cumsum(onehot_int, axis=0) * onehot_int, axis=-1) - 1
    is_kept = slot_index < capacity
    slots = -(-capacity // 16) * 16
    place = jnp.where(is_kept, chosen * slots + slot_index, -1)
    dispatch = (
        place[:, None] == jnp.arange(expert_count * slots, dtype=jnp.int32)[None, :]
    ).astype(jnp.bfloat16)
    dispatched = jnp.sum(onehot_int * is_kept[:, None].astype(jnp.int32), axis=0)
    tally_counts = jnp.stack(
        [dispatched, jnp.sum(onehot_int, axis=0) - dispatched], axis=0
    ).reshape(1, 1, 2, expert_count)

    grad_top = cotangent[0].astype(jnp.float32)
    scaled = (gate_prob[:, None] * grad_top).astype(jnp.bfloat16)
    sent_rows = (
        jnp.einsum(
            "tx,td->xd",
            dispatch,
            jnp.concatenate([mixed_low, scaled], axis=1),
            preferred_element_type=jnp.float32,
        )
        .astype(jnp.bfloat16)
        .reshape(m, local_experts * slots, 2 * D)
    )
    sent_rows, in_far, out_far = lax.optimization_barrier((sent_rows, in_far, out_far))
    maps = [in_own, out_own, in_last, out_last, in_next, out_next, in_far, out_far]
    returned, *terms = run_experts(sent_rows, maps, n, m, slots, 2)
    returned = returned.reshape(expert_count * slots, 2 * D)
    gin_own, gout_own, gin_next, gout_last, gin_last, gout_next = terms
    gout_next = lax.ppermute(gout_next, "seq", to_next)
    gin_last = lax.ppermute(gin_last, "seq", to_last)
    routed = jnp.dot(dispatch, returned, preferred_element_type=jnp.float32)
    combined, grad_mixed = routed[:, :D], routed[:, D:]
    output = (after_cross + gate_prob[:, None] * combined).astype(jnp.bfloat16)

    grad_gate = jnp.sum(grad_top * combined, axis=-1)
    grad_logits = softmax_probs * (onehot - gate_prob[:, None]) * grad_gate[:, None]
    grad_router = jnp.einsum(
        "td,te->de", mixed_low.astype(jnp.float32), grad_logits, precision=highest
    )
    grad_mixed = grad_mixed + jnp.einsum(
        "te,de->td", grad_logits, router.astype(jnp.float32), precision=highest
    )
    grad_cross_part, grad_gain_mix = rms_backward(after_cross, gain_rows[2], grad_mixed)
    grad_after_cross = grad_top + grad_cross_part

    grad_cross_low = grad_after_cross.astype(jnp.bfloat16)
    grad_out_cross = weight_grad(attended_cross_low, grad_cross_low)
    grad_attended_cross = input_grad(grad_cross_low, proj_out[1]).astype(jnp.bfloat16)
    grad_cross_query, grad_memory_keys, grad_memory_values = attend_back(
        seq_at,
        cross_queries,
        memory_key_all,
        memory_value_all,
        grad_attended_cross,
        attended_cross,
        lse_cross,
        None,
    )
    grad_cross_query, gin_last, gout_next, gin_next, gout_last = lax.optimization_barrier(
        (grad_cross_query, gin_last, gout_next, gin_next, gout_last)
    )
    gin_next = lax.ppermute(gin_next, "seq", to_next)
    gout_last = lax.ppermute(gout_last, "seq", to_last)
    grad_query_cross = weight_grad(normed_cross, grad_cross_query)
    grad_self_part, grad_gain_cross = rms_backward(
        after_self, gain_rows[1], input_grad(grad_cross_query, proj_in[3])
    )
    grad_after_self = grad_after_cross + grad_self_part
    grad_memory_part = (
        input_grad(grad_memory_keys, proj_in[4]) + input_grad(grad_memory_values, proj_in[5])
    ).astype(jnp.bfloat16)

    grad_self_low = grad_after_self.astype(jnp.bfloat16)
    grad_out_self = weight_grad(attended_self_low, grad_self_low)
    grad_attended_self = input_grad(grad_self_low, proj_out[0]).astype(jnp.bfloat16)
    early = [
        grad_query_cross,
        weight_grad(memory_all, grad_memory_keys),
        weight_grad(memory_all, grad_memory_values),
        grad_out_self,
        grad_out_cross,
    ]
    grad_attended_self, grad_memory_part, *early = lax.optimization_barrier(
        (grad_attended_self, grad_memory_part, *early)
    )
    grad_self_query, grad_keys, grad_values, near, sums = attend_back(
        seq_at,
        queries,
        key_all,
        value_all,
        grad_attended_self,
        attended_self,
        lse_self,
        lines,
    )
    grad_self_query, grad_keys, grad_values, near, sums, gout_last, gin_next = (
        lax.optimization_barrier(
            (grad_self_query, grad_keys, grad_values, near, sums, gout_last, gin_next)
        )
    )
    grad_expert_in = gin_own + gin_last.astype(jnp.float32) + gin_next.astype(jnp.float32)
    grad_expert_out = gout_own + gout_last.astype(jnp.float32) + gout_next.astype(jnp.float32)
    grad_table = bias_gradient(near, sums)
    grad_normed_query = input_grad(grad_self_query, proj_in[0])
    grad_normed_part = (
        input_grad(grad_keys, proj_in[1]) + input_grad(grad_values, proj_in[2])
    ).astype(jnp.bfloat16)
    grad_normed_part = lax.optimization_barrier(grad_normed_part)
    grad_gain_self = (
        jnp.sum(grad_normed_part.astype(jnp.float32) * normed_all.astype(jnp.float32), axis=0)
        + jnp.sum(grad_normed_query * normed_self.astype(jnp.float32), axis=0)
    ) / gain_rows[0]

    grads = jnp.concatenate(
        [
            weight_grad(normed_self, grad_self_query),
            weight_grad(normed_all, grad_keys),
            weight_grad(normed_all, grad_values),
            *early,
        ]
    )
    grad_gains = jnp.stack([grad_gain_self, grad_gain_cross, grad_gain_mix])
    small = [
        grad_gains.reshape(-1, TILE),
        grad_router.T.reshape(-1, TILE),
        jnp.pad(grad_table, ((0, 0), (0, TILE - HEADS))),
    ]
    ends = [small[0].shape[0], small[0].shape[0] + small[1].shape[0]]
    (grad_normed_own, grad_memory), grads, small = finish(
        [
            grad_normed_part.reshape(n, token_count, D),
            grad_memory_part.reshape(n, memory_count, D),
        ],
        grads,
        jnp.concatenate(small),
        n,
        m,
        4,
    )
    grads = grads.reshape(-1, D, D).astype(jnp.float32)
    grad_token_part, _ = rms_backward(tokens, gain_rows[0], grad_normed_query + grad_normed_own)
    grad_in = (grad_after_self + grad_token_part).astype(jnp.bfloat16)
    return (
        output.reshape(1, token_count, D),
        grad_in.reshape(1, token_count, D),
        grad_memory.astype(jnp.bfloat16).reshape(1, memory_count, D),
        grads[:6],
        grads[6:],
        small[: ends[0]].reshape(grad_gains.shape),
        small[ends[1] : ends[1] + NBUCKET, :HEADS],
        small[ends[0] : ends[1]].reshape(expert_count, D).T,
        grad_expert_in,
        grad_expert_out,
        tally_counts,
    )


def solution(mesh):
    rows = P("exp", "seq", None)
    hidden = P("exp", None, "seq")
    return jax.shard_map(
        functools.partial(body, mesh.shape["seq"], mesh.shape["exp"]),
        mesh=mesh,
        in_specs=(rows, rows, P(), P(), P(), P(), P(), rows, hidden, hidden, rows),
        out_specs=(
            rows,
            rows,
            rows,
            P(),
            P(),
            P(),
            P(),
            P(),
            hidden,
            hidden,
            P("exp", "seq", None, None),
        ),
        check_vma=False,
    )
```

```python
import functools
import math

import jax
import jax.numpy as jnp
from jax import lax
from jax.experimental import pallas as pl
from jax.experimental.pallas import tpu as pltpu
from jax.sharding import PartitionSpec as P

D = 768
HEADS = 12
HEAD_DIM = 64
NBUCKET = 32
MAXDIST = 128
TILE = 128
PAIRS = HEADS * HEAD_DIM // TILE

MESH = pl.DeviceIdType.MESH
ANY = pl.BlockSpec(memory_space=pl.ANY)
SMEM = pl.BlockSpec(memory_space=pltpu.SMEM)

norm_eps = 1e-06
masked_score = -1e30
highest = lax.Precision.HIGHEST
log2e = 1.0 / math.log(2.0)
scale_factor = HEAD_DIM ** (-0.5)


def bucket_edges():
    half_count = NBUCKET // 2
    thresholds = []
    for bucket_number in range(1, NBUCKET):
        if bucket_number < half_count:
            thresholds.append(bucket_number)
        else:
            thresholds.append(
                int(
                    half_count
                    * (MAXDIST / half_count) ** ((bucket_number - half_count) / half_count)
                )
            )
    return thresholds


def rms_apply(values, gain_row):
    return (
        values * lax.rsqrt(jnp.mean(values * values, axis=-1, keepdims=True) + norm_eps) * gain_row
    )


def rms_backward(values, gain_row, upstream):
    _, pullback = jax.vjp(rms_apply, values, gain_row)
    return pullback(upstream)


def cost(us):
    return pl.CostEstimate(flops=us * 10**9, bytes_accessed=0, transcendentals=0)


def seq_cycle(n):
    cols = n // 4
    if n % 4 or cols < 2:
        return list(range(n))
    order = [0]
    for row in range(4):
        span = range(1, cols) if row % 2 == 0 else range(cols - 1, 0, -1)
        order += [row * cols + col for col in span]
    return order + [3 * cols, 2 * cols, cols]


def look_up(index, table):
    value = jnp.int32(table[0])
    for number, entry in enumerate(table[1:], 1):
        value = jnp.where(index == number, jnp.int32(entry), value)
    return value


def greet(others):
    barrier = pltpu.get_barrier_semaphore()
    for other in others:
        pl.semaphore_signal(barrier, inc=1, device_id=other, device_id_type=MESH)
    pl.semaphore_wait(barrier, len(others))


def seq_ring(n):
    order = seq_cycle(n)
    pos = look_up(lax.axis_index("seq"), [order.index(i) for i in range(n)])

    def at(place):
        return look_up(lax.rem(place + 4 * n, n), order)

    return pos, at, ({"seq": at(pos + 1)}, {"seq": at(pos - 1)})


def gather_kernel(n, parts, *refs):
    sources, proj_ref, outs = refs[:2], refs[2], refs[3:10]
    lands, w_buf, bufs = refs[10:12], refs[12], refs[13:18]
    own_sem, w_sem, send_sem, recv_sem, store_sem = refs[18:]
    pos, at, sides = seq_ring(n)
    me = at(pos)
    greet(sides)
    own = [pltpu.make_async_copy(sources[a], lands[a].at[me], own_sem.at[a]) for a in range(2)]
    weights = [
        pltpu.make_async_copy(proj_ref.at[number], w_buf.at[i], w_sem.at[i])
        for i, number in enumerate((0, 1, 2, 4, 5))
    ]
    started, latest, stored = [], {}, []

    def pass_on(step):
        for part in range(parts):
            for a in range(2):
                rows = sources[a].shape[0] // 2 // parts
                for way in range(2):
                    if step:
                        latest[a, way, part].wait_recv()
                    if step == n - 1:
                        continue
                    block = at(pos - step) if way == 0 else at(pos + step)
                    span = pl.ds((way * parts + part) * rows, rows)
                    copy = pltpu.make_async_remote_copy(
                        src_ref=lands[a].at[block, span] if step else sources[a].at[span],
                        dst_ref=lands[a].at[block, span],
                        send_sem=send_sem.at[a, way, step, part],
                        recv_sem=recv_sem.at[a, way, step, part],
                        device_id=sides[way],
                        device_id_type=MESH,
                    )
                    copy.start()
                    started.append(copy)
                    latest[a, way, part] = copy

    def store(source, target, number, step, way):
        copy = pltpu.make_async_copy(source, target, store_sem.at[number, step, way])
        copy.start()
        stored.append(copy)

    def work(step):
        blocks = (at(pos - step), at(pos + step))
        for a in range(2):
            half = sources[a].shape[0] // 2
            spans = (pl.ds(0, half), pl.ds(half, half))
            rows = jnp.concatenate([lands[a][blocks[way], spans[way], :] for way in range(2)], axis=0)
            for i in range(2):
                buf = bufs[1 + 2 * a + i]
                made = dot_plain(rows, w_buf[1 + 2 * a + i]).astype(buf.dtype)
                for way in range(2):
                    buf[blocks[way], spans[way], :] = made[way * half : (way + 1) * half]
            for way in range(2):
                where = (blocks[way], spans[way])
                store(lands[a].at[where], outs[a].at[where], a, step, way)
                for i in range(2):
                    number = 1 + 2 * a + i
                    store(bufs[number].at[where], outs[2 + number].at[where], 2 + number, step, way)

    pass_on(0)
    for copy in own + weights:
        copy.start()
    for copy in own + weights:
        copy.wait()
    bufs[0][...] = dot_plain(lands[0][me], w_buf[0]).astype(bufs[0].dtype)
    store(bufs[0], outs[2], 2, 0, 0)
    work(0)
    for step in range(1, n):
        pass_on(step)
        work(step)
    for copy in started:
        copy.wait_send()
    for copy in stored:
        copy.wait()


def gather_projected(tokens, memory_rows, proj_in, n, number, parts=2):
    both = (tokens, memory_rows)
    copies = (2, 2, n - 1, parts)
    wide = [(n,) + x.shape for x in both]
    shapes = wide + [tokens.shape] + [wide[0]] * 2 + [wide[1]] * 2
    dma = pltpu.SemaphoreType.DMA
    return pl.pallas_call(
        functools.partial(gather_kernel, n, parts),
        out_shape=[jax.ShapeDtypeStruct(shape, tokens.dtype) for shape in shapes],
        in_specs=[ANY] * 3,
        out_specs=[ANY] * 7,
        scratch_shapes=[pltpu.VMEM(shape, tokens.dtype) for shape in wide]
        + [pltpu.VMEM((5,) + proj_in.shape[1:], tokens.dtype)]
        + [pltpu.VMEM(shape, tokens.dtype) for shape in shapes[2:]]
        + [dma((2,)), dma((5,)), dma(copies), dma(copies), dma((7, n, 2))],
        compiler_params=pltpu.CompilerParams(
            collective_id=number, has_side_effects=True, vmem_limit_bytes=58 << 20
        ),
        cost_estimate=cost(60),
        name="gather_projected",
    )(tokens, memory_rows, proj_in)


def scatter_kernel(n, parts, count, *refs):
    sources, outs = refs[:count], refs[count : 2 * count]
    own_bufs, got_bufs = refs[2 * count : 3 * count], refs[3 * count : 4 * count]
    own_sem, send_sem, recv_sem = refs[4 * count :]
    pos, at, sides = seq_ring(n)
    greet(sides)
    lanes = [(a, part, way) for a in range(count) for part in range(parts) for way in range(2)]

    def span(a, part, way):
        rows = sources[a].shape[1] // 2 // parts
        return pl.ds((way * parts + part) * rows, rows)

    def block(way, step):
        return at(pos - 1 - step) if way == 0 else at(pos + 1 + step)

    def send(lane, step, source):
        a, part, way = lane
        copy = pltpu.make_async_remote_copy(
            src_ref=source,
            dst_ref=got_bufs[a].at[way, step, part],
            send_sem=send_sem.at[a, way, step, part],
            recv_sem=recv_sem.at[a, way, step, part],
            device_id=sides[way],
            device_id_type=MESH,
        )
        copy.start()
        return copy

    latest, started, own = {}, [], {}
    for lane in lanes:
        a, part, way = lane
        latest[lane] = send(lane, 0, sources[a].at[block(way, 0), span(a, part, way)])
        started.append(latest[lane])
    for step in range(1, n):
        for lane in lanes:
            a, part, way = lane
            own[lane, step] = pltpu.make_async_copy(
                sources[a].at[block(way, step), span(a, part, way)],
                own_bufs[a].at[way, step - 1, part],
                own_sem.at[a, way, step - 1, part],
            )
            own[lane, step].start()
    for step in range(1, n):
        for lane in lanes:
            a, part, way = lane
            own[lane, step].wait()
            latest[lane].wait_recv()
            total = got_bufs[a][way, step - 1, part].astype(jnp.float32) + own_bufs[a][
                way, step - 1, part
            ].astype(jnp.float32)
            if step == n - 1:
                outs[a][span(a, part, way)] = total.astype(outs[a].dtype)
            else:
                got_bufs[a][way, step - 1, part] = total.astype(got_bufs[a].dtype)
                latest[lane] = send(lane, step, got_bufs[a].at[way, step - 1, part])
                started.append(latest[lane])
    for copy in started:
        copy.wait_send()


def ring_scatter(arrays, n, number, out_dtype, parts=2):
    count = len(arrays)
    copies = (count, 2, n - 1, parts)
    bufs = [
        pltpu.VMEM((2, n - 1, parts, a.shape[1] // 2 // parts, a.shape[2]), a.dtype)
        for a in arrays
    ]
    return pl.pallas_call(
        functools.partial(scatter_kernel, n, parts, count),
        out_shape=[jax.ShapeDtypeStruct(a.shape[1:], out_dtype) for a in arrays],
        in_specs=[ANY] * count,
        out_specs=[pl.BlockSpec(memory_space=pltpu.VMEM)] * count,
        scratch_shapes=bufs + bufs + [pltpu.SemaphoreType.DMA(copies)] * 3,
        compiler_params=pltpu.CompilerParams(
            collective_id=number, has_side_effects=True, vmem_limit_bytes=58 << 20
        ),
        name="ring_scatter",
    )(*arrays)


def finish_kernel(n, counts, *refs):
    few, many = counts
    refs = list(refs)
    take = lambda count: [refs.pop(0) for _ in range(count)]
    blocks, xs, sums, outs = take(few), take(many), take(few), take(many)
    own_bufs, got_bufs = take(few), take(few)
    mines, twins, crosses, gots = take(many), take(many), take(many), take(many)
    near_sem, far_sem, own_sem, pair_sem, cross_sem, ring_sem = refs
    pos, at, sides = seq_ring(n)
    exp = lax.axis_index("exp")
    core, chip = lax.rem(exp, 2), exp // 2
    peer, over = {"exp": exp + 1 - 2 * core}, {"exp": core + 2 * (1 - chip)}
    greet(sides + (peer, over))
    started = []

    def push(source, target, sems, index, to):
        copy = pltpu.make_async_remote_copy(
            src_ref=source,
            dst_ref=target,
            send_sem=sems.at[(0,) + index],
            recv_sem=sems.at[(1,) + index],
            device_id=to,
            device_id_type=MESH,
        )
        copy.start()
        started.append(copy)
        return copy

    def block(way, step):
        return at(pos - 1 - step) if way == 0 else at(pos + 1 + step)

    def fetch(source, target, sem):
        copy = pltpu.make_async_copy(source, target, sem)
        copy.start()
        return copy

    add = lambda *terms: functools.reduce(lambda u, v: u + v, [t.astype(jnp.float32) for t in terms])
    ways = range(2)
    lanes = [(a, way) for a in range(many) for way in ways]
    parts = 2
    rings = [(a, way, part) for part in range(parts) for a in range(few) for way in ways]

    def span(ref, way):
        half = ref.shape[-2] // 2
        return pl.ds(way * half, half)

    def piece(lane):
        a, way, part = lane
        rows = blocks[a].shape[-2] // 2 // parts
        return pl.ds(way * parts * rows + part * rows, rows), pl.ds(part * rows, rows)

    pairs, own, crossing, ring = {}, {}, {}, {}
    for side in range(2):
        for step in range(n):
            for lane in lanes:
                a, way = lane
                place = chip if side else 1 - chip
                where, rows = block(way, step), span(xs[a], way)
                pairs[side, lane, step] = push(
                    xs[a].at[1 - core, place, where, rows],
                    twins[a].at[side, way, step],
                    pair_sem,
                    (0, side) + lane + (0, step),
                    peer,
                )
                own[side, lane, step] = fetch(
                    xs[a].at[core, place, where, rows],
                    mines[a].at[side, way, step],
                    own_sem.at[(side,) + lane + (step,)],
                )
        if side == 0:
            for lane in rings:
                a, way, part = lane
                wide, thin = piece(lane)
                ring[lane] = push(
                    blocks[a].at[block(way, 0), wide],
                    got_bufs[a].at[way, 0, thin],
                    far_sem,
                    lane + (0,),
                    sides[way],
                )
            near = {}
            for step in range(1, n):
                for lane in rings:
                    a, way, part = lane
                    wide, thin = piece(lane)
                    near[lane, step] = fetch(
                        blocks[a].at[block(way, step), wide],
                        own_bufs[a].at[way, step - 1, thin],
                        near_sem.at[lane + (step - 1,)],
                    )

    def scatter(step, which):
        for lane in rings:
            a, way, part = lane
            if part != which:
                continue
            wide, thin = piece(lane)
            near[lane, step].wait()
            ring[lane].wait_recv()
            total = add(got_bufs[a][way, step - 1, thin], own_bufs[a][way, step - 1, thin])
            if step == n - 1:
                sums[a][wide] = total.astype(sums[a].dtype)
            else:
                got_bufs[a][way, step - 1, thin] = total.astype(got_bufs[a].dtype)
                ring[lane] = push(
                    got_bufs[a].at[way, step - 1, thin],
                    got_bufs[a].at[way, step, thin],
                    far_sem,
                    lane + (step,),
                    sides[way],
                )

    for step in range(n):
        for lane in lanes:
            a, way = lane
            own[0, lane, step].wait()
            pairs[0, lane, step].wait_recv()
            mines[a][0, way, step] = add(mines[a][0, way, step], twins[a][0, way, step]).astype(
                mines[a].dtype
            )
            crossing[lane, step] = push(
                mines[a].at[0, way, step],
                crosses[a].at[way, step],
                cross_sem,
                (0,) + lane + (0, step),
                over,
            )
        if step >= n - 2:
            scatter(1, step - n + 2)
    latest = {}
    for step in range(n):
        if step + 2 < n:
            scatter(step + 2, 0)
        for lane in lanes:
            a, way = lane
            own[1, lane, step].wait()
            pairs[1, lane, step].wait_recv()
            crossing[lane, step].wait_recv()
            terms = [mines[a][1, way, step], twins[a][1, way, step], crosses[a][way, step]]
            if step:
                latest[lane].wait_recv()
                terms.append(gots[a][way, step - 1])
            mines[a][1, way, step] = add(*terms).astype(mines[a].dtype)
            if step < n - 1:
                latest[lane] = push(
                    mines[a].at[1, way, step],
                    gots[a].at[way, step],
                    ring_sem,
                    (0,) + lane + (0, step),
                    sides[way],
                )
        if step + 2 < n:
            scatter(step + 2, 1)
    keep, done = [], []
    streams = []
    for a, way in lanes:
        half = xs[a].shape[-2] // 2
        if half % 48 == 0:
            some = half * 2 // 3
            streams += [
                (a, way, 0, way * half, some, False, True),
                (a, way, 1, way * half + some, half - some, False, False),
                (a, way, 2, way * half + some, half - some, True, False),
            ]
        else:
            streams.append((a, way, 0, way * half, half, False, True))
    latest, crossing = {}, {}

    def target_of(stream, step, other):
        a, way, number, first, size = stream[:5]
        where = at(pos - step) if way == 0 else at(pos + step)
        return outs[a].at[core, 1 - chip if other else chip, where, pl.ds(first, size)]

    def hand_on(stream, step):
        a, way, number = stream[:3]
        crossing[stream, step].wait_recv()
        target = target_of(stream, step, True)
        done.append(push(target, target, pair_sem, (1, 1, a, way, number, step), peer))

    for step in range(n):
        for stream in streams:
            a, way, number, first, size, other, always = stream
            if step:
                latest[stream].wait_recv()
            target = target_of(stream, step, other)
            if step or other:
                source = target
            else:
                source = mines[a].at[1, way, n - 1, pl.ds(first - way * (xs[a].shape[-2] // 2), size)]
            if step == 0 and other:
                crossing[streams[streams.index(stream) - 1], 0].wait_recv()
            if step < n - 1:
                latest[stream] = push(
                    source, target, ring_sem, (1, a, way, number, step), sides[way]
                )
            if not other and (always or step == 0):
                crossing[stream, step] = push(
                    source, target, cross_sem, (1, a, way, number, step), over
                )
            done.append(push(source, target, pair_sem, (1, 0, a, way, number, step), peer))
            if step == 0 and not other:
                keep.append(fetch(source, target, own_sem.at[0, a, way, number]))
        if step:
            for stream in streams:
                if stream[6]:
                    hand_on(stream, step - 1)
    for stream in streams:
        if stream[6]:
            hand_on(stream, n - 1)
    for copy in keep:
        copy.wait()
    for copy in done:
        copy.wait_recv()
    for copy in started:
        copy.wait_send()


def finish(blocks, rows_in, small, n, m, number):
    rows, cols = rows_in.shape
    each = rows // (4 * n)
    if m != 4 or rows % (4 * n * 32) or small.shape[0] > 4 * n * 16:
        return (
            ring_scatter(blocks, n, number, jnp.float32),
            *lax.psum((rows_in, small), ("seq", "exp")),
        )
    padded = jnp.pad(small, ((0, 4 * n * 16 - small.shape[0]), (0, 0)))
    arrays = [rows_in.reshape(2, 2, n, each, cols), padded.reshape(2, 2, n, 16, TILE)]
    few, many = len(blocks), len(arrays)
    halves = [(x.shape[-2] // 2, x.shape[-1], x.dtype) for x in blocks + arrays]
    ring_bufs = [pltpu.VMEM((2, n - 1, r, c), t) for r, c, t in halves[:few]]
    two = [pltpu.VMEM((2, 2, n, r, c), t) for r, c, t in halves[few:]]
    one = [pltpu.VMEM((2, n, r, c), t) for r, c, t in halves[few:]]
    dma = pltpu.SemaphoreType.DMA
    results = pl.pallas_call(
        functools.partial(finish_kernel, n, (few, many)),
        out_shape=[jax.ShapeDtypeStruct(x.shape[1:], jnp.float32) for x in blocks]
        + [jax.ShapeDtypeStruct(x.shape, x.dtype) for x in arrays],
        in_specs=[ANY] * (few + many),
        out_specs=[pl.BlockSpec(memory_space=pltpu.VMEM)] * few + [ANY] * many,
        scratch_shapes=ring_bufs * 2
        + two * 2
        + one * 2
        + [
            dma((few, 2, 2, n)),
            dma((2, few, 2, 2, n)),
            dma((2, many, 2, n)),
            dma((2, 2, 2, many, 2, 3, n)),
            dma((2, 2, many, 2, 3, n)),
            dma((2, 2, many, 2, 3, n)),
        ],
        compiler_params=pltpu.CompilerParams(
            collective_id=number, has_side_effects=True, vmem_limit_bytes=58 << 20
        ),
        cost_estimate=cost(120),
        name="finish",
    )(*blocks, *arrays)
    return results[:few], results[few].reshape(rows, cols), results[-1].reshape(-1, TILE)


def dot_last(a, b):
    return lax.dot_general(a, b, (((1,), (1,)), ((), ())), preferred_element_type=jnp.float32)


def dot_first(a, b):
    return lax.dot_general(a, b, (((0,), (0,)), ((), ())), preferred_element_type=jnp.float32)


def dot_plain(a, b):
    return jnp.dot(a, b, preferred_element_type=jnp.float32)


def head_masks(dtype):
    low = lax.broadcasted_iota(jnp.int32, (1, TILE), 1) < HEAD_DIM
    first = jnp.where(low, 1.0, 0.0).astype(jnp.float32)
    return first.astype(dtype), (1.0 - first).astype(dtype)


def split_heads(pair):
    return jnp.concatenate([pair * mask for mask in head_masks(pair.dtype)], axis=0)


def own_bias(tiles, count):
    rows = []
    for r in range(count):
        row = []
        for c in range(count):
            if c == r:
                row.append(tiles[:, TILE:])
            elif c == r - 1:
                row.append(tiles[:, :TILE])
            else:
                row.append(jnp.full((TILE, TILE), 0.0 if c < r else masked_score, jnp.float32))
        rows.append(jnp.concatenate(row, axis=1))
    return jnp.concatenate(rows, axis=0)


def edge_bias(tiles, rows):
    edge = []
    for h in range(2):
        first = jnp.concatenate(
            [jnp.zeros((rows - TILE, TILE), jnp.float32), tiles[h][:, :TILE].T], axis=0
        )
        edge += [first, jnp.zeros((rows, rows - TILE), jnp.float32)]
    return jnp.concatenate(edge, axis=1)


def each_far(s, block, act, times=3):
    far = jnp.maximum(s - 1, 0)
    bundles = far // times

    def bundle(j, carry):
        act(pl.multiple_of(j * times * block, block), times)
        return carry

    def single(j, carry):
        act(pl.multiple_of(j * block, block), 1)
        return carry

    lax.fori_loop(0, bundles, bundle, 0)
    lax.fori_loop(bundles * times, far, single, 0)


def attend_kernel(causal, block, s_ref, q_ref, k_ref, v_ref, *refs):
    if causal:
        line_ref, low_ref, wide_ref, lse_ref, acc_ref, top_ref = refs
    else:
        low_ref, wide_ref, lse_ref, acc_ref, top_ref = refs
    rows = q_ref.shape[0]
    both = split_heads(q_ref[...])

    def visit(start, bias, first, times=1):
        ones = jnp.ones((16, times * block), v_ref.dtype)
        keys = k_ref[pl.ds(start, times * block), :]
        values = v_ref[pl.ds(start, times * block), :]
        t = dot_last(keys, both) * (scale_factor * log2e)
        if bias is not None:
            t = t + bias
        top = jnp.max(t, axis=0, keepdims=True)
        if not first:
            before = top_ref[...]
            top = jnp.maximum(before, top)
            fade = jnp.exp2(before - top)
        top_ref[...] = top
        p = jnp.exp2(t - top).astype(values.dtype)
        part = dot_plain(jnp.concatenate([values.T, ones], axis=0), p)
        if first:
            acc_ref[...] = part
        else:
            acc_ref[...] = acc_ref[...] * fade + part

    if causal:
        s = s_ref[0]
        count = rows // TILE
        tiles = [bias_tile(line_ref, h) for h in range(2)]
        visit(
            pl.multiple_of(s * block, block),
            jnp.concatenate([own_bias(tiles[h], count).T for h in range(2)], axis=1),
            True,
        )

        @pl.when(s > 0)
        def _():
            visit(pl.multiple_of((s - 1) * block, block), edge_bias(tiles, rows), False)

        each_far(s, block, lambda start, times: visit(start, None, False, times))
    else:
        for j in range(k_ref.shape[0] // block):
            visit(j * block, None, j == 0)
    sums = acc_ref[TILE : TILE + 1, :]
    wide = jnp.concatenate(
        [
            acc_ref[:HEAD_DIM, :rows] / sums[:, :rows],
            acc_ref[HEAD_DIM:TILE, rows:] / sums[:, rows:],
        ],
        axis=0,
    ).T
    wide_ref[...] = wide
    low_ref[...] = wide.astype(low_ref.dtype)
    lse = top_ref[...] + jnp.log2(sums)
    lse_ref[0] = jnp.concatenate([lse[:, :rows], lse[:, rows:]], axis=0)


def attend(seq_at, queries, keys, values, lines):
    rows, total = queries.shape[0], keys.shape[0]
    causal = lines is not None
    block = rows if causal else math.gcd(total, 1024)
    pair = pl.BlockSpec((rows, TILE), lambda g: (0, g))
    long = pl.BlockSpec((total, TILE), lambda g: (0, g))
    extra, specs = [], []
    if causal:
        extra, specs = [lines], [pl.BlockSpec((1,) + lines.shape[1:], lambda g: (g, 0, 0))]
    return pl.pallas_call(
        functools.partial(attend_kernel, causal, block),
        grid=(PAIRS,),
        out_shape=[
            jax.ShapeDtypeStruct((rows, D), jnp.bfloat16),
            jax.ShapeDtypeStruct((rows, D), jnp.float32),
            jax.ShapeDtypeStruct((PAIRS, 2, rows), jnp.float32),
        ],
        in_specs=[SMEM, pair, long, long] + specs,
        out_specs=[pair, pair, pl.BlockSpec((1, 2, rows), lambda g: (g, 0, 0))],
        scratch_shapes=[
            pltpu.VMEM((TILE + 16, 2 * rows), jnp.float32),
            pltpu.VMEM((1, 2 * rows), jnp.float32),
        ],
        compiler_params=pltpu.CompilerParams(vmem_limit_bytes=48 << 20),
        cost_estimate=cost(40 if causal else 10),
        name="attend_self" if causal else "attend_cross",
    )(seq_at, queries, keys, values, *extra)


def attend_back_kernel(causal, block, s_ref, q_ref, k_ref, v_ref, up_ref, wide_ref, lse_ref, *refs):
    if causal:
        line_ref, dq_ref, dk_ref, dv_ref, near_ref, sum_ref, acc_ref = refs
    else:
        dq_ref, dk_ref, dv_ref, acc_ref = refs
    rows = q_ref.shape[0]
    both = split_heads(q_ref[...])
    up = up_ref[...]
    up_both = split_heads(up)
    turned = (up.astype(jnp.float32) * wide_ref[...]).T
    delta = jnp.concatenate(
        [
            jnp.sum(turned[:HEAD_DIM], axis=0, keepdims=True),
            jnp.sum(turned[HEAD_DIM:], axis=0, keepdims=True),
        ],
        axis=1,
    )
    lse = jnp.concatenate([lse_ref[0, :1], lse_ref[0, 1:]], axis=1)

    def visit(start, bias, first, times=1):
        ones = jnp.ones((16, times * block), k_ref.dtype)
        keys = k_ref[pl.ds(start, times * block), :]
        values = v_ref[pl.ds(start, times * block), :]
        t = dot_last(keys, both) * (scale_factor * log2e)
        if bias is not None:
            t = t + bias
        p = jnp.exp2(t - lse)
        ds = (p * (dot_last(values, up_both) - delta)).astype(keys.dtype)
        dv_ref[pl.ds(start, times * block), :] = dot_plain(p.astype(keys.dtype), up_both).astype(
            dv_ref.dtype
        )
        dk_ref[pl.ds(start, times * block), :] = (dot_plain(ds, both) * scale_factor).astype(dk_ref.dtype)
        part = dot_plain(jnp.concatenate([keys.T, ones], axis=0), ds)
        if first:
            acc_ref[...] = part
        else:
            acc_ref[...] += part
        return ds

    if causal:
        s = s_ref[0]
        count = rows // TILE
        tiles = [bias_tile(line_ref, h) for h in range(2)]
        ds = visit(
            pl.multiple_of(s * block, block),
            jnp.concatenate([own_bias(tiles[h], count).T for h in range(2)], axis=1),
            True,
        )
        for h in range(2):
            same = before = jnp.zeros((TILE, TILE), jnp.float32)
            for r in range(count):
                columns = slice(h * rows + r * TILE, h * rows + (r + 1) * TILE)
                same = same + ds[r * TILE : (r + 1) * TILE, columns].astype(jnp.float32)
                if r:
                    before = before + ds[(r - 1) * TILE : r * TILE, columns].astype(jnp.float32)
            near_ref[h, :TILE] = before
            near_ref[h, TILE:] = same

        @pl.when(s > 0)
        def _():
            ds = visit(pl.multiple_of((s - 1) * block, block), edge_bias(tiles, rows), False)
            for h in range(2):
                near_ref[h, :TILE] += ds[rows - TILE :, h * rows : h * rows + TILE].astype(
                    jnp.float32
                )

        each_far(s, block, lambda start, times: visit(start, None, False, times))

        def beyond(j, carry):
            start = pl.multiple_of(j * block, block)
            dk_ref[pl.ds(start, block), :] = jnp.zeros((block, TILE), dk_ref.dtype)
            dv_ref[pl.ds(start, block), :] = jnp.zeros((block, TILE), dv_ref.dtype)
            return carry

        lax.fori_loop(s + 1, k_ref.shape[0] // block, beyond, 0)
        sum_ref[0] = jnp.concatenate(
            [acc_ref[TILE : TILE + 1, :rows], acc_ref[TILE : TILE + 1, rows:]], axis=0
        )
    else:
        for j in range(k_ref.shape[0] // block):
            visit(j * block, None, j == 0)
    dq = jnp.concatenate([acc_ref[:HEAD_DIM, :rows], acc_ref[HEAD_DIM:TILE, rows:]], axis=0)
    dq_ref[...] = (dq.T * scale_factor).astype(dq_ref.dtype)


def attend_back(seq_at, queries, keys, values, upstream, wide, lse, lines):
    rows, total = queries.shape[0], keys.shape[0]
    causal = lines is not None
    block = rows if causal else math.gcd(total, 1024)
    pair = pl.BlockSpec((rows, TILE), lambda g: (0, g))
    long = pl.BlockSpec((total, TILE), lambda g: (0, g))
    line = pl.BlockSpec((1, 2, rows), lambda g: (g, 0, 0))
    extra, specs, shapes, out_specs = [], [], [], []
    if causal:
        extra, specs = [lines], [pl.BlockSpec((1,) + lines.shape[1:], lambda g: (g, 0, 0))]
        shapes = [
            jax.ShapeDtypeStruct((HEADS, 2 * TILE, TILE), jnp.float32),
            jax.ShapeDtypeStruct((PAIRS, 2, rows), jnp.float32),
        ]
        out_specs = [pl.BlockSpec((2, 2 * TILE, TILE), lambda g: (g, 0, 0)), line]
    return pl.pallas_call(
        functools.partial(attend_back_kernel, causal, block),
        grid=(PAIRS,),
        out_shape=[
            jax.ShapeDtypeStruct((rows, D), jnp.bfloat16),
            jax.ShapeDtypeStruct((total, D), jnp.bfloat16),
            jax.ShapeDtypeStruct((total, D), jnp.bfloat16),
        ]
        + shapes,
        in_specs=[SMEM, pair, long, long, pair, pair, line] + specs,
        out_specs=[pair, long, long] + out_specs,
        scratch_shapes=[pltpu.VMEM((TILE + 16, 2 * rows), jnp.float32)],
        compiler_params=pltpu.CompilerParams(vmem_limit_bytes=48 << 20),
        cost_estimate=cost(48 if causal else 15),
        name="attend_self_back" if causal else "attend_cross_back",
    )(seq_at, queries, keys, values, upstream, wide, lse, *extra)


def token_back_kernel(x_ref, dk_ref, dv_ref, wk_ref, wv_ref, dx_ref, gk_ref, gv_ref, gain_ref, k_acc, v_acc):
    x, dk, dv = x_ref[...], dk_ref[...], dv_ref[...]
    dx = dot_last(dk, wk_ref[0]) + dot_last(dv, wv_ref[0])
    dx_ref[...] = dx.astype(dx_ref.dtype)
    gain = jnp.sum(dx * x.astype(jnp.float32), axis=0, keepdims=True)
    gk, gv = dot_first(x, dk), dot_first(x, dv)
    step, last = pl.program_id(0), pl.num_programs(0) - 1

    @pl.when(step == 0)
    def _():
        gain_ref[...] = gain
        k_acc[...] = gk
        v_acc[...] = gv

    @pl.when(step > 0)
    def _():
        gain_ref[...] += gain
        k_acc[...] += gk
        v_acc[...] += gv

    @pl.when(step == last)
    def _():
        gk_ref[...] = k_acc[...].astype(gk_ref.dtype)
        gv_ref[...] = v_acc[...].astype(gv_ref.dtype)


def token_back(tokens, grad_keys, grad_values, proj_in, rows, first, name):
    total = tokens.shape[0]
    block = pl.BlockSpec((rows, D), lambda i: (i, 0))
    weight = lambda number: pl.BlockSpec((1, D, D), lambda i: (number, 0, 0))
    whole = lambda r: pl.BlockSpec((r, D), lambda i: (0, 0))
    grad = jax.ShapeDtypeStruct((D, D), tokens.dtype)
    return pl.pallas_call(
        token_back_kernel,
        grid=(total // rows,),
        out_shape=[
            jax.ShapeDtypeStruct(tokens.shape, tokens.dtype),
            grad,
            grad,
            jax.ShapeDtypeStruct((1, D), jnp.float32),
        ],
        in_specs=[block] * 3 + [weight(first), weight(first + 1)],
        out_specs=[block, whole(D), whole(D), whole(1)],
        scratch_shapes=[pltpu.VMEM((D, D), jnp.float32)] * 2,
        compiler_params=pltpu.CompilerParams(vmem_limit_bytes=48 << 20),
        cost_estimate=cost(18 if total > 2048 else 8),
        name=name,
    )(tokens, grad_keys, grad_values, proj_in, proj_in)


def bias_lines(bias_table):
    at = jnp.arange(3 * TILE, dtype=jnp.int32)
    distance = jnp.where(at <= 2 * TILE, TILE - at, 4 * TILE - at)
    table = (bias_table - bias_table[NBUCKET - 1 :]) * log2e
    terms = jnp.broadcast_to(table[0][:, None], (HEADS, 3 * TILE))
    for number, threshold in enumerate(bucket_edges()):
        terms = jnp.where((distance >= threshold)[None], table[number + 1][:, None], terms)
    return jnp.where((distance >= 0)[None], terms, masked_score).reshape(PAIRS, 2, 3 * TILE)


def bias_tile(line_ref, h):
    line = jnp.broadcast_to(line_ref[0, h : h + 1, :], (TILE, 3 * TILE))
    return pltpu.roll(line, 0, 1, stride=1, stride_axis=0)[:, : 2 * TILE]


def bias_gradient(near, sums):
    distance = (
        TILE
        + jnp.arange(TILE, dtype=jnp.int32)[None, :]
        - jnp.arange(2 * TILE, dtype=jnp.int32)[:, None]
    )
    bucket = jnp.zeros(distance.shape, jnp.int32)
    for threshold in bucket_edges():
        bucket = bucket + (distance >= threshold).astype(jnp.int32)
    onehot = (
        bucket.reshape(-1)[None, :] == jnp.arange(NBUCKET, dtype=jnp.int32)[:, None]
    ).astype(jnp.float32)
    flat = near.reshape(HEADS, -1)
    table = lax.dot_general(
        onehot, flat, (((1,), (1,)), ((), ())), precision=highest
    )
    far = jnp.sum(sums, axis=-1).reshape(HEADS) - jnp.sum(flat, axis=-1)
    last = jnp.arange(NBUCKET, dtype=jnp.int32)[:, None] == NBUCKET - 1
    return table + jnp.where(last, far[None, :], 0.0)


def expert_kernel(n, m, slots, *refs):
    x_ref, maps, result_ref, grads = refs[0], refs[1:9], refs[9], refs[10:16]
    rows, parts, backs, up_all, down_all, act_all, du_all = refs[16:23]
    grad_bufs, far_bufs = refs[23:31], refs[31:33]
    map_sem, own_sem, grad_sem, go_sem, back_sem, term_sem = refs[33:]
    seq, exp = lax.axis_index("seq"), lax.axis_index("exp")
    groups, count = n // QUAD, x_ref.shape[1] // slots
    batch = max(1, 128 // slots)
    far = [(g, k) for g in range(1, groups) for k in range(m)]
    moves = far + [(0, k) for k in range(1, m)]
    source_of = lambda k: lax.rem(exp + m - k, m)

    def push(source, target, sems, g, k, to_seq, to_exp):
        copy = pltpu.make_async_remote_copy(
            src_ref=source,
            dst_ref=target,
            send_sem=sems.at[0, g, k],
            recv_sem=sems.at[1, g, k],
            device_id={"seq": to_seq, "exp": to_exp},
            device_id_type=MESH,
        )
        copy.start()
        return copy

    def place(g, k):
        return lax.rem(seq + g * QUAD, n), lax.rem(exp + k, m)

    to_next, to_last = quad_moves(n)
    side = {"next": look_up(seq, [b for _, b in to_next]), "last": look_up(seq, [b for _, b in to_last])}
    greet(
        [dict(zip(("seq", "exp"), place(g, k))) for g, k in moves]
        + [{"seq": side["next"], "exp": exp}, {"seq": side["last"], "exp": exp}]
    )
    going = {}
    for g, k in moves:
        to_seq, to_exp = place(g, k)
        going[g, k] = push(x_ref.at[to_exp], rows.at[g, exp], go_sem, g, k, to_seq, to_exp)
    own = pltpu.make_async_copy(x_ref.at[exp], rows.at[0, exp], own_sem.at[0])
    own.start()
    fetched = []
    for j in range(QUAD):
        for at, (source, target) in enumerate(((maps[2 * j], up_all), (maps[2 * j + 1], down_all))):
            copy = pltpu.make_async_copy(source, target.at[j], map_sem.at[at, j])
            copy.start()
            fetched.append(copy)
    for copy in fetched:
        copy.wait()
    own.wait()
    slope = math.sqrt(2.0 / math.pi)
    coming = {}

    def work(g, first, last):
        for k in range(first, last):
            if g or k:
                going[g, k].wait_recv()
        size = (last - first) * slots
        base = (g * m + first) * slots

        def one(e, carry):
            start = pl.multiple_of(e * slots, slots)
            piece = jnp.concatenate(
                [rows[g, source_of(k), pl.ds(start, slots), :] for k in range(first, last)], axis=0
            )
            tokens, upstream = piece[:, :D], piece[:, D:]
            result = back = None
            for j in range(QUAD):
                up_map, down_map = up_all[j, e], down_all[j, e]
                u = dot_plain(tokens, up_map)
                square = u * u
                bend = jnp.tanh(slope * (u + 0.044715 * (square * u)))
                half = 0.5 * (1.0 + bend)
                act = (u * half).astype(tokens.dtype)
                rise = half + 0.5 * u * (1.0 - bend * bend) * (
                    slope * (1.0 + 3 * 0.044715 * square)
                )
                du = (dot_plain(upstream, down_map) * rise).astype(tokens.dtype)
                act_all[e, j, base : base + size] = act
                du_all[e, j, base : base + size] = du
                y, dn = dot_last(act, down_map), dot_last(du, up_map)
                result = y if result is None else result + y
                back = dn if back is None else back + dn
            for i, k in enumerate(range(first, last)):
                span = slice(i * slots, (i + 1) * slots)
                where = (g, source_of(k), pl.ds(start, slots))
                parts[where + (slice(0, D),)] = result[span].astype(parts.dtype)
                parts[where + (slice(D, 2 * D),)] = back[span].astype(parts.dtype)
            return carry

        lax.fori_loop(0, count, one, 0)
        for k in range(first, last):
            if g or k:
                source = source_of(k)
                coming[g, k] = push(
                    parts.at[g, source],
                    backs.at[g, exp],
                    back_sem,
                    g,
                    k,
                    lax.rem(seq + n - g * QUAD, n),
                    source,
                )

    work(0, 0, m)
    for g in range(1, groups):
        for first in range(0, m, batch):
            work(g, first, min(m, first + batch))

    total = groups * m * slots

    def weigh(j):
        def one(e, carry):
            start = pl.multiple_of(e * slots, slots)
            piece = jnp.concatenate(
                [
                    rows[g, source_of(k), pl.ds(start, slots), :]
                    for g in range(groups)
                    for k in range(m)
                ],
                axis=0,
            )
            tokens, upstream = piece[:, :D], piece[:, D:]
            up_buf, down_buf = grad_bufs[2 * j], grad_bufs[2 * j + 1]
            up_buf[e] = dot_first(tokens, du_all[e, j, :total]).astype(up_buf.dtype)
            down_buf[e] = dot_first(upstream, act_all[e, j, :total]).astype(down_buf.dtype)
            return carry

        lax.fori_loop(0, count, one, 0)

    def term(source, target, number, to):
        return push(source, target, term_sem, 0, number, side[to], exp)

    def store(source, number):
        copy = pltpu.make_async_copy(source, grads[number], grad_sem.at[number])
        copy.start()
        return copy

    weigh(3)
    terms_out = [
        term(grad_bufs[6], far_bufs[0], 0, "next"),
        term(grad_bufs[7], far_bufs[1], 1, "last"),
    ]
    weigh(1)
    weigh(2)
    weigh(0)
    stored = [
        store(grad_bufs[i], number) for number, i in ((0, 0), (1, 1), (4, 2), (5, 5))
    ]
    for number, (buf, far_buf) in enumerate(((grad_bufs[4], far_bufs[0]), (grad_bufs[3], far_bufs[1]))):
        terms_out[number].wait_recv()
        buf[...] = (buf[...].astype(jnp.float32) + far_buf[...].astype(jnp.float32)).astype(buf.dtype)
        stored.append(store(buf, 2 + number))
    for k in range(m):
        where = source_of(k)
        terms = []
        for g in range(groups):
            back_k = (m - k) % m
            if g == 0 and k == 0:
                terms.append(parts[0, exp])
            else:
                coming[g, back_k].wait_recv()
                terms.append(backs[g, where])
        total_row = terms[0].astype(jnp.float32)
        for term in terms[1:]:
            total_row = total_row + term.astype(jnp.float32)
        result_ref[where] = total_row.astype(result_ref.dtype)
    for copy in stored:
        copy.wait()
    for copy in terms_out:
        copy.wait_send()
    for copies in (going, coming):
        for copy in copies.values():
            copy.wait_send()


def run_experts(x, maps, n, m, slots, number):
    groups = n // QUAD
    count, _, hidden = maps[0].shape
    total = groups * m * slots
    big = pltpu.VMEM((groups,) + x.shape, x.dtype)
    stack = pltpu.VMEM((QUAD,) + maps[0].shape, x.dtype)
    kept = pltpu.VMEM((count, QUAD, total, hidden), x.dtype)
    grads = [(w.shape, jnp.float32 if i < 2 else jnp.bfloat16) for i, w in enumerate(maps)]
    dma = pltpu.SemaphoreType.DMA
    return pl.pallas_call(
        functools.partial(expert_kernel, n, m, slots),
        out_shape=[jax.ShapeDtypeStruct(x.shape, x.dtype)]
        + [jax.ShapeDtypeStruct(shape, dtype) for shape, dtype in grads[:6]],
        in_specs=[ANY] * (1 + len(maps)),
        out_specs=[pl.BlockSpec(memory_space=pltpu.VMEM)] + [ANY] * 6,
        scratch_shapes=[big] * 3
        + [stack] * 2
        + [kept] * 2
        + [pltpu.VMEM(shape, dtype) for shape, dtype in grads + grads[6:]]
        + [
            dma((2, QUAD)),
            dma((1,)),
            dma((6,)),
            dma((2, groups, m)),
            dma((2, groups, m)),
            dma((2, 1, 2)),
        ],
        compiler_params=pltpu.CompilerParams(
            collective_id=number, has_side_effects=True, vmem_limit_bytes=60 << 20
        ),
        cost_estimate=cost(150),
        name="run_experts",
    )(x, *maps)


QUAD = 4


def quad_moves(n):
    ring = (0, 1, 3, 2)
    step = lambda i, by: i - i % QUAD + ring[(ring.index(i % QUAD) + by) % QUAD]
    return [(i, step(i, 1)) for i in range(n)], [(i, step(i, -1)) for i in range(n)]


def project(source, matrix):
    return jnp.dot(source, matrix, preferred_element_type=jnp.float32).astype(jnp.bfloat16)


def weight_grad(source, upstream):
    return jnp.einsum("td,te->de", source, upstream, preferred_element_type=jnp.float32).astype(
        jnp.bfloat16
    )


def input_grad(upstream, matrix):
    return jnp.einsum("te,de->td", upstream, matrix, preferred_element_type=jnp.float32)


def body(
    n,
    m,
    hidden_in,
    memory,
    proj_in,
    proj_out,
    norm_gains,
    rel_bias,
    router,
    expert_choice,
    expert_in,
    expert_out,
    cotangent,
):
    tokens = hidden_in[0].astype(jnp.float32)
    memory_rows = memory[0]
    memory_count = memory_rows.shape[0]
    gain_rows = norm_gains.astype(jnp.float32)
    token_count = tokens.shape[0]
    seq_at = lax.axis_index("seq").astype(jnp.int32).reshape(1)
    normed_self = rms_apply(tokens, gain_rows[0]).astype(jnp.bfloat16)
    lines = bias_lines(rel_bias)

    normed_all, memory_all, queries, key_all, value_all, memory_key_all, memory_value_all = (
        gather_projected(normed_self, memory_rows, proj_in, n, 1)
    )
    to_next, to_last = quad_moves(n)
    in_own, out_own, normed_all = lax.optimization_barrier((expert_in, expert_out, normed_all))
    in_last, out_last = (lax.ppermute(w, "seq", to_next) for w in (in_own, out_own))
    in_next, out_next = (lax.ppermute(w, "seq", to_last) for w in (in_own, out_own))
    normed_all = normed_all.reshape(n * token_count, D)
    memory_all = memory_all.reshape(n * memory_count, D)
    key_all, value_all = (x.reshape(n * token_count, D) for x in (key_all, value_all))
    memory_key_all, memory_value_all = (
        x.reshape(n * memory_count, D) for x in (memory_key_all, memory_value_all)
    )
    attended_self_low, attended_self, lse_self = attend(
        seq_at, queries, key_all, value_all, lines
    )
    attended_self_low, in_last, out_next = lax.optimization_barrier(
        (attended_self_low, in_last, out_next)
    )
    in_far = lax.ppermute(in_last, "seq", to_next)
    out_far = lax.ppermute(out_next, "seq", to_last)
    after_self = tokens + jnp.dot(
        attended_self_low, proj_out[0], preferred_element_type=jnp.float32
    )

    normed_cross = rms_apply(after_self, gain_rows[1]).astype(jnp.bfloat16)
    cross_queries = project(normed_cross, proj_in[3])
    attended_cross_low, attended_cross, lse_cross = attend(
        seq_at, cross_queries, memory_key_all, memory_value_all, None
    )
    after_cross = after_self + jnp.dot(
        attended_cross_low, proj_out[1], preferred_element_type=jnp.float32
    )

    mixed_low = rms_apply(after_cross, gain_rows[2]).astype(jnp.bfloat16)
    softmax_probs = jax.nn.softmax(
        jnp.dot(mixed_low, router, preferred_element_type=jnp.float32), axis=-1
    )
    expert_count = router.shape[1]
    local_experts = expert_in.shape[0]
    capacity = max(2, 5 * token_count // (4 * expert_count))
    chosen = expert_choice[0, :, 0]
    onehot_int = (chosen[:, None] == jnp.arange(expert_count, dtype=jnp.int32)[None, :]).astype(
        jnp.int32
    )
    onehot = onehot_int.astype(jnp.float32)
    gate_prob = jnp.sum(softmax_probs * onehot, axis=-1)
    slot_index = jnp.sum(jnp.cumsum(onehot_int, axis=0) * onehot_int, axis=-1) - 1
    is_kept = slot_index < capacity
    slots = -(-capacity // 16) * 16
    place = jnp.where(is_kept, chosen * slots + slot_index, -1)
    dispatch = (
        place[:, None] == jnp.arange(expert_count * slots, dtype=jnp.int32)[None, :]
    ).astype(jnp.bfloat16)
    dispatched = jnp.sum(onehot_int * is_kept[:, None].astype(jnp.int32), axis=0)
    tally_counts = jnp.stack(
        [dispatched, jnp.sum(onehot_int, axis=0) - dispatched], axis=0
    ).reshape(1, 1, 2, expert_count)

    grad_top = cotangent[0].astype(jnp.float32)
    scaled = (gate_prob[:, None] * grad_top).astype(jnp.bfloat16)
    sent_rows = (
        jnp.einsum(
            "tx,td->xd",
            dispatch,
            jnp.concatenate([mixed_low, scaled], axis=1),
            preferred_element_type=jnp.float32,
        )
        .astype(jnp.bfloat16)
        .reshape(m, local_experts * slots, 2 * D)
    )
    sent_rows, in_far, out_far = lax.optimization_barrier((sent_rows, in_far, out_far))
    maps = [in_own, out_own, in_last, out_last, in_next, out_next, in_far, out_far]
    returned, *terms = run_experts(sent_rows, maps, n, m, slots, 2)
    returned = returned.reshape(expert_count * slots, 2 * D)
    gin_own, gout_own, gin_next, gout_last, gin_last, gout_next = terms
    gout_next = lax.ppermute(gout_next, "seq", to_next)
    gin_last = lax.ppermute(gin_last, "seq", to_last)
    routed = jnp.dot(dispatch, returned, preferred_element_type=jnp.float32)
    combined, grad_mixed = routed[:, :D], routed[:, D:]
    output = (after_cross + gate_prob[:, None] * combined).astype(jnp.bfloat16)

    grad_gate = jnp.sum(grad_top * combined, axis=-1)
    grad_logits = softmax_probs * (onehot - gate_prob[:, None]) * grad_gate[:, None]
    grad_router = jnp.einsum(
        "td,te->de", mixed_low.astype(jnp.float32), grad_logits, precision=highest
    )
    grad_mixed = grad_mixed + jnp.einsum(
        "te,de->td", grad_logits, router.astype(jnp.float32), precision=highest
    )
    grad_cross_part, grad_gain_mix = rms_backward(after_cross, gain_rows[2], grad_mixed)
    grad_after_cross = grad_top + grad_cross_part

    grad_cross_low = grad_after_cross.astype(jnp.bfloat16)
    grad_out_cross = weight_grad(attended_cross_low, grad_cross_low)
    grad_attended_cross = input_grad(grad_cross_low, proj_out[1]).astype(jnp.bfloat16)
    grad_cross_query, grad_memory_keys, grad_memory_values = attend_back(
        seq_at,
        cross_queries,
        memory_key_all,
        memory_value_all,
        grad_attended_cross,
        attended_cross,
        lse_cross,
        None,
    )
    grad_cross_query, gin_last, gout_next, gin_next, gout_last = lax.optimization_barrier(
        (grad_cross_query, gin_last, gout_next, gin_next, gout_last)
    )
    gin_next = lax.ppermute(gin_next, "seq", to_next)
    gout_last = lax.ppermute(gout_last, "seq", to_last)
    grad_query_cross = weight_grad(normed_cross, grad_cross_query)
    grad_self_part, grad_gain_cross = rms_backward(
        after_self, gain_rows[1], input_grad(grad_cross_query, proj_in[3])
    )
    grad_after_self = grad_after_cross + grad_self_part
    grad_memory_part, grad_key_cross, grad_value_cross, _ = token_back(
        memory_all,
        grad_memory_keys,
        grad_memory_values,
        proj_in,
        math.gcd(n * memory_count, 512),
        4,
        "memory_back",
    )

    grad_self_low = grad_after_self.astype(jnp.bfloat16)
    grad_out_self = weight_grad(attended_self_low, grad_self_low)
    grad_attended_self = input_grad(grad_self_low, proj_out[0]).astype(jnp.bfloat16)
    grad_self_query, grad_keys, grad_values, near, sums = attend_back(
        seq_at,
        queries,
        key_all,
        value_all,
        grad_attended_self,
        attended_self,
        lse_self,
        lines,
    )
    grad_self_query, grad_keys, grad_values, near, sums, gout_last, gin_next = (
        lax.optimization_barrier(
            (grad_self_query, grad_keys, grad_values, near, sums, gout_last, gin_next)
        )
    )
    grad_expert_in = gin_own + gin_last.astype(jnp.float32) + gin_next.astype(jnp.float32)
    grad_expert_out = gout_own + gout_last.astype(jnp.float32) + gout_next.astype(jnp.float32)
    grad_table = bias_gradient(near, sums)
    grad_normed_query = input_grad(grad_self_query, proj_in[0])
    grad_normed_part, grad_key_self, grad_value_self, grad_gain_part = token_back(
        normed_all, grad_keys, grad_values, proj_in, 2 * token_count, 1, "token_back"
    )
    grad_gain_self = (
        grad_gain_part[0]
        + jnp.sum(grad_normed_query * normed_self.astype(jnp.float32), axis=0)
    ) / gain_rows[0]

    grads = jnp.concatenate(
        [
            weight_grad(normed_self, grad_self_query),
            grad_key_self,
            grad_value_self,
            grad_query_cross,
            grad_key_cross,
            grad_value_cross,
            grad_out_self,
            grad_out_cross,
        ]
    )
    grad_gains = jnp.stack([grad_gain_self, grad_gain_cross, grad_gain_mix])
    small = [
        grad_gains.reshape(-1, TILE),
        grad_router.T.reshape(-1, TILE),
        jnp.pad(grad_table, ((0, 0), (0, TILE - HEADS))),
    ]
    ends = [small[0].shape[0], small[0].shape[0] + small[1].shape[0]]
    (grad_normed_own, grad_memory), grads, small = finish(
        [
            grad_normed_part.reshape(n, token_count, D),
            grad_memory_part.reshape(n, memory_count, D),
        ],
        grads,
        jnp.concatenate(small),
        n,
        m,
        4,
    )
    grads = grads.reshape(-1, D, D).astype(jnp.float32)
    grad_token_part, _ = rms_backward(tokens, gain_rows[0], grad_normed_query + grad_normed_own)
    grad_in = (grad_after_self + grad_token_part).astype(jnp.bfloat16)
    return (
        output.reshape(1, token_count, D),
        grad_in.reshape(1, token_count, D),
        grad_memory.astype(jnp.bfloat16).reshape(1, memory_count, D),
        grads[:6],
        grads[6:],
        small[: ends[0]].reshape(grad_gains.shape),
        small[ends[1] : ends[1] + NBUCKET, :HEADS],
        small[ends[0] : ends[1]].reshape(expert_count, D).T,
        grad_expert_in,
        grad_expert_out,
        tally_counts,
    )


def solution(mesh):
    rows = P("exp", "seq", None)
    hidden = P("exp", None, "seq")
    return jax.shard_map(
        functools.partial(body, mesh.shape["seq"], mesh.shape["exp"]),
        mesh=mesh,
        in_specs=(rows, rows, P(), P(), P(), P(), P(), rows, hidden, hidden, rows),
        out_specs=(
            rows,
            rows,
            rows,
            P(),
            P(),
            P(),
            P(),
            P(),
            hidden,
            hidden,
            P("exp", "seq", None, None),
        ),
        check_vma=False,
    )
```

```python
import functools
import math

import jax
import jax.numpy as jnp
from jax import lax
from jax.experimental import pallas as pl
from jax.experimental.pallas import tpu as pltpu
from jax.sharding import PartitionSpec as P

D = 768
HEADS = 12
HEAD_DIM = 64
NBUCKET = 32
MAXDIST = 128
TILE = 128
PAIRS = HEADS * HEAD_DIM // TILE

MESH = pl.DeviceIdType.MESH
ANY = pl.BlockSpec(memory_space=pl.ANY)
SMEM = pl.BlockSpec(memory_space=pltpu.SMEM)

norm_eps = 1e-06
masked_score = -1e30
highest = lax.Precision.HIGHEST
log2e = 1.0 / math.log(2.0)
scale_factor = HEAD_DIM ** (-0.5)


def bucket_edges():
    half_count = NBUCKET // 2
    thresholds = []
    for bucket_number in range(1, NBUCKET):
        if bucket_number < half_count:
            thresholds.append(bucket_number)
        else:
            thresholds.append(
                int(
                    half_count
                    * (MAXDIST / half_count) ** ((bucket_number - half_count) / half_count)
                )
            )
    return thresholds


def rms_apply(values, gain_row):
    return (
        values * lax.rsqrt(jnp.mean(values * values, axis=-1, keepdims=True) + norm_eps) * gain_row
    )


def rms_backward(values, gain_row, upstream):
    _, pullback = jax.vjp(rms_apply, values, gain_row)
    return pullback(upstream)


def cost(us):
    return pl.CostEstimate(flops=us * 10**9, bytes_accessed=0, transcendentals=0)


def seq_cycle(n):
    cols = n // 4
    if n % 4 or cols < 2:
        return list(range(n))
    order = [0]
    for row in range(4):
        span = range(1, cols) if row % 2 == 0 else range(cols - 1, 0, -1)
        order += [row * cols + col for col in span]
    return order + [3 * cols, 2 * cols, cols]


def look_up(index, table):
    value = jnp.int32(table[0])
    for number, entry in enumerate(table[1:], 1):
        value = jnp.where(index == number, jnp.int32(entry), value)
    return value


def greet(others):
    barrier = pltpu.get_barrier_semaphore()
    for other in others:
        pl.semaphore_signal(barrier, inc=1, device_id=other, device_id_type=MESH)
    pl.semaphore_wait(barrier, len(others))


def seq_ring(n):
    order = seq_cycle(n)
    pos = look_up(lax.axis_index("seq"), [order.index(i) for i in range(n)])

    def at(place):
        return look_up(lax.rem(place + 4 * n, n), order)

    return pos, at, ({"seq": at(pos + 1)}, {"seq": at(pos - 1)})


def gather_kernel(n, parts, *refs):
    sources, proj_ref, outs = refs[:2], refs[2], refs[3:10]
    lands, w_buf, bufs = refs[10:12], refs[12], refs[13:18]
    own_sem, w_sem, send_sem, recv_sem, store_sem = refs[18:]
    pos, at, sides = seq_ring(n)
    me = at(pos)
    greet(sides)
    own = [pltpu.make_async_copy(sources[a], lands[a].at[me], own_sem.at[a]) for a in range(2)]
    weights = [
        pltpu.make_async_copy(proj_ref.at[number], w_buf.at[i], w_sem.at[i])
        for i, number in enumerate((0, 1, 2, 4, 5))
    ]
    started, latest, stored = [], {}, []

    def pass_on(step):
        for part in range(parts):
            for a in range(2):
                rows = sources[a].shape[0] // 2 // parts
                for way in range(2):
                    if step:
                        latest[a, way, part].wait_recv()
                    if step == n - 1:
                        continue
                    block = at(pos - step) if way == 0 else at(pos + step)
                    span = pl.ds((way * parts + part) * rows, rows)
                    copy = pltpu.make_async_remote_copy(
                        src_ref=lands[a].at[block, span] if step else sources[a].at[span],
                        dst_ref=lands[a].at[block, span],
                        send_sem=send_sem.at[a, way, step, part],
                        recv_sem=recv_sem.at[a, way, step, part],
                        device_id=sides[way],
                        device_id_type=MESH,
                    )
                    copy.start()
                    started.append(copy)
                    latest[a, way, part] = copy

    def store(source, target, number, step, way):
        copy = pltpu.make_async_copy(source, target, store_sem.at[number, step, way])
        copy.start()
        stored.append(copy)

    def work(step):
        blocks = (at(pos - step), at(pos + step))
        for a in range(2):
            half = sources[a].shape[0] // 2
            spans = (pl.ds(0, half), pl.ds(half, half))
            rows = jnp.concatenate([lands[a][blocks[way], spans[way], :] for way in range(2)], axis=0)
            for i in range(2):
                buf = bufs[1 + 2 * a + i]
                made = dot_plain(rows, w_buf[1 + 2 * a + i]).astype(buf.dtype)
                for way in range(2):
                    buf[blocks[way], spans[way], :] = made[way * half : (way + 1) * half]
            for way in range(2):
                where = (blocks[way], spans[way])
                store(lands[a].at[where], outs[a].at[where], a, step, way)
                for i in range(2):
                    number = 1 + 2 * a + i
                    store(bufs[number].at[where], outs[2 + number].at[where], 2 + number, step, way)

    pass_on(0)
    for copy in own + weights:
        copy.start()
    for copy in own + weights:
        copy.wait()
    bufs[0][...] = dot_plain(lands[0][me], w_buf[0]).astype(bufs[0].dtype)
    store(bufs[0], outs[2], 2, 0, 0)
    work(0)
    for step in range(1, n):
        pass_on(step)
        work(step)
    for copy in started:
        copy.wait_send()
    for copy in stored:
        copy.wait()


def gather_projected(tokens, memory_rows, proj_in, n, number, parts=2):
    both = (tokens, memory_rows)
    copies = (2, 2, n - 1, parts)
    wide = [(n,) + x.shape for x in both]
    shapes = wide + [tokens.shape] + [wide[0]] * 2 + [wide[1]] * 2
    dma = pltpu.SemaphoreType.DMA
    return pl.pallas_call(
        functools.partial(gather_kernel, n, parts),
        out_shape=[jax.ShapeDtypeStruct(shape, tokens.dtype) for shape in shapes],
        in_specs=[ANY] * 3,
        out_specs=[ANY] * 7,
        scratch_shapes=[pltpu.VMEM(shape, tokens.dtype) for shape in wide]
        + [pltpu.VMEM((5,) + proj_in.shape[1:], tokens.dtype)]
        + [pltpu.VMEM(shape, tokens.dtype) for shape in shapes[2:]]
        + [dma((2,)), dma((5,)), dma(copies), dma(copies), dma((7, n, 2))],
        compiler_params=pltpu.CompilerParams(
            collective_id=number, has_side_effects=True, vmem_limit_bytes=58 << 20
        ),
        cost_estimate=cost(60),
        name="gather_projected",
    )(tokens, memory_rows, proj_in)


def scatter_kernel(n, parts, count, *refs):
    sources, outs = refs[:count], refs[count : 2 * count]
    own_bufs, got_bufs = refs[2 * count : 3 * count], refs[3 * count : 4 * count]
    own_sem, send_sem, recv_sem = refs[4 * count :]
    pos, at, sides = seq_ring(n)
    greet(sides)
    lanes = [(a, part, way) for a in range(count) for part in range(parts) for way in range(2)]

    def span(a, part, way):
        rows = sources[a].shape[1] // 2 // parts
        return pl.ds((way * parts + part) * rows, rows)

    def block(way, step):
        return at(pos - 1 - step) if way == 0 else at(pos + 1 + step)

    def send(lane, step, source):
        a, part, way = lane
        copy = pltpu.make_async_remote_copy(
            src_ref=source,
            dst_ref=got_bufs[a].at[way, step, part],
            send_sem=send_sem.at[a, way, step, part],
            recv_sem=recv_sem.at[a, way, step, part],
            device_id=sides[way],
            device_id_type=MESH,
        )
        copy.start()
        return copy

    latest, started, own = {}, [], {}
    for lane in lanes:
        a, part, way = lane
        latest[lane] = send(lane, 0, sources[a].at[block(way, 0), span(a, part, way)])
        started.append(latest[lane])
    for step in range(1, n):
        for lane in lanes:
            a, part, way = lane
            own[lane, step] = pltpu.make_async_copy(
                sources[a].at[block(way, step), span(a, part, way)],
                own_bufs[a].at[way, step - 1, part],
                own_sem.at[a, way, step - 1, part],
            )
            own[lane, step].start()
    for step in range(1, n):
        for lane in lanes:
            a, part, way = lane
            own[lane, step].wait()
            latest[lane].wait_recv()
            total = got_bufs[a][way, step - 1, part].astype(jnp.float32) + own_bufs[a][
                way, step - 1, part
            ].astype(jnp.float32)
            if step == n - 1:
                outs[a][span(a, part, way)] = total.astype(outs[a].dtype)
            else:
                got_bufs[a][way, step - 1, part] = total.astype(got_bufs[a].dtype)
                latest[lane] = send(lane, step, got_bufs[a].at[way, step - 1, part])
                started.append(latest[lane])
    for copy in started:
        copy.wait_send()


def ring_scatter(arrays, n, number, out_dtype, parts=2):
    count = len(arrays)
    copies = (count, 2, n - 1, parts)
    bufs = [
        pltpu.VMEM((2, n - 1, parts, a.shape[1] // 2 // parts, a.shape[2]), a.dtype)
        for a in arrays
    ]
    return pl.pallas_call(
        functools.partial(scatter_kernel, n, parts, count),
        out_shape=[jax.ShapeDtypeStruct(a.shape[1:], out_dtype) for a in arrays],
        in_specs=[ANY] * count,
        out_specs=[pl.BlockSpec(memory_space=pltpu.VMEM)] * count,
        scratch_shapes=bufs + bufs + [pltpu.SemaphoreType.DMA(copies)] * 3,
        compiler_params=pltpu.CompilerParams(
            collective_id=number, has_side_effects=True, vmem_limit_bytes=58 << 20
        ),
        name="ring_scatter",
    )(*arrays)


def finish_kernel(n, counts, *refs):
    few, many = counts
    refs = list(refs)
    take = lambda count: [refs.pop(0) for _ in range(count)]
    blocks, xs, sums, outs = take(few), take(many), take(few), take(many)
    own_bufs, got_bufs = take(few), take(few)
    mines, twins, crosses, gots = take(many), take(many), take(many), take(many)
    near_sem, far_sem, own_sem, pair_sem, cross_sem, ring_sem = refs
    pos, at, sides = seq_ring(n)
    exp = lax.axis_index("exp")
    core, chip = lax.rem(exp, 2), exp // 2
    peer, over = {"exp": exp + 1 - 2 * core}, {"exp": core + 2 * (1 - chip)}
    greet(sides + (peer, over))
    started = []

    def push(source, target, sems, index, to):
        copy = pltpu.make_async_remote_copy(
            src_ref=source,
            dst_ref=target,
            send_sem=sems.at[(0,) + index],
            recv_sem=sems.at[(1,) + index],
            device_id=to,
            device_id_type=MESH,
        )
        copy.start()
        started.append(copy)
        return copy

    def block(way, step):
        return at(pos - 1 - step) if way == 0 else at(pos + 1 + step)

    def fetch(source, target, sem):
        copy = pltpu.make_async_copy(source, target, sem)
        copy.start()
        return copy

    add = lambda *terms: functools.reduce(lambda u, v: u + v, [t.astype(jnp.float32) for t in terms])
    ways = range(2)
    lanes = [(a, way) for a in range(many) for way in ways]
    parts = 2
    rings = [(a, way, part) for part in range(parts) for a in range(few) for way in ways]

    def span(ref, way):
        half = ref.shape[-2] // 2
        return pl.ds(way * half, half)

    def piece(lane):
        a, way, part = lane
        rows = blocks[a].shape[-2] // 2 // parts
        return pl.ds(way * parts * rows + part * rows, rows), pl.ds(part * rows, rows)

    pairs, own, crossing, ring = {}, {}, {}, {}
    for side in range(2):
        for step in range(n):
            for lane in lanes:
                a, way = lane
                place = chip if side else 1 - chip
                where, rows = block(way, step), span(xs[a], way)
                pairs[side, lane, step] = push(
                    xs[a].at[1 - core, place, where, rows],
                    twins[a].at[side, way, step],
                    pair_sem,
                    (0, side) + lane + (step,),
                    peer,
                )
                own[side, lane, step] = fetch(
                    xs[a].at[core, place, where, rows],
                    mines[a].at[side, way, step],
                    own_sem.at[(side,) + lane + (step,)],
                )
        if side == 0:
            for lane in rings:
                a, way, part = lane
                wide, thin = piece(lane)
                ring[lane] = push(
                    blocks[a].at[block(way, 0), wide],
                    got_bufs[a].at[way, 0, thin],
                    far_sem,
                    lane + (0,),
                    sides[way],
                )
            near = {}
            for step in range(1, n):
                for lane in rings:
                    a, way, part = lane
                    wide, thin = piece(lane)
                    near[lane, step] = fetch(
                        blocks[a].at[block(way, step), wide],
                        own_bufs[a].at[way, step - 1, thin],
                        near_sem.at[lane + (step - 1,)],
                    )

    def scatter(step, which):
        for lane in rings:
            a, way, part = lane
            if part != which:
                continue
            wide, thin = piece(lane)
            near[lane, step].wait()
            ring[lane].wait_recv()
            total = add(got_bufs[a][way, step - 1, thin], own_bufs[a][way, step - 1, thin])
            if step == n - 1:
                sums[a][wide] = total.astype(sums[a].dtype)
            else:
                got_bufs[a][way, step - 1, thin] = total.astype(got_bufs[a].dtype)
                ring[lane] = push(
                    got_bufs[a].at[way, step - 1, thin],
                    got_bufs[a].at[way, step, thin],
                    far_sem,
                    lane + (step,),
                    sides[way],
                )

    for step in range(n):
        for lane in lanes:
            a, way = lane
            own[0, lane, step].wait()
            pairs[0, lane, step].wait_recv()
            mines[a][0, way, step] = add(mines[a][0, way, step], twins[a][0, way, step]).astype(
                mines[a].dtype
            )
            crossing[lane, step] = push(
                mines[a].at[0, way, step],
                crosses[a].at[way, step],
                cross_sem,
                (0,) + lane + (step,),
                over,
            )
    latest = {}
    waiting = [(step, part) for step in range(1, n) for part in range(parts)]
    for step in range(n):
        for lane in lanes:
            a, way = lane
            own[1, lane, step].wait()
            pairs[1, lane, step].wait_recv()
            crossing[lane, step].wait_recv()
            terms = [mines[a][1, way, step], twins[a][1, way, step], crosses[a][way, step]]
            if step:
                latest[lane].wait_recv()
                terms.append(gots[a][way, step - 1])
            mines[a][1, way, step] = add(*terms).astype(mines[a].dtype)
            if step < n - 1:
                latest[lane] = push(
                    mines[a].at[1, way, step],
                    gots[a].at[way, step],
                    ring_sem,
                    (0,) + lane + (step,),
                    sides[way],
                )
        if waiting:
            scatter(*waiting.pop(0))
    keep, done = [], []
    latest, crossing = {}, {}

    def target_of(lane, step, place):
        a, way = lane
        where = at(pos - step) if way == 0 else at(pos + step)
        return outs[a].at[core, place, where, span(outs[a], way)]

    def hand_on(step):
        for lane in lanes:
            crossing[lane, step].wait_recv()
            target = target_of(lane, step, 1 - chip)
            done.append(push(target, target, pair_sem, (1, 1) + lane + (step,), peer))

    for step in range(n):
        for lane in lanes:
            a, way = lane
            if step:
                latest[lane].wait_recv()
            target = target_of(lane, step, chip)
            source = target if step else mines[a].at[1, way, n - 1]
            if step < n - 1:
                latest[lane] = push(source, target, ring_sem, (1,) + lane + (step,), sides[way])
            crossing[lane, step] = push(source, target, cross_sem, (1,) + lane + (step,), over)
            done.append(push(source, target, pair_sem, (1, 0) + lane + (step,), peer))
            if step == 0:
                keep.append(fetch(source, target, own_sem.at[(0,) + lane + (0,)]))
        if waiting:
            scatter(*waiting.pop(0))
        if step:
            hand_on(step - 1)
    hand_on(n - 1)
    while waiting:
        scatter(*waiting.pop(0))
    for copy in keep:
        copy.wait()
    for copy in done:
        copy.wait_recv()
    for copy in started:
        copy.wait_send()


def finish(blocks, rows_in, small, n, m, number):
    rows, cols = rows_in.shape
    each = rows // (4 * n)
    if m != 4 or rows % (4 * n * 32) or small.shape[0] > 4 * n * 16:
        return (
            ring_scatter(blocks, n, number, jnp.float32),
            *lax.psum((rows_in, small), ("seq", "exp")),
        )
    padded = jnp.pad(small, ((0, 4 * n * 16 - small.shape[0]), (0, 0)))
    arrays = [rows_in.reshape(2, 2, n, each, cols), padded.reshape(2, 2, n, 16, TILE)]
    few, many = len(blocks), len(arrays)
    halves = [(x.shape[-2] // 2, x.shape[-1], x.dtype) for x in blocks + arrays]
    ring_bufs = [pltpu.VMEM((2, n - 1, r, c), t) for r, c, t in halves[:few]]
    two = [pltpu.VMEM((2, 2, n, r, c), t) for r, c, t in halves[few:]]
    one = [pltpu.VMEM((2, n, r, c), t) for r, c, t in halves[few:]]
    dma = pltpu.SemaphoreType.DMA
    results = pl.pallas_call(
        functools.partial(finish_kernel, n, (few, many)),
        out_shape=[jax.ShapeDtypeStruct(x.shape[1:], jnp.float32) for x in blocks]
        + [jax.ShapeDtypeStruct(x.shape, x.dtype) for x in arrays],
        in_specs=[ANY] * (few + many),
        out_specs=[pl.BlockSpec(memory_space=pltpu.VMEM)] * few + [ANY] * many,
        scratch_shapes=ring_bufs * 2
        + two * 2
        + one * 2
        + [
            dma((few, 2, 2, n)),
            dma((2, few, 2, 2, n)),
            dma((2, many, 2, n)),
            dma((2, 2, 2, many, 2, n)),
            dma((2, 2, many, 2, n)),
            dma((2, 2, many, 2, n)),
        ],
        compiler_params=pltpu.CompilerParams(
            collective_id=number, has_side_effects=True, vmem_limit_bytes=58 << 20
        ),
        cost_estimate=cost(120),
        name="finish",
    )(*blocks, *arrays)
    return results[:few], results[few].reshape(rows, cols), results[-1].reshape(-1, TILE)


def dot_last(a, b):
    return lax.dot_general(a, b, (((1,), (1,)), ((), ())), preferred_element_type=jnp.float32)


def dot_first(a, b):
    return lax.dot_general(a, b, (((0,), (0,)), ((), ())), preferred_element_type=jnp.float32)


def dot_plain(a, b):
    return jnp.dot(a, b, preferred_element_type=jnp.float32)


def head_masks(dtype):
    low = lax.broadcasted_iota(jnp.int32, (1, TILE), 1) < HEAD_DIM
    first = jnp.where(low, 1.0, 0.0).astype(jnp.float32)
    return first.astype(dtype), (1.0 - first).astype(dtype)


def split_heads(pair):
    return jnp.concatenate([pair * mask for mask in head_masks(pair.dtype)], axis=0)


def own_bias(tiles, count):
    rows = []
    for r in range(count):
        row = []
        for c in range(count):
            if c == r:
                row.append(tiles[:, TILE:])
            elif c == r - 1:
                row.append(tiles[:, :TILE])
            else:
                row.append(jnp.full((TILE, TILE), 0.0 if c < r else masked_score, jnp.float32))
        rows.append(jnp.concatenate(row, axis=1))
    return jnp.concatenate(rows, axis=0)


def edge_bias(tiles, rows):
    edge = []
    for h in range(2):
        first = jnp.concatenate(
            [jnp.zeros((rows - TILE, TILE), jnp.float32), tiles[h][:, :TILE].T], axis=0
        )
        edge += [first, jnp.zeros((rows, rows - TILE), jnp.float32)]
    return jnp.concatenate(edge, axis=1)


def each_far(s, block, act, times=3):
    far = jnp.maximum(s - 1, 0)
    bundles = far // times

    def bundle(j, carry):
        act(pl.multiple_of(j * times * block, block), times)
        return carry

    def single(j, carry):
        act(pl.multiple_of(j * block, block), 1)
        return carry

    lax.fori_loop(0, bundles, bundle, 0)
    lax.fori_loop(bundles * times, far, single, 0)


def attend_kernel(causal, block, s_ref, q_ref, k_ref, v_ref, *refs):
    if causal:
        line_ref, low_ref, wide_ref, lse_ref, acc_ref, top_ref = refs
    else:
        low_ref, wide_ref, lse_ref, acc_ref, top_ref = refs
    rows = q_ref.shape[0]
    both = split_heads(q_ref[...])

    def visit(start, bias, first, times=1):
        ones = jnp.ones((16, times * block), v_ref.dtype)
        keys = k_ref[pl.ds(start, times * block), :]
        values = v_ref[pl.ds(start, times * block), :]
        t = dot_last(keys, both) * (scale_factor * log2e)
        if bias is not None:
            t = t + bias
        top = jnp.max(t, axis=0, keepdims=True)
        if not first:
            before = top_ref[...]
            top = jnp.maximum(before, top)
            fade = jnp.exp2(before - top)
        top_ref[...] = top
        p = jnp.exp2(t - top).astype(values.dtype)
        part = dot_plain(jnp.concatenate([values.T, ones], axis=0), p)
        if first:
            acc_ref[...] = part
        else:
            acc_ref[...] = acc_ref[...] * fade + part

    if causal:
        s = s_ref[0]
        count = rows // TILE
        tiles = [bias_tile(line_ref, h) for h in range(2)]
        visit(
            pl.multiple_of(s * block, block),
            jnp.concatenate([own_bias(tiles[h], count).T for h in range(2)], axis=1),
            True,
        )

        @pl.when(s > 0)
        def _():
            visit(pl.multiple_of((s - 1) * block, block), edge_bias(tiles, rows), False)

        each_far(s, block, lambda start, times: visit(start, None, False, times))
    else:
        for j in range(k_ref.shape[0] // block):
            visit(j * block, None, j == 0)
    sums = acc_ref[TILE : TILE + 1, :]
    wide = jnp.concatenate(
        [
            acc_ref[:HEAD_DIM, :rows] / sums[:, :rows],
            acc_ref[HEAD_DIM:TILE, rows:] / sums[:, rows:],
        ],
        axis=0,
    ).T
    wide_ref[...] = wide
    low_ref[...] = wide.astype(low_ref.dtype)
    lse = top_ref[...] + jnp.log2(sums)
    lse_ref[0] = jnp.concatenate([lse[:, :rows], lse[:, rows:]], axis=0)


def attend(seq_at, queries, keys, values, lines):
    rows, total = queries.shape[0], keys.shape[0]
    causal = lines is not None
    block = rows if causal else math.gcd(total, 1024)
    pair = pl.BlockSpec((rows, TILE), lambda g: (0, g))
    long = pl.BlockSpec((total, TILE), lambda g: (0, g))
    extra, specs = [], []
    if causal:
        extra, specs = [lines], [pl.BlockSpec((1,) + lines.shape[1:], lambda g: (g, 0, 0))]
    return pl.pallas_call(
        functools.partial(attend_kernel, causal, block),
        grid=(PAIRS,),
        out_shape=[
            jax.ShapeDtypeStruct((rows, D), jnp.bfloat16),
            jax.ShapeDtypeStruct((rows, D), jnp.float32),
            jax.ShapeDtypeStruct((PAIRS, 2, rows), jnp.float32),
        ],
        in_specs=[SMEM, pair, long, long] + specs,
        out_specs=[pair, pair, pl.BlockSpec((1, 2, rows), lambda g: (g, 0, 0))],
        scratch_shapes=[
            pltpu.VMEM((TILE + 16, 2 * rows), jnp.float32),
            pltpu.VMEM((1, 2 * rows), jnp.float32),
        ],
        compiler_params=pltpu.CompilerParams(vmem_limit_bytes=48 << 20),
        cost_estimate=cost(40 if causal else 10),
        name="attend_self" if causal else "attend_cross",
    )(seq_at, queries, keys, values, *extra)


def attend_back_kernel(causal, block, s_ref, q_ref, k_ref, v_ref, up_ref, wide_ref, lse_ref, *refs):
    if causal:
        line_ref, dq_ref, dk_ref, dv_ref, near_ref, sum_ref, acc_ref = refs
    else:
        dq_ref, dk_ref, dv_ref, acc_ref = refs
    rows = q_ref.shape[0]
    both = split_heads(q_ref[...])
    up = up_ref[...]
    up_both = split_heads(up)
    turned = (up.astype(jnp.float32) * wide_ref[...]).T
    delta = jnp.concatenate(
        [
            jnp.sum(turned[:HEAD_DIM], axis=0, keepdims=True),
            jnp.sum(turned[HEAD_DIM:], axis=0, keepdims=True),
        ],
        axis=1,
    )
    lse = jnp.concatenate([lse_ref[0, :1], lse_ref[0, 1:]], axis=1)

    def visit(start, bias, first, times=1):
        ones = jnp.ones((16, times * block), k_ref.dtype)
        keys = k_ref[pl.ds(start, times * block), :]
        values = v_ref[pl.ds(start, times * block), :]
        t = dot_last(keys, both) * (scale_factor * log2e)
        if bias is not None:
            t = t + bias
        p = jnp.exp2(t - lse)
        ds = (p * (dot_last(values, up_both) - delta)).astype(keys.dtype)
        dv_ref[pl.ds(start, times * block), :] = dot_plain(p.astype(keys.dtype), up_both).astype(
            dv_ref.dtype
        )
        dk_ref[pl.ds(start, times * block), :] = (dot_plain(ds, both) * scale_factor).astype(dk_ref.dtype)
        part = dot_plain(jnp.concatenate([keys.T, ones], axis=0), ds)
        if first:
            acc_ref[...] = part
        else:
            acc_ref[...] += part
        return ds

    if causal:
        s = s_ref[0]
        count = rows // TILE
        tiles = [bias_tile(line_ref, h) for h in range(2)]
        ds = visit(
            pl.multiple_of(s * block, block),
            jnp.concatenate([own_bias(tiles[h], count).T for h in range(2)], axis=1),
            True,
        )
        for h in range(2):
            same = before = jnp.zeros((TILE, TILE), jnp.float32)
            for r in range(count):
                columns = slice(h * rows + r * TILE, h * rows + (r + 1) * TILE)
                same = same + ds[r * TILE : (r + 1) * TILE, columns].astype(jnp.float32)
                if r:
                    before = before + ds[(r - 1) * TILE : r * TILE, columns].astype(jnp.float32)
            near_ref[h, :TILE] = before
            near_ref[h, TILE:] = same

        @pl.when(s > 0)
        def _():
            ds = visit(pl.multiple_of((s - 1) * block, block), edge_bias(tiles, rows), False)
            for h in range(2):
                near_ref[h, :TILE] += ds[rows - TILE :, h * rows : h * rows + TILE].astype(
                    jnp.float32
                )

        each_far(s, block, lambda start, times: visit(start, None, False, times))

        def beyond(j, carry):
            start = pl.multiple_of(j * block, block)
            dk_ref[pl.ds(start, block), :] = jnp.zeros((block, TILE), dk_ref.dtype)
            dv_ref[pl.ds(start, block), :] = jnp.zeros((block, TILE), dv_ref.dtype)
            return carry

        lax.fori_loop(s + 1, k_ref.shape[0] // block, beyond, 0)
        sum_ref[0] = jnp.concatenate(
            [acc_ref[TILE : TILE + 1, :rows], acc_ref[TILE : TILE + 1, rows:]], axis=0
        )
    else:
        for j in range(k_ref.shape[0] // block):
            visit(j * block, None, j == 0)
    dq = jnp.concatenate([acc_ref[:HEAD_DIM, :rows], acc_ref[HEAD_DIM:TILE, rows:]], axis=0)
    dq_ref[...] = (dq.T * scale_factor).astype(dq_ref.dtype)


def attend_back(seq_at, queries, keys, values, upstream, wide, lse, lines):
    rows, total = queries.shape[0], keys.shape[0]
    causal = lines is not None
    block = rows if causal else math.gcd(total, 1024)
    pair = pl.BlockSpec((rows, TILE), lambda g: (0, g))
    long = pl.BlockSpec((total, TILE), lambda g: (0, g))
    line = pl.BlockSpec((1, 2, rows), lambda g: (g, 0, 0))
    extra, specs, shapes, out_specs = [], [], [], []
    if causal:
        extra, specs = [lines], [pl.BlockSpec((1,) + lines.shape[1:], lambda g: (g, 0, 0))]
        shapes = [
            jax.ShapeDtypeStruct((HEADS, 2 * TILE, TILE), jnp.float32),
            jax.ShapeDtypeStruct((PAIRS, 2, rows), jnp.float32),
        ]
        out_specs = [pl.BlockSpec((2, 2 * TILE, TILE), lambda g: (g, 0, 0)), line]
    return pl.pallas_call(
        functools.partial(attend_back_kernel, causal, block),
        grid=(PAIRS,),
        out_shape=[
            jax.ShapeDtypeStruct((rows, D), jnp.bfloat16),
            jax.ShapeDtypeStruct((total, D), jnp.bfloat16),
            jax.ShapeDtypeStruct((total, D), jnp.bfloat16),
        ]
        + shapes,
        in_specs=[SMEM, pair, long, long, pair, pair, line] + specs,
        out_specs=[pair, long, long] + out_specs,
        scratch_shapes=[pltpu.VMEM((TILE + 16, 2 * rows), jnp.float32)],
        compiler_params=pltpu.CompilerParams(vmem_limit_bytes=48 << 20),
        cost_estimate=cost(48 if causal else 15),
        name="attend_self_back" if causal else "attend_cross_back",
    )(seq_at, queries, keys, values, upstream, wide, lse, *extra)


def key_value_back(x_ref, dk_ref, dv_ref, wk_ref, wv_ref, dx_ref):
    x, dk, dv = x_ref[...], dk_ref[...], dv_ref[...]
    dx = dot_last(dk, wk_ref[0]) + dot_last(dv, wv_ref[0])
    dx_ref[...] = dx.astype(dx_ref.dtype)
    gain = jnp.sum(dx * x.astype(jnp.float32), axis=0, keepdims=True)
    return gain, dot_first(x, dk), dot_first(x, dv)


def add_up(step, last, made, totals, outs):
    @pl.when(step == 0)
    def _():
        for total, term in zip(totals, made):
            total[...] = term

    @pl.when(step > 0)
    def _():
        for total, term in zip(totals, made):
            total[...] += term

    @pl.when(step == last)
    def _():
        for out, total in zip(outs, totals):
            out[...] = total[...].astype(out.dtype)


def memory_back_kernel(x_ref, dk_ref, dv_ref, wk_ref, wv_ref, dx_ref, grad_ref, k_acc, v_acc):
    _, gk, gv = key_value_back(x_ref, dk_ref, dv_ref, wk_ref, wv_ref, dx_ref)
    outs = [grad_ref.at[0], grad_ref.at[1]]
    add_up(pl.program_id(0), pl.num_programs(0) - 1, (gk, gv), (k_acc, v_acc), outs)


def token_back_kernel(*refs):
    x_ref, dk_ref, dv_ref, wk_ref, wv_ref, own_ref, dq_ref, wq_ref = refs[:8]
    terms, (dx_ref, grad_ref, gain_ref, query_ref), sums = refs[8:14], refs[14:18], refs[18:20]
    k_acc, v_acc = refs[20:]
    step, last = pl.program_id(0), pl.num_programs(0) - 1
    for i, out in enumerate(sums):
        own, *others = terms[3 * i : 3 * i + 3]
        total = own[...]
        for other in others:
            total = total + other[...].astype(jnp.float32)
        out[...] = total
    gain, gk, gv = key_value_back(x_ref, dk_ref, dv_ref, wk_ref, wv_ref, dx_ref)
    add_up(step, last, (gk, gv), (k_acc, v_acc), [grad_ref.at[1], grad_ref.at[2]])

    @pl.when(step == 0)
    def _():
        own, dq = own_ref[...], dq_ref[...]
        back = dot_last(dq, wq_ref[0])
        query_ref[...] = back
        gain_ref[...] = gain + jnp.sum(back * own.astype(jnp.float32), axis=0, keepdims=True)
        grad_ref[0] = dot_first(own, dq).astype(grad_ref.dtype)

    @pl.when(step > 0)
    def _():
        gain_ref[...] += gain


def memory_back(tokens, grad_keys, grad_values, proj_in):
    total = tokens.shape[0]
    rows = math.gcd(total, 512)
    block = pl.BlockSpec((rows, D), lambda i: (i, 0))
    weight = lambda number: pl.BlockSpec((1, D, D), lambda i: (number, 0, 0))
    return pl.pallas_call(
        memory_back_kernel,
        grid=(total // rows,),
        out_shape=[
            jax.ShapeDtypeStruct(tokens.shape, tokens.dtype),
            jax.ShapeDtypeStruct((2, D, D), tokens.dtype),
        ],
        in_specs=[block] * 3 + [weight(4), weight(5)],
        out_specs=[block, pl.BlockSpec((2, D, D), lambda i: (0, 0, 0))],
        scratch_shapes=[pltpu.VMEM((D, D), jnp.float32)] * 2,
        compiler_params=pltpu.CompilerParams(vmem_limit_bytes=48 << 20),
        cost_estimate=cost(8),
        name="memory_back",
    )(tokens, grad_keys, grad_values, proj_in, proj_in)


def token_back(tokens, grad_keys, grad_values, own, grad_queries, proj_in, terms):
    steps = tokens.shape[0] // (2 * own.shape[0])
    block = pl.BlockSpec((2 * own.shape[0], D), lambda i: (i, 0))
    weight = lambda number: pl.BlockSpec((1, D, D), lambda i: (number, 0, 0))
    whole = pl.BlockSpec(own.shape, lambda i: (0, 0))
    count, _, hidden = terms[0].shape
    expert = pl.BlockSpec((count, D // steps, hidden), lambda i: (0, i, 0))
    return pl.pallas_call(
        token_back_kernel,
        grid=(steps,),
        out_shape=[
            jax.ShapeDtypeStruct(tokens.shape, tokens.dtype),
            jax.ShapeDtypeStruct((8, D, D), tokens.dtype),
            jax.ShapeDtypeStruct((1, D), jnp.float32),
            jax.ShapeDtypeStruct(own.shape, jnp.float32),
        ]
        + [jax.ShapeDtypeStruct(terms[0].shape, jnp.float32)] * 2,
        in_specs=[block] * 3 + [weight(1), weight(2), whole, whole, weight(0)] + [expert] * 6,
        out_specs=[
            block,
            pl.BlockSpec((3, D, D), lambda i: (0, 0, 0)),
            pl.BlockSpec((1, D), lambda i: (0, 0)),
            whole,
            expert,
            expert,
        ],
        scratch_shapes=[pltpu.VMEM((D, D), jnp.float32)] * 2,
        compiler_params=pltpu.CompilerParams(vmem_limit_bytes=56 << 20),
        cost_estimate=cost(24),
        name="token_back",
    )(tokens, grad_keys, grad_values, proj_in, proj_in, own, grad_queries, proj_in, *terms)


def bias_lines(bias_table):
    at = jnp.arange(3 * TILE, dtype=jnp.int32)
    distance = jnp.where(at <= 2 * TILE, TILE - at, 4 * TILE - at)
    table = (bias_table - bias_table[NBUCKET - 1 :]) * log2e
    terms = jnp.broadcast_to(table[0][:, None], (HEADS, 3 * TILE))
    for number, threshold in enumerate(bucket_edges()):
        terms = jnp.where((distance >= threshold)[None], table[number + 1][:, None], terms)
    return jnp.where((distance >= 0)[None], terms, masked_score).reshape(PAIRS, 2, 3 * TILE)


def bias_tile(line_ref, h):
    line = jnp.broadcast_to(line_ref[0, h : h + 1, :], (TILE, 3 * TILE))
    return pltpu.roll(line, 0, 1, stride=1, stride_axis=0)[:, : 2 * TILE]


def bias_gradient(near, sums):
    distance = (
        TILE
        + jnp.arange(TILE, dtype=jnp.int32)[None, :]
        - jnp.arange(2 * TILE, dtype=jnp.int32)[:, None]
    )
    bucket = jnp.zeros(distance.shape, jnp.int32)
    for threshold in bucket_edges():
        bucket = bucket + (distance >= threshold).astype(jnp.int32)
    onehot = (
        bucket.reshape(-1)[None, :] == jnp.arange(NBUCKET, dtype=jnp.int32)[:, None]
    ).astype(jnp.float32)
    flat = near.reshape(HEADS, -1)
    table = lax.dot_general(
        onehot, flat, (((1,), (1,)), ((), ())), precision=highest
    )
    far = jnp.sum(sums, axis=-1).reshape(HEADS) - jnp.sum(flat, axis=-1)
    last = jnp.arange(NBUCKET, dtype=jnp.int32)[:, None] == NBUCKET - 1
    return table + jnp.where(last, far[None, :], 0.0)


def expert_kernel(n, m, slots, *refs):
    x_ref, maps, result_ref, grads = refs[0], refs[1:7], refs[7], refs[8:14]
    rows, parts, backs, up_all, down_all, act_all, du_all = refs[14:21]
    grad_bufs, far_bufs = refs[21:29], refs[29:31]
    map_sem, own_sem, grad_sem, go_sem, back_sem, term_sem, far_sem = refs[31:]
    seq, exp = lax.axis_index("seq"), lax.axis_index("exp")
    groups, count = n // QUAD, x_ref.shape[1] // slots
    batch = max(1, 128 // slots)
    far = [(g, k) for g in range(1, groups) for k in range(m)]
    moves = far + [(0, k) for k in range(1, m)]
    source_of = lambda k: lax.rem(exp + m - k, m)

    def push(source, target, sems, g, k, to_seq, to_exp):
        copy = pltpu.make_async_remote_copy(
            src_ref=source,
            dst_ref=target,
            send_sem=sems.at[0, g, k],
            recv_sem=sems.at[1, g, k],
            device_id={"seq": to_seq, "exp": to_exp},
            device_id_type=MESH,
        )
        copy.start()
        return copy

    def place(g, k):
        return lax.rem(seq + g * QUAD, n), lax.rem(exp + k, m)

    to_next, to_last = quad_moves(n)
    side = {"next": look_up(seq, [b for _, b in to_next]), "last": look_up(seq, [b for _, b in to_last])}
    greet(
        [dict(zip(("seq", "exp"), place(g, k))) for g, k in moves]
        + [{"seq": side["next"], "exp": exp}, {"seq": side["last"], "exp": exp}]
    )
    going = {}
    for g, k in moves:
        to_seq, to_exp = place(g, k)
        going[g, k] = push(x_ref.at[to_exp], rows.at[g, exp], go_sem, g, k, to_seq, to_exp)
    own = pltpu.make_async_copy(x_ref.at[exp], rows.at[0, exp], own_sem.at[0])
    own.start()
    fetched = []
    for j in range(1, QUAD):
        j = j % (QUAD - 1)
        for at, (source, target) in enumerate(((maps[2 * j], up_all), (maps[2 * j + 1], down_all))):
            copy = pltpu.make_async_copy(source, target.at[j], map_sem.at[at, j])
            copy.start()
            fetched.append(copy)
    for copy in fetched:
        copy.wait()
    far_maps = [
        push(up_all.at[1], up_all.at[3], far_sem, 0, 0, side["next"], exp),
        push(down_all.at[2], down_all.at[3], far_sem, 0, 1, side["last"], exp),
    ]
    own.wait()
    slope = math.sqrt(2.0 / math.pi)
    coming = {}

    def work(g, first, last):
        for k in range(first, last):
            if g or k:
                going[g, k].wait_recv()
        size = (last - first) * slots
        base = (g * m + first) * slots

        def one(e, carry):
            start = pl.multiple_of(e * slots, slots)
            piece = jnp.concatenate(
                [rows[g, source_of(k), pl.ds(start, slots), :] for k in range(first, last)], axis=0
            )
            tokens, upstream = piece[:, :D], piece[:, D:]
            result = back = None
            for j in range(QUAD):
                up_map, down_map = up_all[j, e], down_all[j, e]
                u = dot_plain(tokens, up_map)
                square = u * u
                bend = jnp.tanh(slope * (u + 0.044715 * (square * u)))
                half = 0.5 * (1.0 + bend)
                act = (u * half).astype(tokens.dtype)
                rise = half + 0.5 * u * (1.0 - bend * bend) * (
                    slope * (1.0 + 3 * 0.044715 * square)
                )
                du = (dot_plain(upstream, down_map) * rise).astype(tokens.dtype)
                act_all[e, j, base : base + size] = act
                du_all[e, j, base : base + size] = du
                y, dn = dot_last(act, down_map), dot_last(du, up_map)
                result = y if result is None else result + y
                back = dn if back is None else back + dn
            for i, k in enumerate(range(first, last)):
                span = slice(i * slots, (i + 1) * slots)
                where = (g, source_of(k), pl.ds(start, slots))
                parts[where + (slice(0, D),)] = result[span].astype(parts.dtype)
                parts[where + (slice(D, 2 * D),)] = back[span].astype(parts.dtype)
            return carry

        lax.fori_loop(0, count, one, 0)
        for k in range(first, last):
            if g or k:
                source = source_of(k)
                coming[g, k] = push(
                    parts.at[g, source],
                    backs.at[g, exp],
                    back_sem,
                    g,
                    k,
                    lax.rem(seq + n - g * QUAD, n),
                    source,
                )

    for copy in far_maps:
        copy.wait_recv()
    work(0, 0, m)
    for g in range(1, groups):
        for first in range(0, m, batch):
            work(g, first, min(m, first + batch))

    total = groups * m * slots

    def weigh(j):
        def one(e, carry):
            start = pl.multiple_of(e * slots, slots)
            piece = jnp.concatenate(
                [
                    rows[g, source_of(k), pl.ds(start, slots), :]
                    for g in range(groups)
                    for k in range(m)
                ],
                axis=0,
            )
            tokens, upstream = piece[:, :D], piece[:, D:]
            up_buf, down_buf = grad_bufs[2 * j], grad_bufs[2 * j + 1]
            up_buf[e] = dot_first(tokens, du_all[e, j, :total]).astype(up_buf.dtype)
            down_buf[e] = dot_first(upstream, act_all[e, j, :total]).astype(down_buf.dtype)
            return carry

        lax.fori_loop(0, count, one, 0)

    def term(source, target, number, to):
        return push(source, target, term_sem, 0, number, side[to], exp)

    def store(source, number):
        copy = pltpu.make_async_copy(source, grads[number], grad_sem.at[number])
        copy.start()
        return copy

    weigh(3)
    terms_out = [
        term(grad_bufs[6], far_bufs[0], 0, "next"),
        term(grad_bufs[7], far_bufs[1], 1, "last"),
    ]
    weigh(1)
    weigh(2)
    weigh(0)
    stored = [
        store(grad_bufs[i], number) for number, i in ((0, 0), (1, 1), (4, 2), (5, 5))
    ]
    for number, (buf, far_buf) in enumerate(((grad_bufs[4], far_bufs[0]), (grad_bufs[3], far_bufs[1]))):
        terms_out[number].wait_recv()
        buf[...] = (buf[...].astype(jnp.float32) + far_buf[...].astype(jnp.float32)).astype(buf.dtype)
        stored.append(store(buf, 2 + number))
    for k in range(m):
        where = source_of(k)
        terms = []
        for g in range(groups):
            back_k = (m - k) % m
            if g == 0 and k == 0:
                terms.append(parts[0, exp])
            else:
                coming[g, back_k].wait_recv()
                terms.append(backs[g, where])
        total_row = terms[0].astype(jnp.float32)
        for term in terms[1:]:
            total_row = total_row + term.astype(jnp.float32)
        result_ref[where] = total_row.astype(result_ref.dtype)
    for copy in stored:
        copy.wait()
    for copy in terms_out + far_maps:
        copy.wait_send()
    for copies in (going, coming):
        for copy in copies.values():
            copy.wait_send()


def run_experts(x, maps, n, m, slots, number):
    groups = n // QUAD
    count, _, hidden = maps[0].shape
    total = groups * m * slots
    big = pltpu.VMEM((groups,) + x.shape, x.dtype)
    stack = pltpu.VMEM((QUAD,) + maps[0].shape, x.dtype)
    kept = pltpu.VMEM((count, QUAD, total, hidden), x.dtype)
    grads = [(maps[0].shape, jnp.float32 if i < 2 else jnp.bfloat16) for i in range(2 * QUAD)]
    dma = pltpu.SemaphoreType.DMA
    return pl.pallas_call(
        functools.partial(expert_kernel, n, m, slots),
        out_shape=[jax.ShapeDtypeStruct(x.shape, x.dtype)]
        + [jax.ShapeDtypeStruct(shape, dtype) for shape, dtype in grads[:6]],
        in_specs=[ANY] * (1 + len(maps)),
        out_specs=[pl.BlockSpec(memory_space=pltpu.VMEM)] + [ANY] * 6,
        scratch_shapes=[big] * 3
        + [stack] * 2
        + [kept] * 2
        + [pltpu.VMEM(shape, dtype) for shape, dtype in grads + grads[6:]]
        + [
            dma((2, QUAD)),
            dma((1,)),
            dma((6,)),
            dma((2, groups, m)),
            dma((2, groups, m)),
            dma((2, 1, 2)),
            dma((2, 1, 2)),
        ],
        compiler_params=pltpu.CompilerParams(
            collective_id=number, has_side_effects=True, vmem_limit_bytes=60 << 20
        ),
        cost_estimate=cost(150),
        name="run_experts",
    )(x, *maps)


QUAD = 4


def quad_moves(n):
    ring = (0, 1, 3, 2)
    step = lambda i, by: i - i % QUAD + ring[(ring.index(i % QUAD) + by) % QUAD]
    return [(i, step(i, 1)) for i in range(n)], [(i, step(i, -1)) for i in range(n)]


def project(source, matrix):
    return jnp.dot(source, matrix, preferred_element_type=jnp.float32).astype(jnp.bfloat16)


def weight_grad(source, upstream):
    return jnp.einsum("td,te->de", source, upstream, preferred_element_type=jnp.float32).astype(
        jnp.bfloat16
    )


def input_grad(upstream, matrix):
    return jnp.einsum("te,de->td", upstream, matrix, preferred_element_type=jnp.float32)


def body(
    n,
    m,
    hidden_in,
    memory,
    proj_in,
    proj_out,
    norm_gains,
    rel_bias,
    router,
    expert_choice,
    expert_in,
    expert_out,
    cotangent,
):
    tokens = hidden_in[0].astype(jnp.float32)
    memory_rows = memory[0]
    memory_count = memory_rows.shape[0]
    gain_rows = norm_gains.astype(jnp.float32)
    token_count = tokens.shape[0]
    seq_at = lax.axis_index("seq").astype(jnp.int32).reshape(1)
    normed_self = rms_apply(tokens, gain_rows[0]).astype(jnp.bfloat16)
    lines = bias_lines(rel_bias)

    normed_all, memory_all, queries, key_all, value_all, memory_key_all, memory_value_all = (
        gather_projected(normed_self, memory_rows, proj_in, n, 1)
    )
    to_next, to_last = quad_moves(n)
    in_own, out_own, normed_all = lax.optimization_barrier((expert_in, expert_out, normed_all))
    in_last, out_last = (lax.ppermute(w, "seq", to_next) for w in (in_own, out_own))
    in_next, out_next = (lax.ppermute(w, "seq", to_last) for w in (in_own, out_own))
    normed_all = normed_all.reshape(n * token_count, D)
    memory_all = memory_all.reshape(n * memory_count, D)
    key_all, value_all = (x.reshape(n * token_count, D) for x in (key_all, value_all))
    memory_key_all, memory_value_all = (
        x.reshape(n * memory_count, D) for x in (memory_key_all, memory_value_all)
    )
    attended_self_low, attended_self, lse_self = attend(
        seq_at, queries, key_all, value_all, lines
    )
    after_self = tokens + jnp.dot(
        attended_self_low, proj_out[0], preferred_element_type=jnp.float32
    )

    normed_cross = rms_apply(after_self, gain_rows[1]).astype(jnp.bfloat16)
    cross_queries = project(normed_cross, proj_in[3])
    attended_cross_low, attended_cross, lse_cross = attend(
        seq_at, cross_queries, memory_key_all, memory_value_all, None
    )
    after_cross = after_self + jnp.dot(
        attended_cross_low, proj_out[1], preferred_element_type=jnp.float32
    )

    mixed_low = rms_apply(after_cross, gain_rows[2]).astype(jnp.bfloat16)
    softmax_probs = jax.nn.softmax(
        jnp.dot(mixed_low, router, preferred_element_type=jnp.float32), axis=-1
    )
    expert_count = router.shape[1]
    local_experts = expert_in.shape[0]
    capacity = max(2, 5 * token_count // (4 * expert_count))
    chosen = expert_choice[0, :, 0]
    onehot_int = (chosen[:, None] == jnp.arange(expert_count, dtype=jnp.int32)[None, :]).astype(
        jnp.int32
    )
    onehot = onehot_int.astype(jnp.float32)
    gate_prob = jnp.sum(softmax_probs * onehot, axis=-1)
    slot_index = jnp.sum(jnp.cumsum(onehot_int, axis=0) * onehot_int, axis=-1) - 1
    is_kept = slot_index < capacity
    slots = -(-capacity // 16) * 16
    place = jnp.where(is_kept, chosen * slots + slot_index, -1)
    dispatch = (
        place[:, None] == jnp.arange(expert_count * slots, dtype=jnp.int32)[None, :]
    ).astype(jnp.bfloat16)
    dispatched = jnp.sum(onehot_int * is_kept[:, None].astype(jnp.int32), axis=0)
    tally_counts = jnp.stack(
        [dispatched, jnp.sum(onehot_int, axis=0) - dispatched], axis=0
    ).reshape(1, 1, 2, expert_count)

    grad_top = cotangent[0].astype(jnp.float32)
    scaled = (gate_prob[:, None] * grad_top).astype(jnp.bfloat16)
    sent_rows = (
        jnp.einsum(
            "tx,td->xd",
            dispatch,
            jnp.concatenate([mixed_low, scaled], axis=1),
            preferred_element_type=jnp.float32,
        )
        .astype(jnp.bfloat16)
        .reshape(m, local_experts * slots, 2 * D)
    )
    maps = [in_own, out_own, in_last, out_last, in_next, out_next]
    returned, *terms = run_experts(sent_rows, maps, n, m, slots, 2)
    returned = returned.reshape(expert_count * slots, 2 * D)
    gin_own, gout_own, gin_next, gout_last, gin_last, gout_next = terms
    gout_next = lax.ppermute(gout_next, "seq", to_next)
    gin_last = lax.ppermute(gin_last, "seq", to_last)
    routed = jnp.dot(dispatch, returned, preferred_element_type=jnp.float32)
    combined, grad_mixed = routed[:, :D], routed[:, D:]
    output = (after_cross + gate_prob[:, None] * combined).astype(jnp.bfloat16)

    grad_gate = jnp.sum(grad_top * combined, axis=-1)
    grad_logits = softmax_probs * (onehot - gate_prob[:, None]) * grad_gate[:, None]
    grad_router = jnp.einsum(
        "td,te->de", mixed_low.astype(jnp.float32), grad_logits, precision=highest
    )
    grad_mixed = grad_mixed + jnp.einsum(
        "te,de->td", grad_logits, router.astype(jnp.float32), precision=highest
    )
    grad_cross_part, grad_gain_mix = rms_backward(after_cross, gain_rows[2], grad_mixed)
    grad_after_cross = grad_top + grad_cross_part

    grad_cross_low = grad_after_cross.astype(jnp.bfloat16)
    grad_out_cross = weight_grad(attended_cross_low, grad_cross_low)
    grad_attended_cross = input_grad(grad_cross_low, proj_out[1]).astype(jnp.bfloat16)
    grad_cross_query, grad_memory_keys, grad_memory_values = attend_back(
        seq_at,
        cross_queries,
        memory_key_all,
        memory_value_all,
        grad_attended_cross,
        attended_cross,
        lse_cross,
        None,
    )
    grad_cross_query, gin_last, gout_next, gin_next, gout_last = lax.optimization_barrier(
        (grad_cross_query, gin_last, gout_next, gin_next, gout_last)
    )
    gin_next = lax.ppermute(gin_next, "seq", to_next)
    gout_last = lax.ppermute(gout_last, "seq", to_last)
    grad_query_cross = weight_grad(normed_cross, grad_cross_query)
    grad_self_part, grad_gain_cross = rms_backward(
        after_self, gain_rows[1], input_grad(grad_cross_query, proj_in[3])
    )
    grad_after_self = grad_after_cross + grad_self_part
    grad_memory_part, grads_cross = memory_back(
        memory_all, grad_memory_keys, grad_memory_values, proj_in
    )

    grad_self_low = grad_after_self.astype(jnp.bfloat16)
    grad_out_self = weight_grad(attended_self_low, grad_self_low)
    grad_attended_self = input_grad(grad_self_low, proj_out[0]).astype(jnp.bfloat16)
    grad_self_query, grad_keys, grad_values, near, sums = attend_back(
        seq_at,
        queries,
        key_all,
        value_all,
        grad_attended_self,
        attended_self,
        lse_self,
        lines,
    )
    grad_self_query, grad_keys, grad_values, near, sums, gout_last, gin_next = (
        lax.optimization_barrier(
            (grad_self_query, grad_keys, grad_values, near, sums, gout_last, gin_next)
        )
    )
    grad_table = bias_gradient(near, sums)
    (
        grad_normed_part,
        grads,
        grad_gain_part,
        grad_normed_query,
        grad_expert_in,
        grad_expert_out,
    ) = token_back(
        normed_all,
        grad_keys,
        grad_values,
        normed_self,
        grad_self_query,
        proj_in,
        [gin_own, gin_last, gin_next, gout_own, gout_last, gout_next],
    )
    grad_gain_self = grad_gain_part[0] / gain_rows[0]

    grads = lax.dynamic_update_slice(grads, grads_cross, (4, 0, 0))
    for number, grad in ((3, grad_query_cross), (6, grad_out_self), (7, grad_out_cross)):
        grads = lax.dynamic_update_slice(grads, grad[None], (number, 0, 0))
    grad_gains = jnp.stack([grad_gain_self, grad_gain_cross, grad_gain_mix])
    small = [
        grad_gains.reshape(-1, TILE),
        grad_router.T.reshape(-1, TILE),
        jnp.pad(grad_table, ((0, 0), (0, TILE - HEADS))),
    ]
    ends = [small[0].shape[0], small[0].shape[0] + small[1].shape[0]]
    (grad_normed_own, grad_memory), grads, small = finish(
        [
            grad_normed_part.reshape(n, token_count, D),
            grad_memory_part.reshape(n, memory_count, D),
        ],
        grads.reshape(-1, D),
        jnp.concatenate(small),
        n,
        m,
        4,
    )
    grads = grads.reshape(-1, D, D).astype(jnp.float32)
    grad_token_part, _ = rms_backward(tokens, gain_rows[0], grad_normed_query + grad_normed_own)
    grad_in = (grad_after_self + grad_token_part).astype(jnp.bfloat16)
    return (
        output.reshape(1, token_count, D),
        grad_in.reshape(1, token_count, D),
        grad_memory.astype(jnp.bfloat16).reshape(1, memory_count, D),
        grads[:6],
        grads[6:],
        small[: ends[0]].reshape(grad_gains.shape),
        small[ends[1] : ends[1] + NBUCKET, :HEADS],
        small[ends[0] : ends[1]].reshape(expert_count, D).T,
        grad_expert_in,
        grad_expert_out,
        tally_counts,
    )


def solution(mesh):
    rows = P("exp", "seq", None)
    hidden = P("exp", None, "seq")
    return jax.shard_map(
        functools.partial(body, mesh.shape["seq"], mesh.shape["exp"]),
        mesh=mesh,
        in_specs=(rows, rows, P(), P(), P(), P(), P(), rows, hidden, hidden, rows),
        out_specs=(
            rows,
            rows,
            rows,
            P(),
            P(),
            P(),
            P(),
            P(),
            hidden,
            hidden,
            P("exp", "seq", None, None),
        ),
        check_vma=False,
    )
```

```python
import functools
import math

import jax
import jax.numpy as jnp
from jax import lax
from jax.experimental import pallas as pl
from jax.experimental.pallas import tpu as pltpu
from jax.sharding import PartitionSpec as P

D = 768
HEADS = 12
HEAD_DIM = 64
NBUCKET = 32
MAXDIST = 128
TILE = 128
PAIRS = HEADS * HEAD_DIM // TILE

MESH = pl.DeviceIdType.MESH
ANY = pl.BlockSpec(memory_space=pl.ANY)
SMEM = pl.BlockSpec(memory_space=pltpu.SMEM)

norm_eps = 1e-06
masked_score = -1e30
highest = lax.Precision.HIGHEST
log2e = 1.0 / math.log(2.0)
scale_factor = HEAD_DIM ** (-0.5)


def bucket_edges():
    half_count = NBUCKET // 2
    thresholds = []
    for bucket_number in range(1, NBUCKET):
        if bucket_number < half_count:
            thresholds.append(bucket_number)
        else:
            thresholds.append(
                int(
                    half_count
                    * (MAXDIST / half_count) ** ((bucket_number - half_count) / half_count)
                )
            )
    return thresholds


def rms_apply(values, gain_row):
    return (
        values * lax.rsqrt(jnp.mean(values * values, axis=-1, keepdims=True) + norm_eps) * gain_row
    )


def rms_backward(values, gain_row, upstream):
    _, pullback = jax.vjp(rms_apply, values, gain_row)
    return pullback(upstream)


def cost(us):
    return pl.CostEstimate(flops=us * 10**9, bytes_accessed=0, transcendentals=0)


def seq_cycle(n):
    cols = n // 4
    if n % 4 or cols < 2:
        return list(range(n))
    order = [0]
    for row in range(4):
        span = range(1, cols) if row % 2 == 0 else range(cols - 1, 0, -1)
        order += [row * cols + col for col in span]
    return order + [3 * cols, 2 * cols, cols]


def look_up(index, table):
    value = jnp.int32(table[0])
    for number, entry in enumerate(table[1:], 1):
        value = jnp.where(index == number, jnp.int32(entry), value)
    return value


def greet(others):
    barrier = pltpu.get_barrier_semaphore()
    for other in others:
        pl.semaphore_signal(barrier, inc=1, device_id=other, device_id_type=MESH)
    pl.semaphore_wait(barrier, len(others))


def seq_ring(n):
    order = seq_cycle(n)
    pos = look_up(lax.axis_index("seq"), [order.index(i) for i in range(n)])

    def at(place):
        return look_up(lax.rem(place + 4 * n, n), order)

    return pos, at, ({"seq": at(pos + 1)}, {"seq": at(pos - 1)})


def gather_kernel(n, parts, *refs):
    sources, proj_ref, outs = refs[:2], refs[2], refs[3:10]
    lands, w_buf, bufs = refs[10:12], refs[12], refs[13:18]
    own_sem, w_sem, send_sem, recv_sem, store_sem = refs[18:]
    pos, at, sides = seq_ring(n)
    me = at(pos)
    greet(sides)
    own = [pltpu.make_async_copy(sources[a], lands[a].at[me], own_sem.at[a]) for a in range(2)]
    weights = [
        pltpu.make_async_copy(proj_ref.at[number], w_buf.at[i], w_sem.at[i])
        for i, number in enumerate((0, 1, 2, 4, 5))
    ]
    started, latest, stored = [], {}, []

    def pass_on(step):
        for part in range(parts):
            for a in range(2):
                rows = sources[a].shape[0] // 2 // parts
                for way in range(2):
                    if step:
                        latest[a, way, part].wait_recv()
                    if step == n - 1:
                        continue
                    block = at(pos - step) if way == 0 else at(pos + step)
                    span = pl.ds((way * parts + part) * rows, rows)
                    copy = pltpu.make_async_remote_copy(
                        src_ref=lands[a].at[block, span] if step else sources[a].at[span],
                        dst_ref=lands[a].at[block, span],
                        send_sem=send_sem.at[a, way, step, part],
                        recv_sem=recv_sem.at[a, way, step, part],
                        device_id=sides[way],
                        device_id_type=MESH,
                    )
                    copy.start()
                    started.append(copy)
                    latest[a, way, part] = copy

    def store(source, target, number, step, way):
        copy = pltpu.make_async_copy(source, target, store_sem.at[number, step, way])
        copy.start()
        stored.append(copy)

    def work(step):
        blocks = (at(pos - step), at(pos + step))
        for a in range(2):
            half = sources[a].shape[0] // 2
            spans = (pl.ds(0, half), pl.ds(half, half))
            rows = jnp.concatenate([lands[a][blocks[way], spans[way], :] for way in range(2)], axis=0)
            for i in range(2):
                buf = bufs[1 + 2 * a + i]
                made = dot_plain(rows, w_buf[1 + 2 * a + i]).astype(buf.dtype)
                for way in range(2):
                    buf[blocks[way], spans[way], :] = made[way * half : (way + 1) * half]
            for way in range(2):
                where = (blocks[way], spans[way])
                store(lands[a].at[where], outs[a].at[where], a, step, way)
                for i in range(2):
                    number = 1 + 2 * a + i
                    store(bufs[number].at[where], outs[2 + number].at[where], 2 + number, step, way)

    pass_on(0)
    for copy in own + weights:
        copy.start()
    for copy in own + weights:
        copy.wait()
    bufs[0][...] = dot_plain(lands[0][me], w_buf[0]).astype(bufs[0].dtype)
    store(bufs[0], outs[2], 2, 0, 0)
    work(0)
    for step in range(1, n):
        pass_on(step)
        work(step)
    for copy in started:
        copy.wait_send()
    for copy in stored:
        copy.wait()


def gather_projected(tokens, memory_rows, proj_in, n, number, parts=2):
    both = (tokens, memory_rows)
    copies = (2, 2, n - 1, parts)
    wide = [(n,) + x.shape for x in both]
    shapes = wide + [tokens.shape] + [wide[0]] * 2 + [wide[1]] * 2
    dma = pltpu.SemaphoreType.DMA
    return pl.pallas_call(
        functools.partial(gather_kernel, n, parts),
        out_shape=[jax.ShapeDtypeStruct(shape, tokens.dtype) for shape in shapes],
        in_specs=[ANY] * 3,
        out_specs=[ANY] * 7,
        scratch_shapes=[pltpu.VMEM(shape, tokens.dtype) for shape in wide]
        + [pltpu.VMEM((5,) + proj_in.shape[1:], tokens.dtype)]
        + [pltpu.VMEM(shape, tokens.dtype) for shape in shapes[2:]]
        + [dma((2,)), dma((5,)), dma(copies), dma(copies), dma((7, n, 2))],
        compiler_params=pltpu.CompilerParams(
            collective_id=number, has_side_effects=True, vmem_limit_bytes=58 << 20
        ),
        cost_estimate=cost(60),
        name="gather_projected",
    )(tokens, memory_rows, proj_in)


def scatter_kernel(n, parts, count, *refs):
    sources, outs = refs[:count], refs[count : 2 * count]
    own_bufs, got_bufs = refs[2 * count : 3 * count], refs[3 * count : 4 * count]
    own_sem, send_sem, recv_sem = refs[4 * count :]
    pos, at, sides = seq_ring(n)
    greet(sides)
    lanes = [(a, part, way) for a in range(count) for part in range(parts) for way in range(2)]

    def span(a, part, way):
        rows = sources[a].shape[1] // 2 // parts
        return pl.ds((way * parts + part) * rows, rows)

    def block(way, step):
        return at(pos - 1 - step) if way == 0 else at(pos + 1 + step)

    def send(lane, step, source):
        a, part, way = lane
        copy = pltpu.make_async_remote_copy(
            src_ref=source,
            dst_ref=got_bufs[a].at[way, step, part],
            send_sem=send_sem.at[a, way, step, part],
            recv_sem=recv_sem.at[a, way, step, part],
            device_id=sides[way],
            device_id_type=MESH,
        )
        copy.start()
        return copy

    latest, started, own = {}, [], {}
    for lane in lanes:
        a, part, way = lane
        latest[lane] = send(lane, 0, sources[a].at[block(way, 0), span(a, part, way)])
        started.append(latest[lane])
    for step in range(1, n):
        for lane in lanes:
            a, part, way = lane
            own[lane, step] = pltpu.make_async_copy(
                sources[a].at[block(way, step), span(a, part, way)],
                own_bufs[a].at[way, step - 1, part],
                own_sem.at[a, way, step - 1, part],
            )
            own[lane, step].start()
    for step in range(1, n):
        for lane in lanes:
            a, part, way = lane
            own[lane, step].wait()
            latest[lane].wait_recv()
            total = got_bufs[a][way, step - 1, part].astype(jnp.float32) + own_bufs[a][
                way, step - 1, part
            ].astype(jnp.float32)
            if step == n - 1:
                outs[a][span(a, part, way)] = total.astype(outs[a].dtype)
            else:
                got_bufs[a][way, step - 1, part] = total.astype(got_bufs[a].dtype)
                latest[lane] = send(lane, step, got_bufs[a].at[way, step - 1, part])
                started.append(latest[lane])
    for copy in started:
        copy.wait_send()


def ring_scatter(arrays, n, number, out_dtype, parts=2):
    count = len(arrays)
    copies = (count, 2, n - 1, parts)
    bufs = [
        pltpu.VMEM((2, n - 1, parts, a.shape[1] // 2 // parts, a.shape[2]), a.dtype)
        for a in arrays
    ]
    return pl.pallas_call(
        functools.partial(scatter_kernel, n, parts, count),
        out_shape=[jax.ShapeDtypeStruct(a.shape[1:], out_dtype) for a in arrays],
        in_specs=[ANY] * count,
        out_specs=[pl.BlockSpec(memory_space=pltpu.VMEM)] * count,
        scratch_shapes=bufs + bufs + [pltpu.SemaphoreType.DMA(copies)] * 3,
        compiler_params=pltpu.CompilerParams(
            collective_id=number, has_side_effects=True, vmem_limit_bytes=58 << 20
        ),
        name="ring_scatter",
    )(*arrays)


def finish_kernel(n, counts, *refs):
    few, many = counts
    refs = list(refs)
    take = lambda count: [refs.pop(0) for _ in range(count)]
    blocks, xs, sums, outs = take(few), take(many), take(few), take(many)
    own_bufs, got_bufs = take(few), take(few)
    mines, twins, crosses, gots = take(many), take(many), take(many), take(many)
    near_sem, far_sem, own_sem, pair_sem, cross_sem, ring_sem = refs
    pos, at, sides = seq_ring(n)
    exp = lax.axis_index("exp")
    core, chip = lax.rem(exp, 2), exp // 2
    peer, over = {"exp": exp + 1 - 2 * core}, {"exp": core + 2 * (1 - chip)}
    greet(sides + (peer, over))
    started = []

    def push(source, target, sems, index, to):
        copy = pltpu.make_async_remote_copy(
            src_ref=source,
            dst_ref=target,
            send_sem=sems.at[(0,) + index],
            recv_sem=sems.at[(1,) + index],
            device_id=to,
            device_id_type=MESH,
        )
        copy.start()
        started.append(copy)
        return copy

    def block(way, step):
        return at(pos - 1 - step) if way == 0 else at(pos + 1 + step)

    def fetch(source, target, sem):
        copy = pltpu.make_async_copy(source, target, sem)
        copy.start()
        return copy

    add = lambda *terms: functools.reduce(lambda u, v: u + v, [t.astype(jnp.float32) for t in terms])
    ways = range(2)
    lanes = [(a, way) for a in range(many) for way in ways]
    parts = 2
    rings = [(a, way, part) for part in range(parts) for a in range(few) for way in ways]

    def span(ref, way):
        half = ref.shape[-2] // 2
        return pl.ds(way * half, half)

    def piece(lane):
        a, way, part = lane
        rows = blocks[a].shape[-2] // 2 // parts
        return pl.ds(way * parts * rows + part * rows, rows), pl.ds(part * rows, rows)

    pairs, own, crossing, ring = {}, {}, {}, {}
    for side in range(2):
        for step in range(n):
            for lane in lanes:
                a, way = lane
                place = chip if side else 1 - chip
                where, rows = block(way, step), span(xs[a], way)
                pairs[side, lane, step] = push(
                    xs[a].at[1 - core, place, where, rows],
                    twins[a].at[side, way, step],
                    pair_sem,
                    (0, side) + lane + (step,),
                    peer,
                )
                own[side, lane, step] = fetch(
                    xs[a].at[core, place, where, rows],
                    mines[a].at[side, way, step],
                    own_sem.at[(side,) + lane + (step,)],
                )
        if side == 0:
            for lane in rings:
                a, way, part = lane
                wide, thin = piece(lane)
                ring[lane] = push(
                    blocks[a].at[block(way, 0), wide],
                    got_bufs[a].at[way, 0, thin],
                    far_sem,
                    lane + (0,),
                    sides[way],
                )
            near = {}
            for step in range(1, n):
                for lane in rings:
                    a, way, part = lane
                    wide, thin = piece(lane)
                    near[lane, step] = fetch(
                        blocks[a].at[block(way, step), wide],
                        own_bufs[a].at[way, step - 1, thin],
                        near_sem.at[lane + (step - 1,)],
                    )

    def scatter(step, which):
        for lane in rings:
            a, way, part = lane
            if part != which:
                continue
            wide, thin = piece(lane)
            near[lane, step].wait()
            ring[lane].wait_recv()
            total = add(got_bufs[a][way, step - 1, thin], own_bufs[a][way, step - 1, thin])
            if step == n - 1:
                sums[a][wide] = total.astype(sums[a].dtype)
            else:
                got_bufs[a][way, step - 1, thin] = total.astype(got_bufs[a].dtype)
                ring[lane] = push(
                    got_bufs[a].at[way, step - 1, thin],
                    got_bufs[a].at[way, step, thin],
                    far_sem,
                    lane + (step,),
                    sides[way],
                )

    for step in range(n):
        for lane in lanes:
            a, way = lane
            own[0, lane, step].wait()
            pairs[0, lane, step].wait_recv()
            mines[a][0, way, step] = add(mines[a][0, way, step], twins[a][0, way, step]).astype(
                mines[a].dtype
            )
            crossing[lane, step] = push(
                mines[a].at[0, way, step],
                crosses[a].at[way, step],
                cross_sem,
                (0,) + lane + (step,),
                over,
            )
    latest = {}
    waiting = [(step, part) for step in range(1, n) for part in range(parts)]
    for step in range(n):
        for lane in lanes:
            a, way = lane
            own[1, lane, step].wait()
            pairs[1, lane, step].wait_recv()
            crossing[lane, step].wait_recv()
            terms = [mines[a][1, way, step], twins[a][1, way, step], crosses[a][way, step]]
            if step:
                latest[lane].wait_recv()
                terms.append(gots[a][way, step - 1])
            mines[a][1, way, step] = add(*terms).astype(mines[a].dtype)
            if step < n - 1:
                latest[lane] = push(
                    mines[a].at[1, way, step],
                    gots[a].at[way, step],
                    ring_sem,
                    (0,) + lane + (step,),
                    sides[way],
                )
        if waiting:
            scatter(*waiting.pop(0))
    keep, done = [], []
    latest, crossing = {}, {}

    def target_of(lane, step, place):
        a, way = lane
        where = at(pos - step) if way == 0 else at(pos + step)
        return outs[a].at[core, place, where, span(outs[a], way)]

    def hand_on(step):
        for lane in lanes:
            crossing[lane, step].wait_recv()
            target = target_of(lane, step, 1 - chip)
            done.append(push(target, target, pair_sem, (1, 1) + lane + (step,), peer))

    for step in range(n):
        for lane in lanes:
            a, way = lane
            if step:
                latest[lane].wait_recv()
            target = target_of(lane, step, chip)
            source = target if step else mines[a].at[1, way, n - 1]
            if step < n - 1:
                latest[lane] = push(source, target, ring_sem, (1,) + lane + (step,), sides[way])
            crossing[lane, step] = push(source, target, cross_sem, (1,) + lane + (step,), over)
            done.append(push(source, target, pair_sem, (1, 0) + lane + (step,), peer))
            if step == 0:
                keep.append(fetch(source, target, own_sem.at[(0,) + lane + (0,)]))
        if waiting:
            scatter(*waiting.pop(0))
        if step:
            hand_on(step - 1)
    hand_on(n - 1)
    while waiting:
        scatter(*waiting.pop(0))
    for copy in keep:
        copy.wait()
    for copy in done:
        copy.wait_recv()
    for copy in started:
        copy.wait_send()


def finish(blocks, rows_in, small, n, m, number):
    rows, cols = rows_in.shape
    each = rows // (4 * n)
    if m != 4 or rows % (4 * n * 32) or small.shape[0] > 4 * n * 16:
        return (
            ring_scatter(blocks, n, number, jnp.float32),
            *lax.psum((rows_in, small), ("seq", "exp")),
        )
    padded = jnp.pad(small, ((0, 4 * n * 16 - small.shape[0]), (0, 0)))
    arrays = [rows_in.reshape(2, 2, n, each, cols), padded.reshape(2, 2, n, 16, TILE)]
    few, many = len(blocks), len(arrays)
    halves = [(x.shape[-2] // 2, x.shape[-1], x.dtype) for x in blocks + arrays]
    ring_bufs = [pltpu.VMEM((2, n - 1, r, c), t) for r, c, t in halves[:few]]
    two = [pltpu.VMEM((2, 2, n, r, c), t) for r, c, t in halves[few:]]
    one = [pltpu.VMEM((2, n, r, c), t) for r, c, t in halves[few:]]
    dma = pltpu.SemaphoreType.DMA
    results = pl.pallas_call(
        functools.partial(finish_kernel, n, (few, many)),
        out_shape=[jax.ShapeDtypeStruct(x.shape[1:], jnp.float32) for x in blocks]
        + [jax.ShapeDtypeStruct(x.shape, x.dtype) for x in arrays],
        in_specs=[ANY] * (few + many),
        out_specs=[pl.BlockSpec(memory_space=pltpu.VMEM)] * few + [ANY] * many,
        scratch_shapes=ring_bufs * 2
        + two * 2
        + one * 2
        + [
            dma((few, 2, 2, n)),
            dma((2, few, 2, 2, n)),
            dma((2, many, 2, n)),
            dma((2, 2, 2, many, 2, n)),
            dma((2, 2, many, 2, n)),
            dma((2, 2, many, 2, n)),
        ],
        compiler_params=pltpu.CompilerParams(
            collective_id=number, has_side_effects=True, vmem_limit_bytes=58 << 20
        ),
        cost_estimate=cost(120),
        name="finish",
    )(*blocks, *arrays)
    return results[:few], results[few].reshape(rows, cols), results[-1].reshape(-1, TILE)


def dot_last(a, b):
    return lax.dot_general(a, b, (((1,), (1,)), ((), ())), preferred_element_type=jnp.float32)


def dot_first(a, b):
    return lax.dot_general(a, b, (((0,), (0,)), ((), ())), preferred_element_type=jnp.float32)


def dot_plain(a, b):
    return jnp.dot(a, b, preferred_element_type=jnp.float32)


def head_masks(dtype):
    low = lax.broadcasted_iota(jnp.int32, (1, TILE), 1) < HEAD_DIM
    first = jnp.where(low, 1.0, 0.0).astype(jnp.float32)
    return first.astype(dtype), (1.0 - first).astype(dtype)


def split_heads(pair):
    return jnp.concatenate([pair * mask for mask in head_masks(pair.dtype)], axis=0)


def own_bias(tiles, count):
    rows = []
    for r in range(count):
        row = []
        for c in range(count):
            if c == r:
                row.append(tiles[:, TILE:])
            elif c == r - 1:
                row.append(tiles[:, :TILE])
            else:
                row.append(jnp.full((TILE, TILE), 0.0 if c < r else masked_score, jnp.float32))
        rows.append(jnp.concatenate(row, axis=1))
    return jnp.concatenate(rows, axis=0)


def edge_bias(tiles, rows):
    edge = []
    for h in range(2):
        first = jnp.concatenate(
            [jnp.zeros((rows - TILE, TILE), jnp.float32), tiles[h][:, :TILE].T], axis=0
        )
        edge += [first, jnp.zeros((rows, rows - TILE), jnp.float32)]
    return jnp.concatenate(edge, axis=1)


def each_far(s, block, act, times=3):
    far = jnp.maximum(s - 1, 0)
    bundles = far // times

    def bundle(j, carry):
        act(pl.multiple_of(j * times * block, block), times)
        return carry

    def single(j, carry):
        act(pl.multiple_of(j * block, block), 1)
        return carry

    lax.fori_loop(0, bundles, bundle, 0)
    lax.fori_loop(bundles * times, far, single, 0)


def attend_kernel(causal, block, s_ref, q_ref, k_ref, v_ref, *refs):
    if causal:
        line_ref, low_ref, wide_ref, lse_ref, acc_ref, top_ref = refs
    else:
        low_ref, wide_ref, lse_ref, acc_ref, top_ref = refs
    rows = q_ref.shape[0]
    both = split_heads(q_ref[...])

    def visit(start, bias, first, times=1):
        ones = jnp.ones((16, times * block), v_ref.dtype)
        keys = k_ref[pl.ds(start, times * block), :]
        values = v_ref[pl.ds(start, times * block), :]
        t = dot_last(keys, both) * (scale_factor * log2e)
        if bias is not None:
            t = t + bias
        top = jnp.max(t, axis=0, keepdims=True)
        if not first:
            before = top_ref[...]
            top = jnp.maximum(before, top)
            fade = jnp.exp2(before - top)
        top_ref[...] = top
        p = jnp.exp2(t - top).astype(values.dtype)
        part = dot_plain(jnp.concatenate([values.T, ones], axis=0), p)
        if first:
            acc_ref[...] = part
        else:
            acc_ref[...] = acc_ref[...] * fade + part

    if causal:
        s = s_ref[0]
        count = rows // TILE
        tiles = [bias_tile(line_ref, h) for h in range(2)]
        visit(
            pl.multiple_of(s * block, block),
            jnp.concatenate([own_bias(tiles[h], count).T for h in range(2)], axis=1),
            True,
        )

        @pl.when(s > 0)
        def _():
            visit(pl.multiple_of((s - 1) * block, block), edge_bias(tiles, rows), False)

        each_far(s, block, lambda start, times: visit(start, None, False, times))
    else:
        for j in range(k_ref.shape[0] // block):
            visit(j * block, None, j == 0)
    sums = acc_ref[TILE : TILE + 1, :]
    wide = jnp.concatenate(
        [
            acc_ref[:HEAD_DIM, :rows] / sums[:, :rows],
            acc_ref[HEAD_DIM:TILE, rows:] / sums[:, rows:],
        ],
        axis=0,
    ).T
    wide_ref[...] = wide
    low_ref[...] = wide.astype(low_ref.dtype)
    lse = top_ref[...] + jnp.log2(sums)
    lse_ref[0] = jnp.concatenate([lse[:, :rows], lse[:, rows:]], axis=0)


def attend(seq_at, queries, keys, values, lines):
    rows, total = queries.shape[0], keys.shape[0]
    causal = lines is not None
    block = rows if causal else math.gcd(total, 1024)
    pair = pl.BlockSpec((rows, TILE), lambda g: (0, g))
    long = pl.BlockSpec((total, TILE), lambda g: (0, g))
    extra, specs = [], []
    if causal:
        extra, specs = [lines], [pl.BlockSpec((1,) + lines.shape[1:], lambda g: (g, 0, 0))]
    return pl.pallas_call(
        functools.partial(attend_kernel, causal, block),
        grid=(PAIRS,),
        out_shape=[
            jax.ShapeDtypeStruct((rows, D), jnp.bfloat16),
            jax.ShapeDtypeStruct((rows, D), jnp.float32),
            jax.ShapeDtypeStruct((PAIRS, 2, rows), jnp.float32),
        ],
        in_specs=[SMEM, pair, long, long] + specs,
        out_specs=[pair, pair, pl.BlockSpec((1, 2, rows), lambda g: (g, 0, 0))],
        scratch_shapes=[
            pltpu.VMEM((TILE + 16, 2 * rows), jnp.float32),
            pltpu.VMEM((1, 2 * rows), jnp.float32),
        ],
        compiler_params=pltpu.CompilerParams(vmem_limit_bytes=48 << 20),
        cost_estimate=cost(40 if causal else 10),
        name="attend_self" if causal else "attend_cross",
    )(seq_at, queries, keys, values, *extra)


def attend_back_kernel(causal, block, s_ref, q_ref, k_ref, v_ref, up_ref, wide_ref, lse_ref, *refs):
    if causal:
        line_ref, dq_ref, dk_ref, dv_ref, bias_ref, sum_ref, acc_ref, near_ref = refs
    else:
        dq_ref, dk_ref, dv_ref, acc_ref = refs
    rows = q_ref.shape[0]
    both = split_heads(q_ref[...])
    up = up_ref[...]
    up_both = split_heads(up)
    turned = (up.astype(jnp.float32) * wide_ref[...]).T
    delta = jnp.concatenate(
        [
            jnp.sum(turned[:HEAD_DIM], axis=0, keepdims=True),
            jnp.sum(turned[HEAD_DIM:], axis=0, keepdims=True),
        ],
        axis=1,
    )
    lse = jnp.concatenate([lse_ref[0, :1], lse_ref[0, 1:]], axis=1)

    def visit(start, bias, first, times=1):
        ones = jnp.ones((16, times * block), k_ref.dtype)
        keys = k_ref[pl.ds(start, times * block), :]
        values = v_ref[pl.ds(start, times * block), :]
        t = dot_last(keys, both) * (scale_factor * log2e)
        if bias is not None:
            t = t + bias
        p = jnp.exp2(t - lse)
        ds = (p * (dot_last(values, up_both) - delta)).astype(keys.dtype)
        dv_ref[pl.ds(start, times * block), :] = dot_plain(p.astype(keys.dtype), up_both).astype(
            dv_ref.dtype
        )
        dk_ref[pl.ds(start, times * block), :] = (dot_plain(ds, both) * scale_factor).astype(dk_ref.dtype)
        part = dot_plain(jnp.concatenate([keys.T, ones], axis=0), ds)
        if first:
            acc_ref[...] = part
        else:
            acc_ref[...] += part
        return ds

    if causal:
        s = s_ref[0]
        count = rows // TILE
        tiles = [bias_tile(line_ref, h) for h in range(2)]
        ds = visit(
            pl.multiple_of(s * block, block),
            jnp.concatenate([own_bias(tiles[h], count).T for h in range(2)], axis=1),
            True,
        )
        for h in range(2):
            same = before = jnp.zeros((TILE, TILE), jnp.float32)
            for r in range(count):
                columns = slice(h * rows + r * TILE, h * rows + (r + 1) * TILE)
                same = same + ds[r * TILE : (r + 1) * TILE, columns].astype(jnp.float32)
                if r:
                    before = before + ds[(r - 1) * TILE : r * TILE, columns].astype(jnp.float32)
            near_ref[h, :TILE] = before
            near_ref[h, TILE:] = same

        @pl.when(s > 0)
        def _():
            ds = visit(pl.multiple_of((s - 1) * block, block), edge_bias(tiles, rows), False)
            for h in range(2):
                near_ref[h, :TILE] += ds[rows - TILE :, h * rows : h * rows + TILE].astype(
                    jnp.float32
                )

        each_far(s, block, lambda start, times: visit(start, None, False, times))

        def beyond(j, carry):
            start = pl.multiple_of(j * block, block)
            dk_ref[pl.ds(start, block), :] = jnp.zeros((block, TILE), dk_ref.dtype)
            dv_ref[pl.ds(start, block), :] = jnp.zeros((block, TILE), dv_ref.dtype)
            return carry

        lax.fori_loop(s + 1, k_ref.shape[0] // block, beyond, 0)
        turn = (
            lax.broadcasted_iota(jnp.int32, (TILE, TILE), 0)
            + lax.broadcasted_iota(jnp.int32, (TILE, TILE), 1)
            == TILE - 1
        ).astype(jnp.float32)
        diagonals = []
        for h in range(2):
            near = jnp.dot(turn, near_ref[h].T, precision=highest, preferred_element_type=jnp.float32)
            near = jnp.concatenate([near, jnp.zeros((TILE, TILE), jnp.float32)], axis=1)
            near = pltpu.roll(near, 0, 1, stride=1, stride_axis=0)
            diagonals.append(jnp.sum(near, axis=0, keepdims=True))
        bias_ref[0] = jnp.concatenate(diagonals, axis=0)
        sum_ref[0] = jnp.concatenate(
            [acc_ref[TILE : TILE + 1, :rows], acc_ref[TILE : TILE + 1, rows:]], axis=0
        )
    else:
        for j in range(k_ref.shape[0] // block):
            visit(j * block, None, j == 0)
    dq = jnp.concatenate([acc_ref[:HEAD_DIM, :rows], acc_ref[HEAD_DIM:TILE, rows:]], axis=0)
    dq_ref[...] = (dq.T * scale_factor).astype(dq_ref.dtype)


def attend_back(seq_at, queries, keys, values, upstream, wide, lse, lines):
    rows, total = queries.shape[0], keys.shape[0]
    causal = lines is not None
    block = rows if causal else math.gcd(total, 1024)
    pair = pl.BlockSpec((rows, TILE), lambda g: (0, g))
    long = pl.BlockSpec((total, TILE), lambda g: (0, g))
    line = pl.BlockSpec((1, 2, rows), lambda g: (g, 0, 0))
    extra, specs, shapes, out_specs, scratch = [], [], [], [], []
    if causal:
        extra, specs = [lines], [pl.BlockSpec((1,) + lines.shape[1:], lambda g: (g, 0, 0))]
        shapes = [
            jax.ShapeDtypeStruct((PAIRS, 2, 3 * TILE), jnp.float32),
            jax.ShapeDtypeStruct((PAIRS, 2, rows), jnp.float32),
        ]
        out_specs = [pl.BlockSpec((1, 2, 3 * TILE), lambda g: (g, 0, 0)), line]
        scratch = [pltpu.VMEM((2, 2 * TILE, TILE), jnp.float32)]
    return pl.pallas_call(
        functools.partial(attend_back_kernel, causal, block),
        grid=(PAIRS,),
        out_shape=[
            jax.ShapeDtypeStruct((rows, D), jnp.bfloat16),
            jax.ShapeDtypeStruct((total, D), jnp.bfloat16),
            jax.ShapeDtypeStruct((total, D), jnp.bfloat16),
        ]
        + shapes,
        in_specs=[SMEM, pair, long, long, pair, pair, line] + specs,
        out_specs=[pair, long, long] + out_specs,
        scratch_shapes=[pltpu.VMEM((TILE + 16, 2 * rows), jnp.float32)] + scratch,
        compiler_params=pltpu.CompilerParams(vmem_limit_bytes=48 << 20),
        cost_estimate=cost(48 if causal else 15),
        name="attend_self_back" if causal else "attend_cross_back",
    )(seq_at, queries, keys, values, upstream, wide, lse, *extra)


def key_value_back(x_ref, dk_ref, dv_ref, wk_ref, wv_ref, dx_ref):
    x, both = x_ref[...], jnp.concatenate([dk_ref[...], dv_ref[...]], axis=1)
    dx = dot_last(both, jnp.concatenate([wk_ref[0], wv_ref[0]], axis=1))
    dx_ref[...] = dx.astype(dx_ref.dtype)
    gain = jnp.sum(dx * x.astype(jnp.float32), axis=0, keepdims=True)
    return gain, dot_first(x, both)


def add_up(step, last, made, total, outs):
    @pl.when(step == 0)
    def _():
        total[...] = made

    @pl.when(step > 0)
    def _():
        total[...] += made

    @pl.when(step == last)
    def _():
        for i, out in enumerate(outs):
            out[...] = total[:, i * D : (i + 1) * D].astype(out.dtype)


def memory_back_kernel(x_ref, dk_ref, dv_ref, wk_ref, wv_ref, dx_ref, grad_ref, acc_ref):
    _, made = key_value_back(x_ref, dk_ref, dv_ref, wk_ref, wv_ref, dx_ref)
    outs = [grad_ref.at[0], grad_ref.at[1]]
    add_up(pl.program_id(0), pl.num_programs(0) - 1, made, acc_ref, outs)


def token_back_kernel(*refs):
    x_ref, dk_ref, dv_ref, wk_ref, wv_ref, own_ref, dq_ref, wq_ref = refs[:8]
    terms, others, cross_ref = refs[8:14], refs[14:20], refs[20]
    (dx_ref, grad_ref, gain_ref, query_ref), sums = refs[21:25], refs[25:27]
    acc_ref = refs[27]
    step, last = pl.program_id(0), pl.num_programs(0) - 1
    for i, out in enumerate(sums):
        first, *rest = terms[3 * i : 3 * i + 3]
        total = first[...]
        for term in rest:
            total = total + term[...].astype(jnp.float32)
        out[...] = total
    gain, made = key_value_back(x_ref, dk_ref, dv_ref, wk_ref, wv_ref, dx_ref)
    add_up(step, last, made, acc_ref, [grad_ref.at[1], grad_ref.at[2]])

    @pl.when(step == 0)
    def _():
        own, dq = own_ref[...], dq_ref[...]
        back = dot_last(dq, wq_ref[0])
        query_ref[...] = back
        gain_ref[...] = gain + jnp.sum(back * own.astype(jnp.float32), axis=0, keepdims=True)
        grad_ref[0] = dot_first(own, dq).astype(grad_ref.dtype)
        grad_ref[4:6] = cross_ref[...]

    @pl.when(step > 0)
    def _():
        gain_ref[...] += gain

    for i, number in enumerate((3, 6, 7)):

        @pl.when(step == jnp.minimum(i + 1, last))
        def _(i=i, number=number):
            product = dot_first(others[2 * i][...], others[2 * i + 1][...])
            grad_ref[number] = product.astype(grad_ref.dtype)


def memory_back(tokens, grad_keys, grad_values, proj_in):
    total = tokens.shape[0]
    rows = math.gcd(total, 512)
    block = pl.BlockSpec((rows, D), lambda i: (i, 0))
    weight = lambda number: pl.BlockSpec((1, D, D), lambda i: (number, 0, 0))
    return pl.pallas_call(
        memory_back_kernel,
        grid=(total // rows,),
        out_shape=[
            jax.ShapeDtypeStruct(tokens.shape, tokens.dtype),
            jax.ShapeDtypeStruct((2, D, D), tokens.dtype),
        ],
        in_specs=[block] * 3 + [weight(4), weight(5)],
        out_specs=[block, pl.BlockSpec((2, D, D), lambda i: (0, 0, 0))],
        scratch_shapes=[pltpu.VMEM((D, 2 * D), jnp.float32)],
        compiler_params=pltpu.CompilerParams(vmem_limit_bytes=48 << 20),
        cost_estimate=cost(8),
        name="memory_back",
    )(tokens, grad_keys, grad_values, proj_in, proj_in)


def token_back(tokens, grad_keys, grad_values, own, grad_queries, proj_in, terms, others, grads_cross):
    steps = tokens.shape[0] // (2 * own.shape[0])
    block = pl.BlockSpec((2 * own.shape[0], D), lambda i: (i, 0))
    once = pl.Buffered(1)
    weight = lambda number: pl.BlockSpec((1, D, D), lambda i: (number, 0, 0), pipeline_mode=once)
    whole = pl.BlockSpec(own.shape, lambda i: (0, 0), pipeline_mode=once)
    pair = pl.BlockSpec((2, D, D), lambda i: (0, 0, 0), pipeline_mode=once)
    count, _, hidden = terms[0].shape
    expert = pl.BlockSpec((count, D // steps, hidden), lambda i: (0, i, 0))
    return pl.pallas_call(
        token_back_kernel,
        grid=(steps,),
        out_shape=[
            jax.ShapeDtypeStruct(tokens.shape, tokens.dtype),
            jax.ShapeDtypeStruct((8, D, D), tokens.dtype),
            jax.ShapeDtypeStruct((1, D), jnp.float32),
            jax.ShapeDtypeStruct(own.shape, jnp.float32),
        ]
        + [jax.ShapeDtypeStruct(terms[0].shape, jnp.float32)] * 2,
        in_specs=[block] * 3
        + [weight(1), weight(2), whole, whole, weight(0)]
        + [expert] * 6
        + [whole] * 6
        + [pair],
        out_specs=[
            block,
            pl.BlockSpec((8, D, D), lambda i: (0, 0, 0), pipeline_mode=once),
            pl.BlockSpec((1, D), lambda i: (0, 0)),
            pl.BlockSpec(own.shape, lambda i: (0, 0)),
            expert,
            expert,
        ],
        scratch_shapes=[pltpu.VMEM((D, 2 * D), jnp.float32)],
        compiler_params=pltpu.CompilerParams(vmem_limit_bytes=56 << 20),
        cost_estimate=cost(28),
        name="token_back",
    )(
        tokens,
        grad_keys,
        grad_values,
        proj_in,
        proj_in,
        own,
        grad_queries,
        proj_in,
        *terms,
        *others,
        grads_cross,
    )


def bias_lines(bias_table):
    at = jnp.arange(3 * TILE, dtype=jnp.int32)
    distance = jnp.where(at <= 2 * TILE, TILE - at, 4 * TILE - at)
    table = (bias_table - bias_table[NBUCKET - 1 :]) * log2e
    terms = jnp.broadcast_to(table[0][:, None], (HEADS, 3 * TILE))
    for number, threshold in enumerate(bucket_edges()):
        terms = jnp.where((distance >= threshold)[None], table[number + 1][:, None], terms)
    return jnp.where((distance >= 0)[None], terms, masked_score).reshape(PAIRS, 2, 3 * TILE)


def bias_tile(line_ref, h):
    line = jnp.broadcast_to(line_ref[0, h : h + 1, :], (TILE, 3 * TILE))
    return pltpu.roll(line, 0, 1, stride=1, stride_axis=0)[:, : 2 * TILE]


def bias_gradient(diagonals, sums):
    distance = 2 * TILE - 1 - jnp.arange(3 * TILE, dtype=jnp.int32)
    bucket = jnp.zeros(distance.shape, jnp.int32)
    for threshold in bucket_edges():
        bucket = bucket + (distance >= threshold).astype(jnp.int32)
    buckets = jnp.arange(NBUCKET, dtype=jnp.int32)[:, None]
    flat = diagonals.reshape(HEADS, -1)
    far = jnp.sum(sums, axis=-1).reshape(HEADS) - jnp.sum(flat, axis=-1)
    table = lax.dot_general(
        (bucket[None, :] == buckets).astype(jnp.float32),
        flat,
        (((1,), (1,)), ((), ())),
        precision=highest,
    )
    return table + jnp.where(buckets == NBUCKET - 1, far[None, :], 0.0)


def expert_kernel(n, m, slots, *refs):
    x_ref, maps, result_ref, grads = refs[0], refs[1:7], refs[7], refs[8:14]
    rows, parts, backs, up_all, down_all, act_all, du_all = refs[14:21]
    grad_bufs, far_bufs = refs[21:29], refs[29:31]
    map_sem, own_sem, grad_sem, go_sem, back_sem, term_sem, far_sem = refs[31:]
    seq, exp = lax.axis_index("seq"), lax.axis_index("exp")
    groups, count = n // QUAD, x_ref.shape[1] // slots
    batch = max(1, 128 // slots)
    far = [(g, k) for g in range(1, groups) for k in range(m)]
    moves = far + [(0, k) for k in range(1, m)]
    source_of = lambda k: lax.rem(exp + m - k, m)

    def push(source, target, sems, g, k, to_seq, to_exp):
        copy = pltpu.make_async_remote_copy(
            src_ref=source,
            dst_ref=target,
            send_sem=sems.at[0, g, k],
            recv_sem=sems.at[1, g, k],
            device_id={"seq": to_seq, "exp": to_exp},
            device_id_type=MESH,
        )
        copy.start()
        return copy

    def place(g, k):
        return lax.rem(seq + g * QUAD, n), lax.rem(exp + k, m)

    to_next, to_last = quad_moves(n)
    side = {"next": look_up(seq, [b for _, b in to_next]), "last": look_up(seq, [b for _, b in to_last])}
    greet(
        [dict(zip(("seq", "exp"), place(g, k))) for g, k in moves]
        + [{"seq": side["next"], "exp": exp}, {"seq": side["last"], "exp": exp}]
    )
    going = {}
    for g, k in moves:
        to_seq, to_exp = place(g, k)
        going[g, k] = push(x_ref.at[to_exp], rows.at[g, exp], go_sem, g, k, to_seq, to_exp)
    own = pltpu.make_async_copy(x_ref.at[exp], rows.at[0, exp], own_sem.at[0])
    own.start()
    fetched = []
    for j in range(1, QUAD):
        j = j % (QUAD - 1)
        for at, (source, target) in enumerate(((maps[2 * j], up_all), (maps[2 * j + 1], down_all))):
            copy = pltpu.make_async_copy(source, target.at[j], map_sem.at[at, j])
            copy.start()
            fetched.append(copy)
    for copy in fetched:
        copy.wait()
    far_maps = [
        push(up_all.at[1], up_all.at[3], far_sem, 0, 0, side["next"], exp),
        push(down_all.at[2], down_all.at[3], far_sem, 0, 1, side["last"], exp),
    ]
    own.wait()
    slope = math.sqrt(2.0 / math.pi)
    coming = {}

    def work(g, first, last):
        for k in range(first, last):
            if g or k:
                going[g, k].wait_recv()
        size = (last - first) * slots
        base = (g * m + first) * slots

        def one(e, carry):
            start = pl.multiple_of(e * slots, slots)
            piece = jnp.concatenate(
                [rows[g, source_of(k), pl.ds(start, slots), :] for k in range(first, last)], axis=0
            )
            tokens, upstream = piece[:, :D], piece[:, D:]
            result = back = None
            for j in range(QUAD):
                up_map, down_map = up_all[j, e], down_all[j, e]
                u = dot_plain(tokens, up_map)
                square = u * u
                bend = jnp.tanh(slope * (u + 0.044715 * (square * u)))
                half = 0.5 * (1.0 + bend)
                act = (u * half).astype(tokens.dtype)
                rise = half + 0.5 * u * (1.0 - bend * bend) * (
                    slope * (1.0 + 3 * 0.044715 * square)
                )
                du = (dot_plain(upstream, down_map) * rise).astype(tokens.dtype)
                act_all[e, j, base : base + size] = act
                du_all[e, j, base : base + size] = du
                y, dn = dot_last(act, down_map), dot_last(du, up_map)
                result = y if result is None else result + y
                back = dn if back is None else back + dn
            for i, k in enumerate(range(first, last)):
                span = slice(i * slots, (i + 1) * slots)
                where = (g, source_of(k), pl.ds(start, slots))
                parts[where + (slice(0, D),)] = result[span].astype(parts.dtype)
                parts[where + (slice(D, 2 * D),)] = back[span].astype(parts.dtype)
            return carry

        lax.fori_loop(0, count, one, 0)
        for k in range(first, last):
            if g or k:
                source = source_of(k)
                coming[g, k] = push(
                    parts.at[g, source],
                    backs.at[g, exp],
                    back_sem,
                    g,
                    k,
                    lax.rem(seq + n - g * QUAD, n),
                    source,
                )

    for copy in far_maps:
        copy.wait_recv()
    work(0, 0, m)
    for g in range(1, groups):
        for first in range(0, m, batch):
            work(g, first, min(m, first + batch))

    total = groups * m * slots

    def weigh(j):
        def one(e, carry):
            start = pl.multiple_of(e * slots, slots)
            piece = jnp.concatenate(
                [
                    rows[g, source_of(k), pl.ds(start, slots), :]
                    for g in range(groups)
                    for k in range(m)
                ],
                axis=0,
            )
            tokens, upstream = piece[:, :D], piece[:, D:]
            up_buf, down_buf = grad_bufs[2 * j], grad_bufs[2 * j + 1]
            up_buf[e] = dot_first(tokens, du_all[e, j, :total]).astype(up_buf.dtype)
            down_buf[e] = dot_first(upstream, act_all[e, j, :total]).astype(down_buf.dtype)
            return carry

        lax.fori_loop(0, count, one, 0)

    def term(source, target, number, to):
        return push(source, target, term_sem, 0, number, side[to], exp)

    def store(source, number):
        copy = pltpu.make_async_copy(source, grads[number], grad_sem.at[number])
        copy.start()
        return copy

    weigh(3)
    terms_out = [
        term(grad_bufs[6], far_bufs[0], 0, "next"),
        term(grad_bufs[7], far_bufs[1], 1, "last"),
    ]
    weigh(1)
    weigh(2)
    weigh(0)
    stored = [
        store(grad_bufs[i], number) for number, i in ((0, 0), (1, 1), (4, 2), (5, 5))
    ]
    for number, (buf, far_buf) in enumerate(((grad_bufs[4], far_bufs[0]), (grad_bufs[3], far_bufs[1]))):
        terms_out[number].wait_recv()
        buf[...] = (buf[...].astype(jnp.float32) + far_buf[...].astype(jnp.float32)).astype(buf.dtype)
        stored.append(store(buf, 2 + number))
    for k in range(m):
        where = source_of(k)
        terms = []
        for g in range(groups):
            back_k = (m - k) % m
            if g == 0 and k == 0:
                terms.append(parts[0, exp])
            else:
                coming[g, back_k].wait_recv()
                terms.append(backs[g, where])
        total_row = terms[0].astype(jnp.float32)
        for term in terms[1:]:
            total_row = total_row + term.astype(jnp.float32)
        result_ref[where] = total_row.astype(result_ref.dtype)
    for copy in stored:
        copy.wait()
    for copy in terms_out + far_maps:
        copy.wait_send()
    for copies in (going, coming):
        for copy in copies.values():
            copy.wait_send()


def run_experts(x, maps, n, m, slots, number):
    groups = n // QUAD
    count, _, hidden = maps[0].shape
    total = groups * m * slots
    big = pltpu.VMEM((groups,) + x.shape, x.dtype)
    stack = pltpu.VMEM((QUAD,) + maps[0].shape, x.dtype)
    kept = pltpu.VMEM((count, QUAD, total, hidden), x.dtype)
    grads = [(maps[0].shape, jnp.float32 if i < 2 else jnp.bfloat16) for i in range(2 * QUAD)]
    dma = pltpu.SemaphoreType.DMA
    return pl.pallas_call(
        functools.partial(expert_kernel, n, m, slots),
        out_shape=[jax.ShapeDtypeStruct(x.shape, x.dtype)]
        + [jax.ShapeDtypeStruct(shape, dtype) for shape, dtype in grads[:6]],
        in_specs=[ANY] * (1 + len(maps)),
        out_specs=[pl.BlockSpec(memory_space=pltpu.VMEM)] + [ANY] * 6,
        scratch_shapes=[big] * 3
        + [stack] * 2
        + [kept] * 2
        + [pltpu.VMEM(shape, dtype) for shape, dtype in grads + grads[6:]]
        + [
            dma((2, QUAD)),
            dma((1,)),
            dma((6,)),
            dma((2, groups, m)),
            dma((2, groups, m)),
            dma((2, 1, 2)),
            dma((2, 1, 2)),
        ],
        compiler_params=pltpu.CompilerParams(
            collective_id=number, has_side_effects=True, vmem_limit_bytes=60 << 20
        ),
        cost_estimate=cost(150),
        name="run_experts",
    )(x, *maps)


QUAD = 4


def quad_moves(n):
    ring = (0, 1, 3, 2)
    step = lambda i, by: i - i % QUAD + ring[(ring.index(i % QUAD) + by) % QUAD]
    return [(i, step(i, 1)) for i in range(n)], [(i, step(i, -1)) for i in range(n)]


def present_kernel(grad_ref, small_ref, in_ref, out_ref, gain_ref, table_ref, router_ref):
    step = pl.program_id(0)
    value = grad_ref[...].astype(jnp.float32)

    @pl.when(step < 6)
    def _():
        in_ref[...] = value

    @pl.when(step >= 6)
    def _():
        out_ref[...] = value

    @pl.when(step == 0)
    def _():
        experts = router_ref.shape[1]
        each = experts + 8
        pieces = D // TILE
        lines = jnp.concatenate(
            [small_ref[i * each : (i + 1) * each, :] for i in range(pieces)], axis=1
        )
        router_ref[...] = lines[:experts].T
        gain_ref[...] = lines[experts : experts + 3]
        table_ref[...] = small_ref[pieces * each : pieces * each + NBUCKET, :HEADS]


def present(grads, small, experts):
    whole = lambda shape: pl.BlockSpec(shape, lambda i: (0, 0))
    shapes = [(6, D, D), (2, D, D), (3, D), (NBUCKET, HEADS), (D, experts)]
    return pl.pallas_call(
        present_kernel,
        grid=(8,),
        out_shape=[jax.ShapeDtypeStruct(shape, jnp.float32) for shape in shapes],
        in_specs=[pl.BlockSpec((1, D, D), lambda i: (i, 0, 0)), whole(small.shape)],
        out_specs=[
            pl.BlockSpec((1, D, D), lambda i: (jnp.minimum(i, 5), 0, 0)),
            pl.BlockSpec((1, D, D), lambda i: (jnp.maximum(i - 6, 0), 0, 0)),
        ]
        + [whole(shape) for shape in shapes[2:]],
        compiler_params=pltpu.CompilerParams(vmem_limit_bytes=48 << 20),
        cost_estimate=cost(8),
        name="present",
    )(grads, small)


def project(source, matrix):
    return jnp.dot(source, matrix, preferred_element_type=jnp.float32).astype(jnp.bfloat16)


def input_grad(upstream, matrix):
    return jnp.einsum("te,de->td", upstream, matrix, preferred_element_type=jnp.float32)


def body(
    n,
    m,
    hidden_in,
    memory,
    proj_in,
    proj_out,
    norm_gains,
    rel_bias,
    router,
    expert_choice,
    expert_in,
    expert_out,
    cotangent,
):
    tokens = hidden_in[0].astype(jnp.float32)
    memory_rows = memory[0]
    memory_count = memory_rows.shape[0]
    gain_rows = norm_gains.astype(jnp.float32)
    token_count = tokens.shape[0]
    seq_at = lax.axis_index("seq").astype(jnp.int32).reshape(1)
    normed_self = rms_apply(tokens, gain_rows[0]).astype(jnp.bfloat16)
    lines = bias_lines(rel_bias)

    normed_all, memory_all, queries, key_all, value_all, memory_key_all, memory_value_all = (
        gather_projected(normed_self, memory_rows, proj_in, n, 1)
    )
    to_next, to_last = quad_moves(n)
    in_own, out_own, normed_all = lax.optimization_barrier((expert_in, expert_out, normed_all))
    in_last, out_last = (lax.ppermute(w, "seq", to_next) for w in (in_own, out_own))
    in_next, out_next = (lax.ppermute(w, "seq", to_last) for w in (in_own, out_own))
    normed_all = normed_all.reshape(n * token_count, D)
    memory_all = memory_all.reshape(n * memory_count, D)
    key_all, value_all = (x.reshape(n * token_count, D) for x in (key_all, value_all))
    memory_key_all, memory_value_all = (
        x.reshape(n * memory_count, D) for x in (memory_key_all, memory_value_all)
    )
    attended_self_low, attended_self, lse_self = attend(
        seq_at, queries, key_all, value_all, lines
    )
    after_self = tokens + jnp.dot(
        attended_self_low, proj_out[0], preferred_element_type=jnp.float32
    )

    normed_cross = rms_apply(after_self, gain_rows[1]).astype(jnp.bfloat16)
    cross_queries = project(normed_cross, proj_in[3])
    attended_cross_low, attended_cross, lse_cross = attend(
        seq_at, cross_queries, memory_key_all, memory_value_all, None
    )
    after_cross = after_self + jnp.dot(
        attended_cross_low, proj_out[1], preferred_element_type=jnp.float32
    )

    mixed_low = rms_apply(after_cross, gain_rows[2]).astype(jnp.bfloat16)
    softmax_probs = jax.nn.softmax(
        jnp.dot(mixed_low, router, preferred_element_type=jnp.float32), axis=-1
    )
    expert_count = router.shape[1]
    local_experts = expert_in.shape[0]
    capacity = max(2, 5 * token_count // (4 * expert_count))
    chosen = expert_choice[0, :, 0]
    onehot_int = (chosen[:, None] == jnp.arange(expert_count, dtype=jnp.int32)[None, :]).astype(
        jnp.int32
    )
    onehot = onehot_int.astype(jnp.float32)
    gate_prob = jnp.sum(softmax_probs * onehot, axis=-1)
    slot_index = jnp.sum(jnp.cumsum(onehot_int, axis=0) * onehot_int, axis=-1) - 1
    is_kept = slot_index < capacity
    slots = -(-capacity // 16) * 16
    place = jnp.where(is_kept, chosen * slots + slot_index, -1)
    dispatch = (
        place[:, None] == jnp.arange(expert_count * slots, dtype=jnp.int32)[None, :]
    ).astype(jnp.bfloat16)
    dispatched = jnp.sum(onehot_int * is_kept[:, None].astype(jnp.int32), axis=0)
    tally_counts = jnp.stack(
        [dispatched, jnp.sum(onehot_int, axis=0) - dispatched], axis=0
    ).reshape(1, 1, 2, expert_count)

    grad_top = cotangent[0].astype(jnp.float32)
    scaled = (gate_prob[:, None] * grad_top).astype(jnp.bfloat16)
    sent_rows = (
        jnp.einsum(
            "tx,td->xd",
            dispatch,
            jnp.concatenate([mixed_low, scaled], axis=1),
            preferred_element_type=jnp.float32,
        )
        .astype(jnp.bfloat16)
        .reshape(m, local_experts * slots, 2 * D)
    )
    maps = [in_own, out_own, in_last, out_last, in_next, out_next]
    returned, *terms = run_experts(sent_rows, maps, n, m, slots, 2)
    returned = returned.reshape(expert_count * slots, 2 * D)
    gin_own, gout_own, gin_next, gout_last, gin_last, gout_next = terms
    gout_next = lax.ppermute(gout_next, "seq", to_next)
    gin_last = lax.ppermute(gin_last, "seq", to_last)
    routed = jnp.dot(dispatch, returned, preferred_element_type=jnp.float32)
    combined, grad_mixed = routed[:, :D], routed[:, D:]
    output = (after_cross + gate_prob[:, None] * combined).astype(jnp.bfloat16)

    grad_gate = jnp.sum(grad_top * combined, axis=-1)
    grad_logits = softmax_probs * (onehot - gate_prob[:, None]) * grad_gate[:, None]
    grad_router = jnp.einsum(
        "td,te->de", mixed_low.astype(jnp.float32), grad_logits, precision=highest
    )
    grad_mixed = grad_mixed + jnp.einsum(
        "te,de->td", grad_logits, router.astype(jnp.float32), precision=highest
    )
    grad_cross_part, grad_gain_mix = rms_backward(after_cross, gain_rows[2], grad_mixed)
    grad_after_cross = grad_top + grad_cross_part

    grad_cross_low = grad_after_cross.astype(jnp.bfloat16)
    grad_attended_cross = input_grad(grad_cross_low, proj_out[1]).astype(jnp.bfloat16)
    grad_cross_query, grad_memory_keys, grad_memory_values = attend_back(
        seq_at,
        cross_queries,
        memory_key_all,
        memory_value_all,
        grad_attended_cross,
        attended_cross,
        lse_cross,
        None,
    )
    grad_cross_query, gin_last, gout_next, gin_next, gout_last = lax.optimization_barrier(
        (grad_cross_query, gin_last, gout_next, gin_next, gout_last)
    )
    gin_next = lax.ppermute(gin_next, "seq", to_next)
    gout_last = lax.ppermute(gout_last, "seq", to_last)
    grad_self_part, grad_gain_cross = rms_backward(
        after_self, gain_rows[1], input_grad(grad_cross_query, proj_in[3])
    )
    grad_after_self = grad_after_cross + grad_self_part
    grad_memory_part, grads_cross = memory_back(
        memory_all, grad_memory_keys, grad_memory_values, proj_in
    )

    grad_self_low = grad_after_self.astype(jnp.bfloat16)
    grad_attended_self = input_grad(grad_self_low, proj_out[0]).astype(jnp.bfloat16)
    grad_self_query, grad_keys, grad_values, near, sums = attend_back(
        seq_at,
        queries,
        key_all,
        value_all,
        grad_attended_self,
        attended_self,
        lse_self,
        lines,
    )
    grad_self_query, grad_keys, grad_values, near, sums, gout_last, gin_next = (
        lax.optimization_barrier(
            (grad_self_query, grad_keys, grad_values, near, sums, gout_last, gin_next)
        )
    )
    grad_table = bias_gradient(near, sums)
    (
        grad_normed_part,
        grads,
        grad_gain_part,
        grad_normed_query,
        grad_expert_in,
        grad_expert_out,
    ) = token_back(
        normed_all,
        grad_keys,
        grad_values,
        normed_self,
        grad_self_query,
        proj_in,
        [gin_own, gin_last, gin_next, gout_own, gout_last, gout_next],
        [
            normed_cross,
            grad_cross_query,
            attended_self_low,
            grad_self_low,
            attended_cross_low,
            grad_cross_low,
        ],
        grads_cross,
    )
    grad_gain_self = grad_gain_part[0] / gain_rows[0]

    grad_gains = jnp.stack([grad_gain_self, grad_gain_cross, grad_gain_mix])
    lines = jnp.concatenate(
        [grad_router.T, grad_gains, jnp.zeros((8 - grad_gains.shape[0], D), jnp.float32)]
    )
    small = [lines[:, i * TILE : (i + 1) * TILE] for i in range(D // TILE)]
    small.append(jnp.pad(grad_table, ((0, 0), (0, TILE - HEADS))))
    (grad_normed_own, grad_memory), grads, small = finish(
        [
            grad_normed_part.reshape(n, token_count, D),
            grad_memory_part.reshape(n, memory_count, D),
        ],
        grads.reshape(-1, D),
        jnp.concatenate(small),
        n,
        m,
        4,
    )
    wide = present(grads.reshape(8, D, D), small, expert_count)
    grad_token_part, _ = rms_backward(tokens, gain_rows[0], grad_normed_query + grad_normed_own)
    grad_in = (grad_after_self + grad_token_part).astype(jnp.bfloat16)
    return (
        output.reshape(1, token_count, D),
        grad_in.reshape(1, token_count, D),
        grad_memory.astype(jnp.bfloat16).reshape(1, memory_count, D),
        *wide,
        grad_expert_in,
        grad_expert_out,
        tally_counts,
    )


def solution(mesh):
    rows = P("exp", "seq", None)
    hidden = P("exp", None, "seq")
    return jax.shard_map(
        functools.partial(body, mesh.shape["seq"], mesh.shape["exp"]),
        mesh=mesh,
        in_specs=(rows, rows, P(), P(), P(), P(), P(), rows, hidden, hidden, rows),
        out_specs=(
            rows,
            rows,
            rows,
            P(),
            P(),
            P(),
            P(),
            P(),
            hidden,
            hidden,
            P("exp", "seq", None, None),
        ),
        check_vma=False,
    )
```

```python
import functools
import math

import jax
import jax.numpy as jnp
from jax import lax
from jax.experimental import pallas as pl
from jax.experimental.pallas import tpu as pltpu
from jax.sharding import PartitionSpec as P

D = 768
HEADS = 12
HEAD_DIM = 64
NBUCKET = 32
MAXDIST = 128
TILE = 128
PAIRS = HEADS * HEAD_DIM // TILE

MESH = pl.DeviceIdType.MESH
ANY = pl.BlockSpec(memory_space=pl.ANY)
SMEM = pl.BlockSpec(memory_space=pltpu.SMEM)

norm_eps = 1e-06
masked_score = -1e30
highest = lax.Precision.HIGHEST
log2e = 1.0 / math.log(2.0)
scale_factor = HEAD_DIM ** (-0.5)


def bucket_edges():
    half_count = NBUCKET // 2
    thresholds = []
    for bucket_number in range(1, NBUCKET):
        if bucket_number < half_count:
            thresholds.append(bucket_number)
        else:
            thresholds.append(
                int(
                    half_count
                    * (MAXDIST / half_count) ** ((bucket_number - half_count) / half_count)
                )
            )
    return thresholds


def rms_apply(values, gain_row):
    return (
        values * lax.rsqrt(jnp.mean(values * values, axis=-1, keepdims=True) + norm_eps) * gain_row
    )


def rms_backward(values, gain_row, upstream):
    _, pullback = jax.vjp(rms_apply, values, gain_row)
    return pullback(upstream)


def cost(us):
    return pl.CostEstimate(flops=us * 10**9, bytes_accessed=0, transcendentals=0)


def seq_cycle(n):
    cols = n // 4
    if n % 4 or cols < 2:
        return list(range(n))
    order = [0]
    for row in range(4):
        span = range(1, cols) if row % 2 == 0 else range(cols - 1, 0, -1)
        order += [row * cols + col for col in span]
    return order + [3 * cols, 2 * cols, cols]


def look_up(index, table):
    value = jnp.int32(table[0])
    for number, entry in enumerate(table[1:], 1):
        value = jnp.where(index == number, jnp.int32(entry), value)
    return value


def greet(others):
    barrier = pltpu.get_barrier_semaphore()
    for other in others:
        pl.semaphore_signal(barrier, inc=1, device_id=other, device_id_type=MESH)
    pl.semaphore_wait(barrier, len(others))


def seq_ring(n):
    order = seq_cycle(n)
    pos = look_up(lax.axis_index("seq"), [order.index(i) for i in range(n)])

    def at(place):
        return look_up(lax.rem(place + 4 * n, n), order)

    return pos, at, ({"seq": at(pos + 1)}, {"seq": at(pos - 1)})


def gather_kernel(n, parts, *refs):
    sources, proj_ref, outs = refs[:2], refs[2], refs[3:10]
    lands, w_buf, bufs = refs[10:12], refs[12], refs[13:18]
    own_sem, w_sem, send_sem, recv_sem, store_sem = refs[18:]
    pos, at, sides = seq_ring(n)
    me = at(pos)
    greet(sides)
    own = [pltpu.make_async_copy(sources[a], lands[a].at[me], own_sem.at[a]) for a in range(2)]
    weights = [
        pltpu.make_async_copy(proj_ref.at[number], w_buf.at[i], w_sem.at[i])
        for i, number in enumerate((0, 1, 2, 4, 5))
    ]
    started, latest, stored = [], {}, []

    def pass_on(step):
        for part in range(parts):
            for a in range(2):
                rows = sources[a].shape[0] // 2 // parts
                for way in range(2):
                    if step:
                        latest[a, way, part].wait_recv()
                    if step == n - 1:
                        continue
                    block = at(pos - step) if way == 0 else at(pos + step)
                    span = pl.ds((way * parts + part) * rows, rows)
                    copy = pltpu.make_async_remote_copy(
                        src_ref=lands[a].at[block, span] if step else sources[a].at[span],
                        dst_ref=lands[a].at[block, span],
                        send_sem=send_sem.at[a, way, step, part],
                        recv_sem=recv_sem.at[a, way, step, part],
                        device_id=sides[way],
                        device_id_type=MESH,
                    )
                    copy.start()
                    started.append(copy)
                    latest[a, way, part] = copy

    def store(source, target, number, step, way):
        copy = pltpu.make_async_copy(source, target, store_sem.at[number, step, way])
        copy.start()
        stored.append(copy)

    def work(step):
        blocks = (at(pos - step), at(pos + step))
        for a in range(2):
            half = sources[a].shape[0] // 2
            spans = (pl.ds(0, half), pl.ds(half, half))
            rows = jnp.concatenate([lands[a][blocks[way], spans[way], :] for way in range(2)], axis=0)
            for i in range(2):
                buf = bufs[1 + 2 * a + i]
                made = dot_plain(rows, w_buf[1 + 2 * a + i]).astype(buf.dtype)
                for way in range(2):
                    buf[blocks[way], spans[way], :] = made[way * half : (way + 1) * half]
            for way in range(2):
                where = (blocks[way], spans[way])
                store(lands[a].at[where], outs[a].at[where], a, step, way)
                for i in range(2):
                    number = 1 + 2 * a + i
                    store(bufs[number].at[where], outs[2 + number].at[where], 2 + number, step, way)

    pass_on(0)
    for copy in own + weights:
        copy.start()
    for copy in own + weights:
        copy.wait()
    bufs[0][...] = dot_plain(lands[0][me], w_buf[0]).astype(bufs[0].dtype)
    store(bufs[0], outs[2], 2, 0, 0)
    work(0)
    for step in range(1, n):
        pass_on(step)
        work(step)
    for copy in started:
        copy.wait_send()
    for copy in stored:
        copy.wait()


def gather_projected(tokens, memory_rows, proj_in, n, number, parts=2):
    both = (tokens, memory_rows)
    copies = (2, 2, n - 1, parts)
    wide = [(n,) + x.shape for x in both]
    shapes = wide + [tokens.shape] + [wide[0]] * 2 + [wide[1]] * 2
    dma = pltpu.SemaphoreType.DMA
    return pl.pallas_call(
        functools.partial(gather_kernel, n, parts),
        out_shape=[jax.ShapeDtypeStruct(shape, tokens.dtype) for shape in shapes],
        in_specs=[ANY] * 3,
        out_specs=[ANY] * 7,
        scratch_shapes=[pltpu.VMEM(shape, tokens.dtype) for shape in wide]
        + [pltpu.VMEM((5,) + proj_in.shape[1:], tokens.dtype)]
        + [pltpu.VMEM(shape, tokens.dtype) for shape in shapes[2:]]
        + [dma((2,)), dma((5,)), dma(copies), dma(copies), dma((7, n, 2))],
        compiler_params=pltpu.CompilerParams(
            collective_id=number, has_side_effects=True, vmem_limit_bytes=58 << 20
        ),
        cost_estimate=cost(60),
        name="gather_projected",
    )(tokens, memory_rows, proj_in)


def scatter_kernel(n, parts, count, *refs):
    sources, outs = refs[:count], refs[count : 2 * count]
    own_bufs, got_bufs = refs[2 * count : 3 * count], refs[3 * count : 4 * count]
    own_sem, send_sem, recv_sem = refs[4 * count :]
    pos, at, sides = seq_ring(n)
    greet(sides)
    lanes = [(a, part, way) for a in range(count) for part in range(parts) for way in range(2)]

    def span(a, part, way):
        rows = sources[a].shape[1] // 2 // parts
        return pl.ds((way * parts + part) * rows, rows)

    def block(way, step):
        return at(pos - 1 - step) if way == 0 else at(pos + 1 + step)

    def send(lane, step, source):
        a, part, way = lane
        copy = pltpu.make_async_remote_copy(
            src_ref=source,
            dst_ref=got_bufs[a].at[way, step, part],
            send_sem=send_sem.at[a, way, step, part],
            recv_sem=recv_sem.at[a, way, step, part],
            device_id=sides[way],
            device_id_type=MESH,
        )
        copy.start()
        return copy

    latest, started, own = {}, [], {}
    for lane in lanes:
        a, part, way = lane
        latest[lane] = send(lane, 0, sources[a].at[block(way, 0), span(a, part, way)])
        started.append(latest[lane])
    for step in range(1, n):
        for lane in lanes:
            a, part, way = lane
            own[lane, step] = pltpu.make_async_copy(
                sources[a].at[block(way, step), span(a, part, way)],
                own_bufs[a].at[way, step - 1, part],
                own_sem.at[a, way, step - 1, part],
            )
            own[lane, step].start()
    for step in range(1, n):
        for lane in lanes:
            a, part, way = lane
            own[lane, step].wait()
            latest[lane].wait_recv()
            total = got_bufs[a][way, step - 1, part].astype(jnp.float32) + own_bufs[a][
                way, step - 1, part
            ].astype(jnp.float32)
            if step == n - 1:
                outs[a][span(a, part, way)] = total.astype(outs[a].dtype)
            else:
                got_bufs[a][way, step - 1, part] = total.astype(got_bufs[a].dtype)
                latest[lane] = send(lane, step, got_bufs[a].at[way, step - 1, part])
                started.append(latest[lane])
    for copy in started:
        copy.wait_send()


def ring_scatter(arrays, n, number, out_dtype, parts=2):
    count = len(arrays)
    copies = (count, 2, n - 1, parts)
    bufs = [
        pltpu.VMEM((2, n - 1, parts, a.shape[1] // 2 // parts, a.shape[2]), a.dtype)
        for a in arrays
    ]
    return pl.pallas_call(
        functools.partial(scatter_kernel, n, parts, count),
        out_shape=[jax.ShapeDtypeStruct(a.shape[1:], out_dtype) for a in arrays],
        in_specs=[ANY] * count,
        out_specs=[pl.BlockSpec(memory_space=pltpu.VMEM)] * count,
        scratch_shapes=bufs + bufs + [pltpu.SemaphoreType.DMA(copies)] * 3,
        compiler_params=pltpu.CompilerParams(
            collective_id=number, has_side_effects=True, vmem_limit_bytes=58 << 20
        ),
        name="ring_scatter",
    )(*arrays)


def finish_kernel(n, counts, *refs):
    few, many = counts
    refs = list(refs)
    take = lambda count: [refs.pop(0) for _ in range(count)]
    blocks, xs, sums, outs = take(few), take(many), take(few), take(many)
    own_bufs, got_bufs = take(few), take(few)
    mines, twins, crosses, gots = take(many), take(many), take(many), take(many)
    near_sem, far_sem, own_sem, pair_sem, cross_sem, ring_sem = refs
    pos, at, sides = seq_ring(n)
    exp = lax.axis_index("exp")
    core, chip = lax.rem(exp, 2), exp // 2
    peer, over = {"exp": exp + 1 - 2 * core}, {"exp": core + 2 * (1 - chip)}
    greet(sides + (peer, over))
    started = []

    def push(source, target, sems, index, to):
        copy = pltpu.make_async_remote_copy(
            src_ref=source,
            dst_ref=target,
            send_sem=sems.at[(0,) + index],
            recv_sem=sems.at[(1,) + index],
            device_id=to,
            device_id_type=MESH,
        )
        copy.start()
        started.append(copy)
        return copy

    def block(way, step):
        return at(pos - 1 - step) if way == 0 else at(pos + 1 + step)

    def fetch(source, target, sem):
        copy = pltpu.make_async_copy(source, target, sem)
        copy.start()
        return copy

    add = lambda *terms: functools.reduce(lambda u, v: u + v, [t.astype(jnp.float32) for t in terms])
    ways = range(2)
    lanes = [(a, way) for a in range(many) for way in ways]
    parts = 2
    rings = [(a, way, part) for part in range(parts) for a in range(few) for way in ways]

    def span(ref, way):
        half = ref.shape[-2] // 2
        return pl.ds(way * half, half)

    def piece(lane):
        a, way, part = lane
        rows = blocks[a].shape[-2] // 2 // parts
        return pl.ds(way * parts * rows + part * rows, rows), pl.ds(part * rows, rows)

    pairs, own, crossing, ring = {}, {}, {}, {}
    for side in range(2):
        for step in range(n):
            for lane in lanes:
                a, way = lane
                place = chip if side else 1 - chip
                where, rows = block(way, step), span(xs[a], way)
                pairs[side, lane, step] = push(
                    xs[a].at[1 - core, place, where, rows],
                    twins[a].at[side, way, step],
                    pair_sem,
                    (0, side) + lane + (step,),
                    peer,
                )
                own[side, lane, step] = fetch(
                    xs[a].at[core, place, where, rows],
                    mines[a].at[side, way, step],
                    own_sem.at[(side,) + lane + (step,)],
                )
        if side == 0:
            for lane in rings:
                a, way, part = lane
                wide, thin = piece(lane)
                ring[lane] = push(
                    blocks[a].at[block(way, 0), wide],
                    got_bufs[a].at[way, 0, thin],
                    far_sem,
                    lane + (0,),
                    sides[way],
                )
            near = {}
            for step in range(1, n):
                for lane in rings:
                    a, way, part = lane
                    wide, thin = piece(lane)
                    near[lane, step] = fetch(
                        blocks[a].at[block(way, step), wide],
                        own_bufs[a].at[way, step - 1, thin],
                        near_sem.at[lane + (step - 1,)],
                    )

    def scatter(step, which):
        for lane in rings:
            a, way, part = lane
            if part != which:
                continue
            wide, thin = piece(lane)
            near[lane, step].wait()
            ring[lane].wait_recv()
            total = add(got_bufs[a][way, step - 1, thin], own_bufs[a][way, step - 1, thin])
            if step == n - 1:
                sums[a][wide] = total.astype(sums[a].dtype)
            else:
                got_bufs[a][way, step - 1, thin] = total.astype(got_bufs[a].dtype)
                ring[lane] = push(
                    got_bufs[a].at[way, step - 1, thin],
                    got_bufs[a].at[way, step, thin],
                    far_sem,
                    lane + (step,),
                    sides[way],
                )

    for step in range(n):
        for lane in lanes:
            a, way = lane
            own[0, lane, step].wait()
            pairs[0, lane, step].wait_recv()
            mines[a][0, way, step] = add(mines[a][0, way, step], twins[a][0, way, step]).astype(
                mines[a].dtype
            )
            crossing[lane, step] = push(
                mines[a].at[0, way, step],
                crosses[a].at[way, step],
                cross_sem,
                (0,) + lane + (step,),
                over,
            )
    latest = {}
    waiting = [(step, part) for step in range(1, n) for part in range(parts)]
    for step in range(n):
        for lane in lanes:
            a, way = lane
            own[1, lane, step].wait()
            pairs[1, lane, step].wait_recv()
            crossing[lane, step].wait_recv()
            terms = [mines[a][1, way, step], twins[a][1, way, step], crosses[a][way, step]]
            if step:
                latest[lane].wait_recv()
                terms.append(gots[a][way, step - 1])
            mines[a][1, way, step] = add(*terms).astype(mines[a].dtype)
            if step < n - 1:
                latest[lane] = push(
                    mines[a].at[1, way, step],
                    gots[a].at[way, step],
                    ring_sem,
                    (0,) + lane + (step,),
                    sides[way],
                )
        if waiting:
            scatter(*waiting.pop(0))
    keep, done = [], []
    latest, crossing = {}, {}

    def target_of(lane, step, place):
        a, way = lane
        where = at(pos - step) if way == 0 else at(pos + step)
        return outs[a].at[core, place, where, span(outs[a], way)]

    def hand_on(step):
        for lane in lanes:
            crossing[lane, step].wait_recv()
            target = target_of(lane, step, 1 - chip)
            done.append(push(target, target, pair_sem, (1, 1) + lane + (step,), peer))

    for step in range(n):
        for lane in lanes:
            a, way = lane
            if step:
                latest[lane].wait_recv()
            target = target_of(lane, step, chip)
            source = target if step else mines[a].at[1, way, n - 1]
            if step < n - 1:
                latest[lane] = push(source, target, ring_sem, (1,) + lane + (step,), sides[way])
            crossing[lane, step] = push(source, target, cross_sem, (1,) + lane + (step,), over)
            done.append(push(source, target, pair_sem, (1, 0) + lane + (step,), peer))
            if step == 0:
                keep.append(fetch(source, target, own_sem.at[(0,) + lane + (0,)]))
        if waiting:
            scatter(*waiting.pop(0))
        if step:
            hand_on(step - 1)
    hand_on(n - 1)
    while waiting:
        scatter(*waiting.pop(0))
    for copy in keep:
        copy.wait()
    for copy in done:
        copy.wait_recv()
    for copy in started:
        copy.wait_send()


def finish(blocks, rows_in, small, n, m, number):
    rows, cols = rows_in.shape
    each = rows // (4 * n)
    if m != 4 or rows % (4 * n * 32) or small.shape[0] > 4 * n * 16:
        return (
            ring_scatter(blocks, n, number, jnp.float32),
            *lax.psum((rows_in, small), ("seq", "exp")),
        )
    padded = jnp.pad(small, ((0, 4 * n * 16 - small.shape[0]), (0, 0)))
    arrays = [rows_in.reshape(2, 2, n, each, cols), padded.reshape(2, 2, n, 16, TILE)]
    few, many = len(blocks), len(arrays)
    halves = [(x.shape[-2] // 2, x.shape[-1], x.dtype) for x in blocks + arrays]
    ring_bufs = [pltpu.VMEM((2, n - 1, r, c), t) for r, c, t in halves[:few]]
    two = [pltpu.VMEM((2, 2, n, r, c), t) for r, c, t in halves[few:]]
    one = [pltpu.VMEM((2, n, r, c), t) for r, c, t in halves[few:]]
    dma = pltpu.SemaphoreType.DMA
    results = pl.pallas_call(
        functools.partial(finish_kernel, n, (few, many)),
        out_shape=[jax.ShapeDtypeStruct(x.shape[1:], jnp.float32) for x in blocks]
        + [jax.ShapeDtypeStruct(x.shape, x.dtype) for x in arrays],
        in_specs=[ANY] * (few + many),
        out_specs=[pl.BlockSpec(memory_space=pltpu.VMEM)] * few + [ANY] * many,
        scratch_shapes=ring_bufs * 2
        + two * 2
        + one * 2
        + [
            dma((few, 2, 2, n)),
            dma((2, few, 2, 2, n)),
            dma((2, many, 2, n)),
            dma((2, 2, 2, many, 2, n)),
            dma((2, 2, many, 2, n)),
            dma((2, 2, many, 2, n)),
        ],
        compiler_params=pltpu.CompilerParams(
            collective_id=number, has_side_effects=True, vmem_limit_bytes=58 << 20
        ),
        cost_estimate=cost(120),
        name="finish",
    )(*blocks, *arrays)
    return results[:few], results[few].reshape(rows, cols), results[-1].reshape(-1, TILE)


def dot_last(a, b):
    return lax.dot_general(a, b, (((1,), (1,)), ((), ())), preferred_element_type=jnp.float32)


def dot_first(a, b):
    return lax.dot_general(a, b, (((0,), (0,)), ((), ())), preferred_element_type=jnp.float32)


def dot_plain(a, b):
    return jnp.dot(a, b, preferred_element_type=jnp.float32)


def head_masks(dtype):
    low = lax.broadcasted_iota(jnp.int32, (1, TILE), 1) < HEAD_DIM
    first = jnp.where(low, 1.0, 0.0).astype(jnp.float32)
    return first.astype(dtype), (1.0 - first).astype(dtype)


def split_heads(pair):
    return jnp.concatenate([pair * mask for mask in head_masks(pair.dtype)], axis=0)


def own_bias(tiles, count):
    rows = []
    for r in range(count):
        row = []
        for c in range(count):
            if c == r:
                row.append(tiles[:, TILE:])
            elif c == r - 1:
                row.append(tiles[:, :TILE])
            else:
                row.append(jnp.full((TILE, TILE), 0.0 if c < r else masked_score, jnp.float32))
        rows.append(jnp.concatenate(row, axis=1))
    return jnp.concatenate(rows, axis=0)


def edge_bias(tiles, rows):
    edge = []
    for h in range(2):
        first = jnp.concatenate(
            [jnp.zeros((rows - TILE, TILE), jnp.float32), tiles[h][:, :TILE].T], axis=0
        )
        edge += [first, jnp.zeros((rows, rows - TILE), jnp.float32)]
    return jnp.concatenate(edge, axis=1)


def each_far(s, block, act, times=3):
    far = jnp.maximum(s - 1, 0)
    bundles = far // times

    def bundle(j, carry):
        act(pl.multiple_of(j * times * block, block), times)
        return carry

    def single(j, carry):
        act(pl.multiple_of(j * block, block), 1)
        return carry

    lax.fori_loop(0, bundles, bundle, 0)
    lax.fori_loop(bundles * times, far, single, 0)


def attend_kernel(causal, block, s_ref, q_ref, k_ref, v_ref, *refs):
    if causal:
        line_ref, low_ref, wide_ref, lse_ref, acc_ref, top_ref = refs
    else:
        low_ref, wide_ref, lse_ref, acc_ref, top_ref = refs
    rows = q_ref.shape[0]
    both = split_heads(q_ref[...])

    def visit(start, bias, first, times=1):
        ones = jnp.ones((16, times * block), v_ref.dtype)
        keys = k_ref[pl.ds(start, times * block), :]
        values = v_ref[pl.ds(start, times * block), :]
        t = dot_last(keys, both) * (scale_factor * log2e)
        if bias is not None:
            t = t + bias
        top = jnp.max(t, axis=0, keepdims=True)
        if not first:
            before = top_ref[...]
            top = jnp.maximum(before, top)
            fade = jnp.exp2(before - top)
        top_ref[...] = top
        p = jnp.exp2(t - top).astype(values.dtype)
        part = dot_plain(jnp.concatenate([values.T, ones], axis=0), p)
        if first:
            acc_ref[...] = part
        else:
            acc_ref[...] = acc_ref[...] * fade + part

    if causal:
        s = s_ref[0]
        count = rows // TILE
        tiles = [bias_tile(line_ref, h) for h in range(2)]
        visit(
            pl.multiple_of(s * block, block),
            jnp.concatenate([own_bias(tiles[h], count).T for h in range(2)], axis=1),
            True,
        )

        @pl.when(s > 0)
        def _():
            visit(pl.multiple_of((s - 1) * block, block), edge_bias(tiles, rows), False)

        each_far(s, block, lambda start, times: visit(start, None, False, times))
    else:
        for j in range(k_ref.shape[0] // block):
            visit(j * block, None, j == 0)
    sums = acc_ref[TILE : TILE + 1, :]
    wide = jnp.concatenate(
        [
            acc_ref[:HEAD_DIM, :rows] / sums[:, :rows],
            acc_ref[HEAD_DIM:TILE, rows:] / sums[:, rows:],
        ],
        axis=0,
    ).T
    wide_ref[...] = wide
    low_ref[...] = wide.astype(low_ref.dtype)
    lse = top_ref[...] + jnp.log2(sums)
    lse_ref[0] = jnp.concatenate([lse[:, :rows], lse[:, rows:]], axis=0)


def attend(seq_at, queries, keys, values, lines):
    rows, total = queries.shape[0], keys.shape[0]
    causal = lines is not None
    block = rows if causal else math.gcd(total, 1024)
    pair = pl.BlockSpec((rows, TILE), lambda g: (0, g))
    long = pl.BlockSpec((total, TILE), lambda g: (0, g))
    extra, specs = [], []
    if causal:
        extra, specs = [lines], [pl.BlockSpec((1,) + lines.shape[1:], lambda g: (g, 0, 0))]
    return pl.pallas_call(
        functools.partial(attend_kernel, causal, block),
        grid=(PAIRS,),
        out_shape=[
            jax.ShapeDtypeStruct((rows, D), jnp.bfloat16),
            jax.ShapeDtypeStruct((rows, D), jnp.float32),
            jax.ShapeDtypeStruct((PAIRS, 2, rows), jnp.float32),
        ],
        in_specs=[SMEM, pair, long, long] + specs,
        out_specs=[pair, pair, pl.BlockSpec((1, 2, rows), lambda g: (g, 0, 0))],
        scratch_shapes=[
            pltpu.VMEM((TILE + 16, 2 * rows), jnp.float32),
            pltpu.VMEM((1, 2 * rows), jnp.float32),
        ],
        compiler_params=pltpu.CompilerParams(vmem_limit_bytes=48 << 20),
        cost_estimate=cost(40 if causal else 10),
        name="attend_self" if causal else "attend_cross",
    )(seq_at, queries, keys, values, *extra)


def attend_back_kernel(causal, block, s_ref, q_ref, k_ref, v_ref, up_ref, wide_ref, lse_ref, *refs):
    if causal:
        line_ref, dq_ref, dk_ref, dv_ref, bias_ref, sum_ref, acc_ref, near_ref = refs
    else:
        dq_ref, dk_ref, dv_ref, acc_ref = refs
    rows = q_ref.shape[0]
    both = split_heads(q_ref[...])
    up = up_ref[...]
    up_both = split_heads(up)
    turned = (up.astype(jnp.float32) * wide_ref[...]).T
    delta = jnp.concatenate(
        [
            jnp.sum(turned[:HEAD_DIM], axis=0, keepdims=True),
            jnp.sum(turned[HEAD_DIM:], axis=0, keepdims=True),
        ],
        axis=1,
    )
    lse = jnp.concatenate([lse_ref[0, :1], lse_ref[0, 1:]], axis=1)

    def visit(start, bias, first, times=1):
        ones = jnp.ones((16, times * block), k_ref.dtype)
        keys = k_ref[pl.ds(start, times * block), :]
        values = v_ref[pl.ds(start, times * block), :]
        t = dot_last(keys, both) * (scale_factor * log2e)
        if bias is not None:
            t = t + bias
        p = jnp.exp2(t - lse)
        ds = (p * (dot_last(values, up_both) - delta)).astype(keys.dtype)
        dv_ref[pl.ds(start, times * block), :] = dot_plain(p.astype(keys.dtype), up_both).astype(
            dv_ref.dtype
        )
        dk_ref[pl.ds(start, times * block), :] = (dot_plain(ds, both) * scale_factor).astype(dk_ref.dtype)
        part = dot_plain(jnp.concatenate([keys.T, ones], axis=0), ds)
        if first:
            acc_ref[...] = part
        else:
            acc_ref[...] += part
        return ds

    if causal:
        s = s_ref[0]
        count = rows // TILE
        tiles = [bias_tile(line_ref, h) for h in range(2)]
        ds = visit(
            pl.multiple_of(s * block, block),
            jnp.concatenate([own_bias(tiles[h], count).T for h in range(2)], axis=1),
            True,
        )
        for h in range(2):
            same = before = jnp.zeros((TILE, TILE), jnp.float32)
            for r in range(count):
                columns = slice(h * rows + r * TILE, h * rows + (r + 1) * TILE)
                same = same + ds[r * TILE : (r + 1) * TILE, columns].astype(jnp.float32)
                if r:
                    before = before + ds[(r - 1) * TILE : r * TILE, columns].astype(jnp.float32)
            near_ref[h, :TILE] = before
            near_ref[h, TILE:] = same

        @pl.when(s > 0)
        def _():
            ds = visit(pl.multiple_of((s - 1) * block, block), edge_bias(tiles, rows), False)
            for h in range(2):
                near_ref[h, :TILE] += ds[rows - TILE :, h * rows : h * rows + TILE].astype(
                    jnp.float32
                )

        each_far(s, block, lambda start, times: visit(start, None, False, times))

        def beyond(j, carry):
            start = pl.multiple_of(j * block, block)
            dk_ref[pl.ds(start, block), :] = jnp.zeros((block, TILE), dk_ref.dtype)
            dv_ref[pl.ds(start, block), :] = jnp.zeros((block, TILE), dv_ref.dtype)
            return carry

        lax.fori_loop(s + 1, k_ref.shape[0] // block, beyond, 0)
        turn = (
            lax.broadcasted_iota(jnp.int32, (TILE, TILE), 0)
            + lax.broadcasted_iota(jnp.int32, (TILE, TILE), 1)
            == TILE - 1
        ).astype(jnp.float32)
        diagonals = []
        for h in range(2):
            near = jnp.dot(turn, near_ref[h].T, precision=highest, preferred_element_type=jnp.float32)
            near = jnp.concatenate([near, jnp.zeros((TILE, TILE), jnp.float32)], axis=1)
            near = pltpu.roll(near, 0, 1, stride=1, stride_axis=0)
            diagonals.append(jnp.sum(near, axis=0, keepdims=True))
        bias_ref[0] = jnp.concatenate(diagonals, axis=0)
        sum_ref[0] = jnp.concatenate(
            [acc_ref[TILE : TILE + 1, :rows], acc_ref[TILE : TILE + 1, rows:]], axis=0
        )
    else:
        for j in range(k_ref.shape[0] // block):
            visit(j * block, None, j == 0)
    dq = jnp.concatenate([acc_ref[:HEAD_DIM, :rows], acc_ref[HEAD_DIM:TILE, rows:]], axis=0)
    dq_ref[...] = (dq.T * scale_factor).astype(dq_ref.dtype)


def attend_back(seq_at, queries, keys, values, upstream, wide, lse, lines):
    rows, total = queries.shape[0], keys.shape[0]
    causal = lines is not None
    block = rows if causal else math.gcd(total, 1024)
    pair = pl.BlockSpec((rows, TILE), lambda g: (0, g))
    long = pl.BlockSpec((total, TILE), lambda g: (0, g))
    line = pl.BlockSpec((1, 2, rows), lambda g: (g, 0, 0))
    extra, specs, shapes, out_specs, scratch = [], [], [], [], []
    if causal:
        extra, specs = [lines], [pl.BlockSpec((1,) + lines.shape[1:], lambda g: (g, 0, 0))]
        shapes = [
            jax.ShapeDtypeStruct((PAIRS, 2, 3 * TILE), jnp.float32),
            jax.ShapeDtypeStruct((PAIRS, 2, rows), jnp.float32),
        ]
        out_specs = [pl.BlockSpec((1, 2, 3 * TILE), lambda g: (g, 0, 0)), line]
        scratch = [pltpu.VMEM((2, 2 * TILE, TILE), jnp.float32)]
    return pl.pallas_call(
        functools.partial(attend_back_kernel, causal, block),
        grid=(PAIRS,),
        out_shape=[
            jax.ShapeDtypeStruct((rows, D), jnp.bfloat16),
            jax.ShapeDtypeStruct((total, D), jnp.bfloat16),
            jax.ShapeDtypeStruct((total, D), jnp.bfloat16),
        ]
        + shapes,
        in_specs=[SMEM, pair, long, long, pair, pair, line] + specs,
        out_specs=[pair, long, long] + out_specs,
        scratch_shapes=[pltpu.VMEM((TILE + 16, 2 * rows), jnp.float32)] + scratch,
        compiler_params=pltpu.CompilerParams(vmem_limit_bytes=48 << 20),
        cost_estimate=cost(48 if causal else 15),
        name="attend_self_back" if causal else "attend_cross_back",
    )(seq_at, queries, keys, values, upstream, wide, lse, *extra)


def key_value_back(x_ref, dk_ref, dv_ref, wk_ref, wv_ref, dx_ref):
    x, both = x_ref[...], jnp.concatenate([dk_ref[...], dv_ref[...]], axis=1)
    dx = dot_last(both, jnp.concatenate([wk_ref[0], wv_ref[0]], axis=1))
    dx_ref[...] = dx.astype(dx_ref.dtype)
    gain = jnp.sum(dx * x.astype(jnp.float32), axis=0, keepdims=True)
    return gain, dot_first(x, both)


def add_up(step, last, made, total, outs):
    @pl.when(step == 0)
    def _():
        total[...] = made

    @pl.when(step > 0)
    def _():
        total[...] += made

    @pl.when(step == last)
    def _():
        for i, out in enumerate(outs):
            out[...] = total[:, i * D : (i + 1) * D].astype(out.dtype)


def memory_back_kernel(x_ref, dk_ref, dv_ref, wk_ref, wv_ref, dx_ref, grad_ref, acc_ref):
    _, made = key_value_back(x_ref, dk_ref, dv_ref, wk_ref, wv_ref, dx_ref)
    outs = [grad_ref.at[0], grad_ref.at[1]]
    add_up(pl.program_id(0), pl.num_programs(0) - 1, made, acc_ref, outs)


def token_back_kernel(*refs):
    x_ref, dk_ref, dv_ref, wk_ref, wv_ref, own_ref, dq_ref, wq_ref = refs[:8]
    terms, others, cross_ref = refs[8:14], refs[14:20], refs[20]
    (dx_ref, grad_ref, gain_ref, query_ref), sums = refs[21:25], refs[25:27]
    acc_ref = refs[27]
    step, last = pl.program_id(0), pl.num_programs(0) - 1
    for i, out in enumerate(sums):
        first, *rest = terms[3 * i : 3 * i + 3]
        total = first[...]
        for term in rest:
            total = total + term[...].astype(jnp.float32)
        out[...] = total
    gain, made = key_value_back(x_ref, dk_ref, dv_ref, wk_ref, wv_ref, dx_ref)
    add_up(step, last, made, acc_ref, [grad_ref.at[1], grad_ref.at[2]])

    @pl.when(step == 0)
    def _():
        own, dq = own_ref[...], dq_ref[...]
        back = dot_last(dq, wq_ref[0])
        query_ref[...] = back
        gain_ref[...] = gain + jnp.sum(back * own.astype(jnp.float32), axis=0, keepdims=True)
        grad_ref[0] = dot_first(own, dq).astype(grad_ref.dtype)
        grad_ref[4:6] = cross_ref[...]

    @pl.when(step > 0)
    def _():
        gain_ref[...] += gain

    for i, number in enumerate((3, 6, 7)):

        @pl.when(step == jnp.minimum(i + 1, last))
        def _(i=i, number=number):
            product = dot_first(others[2 * i][...], others[2 * i + 1][...])
            grad_ref[number] = product.astype(grad_ref.dtype)


def memory_back(tokens, grad_keys, grad_values, proj_in):
    total = tokens.shape[0]
    rows = math.gcd(total, 512)
    block = pl.BlockSpec((rows, D), lambda i: (i, 0))
    weight = lambda number: pl.BlockSpec((1, D, D), lambda i: (number, 0, 0))
    return pl.pallas_call(
        memory_back_kernel,
        grid=(total // rows,),
        out_shape=[
            jax.ShapeDtypeStruct(tokens.shape, tokens.dtype),
            jax.ShapeDtypeStruct((2, D, D), tokens.dtype),
        ],
        in_specs=[block] * 3 + [weight(4), weight(5)],
        out_specs=[block, pl.BlockSpec((2, D, D), lambda i: (0, 0, 0))],
        scratch_shapes=[pltpu.VMEM((D, 2 * D), jnp.float32)],
        compiler_params=pltpu.CompilerParams(vmem_limit_bytes=48 << 20),
        cost_estimate=cost(8),
        name="memory_back",
    )(tokens, grad_keys, grad_values, proj_in, proj_in)


def token_back(tokens, grad_keys, grad_values, own, grad_queries, proj_in, terms, others, grads_cross):
    steps = tokens.shape[0] // (2 * own.shape[0])
    block = pl.BlockSpec((2 * own.shape[0], D), lambda i: (i, 0))
    once = pl.Buffered(1)
    weight = lambda number: pl.BlockSpec((1, D, D), lambda i: (number, 0, 0), pipeline_mode=once)
    whole = pl.BlockSpec(own.shape, lambda i: (0, 0), pipeline_mode=once)
    pair = pl.BlockSpec((2, D, D), lambda i: (0, 0, 0), pipeline_mode=once)
    count, _, hidden = terms[0].shape
    expert = pl.BlockSpec((count, D // steps, hidden), lambda i: (0, i, 0))
    return pl.pallas_call(
        token_back_kernel,
        grid=(steps,),
        out_shape=[
            jax.ShapeDtypeStruct(tokens.shape, tokens.dtype),
            jax.ShapeDtypeStruct((8, D, D), tokens.dtype),
            jax.ShapeDtypeStruct((1, D), jnp.float32),
            jax.ShapeDtypeStruct(own.shape, jnp.float32),
        ]
        + [jax.ShapeDtypeStruct(terms[0].shape, jnp.float32)] * 2,
        in_specs=[block] * 3
        + [weight(1), weight(2), whole, whole, weight(0)]
        + [expert] * 6
        + [whole] * 6
        + [pair],
        out_specs=[
            block,
            pl.BlockSpec((8, D, D), lambda i: (0, 0, 0), pipeline_mode=once),
            pl.BlockSpec((1, D), lambda i: (0, 0)),
            pl.BlockSpec(own.shape, lambda i: (0, 0)),
            expert,
            expert,
        ],
        scratch_shapes=[pltpu.VMEM((D, 2 * D), jnp.float32)],
        compiler_params=pltpu.CompilerParams(vmem_limit_bytes=56 << 20),
        cost_estimate=cost(28),
        name="token_back",
    )(
        tokens,
        grad_keys,
        grad_values,
        proj_in,
        proj_in,
        own,
        grad_queries,
        proj_in,
        *terms,
        *others,
        grads_cross,
    )


def bias_lines(bias_table):
    at = jnp.arange(3 * TILE, dtype=jnp.int32)
    distance = jnp.where(at <= 2 * TILE, TILE - at, 4 * TILE - at)
    table = (bias_table - bias_table[NBUCKET - 1 :]) * log2e
    terms = jnp.broadcast_to(table[0][:, None], (HEADS, 3 * TILE))
    for number, threshold in enumerate(bucket_edges()):
        terms = jnp.where((distance >= threshold)[None], table[number + 1][:, None], terms)
    return jnp.where((distance >= 0)[None], terms, masked_score).reshape(PAIRS, 2, 3 * TILE)


def bias_tile(line_ref, h):
    line = jnp.broadcast_to(line_ref[0, h : h + 1, :], (TILE, 3 * TILE))
    return pltpu.roll(line, 0, 1, stride=1, stride_axis=0)[:, : 2 * TILE]


def bias_gradient(diagonals, sums):
    distance = 2 * TILE - 1 - jnp.arange(3 * TILE, dtype=jnp.int32)
    bucket = jnp.zeros(distance.shape, jnp.int32)
    for threshold in bucket_edges():
        bucket = bucket + (distance >= threshold).astype(jnp.int32)
    buckets = jnp.arange(NBUCKET, dtype=jnp.int32)[:, None]
    flat = diagonals.reshape(HEADS, -1)
    far = jnp.sum(sums, axis=-1).reshape(HEADS) - jnp.sum(flat, axis=-1)
    table = lax.dot_general(
        (bucket[None, :] == buckets).astype(jnp.float32),
        flat,
        (((1,), (1,)), ((), ())),
        precision=highest,
    )
    return table + jnp.where(buckets == NBUCKET - 1, far[None, :], 0.0)


def expert_kernel(n, m, slots, *refs):
    x_ref, maps, result_ref, grads = refs[0], refs[1:7], refs[7], refs[8:14]
    rows, parts, backs, up_all, down_all, act_all, du_all = refs[14:21]
    grad_bufs, far_bufs = refs[21:29], refs[29:31]
    map_sem, own_sem, grad_sem, go_sem, back_sem, term_sem, far_sem = refs[31:]
    seq, exp = lax.axis_index("seq"), lax.axis_index("exp")
    groups, count = n // QUAD, x_ref.shape[1] // slots
    batch = max(1, 128 // slots)
    far = [(g, k) for g in range(1, groups) for k in range(m)]
    moves = far + [(0, k) for k in range(1, m)]
    source_of = lambda k: lax.rem(exp + m - k, m)

    def push(source, target, sems, g, k, to_seq, to_exp):
        copy = pltpu.make_async_remote_copy(
            src_ref=source,
            dst_ref=target,
            send_sem=sems.at[0, g, k],
            recv_sem=sems.at[1, g, k],
            device_id={"seq": to_seq, "exp": to_exp},
            device_id_type=MESH,
        )
        copy.start()
        return copy

    def place(g, k):
        return lax.rem(seq + g * QUAD, n), lax.rem(exp + k, m)

    to_next, to_last = quad_moves(n)
    side = {"next": look_up(seq, [b for _, b in to_next]), "last": look_up(seq, [b for _, b in to_last])}
    greet(
        [dict(zip(("seq", "exp"), place(g, k))) for g, k in moves]
        + [{"seq": side["next"], "exp": exp}, {"seq": side["last"], "exp": exp}]
    )
    going = {}

    def go(some):
        for g, k in some:
            to_seq, to_exp = place(g, k)
            going[g, k] = push(x_ref.at[to_exp], rows.at[g, exp], go_sem, g, k, to_seq, to_exp)

    early = far[: len(far) // 2]
    go(early + moves[len(far) :])
    own = pltpu.make_async_copy(x_ref.at[exp], rows.at[0, exp], own_sem.at[0])
    own.start()
    fetched = []
    for j in range(1, QUAD):
        j = j % (QUAD - 1)
        for at, (source, target) in enumerate(((maps[2 * j], up_all), (maps[2 * j + 1], down_all))):
            copy = pltpu.make_async_copy(source, target.at[j], map_sem.at[at, j])
            copy.start()
            fetched.append(copy)
    for copy in fetched:
        copy.wait()
    far_maps = [
        push(up_all.at[1], up_all.at[3], far_sem, 0, 0, side["next"], exp),
        push(down_all.at[2], down_all.at[3], far_sem, 0, 1, side["last"], exp),
    ]
    own.wait()
    slope = math.sqrt(2.0 / math.pi)
    coming = {}

    def work(g, first, last):
        for k in range(first, last):
            if g or k:
                going[g, k].wait_recv()
        size = (last - first) * slots
        base = (g * m + first) * slots

        def one(e, carry):
            start = pl.multiple_of(e * slots, slots)
            piece = jnp.concatenate(
                [rows[g, source_of(k), pl.ds(start, slots), :] for k in range(first, last)], axis=0
            )
            tokens, upstream = piece[:, :D], piece[:, D:]
            result = back = None
            for j in range(QUAD):
                up_map, down_map = up_all[j, e], down_all[j, e]
                u = dot_plain(tokens, up_map)
                square = u * u
                bend = jnp.tanh(slope * (u + 0.044715 * (square * u)))
                half = 0.5 * (1.0 + bend)
                act = (u * half).astype(tokens.dtype)
                rise = half + 0.5 * u * (1.0 - bend * bend) * (
                    slope * (1.0 + 3 * 0.044715 * square)
                )
                du = (dot_plain(upstream, down_map) * rise).astype(tokens.dtype)
                act_all[e, j, base : base + size] = act
                du_all[e, j, base : base + size] = du
                y, dn = dot_last(act, down_map), dot_last(du, up_map)
                result = y if result is None else result + y
                back = dn if back is None else back + dn
            for i, k in enumerate(range(first, last)):
                span = slice(i * slots, (i + 1) * slots)
                where = (g, source_of(k), pl.ds(start, slots))
                parts[where + (slice(0, D),)] = result[span].astype(parts.dtype)
                parts[where + (slice(D, 2 * D),)] = back[span].astype(parts.dtype)
            return carry

        lax.fori_loop(0, count, one, 0)
        for k in range(first, last):
            if g or k:
                source = source_of(k)
                coming[g, k] = push(
                    parts.at[g, source],
                    backs.at[g, exp],
                    back_sem,
                    g,
                    k,
                    lax.rem(seq + n - g * QUAD, n),
                    source,
                )

    for move in early:
        going[move].wait_send()
    go(far[len(early) :])
    for copy in far_maps:
        copy.wait_recv()
    work(0, 0, m)
    for g in range(1, groups):
        for first in range(0, m, batch):
            work(g, first, min(m, first + batch))

    total = groups * m * slots

    def weigh(j):
        def one(e, carry):
            start = pl.multiple_of(e * slots, slots)
            piece = jnp.concatenate(
                [
                    rows[g, source_of(k), pl.ds(start, slots), :]
                    for g in range(groups)
                    for k in range(m)
                ],
                axis=0,
            )
            tokens, upstream = piece[:, :D], piece[:, D:]
            up_buf, down_buf = grad_bufs[2 * j], grad_bufs[2 * j + 1]
            up_buf[e] = dot_first(tokens, du_all[e, j, :total]).astype(up_buf.dtype)
            down_buf[e] = dot_first(upstream, act_all[e, j, :total]).astype(down_buf.dtype)
            return carry

        lax.fori_loop(0, count, one, 0)

    def term(source, target, number, to):
        return push(source, target, term_sem, 0, number, side[to], exp)

    def store(source, number):
        copy = pltpu.make_async_copy(source, grads[number], grad_sem.at[number])
        copy.start()
        return copy

    weigh(3)
    terms_out = [
        term(grad_bufs[6], far_bufs[0], 0, "next"),
        term(grad_bufs[7], far_bufs[1], 1, "last"),
    ]
    weigh(1)
    weigh(2)
    weigh(0)
    stored = [
        store(grad_bufs[i], number) for number, i in ((0, 0), (1, 1), (4, 2), (5, 5))
    ]
    for number, (buf, far_buf) in enumerate(((grad_bufs[4], far_bufs[0]), (grad_bufs[3], far_bufs[1]))):
        terms_out[number].wait_recv()
        buf[...] = (buf[...].astype(jnp.float32) + far_buf[...].astype(jnp.float32)).astype(buf.dtype)
        stored.append(store(buf, 2 + number))
    for k in range(m):
        where = source_of(k)
        terms = []
        for g in range(groups):
            back_k = (m - k) % m
            if g == 0 and k == 0:
                terms.append(parts[0, exp])
            else:
                coming[g, back_k].wait_recv()
                terms.append(backs[g, where])
        total_row = terms[0].astype(jnp.float32)
        for term in terms[1:]:
            total_row = total_row + term.astype(jnp.float32)
        result_ref[where] = total_row.astype(result_ref.dtype)
    for copy in stored:
        copy.wait()
    for copy in terms_out + far_maps:
        copy.wait_send()
    for move in moves[len(early) :]:
        going[move].wait_send()
    for copy in coming.values():
        copy.wait_send()


def run_experts(x, maps, n, m, slots, number):
    groups = n // QUAD
    count, _, hidden = maps[0].shape
    total = groups * m * slots
    big = pltpu.VMEM((groups,) + x.shape, x.dtype)
    stack = pltpu.VMEM((QUAD,) + maps[0].shape, x.dtype)
    kept = pltpu.VMEM((count, QUAD, total, hidden), x.dtype)
    grads = [(maps[0].shape, jnp.float32 if i < 2 else jnp.bfloat16) for i in range(2 * QUAD)]
    dma = pltpu.SemaphoreType.DMA
    return pl.pallas_call(
        functools.partial(expert_kernel, n, m, slots),
        out_shape=[jax.ShapeDtypeStruct(x.shape, x.dtype)]
        + [jax.ShapeDtypeStruct(shape, dtype) for shape, dtype in grads[:6]],
        in_specs=[ANY] * (1 + len(maps)),
        out_specs=[pl.BlockSpec(memory_space=pltpu.VMEM)] + [ANY] * 6,
        scratch_shapes=[big] * 3
        + [stack] * 2
        + [kept] * 2
        + [pltpu.VMEM(shape, dtype) for shape, dtype in grads + grads[6:]]
        + [
            dma((2, QUAD)),
            dma((1,)),
            dma((6,)),
            dma((2, groups, m)),
            dma((2, groups, m)),
            dma((2, 1, 2)),
            dma((2, 1, 2)),
        ],
        compiler_params=pltpu.CompilerParams(
            collective_id=number, has_side_effects=True, vmem_limit_bytes=60 << 20
        ),
        cost_estimate=cost(150),
        name="run_experts",
    )(x, *maps)


QUAD = 4


def quad_moves(n):
    ring = (0, 1, 3, 2)
    step = lambda i, by: i - i % QUAD + ring[(ring.index(i % QUAD) + by) % QUAD]
    return [(i, step(i, 1)) for i in range(n)], [(i, step(i, -1)) for i in range(n)]


def present_kernel(grad_ref, small_ref, in_ref, out_ref, gain_ref, table_ref, router_ref):
    step = pl.program_id(0)
    value = grad_ref[...].astype(jnp.float32)

    @pl.when(step < 6)
    def _():
        in_ref[...] = value

    @pl.when(step >= 6)
    def _():
        out_ref[...] = value

    @pl.when(step == 0)
    def _():
        experts = router_ref.shape[1]
        each = experts + 8
        pieces = D // TILE
        lines = jnp.concatenate(
            [small_ref[i * each : (i + 1) * each, :] for i in range(pieces)], axis=1
        )
        router_ref[...] = lines[:experts].T
        gain_ref[...] = lines[experts : experts + 3]
        table_ref[...] = small_ref[pieces * each : pieces * each + NBUCKET, :HEADS]


def present(grads, small, experts):
    whole = lambda shape: pl.BlockSpec(shape, lambda i: (0, 0))
    shapes = [(6, D, D), (2, D, D), (3, D), (NBUCKET, HEADS), (D, experts)]
    return pl.pallas_call(
        present_kernel,
        grid=(8,),
        out_shape=[jax.ShapeDtypeStruct(shape, jnp.float32) for shape in shapes],
        in_specs=[pl.BlockSpec((1, D, D), lambda i: (i, 0, 0)), whole(small.shape)],
        out_specs=[
            pl.BlockSpec((1, D, D), lambda i: (jnp.minimum(i, 5), 0, 0)),
            pl.BlockSpec((1, D, D), lambda i: (jnp.maximum(i - 6, 0), 0, 0)),
        ]
        + [whole(shape) for shape in shapes[2:]],
        compiler_params=pltpu.CompilerParams(vmem_limit_bytes=48 << 20),
        cost_estimate=cost(8),
        name="present",
    )(grads, small)


def project(source, matrix):
    return jnp.dot(source, matrix, preferred_element_type=jnp.float32).astype(jnp.bfloat16)


def input_grad(upstream, matrix):
    return jnp.einsum("te,de->td", upstream, matrix, preferred_element_type=jnp.float32)


def body(
    n,
    m,
    hidden_in,
    memory,
    proj_in,
    proj_out,
    norm_gains,
    rel_bias,
    router,
    expert_choice,
    expert_in,
    expert_out,
    cotangent,
):
    tokens = hidden_in[0].astype(jnp.float32)
    memory_rows = memory[0]
    memory_count = memory_rows.shape[0]
    gain_rows = norm_gains.astype(jnp.float32)
    token_count = tokens.shape[0]
    seq_at = lax.axis_index("seq").astype(jnp.int32).reshape(1)
    normed_self = rms_apply(tokens, gain_rows[0]).astype(jnp.bfloat16)
    lines = bias_lines(rel_bias)

    normed_all, memory_all, queries, key_all, value_all, memory_key_all, memory_value_all = (
        gather_projected(normed_self, memory_rows, proj_in, n, 1)
    )
    to_next, to_last = quad_moves(n)
    in_own, out_own, normed_all = lax.optimization_barrier((expert_in, expert_out, normed_all))
    in_last, out_last = (lax.ppermute(w, "seq", to_next) for w in (in_own, out_own))
    in_next, out_next = (lax.ppermute(w, "seq", to_last) for w in (in_own, out_own))
    normed_all = normed_all.reshape(n * token_count, D)
    memory_all = memory_all.reshape(n * memory_count, D)
    key_all, value_all = (x.reshape(n * token_count, D) for x in (key_all, value_all))
    memory_key_all, memory_value_all = (
        x.reshape(n * memory_count, D) for x in (memory_key_all, memory_value_all)
    )
    attended_self_low, attended_self, lse_self = attend(
        seq_at, queries, key_all, value_all, lines
    )
    after_self = tokens + jnp.dot(
        attended_self_low, proj_out[0], preferred_element_type=jnp.float32
    )

    normed_cross = rms_apply(after_self, gain_rows[1]).astype(jnp.bfloat16)
    cross_queries = project(normed_cross, proj_in[3])
    attended_cross_low, attended_cross, lse_cross = attend(
        seq_at, cross_queries, memory_key_all, memory_value_all, None
    )
    after_cross = after_self + jnp.dot(
        attended_cross_low, proj_out[1], preferred_element_type=jnp.float32
    )

    mixed_low = rms_apply(after_cross, gain_rows[2]).astype(jnp.bfloat16)
    softmax_probs = jax.nn.softmax(
        jnp.dot(mixed_low, router, preferred_element_type=jnp.float32), axis=-1
    )
    expert_count = router.shape[1]
    local_experts = expert_in.shape[0]
    capacity = max(2, 5 * token_count // (4 * expert_count))
    chosen = expert_choice[0, :, 0]
    onehot_int = (chosen[:, None] == jnp.arange(expert_count, dtype=jnp.int32)[None, :]).astype(
        jnp.int32
    )
    onehot = onehot_int.astype(jnp.float32)
    gate_prob = jnp.sum(softmax_probs * onehot, axis=-1)
    slot_index = jnp.sum(jnp.cumsum(onehot_int, axis=0) * onehot_int, axis=-1) - 1
    is_kept = slot_index < capacity
    slots = -(-capacity // 16) * 16
    place = jnp.where(is_kept, chosen * slots + slot_index, -1)
    dispatch = (
        place[:, None] == jnp.arange(expert_count * slots, dtype=jnp.int32)[None, :]
    ).astype(jnp.bfloat16)
    dispatched = jnp.sum(onehot_int * is_kept[:, None].astype(jnp.int32), axis=0)
    tally_counts = jnp.stack(
        [dispatched, jnp.sum(onehot_int, axis=0) - dispatched], axis=0
    ).reshape(1, 1, 2, expert_count)

    grad_top = cotangent[0].astype(jnp.float32)
    scaled = (gate_prob[:, None] * grad_top).astype(jnp.bfloat16)
    sent_rows = (
        jnp.einsum(
            "tx,td->xd",
            dispatch,
            jnp.concatenate([mixed_low, scaled], axis=1),
            preferred_element_type=jnp.float32,
        )
        .astype(jnp.bfloat16)
        .reshape(m, local_experts * slots, 2 * D)
    )
    maps = [in_own, out_own, in_last, out_last, in_next, out_next]
    returned, *terms = run_experts(sent_rows, maps, n, m, slots, 2)
    returned = returned.reshape(expert_count * slots, 2 * D)
    gin_own, gout_own, gin_next, gout_last, gin_last, gout_next = terms
    gout_next = lax.ppermute(gout_next, "seq", to_next)
    gin_last = lax.ppermute(gin_last, "seq", to_last)
    routed = jnp.dot(dispatch, returned, preferred_element_type=jnp.float32)
    combined, grad_mixed = routed[:, :D], routed[:, D:]
    output = (after_cross + gate_prob[:, None] * combined).astype(jnp.bfloat16)

    grad_gate = jnp.sum(grad_top * combined, axis=-1)
    grad_logits = softmax_probs * (onehot - gate_prob[:, None]) * grad_gate[:, None]
    grad_router = jnp.einsum(
        "td,te->de", mixed_low.astype(jnp.float32), grad_logits, precision=highest
    )
    grad_mixed = grad_mixed + jnp.einsum(
        "te,de->td", grad_logits, router.astype(jnp.float32), precision=highest
    )
    grad_cross_part, grad_gain_mix = rms_backward(after_cross, gain_rows[2], grad_mixed)
    grad_after_cross = grad_top + grad_cross_part

    grad_cross_low = grad_after_cross.astype(jnp.bfloat16)
    grad_attended_cross = input_grad(grad_cross_low, proj_out[1]).astype(jnp.bfloat16)
    grad_cross_query, grad_memory_keys, grad_memory_values = attend_back(
        seq_at,
        cross_queries,
        memory_key_all,
        memory_value_all,
        grad_attended_cross,
        attended_cross,
        lse_cross,
        None,
    )
    grad_cross_query, gin_last, gout_next, gin_next, gout_last = lax.optimization_barrier(
        (grad_cross_query, gin_last, gout_next, gin_next, gout_last)
    )
    gin_next = lax.ppermute(gin_next, "seq", to_next)
    gout_last = lax.ppermute(gout_last, "seq", to_last)
    grad_self_part, grad_gain_cross = rms_backward(
        after_self, gain_rows[1], input_grad(grad_cross_query, proj_in[3])
    )
    grad_after_self = grad_after_cross + grad_self_part
    grad_memory_part, grads_cross = memory_back(
        memory_all, grad_memory_keys, grad_memory_values, proj_in
    )

    grad_self_low = grad_after_self.astype(jnp.bfloat16)
    grad_attended_self = input_grad(grad_self_low, proj_out[0]).astype(jnp.bfloat16)
    grad_self_query, grad_keys, grad_values, near, sums = attend_back(
        seq_at,
        queries,
        key_all,
        value_all,
        grad_attended_self,
        attended_self,
        lse_self,
        lines,
    )
    grad_self_query, grad_keys, grad_values, near, sums, gout_last, gin_next = (
        lax.optimization_barrier(
            (grad_self_query, grad_keys, grad_values, near, sums, gout_last, gin_next)
        )
    )
    grad_table = bias_gradient(near, sums)
    (
        grad_normed_part,
        grads,
        grad_gain_part,
        grad_normed_query,
        grad_expert_in,
        grad_expert_out,
    ) = token_back(
        normed_all,
        grad_keys,
        grad_values,
        normed_self,
        grad_self_query,
        proj_in,
        [gin_own, gin_last, gin_next, gout_own, gout_last, gout_next],
        [
            normed_cross,
            grad_cross_query,
            attended_self_low,
            grad_self_low,
            attended_cross_low,
            grad_cross_low,
        ],
        grads_cross,
    )
    grad_gain_self = grad_gain_part[0] / gain_rows[0]

    grad_gains = jnp.stack([grad_gain_self, grad_gain_cross, grad_gain_mix])
    lines = jnp.concatenate(
        [grad_router.T, grad_gains, jnp.zeros((8 - grad_gains.shape[0], D), jnp.float32)]
    )
    small = [lines[:, i * TILE : (i + 1) * TILE] for i in range(D // TILE)]
    small.append(jnp.pad(grad_table, ((0, 0), (0, TILE - HEADS))))
    (grad_normed_own, grad_memory), grads, small = finish(
        [
            grad_normed_part.reshape(n, token_count, D),
            grad_memory_part.reshape(n, memory_count, D),
        ],
        grads.reshape(-1, D),
        jnp.concatenate(small),
        n,
        m,
        4,
    )
    wide = present(grads.reshape(8, D, D), small, expert_count)
    grad_token_part, _ = rms_backward(tokens, gain_rows[0], grad_normed_query + grad_normed_own)
    grad_in = (grad_after_self + grad_token_part).astype(jnp.bfloat16)
    return (
        output.reshape(1, token_count, D),
        grad_in.reshape(1, token_count, D),
        grad_memory.astype(jnp.bfloat16).reshape(1, memory_count, D),
        *wide,
        grad_expert_in,
        grad_expert_out,
        tally_counts,
    )


def solution(mesh):
    rows = P("exp", "seq", None)
    hidden = P("exp", None, "seq")
    return jax.shard_map(
        functools.partial(body, mesh.shape["seq"], mesh.shape["exp"]),
        mesh=mesh,
        in_specs=(rows, rows, P(), P(), P(), P(), P(), rows, hidden, hidden, rows),
        out_specs=(
            rows,
            rows,
            rows,
            P(),
            P(),
            P(),
            P(),
            P(),
            hidden,
            hidden,
            P("exp", "seq", None, None),
        ),
        check_vma=False,
    )
```

```python
import functools
import math

import jax
import jax.numpy as jnp
from jax import lax
from jax.experimental import pallas as pl
from jax.experimental.pallas import tpu as pltpu
from jax.sharding import PartitionSpec as P

D = 768
HEADS = 12
HEAD_DIM = 64
NBUCKET = 32
MAXDIST = 128
TILE = 128
PAIRS = HEADS * HEAD_DIM // TILE

MESH = pl.DeviceIdType.MESH
ANY = pl.BlockSpec(memory_space=pl.ANY)
SMEM = pl.BlockSpec(memory_space=pltpu.SMEM)

norm_eps = 1e-06
masked_score = -1e30
highest = lax.Precision.HIGHEST
log2e = 1.0 / math.log(2.0)
scale_factor = HEAD_DIM ** (-0.5)


def bucket_edges():
    half_count = NBUCKET // 2
    thresholds = []
    for bucket_number in range(1, NBUCKET):
        if bucket_number < half_count:
            thresholds.append(bucket_number)
        else:
            thresholds.append(
                int(
                    half_count
                    * (MAXDIST / half_count) ** ((bucket_number - half_count) / half_count)
                )
            )
    return thresholds


def rms_apply(values, gain_row):
    return (
        values * lax.rsqrt(jnp.mean(values * values, axis=-1, keepdims=True) + norm_eps) * gain_row
    )


def rms_backward(values, gain_row, upstream):
    _, pullback = jax.vjp(rms_apply, values, gain_row)
    return pullback(upstream)


def cost(us):
    return pl.CostEstimate(flops=us * 10**9, bytes_accessed=0, transcendentals=0)


def seq_cycle(n):
    cols = n // 4
    if n % 4 or cols < 2:
        return list(range(n))
    order = [0]
    for row in range(4):
        span = range(1, cols) if row % 2 == 0 else range(cols - 1, 0, -1)
        order += [row * cols + col for col in span]
    return order + [3 * cols, 2 * cols, cols]


def look_up(index, table):
    value = jnp.int32(table[0])
    for number, entry in enumerate(table[1:], 1):
        value = jnp.where(index == number, jnp.int32(entry), value)
    return value


def greet(others):
    barrier = pltpu.get_barrier_semaphore()
    for other in others:
        pl.semaphore_signal(barrier, inc=1, device_id=other, device_id_type=MESH)
    pl.semaphore_wait(barrier, len(others))


def seq_ring(n):
    order = seq_cycle(n)
    pos = look_up(lax.axis_index("seq"), [order.index(i) for i in range(n)])

    def at(place):
        return look_up(lax.rem(place + 4 * n, n), order)

    return pos, at, ({"seq": at(pos + 1)}, {"seq": at(pos - 1)})


def gather_kernel(n, parts, *refs):
    sources, proj_ref, outs = refs[:2], refs[2], refs[3:10]
    lands, w_buf, bufs = refs[10:12], refs[12], refs[13:18]
    own_sem, w_sem, send_sem, recv_sem, store_sem = refs[18:]
    pos, at, sides = seq_ring(n)
    me = at(pos)
    greet(sides)
    own = [pltpu.make_async_copy(sources[a], lands[a].at[me], own_sem.at[a]) for a in range(2)]
    weights = [
        pltpu.make_async_copy(proj_ref.at[number], w_buf.at[i], w_sem.at[i])
        for i, number in enumerate((0, 1, 2, 4, 5))
    ]
    started, latest, stored = [], {}, []

    def pass_on(step):
        for part in range(parts):
            for a in range(2):
                rows = sources[a].shape[0] // 2 // parts
                for way in range(2):
                    if step:
                        latest[a, way, part].wait_recv()
                    if step == n - 1:
                        continue
                    block = at(pos - step) if way == 0 else at(pos + step)
                    span = pl.ds((way * parts + part) * rows, rows)
                    copy = pltpu.make_async_remote_copy(
                        src_ref=lands[a].at[block, span] if step else sources[a].at[span],
                        dst_ref=lands[a].at[block, span],
                        send_sem=send_sem.at[a, way, step, part],
                        recv_sem=recv_sem.at[a, way, step, part],
                        device_id=sides[way],
                        device_id_type=MESH,
                    )
                    copy.start()
                    started.append(copy)
                    latest[a, way, part] = copy

    def store(source, target, number, step, way):
        copy = pltpu.make_async_copy(source, target, store_sem.at[number, step, way])
        copy.start()
        stored.append(copy)

    def work(step):
        blocks = (at(pos - step), at(pos + step))
        for a in range(2):
            half = sources[a].shape[0] // 2
            spans = (pl.ds(0, half), pl.ds(half, half))
            rows = jnp.concatenate([lands[a][blocks[way], spans[way], :] for way in range(2)], axis=0)
            for i in range(2):
                buf = bufs[1 + 2 * a + i]
                made = dot_plain(rows, w_buf[1 + 2 * a + i]).astype(buf.dtype)
                for way in range(2):
                    buf[blocks[way], spans[way], :] = made[way * half : (way + 1) * half]
            for way in range(2):
                where = (blocks[way], spans[way])
                store(lands[a].at[where], outs[a].at[where], a, step, way)
                for i in range(2):
                    number = 1 + 2 * a + i
                    store(bufs[number].at[where], outs[2 + number].at[where], 2 + number, step, way)

    pass_on(0)
    for copy in own + weights:
        copy.start()
    for copy in own + weights:
        copy.wait()
    bufs[0][...] = dot_plain(lands[0][me], w_buf[0]).astype(bufs[0].dtype)
    store(bufs[0], outs[2], 2, 0, 0)
    work(0)
    for step in range(1, n):
        pass_on(step)
        work(step)
    for copy in started:
        copy.wait_send()
    for copy in stored:
        copy.wait()


def gather_projected(tokens, memory_rows, proj_in, n, number, parts=2):
    both = (tokens, memory_rows)
    copies = (2, 2, n - 1, parts)
    wide = [(n,) + x.shape for x in both]
    shapes = wide + [tokens.shape] + [wide[0]] * 2 + [wide[1]] * 2
    dma = pltpu.SemaphoreType.DMA
    return pl.pallas_call(
        functools.partial(gather_kernel, n, parts),
        out_shape=[jax.ShapeDtypeStruct(shape, tokens.dtype) for shape in shapes],
        in_specs=[ANY] * 3,
        out_specs=[ANY] * 7,
        scratch_shapes=[pltpu.VMEM(shape, tokens.dtype) for shape in wide]
        + [pltpu.VMEM((5,) + proj_in.shape[1:], tokens.dtype)]
        + [pltpu.VMEM(shape, tokens.dtype) for shape in shapes[2:]]
        + [dma((2,)), dma((5,)), dma(copies), dma(copies), dma((7, n, 2))],
        compiler_params=pltpu.CompilerParams(
            collective_id=number, has_side_effects=True, vmem_limit_bytes=58 << 20
        ),
        cost_estimate=cost(60),
        name="gather_projected",
    )(tokens, memory_rows, proj_in)


def scatter_kernel(n, parts, count, *refs):
    sources, outs = refs[:count], refs[count : 2 * count]
    own_bufs, got_bufs = refs[2 * count : 3 * count], refs[3 * count : 4 * count]
    own_sem, send_sem, recv_sem = refs[4 * count :]
    pos, at, sides = seq_ring(n)
    greet(sides)
    lanes = [(a, part, way) for a in range(count) for part in range(parts) for way in range(2)]

    def span(a, part, way):
        rows = sources[a].shape[1] // 2 // parts
        return pl.ds((way * parts + part) * rows, rows)

    def block(way, step):
        return at(pos - 1 - step) if way == 0 else at(pos + 1 + step)

    def send(lane, step, source):
        a, part, way = lane
        copy = pltpu.make_async_remote_copy(
            src_ref=source,
            dst_ref=got_bufs[a].at[way, step, part],
            send_sem=send_sem.at[a, way, step, part],
            recv_sem=recv_sem.at[a, way, step, part],
            device_id=sides[way],
            device_id_type=MESH,
        )
        copy.start()
        return copy

    latest, started, own = {}, [], {}
    for lane in lanes:
        a, part, way = lane
        latest[lane] = send(lane, 0, sources[a].at[block(way, 0), span(a, part, way)])
        started.append(latest[lane])
    for step in range(1, n):
        for lane in lanes:
            a, part, way = lane
            own[lane, step] = pltpu.make_async_copy(
                sources[a].at[block(way, step), span(a, part, way)],
                own_bufs[a].at[way, step - 1, part],
                own_sem.at[a, way, step - 1, part],
            )
            own[lane, step].start()
    for step in range(1, n):
        for lane in lanes:
            a, part, way = lane
            own[lane, step].wait()
            latest[lane].wait_recv()
            total = got_bufs[a][way, step - 1, part].astype(jnp.float32) + own_bufs[a][
                way, step - 1, part
            ].astype(jnp.float32)
            if step == n - 1:
                outs[a][span(a, part, way)] = total.astype(outs[a].dtype)
            else:
                got_bufs[a][way, step - 1, part] = total.astype(got_bufs[a].dtype)
                latest[lane] = send(lane, step, got_bufs[a].at[way, step - 1, part])
                started.append(latest[lane])
    for copy in started:
        copy.wait_send()


def ring_scatter(arrays, n, number, out_dtype, parts=2):
    count = len(arrays)
    copies = (count, 2, n - 1, parts)
    bufs = [
        pltpu.VMEM((2, n - 1, parts, a.shape[1] // 2 // parts, a.shape[2]), a.dtype)
        for a in arrays
    ]
    return pl.pallas_call(
        functools.partial(scatter_kernel, n, parts, count),
        out_shape=[jax.ShapeDtypeStruct(a.shape[1:], out_dtype) for a in arrays],
        in_specs=[ANY] * count,
        out_specs=[pl.BlockSpec(memory_space=pltpu.VMEM)] * count,
        scratch_shapes=bufs + bufs + [pltpu.SemaphoreType.DMA(copies)] * 3,
        compiler_params=pltpu.CompilerParams(
            collective_id=number, has_side_effects=True, vmem_limit_bytes=58 << 20
        ),
        name="ring_scatter",
    )(*arrays)


def finish_kernel(n, counts, *refs):
    few, many = counts
    refs = list(refs)
    take = lambda count: [refs.pop(0) for _ in range(count)]
    blocks, xs, sums, outs = take(few), take(many), take(few), take(many)
    own_bufs, got_bufs = take(few), take(few)
    mines, twins, crosses, gots = take(many), take(many), take(many), take(many)
    near_sem, far_sem, own_sem, pair_sem, cross_sem, ring_sem = refs
    pos, at, sides = seq_ring(n)
    exp = lax.axis_index("exp")
    core, chip = lax.rem(exp, 2), exp // 2
    peer, over = {"exp": exp + 1 - 2 * core}, {"exp": core + 2 * (1 - chip)}
    greet(sides + (peer, over))
    started = []

    def push(source, target, sems, index, to):
        copy = pltpu.make_async_remote_copy(
            src_ref=source,
            dst_ref=target,
            send_sem=sems.at[(0,) + index],
            recv_sem=sems.at[(1,) + index],
            device_id=to,
            device_id_type=MESH,
        )
        copy.start()
        started.append(copy)
        return copy

    def block(way, step):
        return at(pos - 1 - step) if way == 0 else at(pos + 1 + step)

    def fetch(source, target, sem):
        copy = pltpu.make_async_copy(source, target, sem)
        copy.start()
        return copy

    add = lambda *terms: functools.reduce(lambda u, v: u + v, [t.astype(jnp.float32) for t in terms])
    ways = range(2)
    lanes = [(a, way) for a in range(many) for way in ways]
    parts = 2
    rings = [(a, way, part) for part in range(parts) for a in range(few) for way in ways]

    def span(ref, way):
        half = ref.shape[-2] // 2
        return pl.ds(way * half, half)

    def piece(lane):
        a, way, part = lane
        rows = blocks[a].shape[-2] // 2 // parts
        return pl.ds(way * parts * rows + part * rows, rows), pl.ds(part * rows, rows)

    pairs, own, crossing, ring = {}, {}, {}, {}
    for lane in rings:
        a, way, part = lane
        wide, thin = piece(lane)
        ring[lane] = push(
            blocks[a].at[block(way, 0), wide],
            got_bufs[a].at[way, 0, thin],
            far_sem,
            lane + (0,),
            sides[way],
        )
    for side in range(2):
        for step in range(n):
            for lane in lanes:
                a, way = lane
                place = chip if side else 1 - chip
                where, rows = block(way, step), span(xs[a], way)
                pairs[side, lane, step] = push(
                    xs[a].at[1 - core, place, where, rows],
                    twins[a].at[side, way, step],
                    pair_sem,
                    (0, side) + lane + (step,),
                    peer,
                )
                own[side, lane, step] = fetch(
                    xs[a].at[core, place, where, rows],
                    mines[a].at[side, way, step],
                    own_sem.at[(side,) + lane + (step,)],
                )
        if side == 0:
            near = {}
            for step in range(1, n):
                for lane in rings:
                    a, way, part = lane
                    wide, thin = piece(lane)
                    near[lane, step] = fetch(
                        blocks[a].at[block(way, step), wide],
                        own_bufs[a].at[way, step - 1, thin],
                        near_sem.at[lane + (step - 1,)],
                    )

    def scatter(step, which):
        for lane in rings:
            a, way, part = lane
            if part != which:
                continue
            wide, thin = piece(lane)
            near[lane, step].wait()
            ring[lane].wait_recv()
            total = add(got_bufs[a][way, step - 1, thin], own_bufs[a][way, step - 1, thin])
            if step == n - 1:
                sums[a][wide] = total.astype(sums[a].dtype)
            else:
                got_bufs[a][way, step - 1, thin] = total.astype(got_bufs[a].dtype)
                ring[lane] = push(
                    got_bufs[a].at[way, step - 1, thin],
                    got_bufs[a].at[way, step, thin],
                    far_sem,
                    lane + (step,),
                    sides[way],
                )

    for step in range(n):
        for lane in lanes:
            a, way = lane
            own[0, lane, step].wait()
            pairs[0, lane, step].wait_recv()
            mines[a][0, way, step] = add(mines[a][0, way, step], twins[a][0, way, step]).astype(
                mines[a].dtype
            )
            crossing[lane, step] = push(
                mines[a].at[0, way, step],
                crosses[a].at[way, step],
                cross_sem,
                (0,) + lane + (step,),
                over,
            )
    latest = {}
    waiting = [(step, part) for step in range(1, n) for part in range(parts)]
    for step in range(n):
        for lane in lanes:
            a, way = lane
            own[1, lane, step].wait()
            pairs[1, lane, step].wait_recv()
            crossing[lane, step].wait_recv()
            terms = [mines[a][1, way, step], twins[a][1, way, step], crosses[a][way, step]]
            if step:
                latest[lane].wait_recv()
                terms.append(gots[a][way, step - 1])
            mines[a][1, way, step] = add(*terms).astype(mines[a].dtype)
            if step < n - 1:
                latest[lane] = push(
                    mines[a].at[1, way, step],
                    gots[a].at[way, step],
                    ring_sem,
                    (0,) + lane + (step,),
                    sides[way],
                )
        if waiting:
            scatter(*waiting.pop(0))
    keep, done = [], []
    latest, crossing = {}, {}

    def target_of(lane, step, place):
        a, way = lane
        where = at(pos - step) if way == 0 else at(pos + step)
        return outs[a].at[core, place, where, span(outs[a], way)]

    def hand_on(step):
        for lane in lanes:
            crossing[lane, step].wait_recv()
            target = target_of(lane, step, 1 - chip)
            done.append(push(target, target, pair_sem, (1, 1) + lane + (step,), peer))

    for step in range(n):
        for lane in lanes:
            a, way = lane
            if step:
                latest[lane].wait_recv()
            target = target_of(lane, step, chip)
            source = target if step else mines[a].at[1, way, n - 1]
            if step < n - 1:
                latest[lane] = push(source, target, ring_sem, (1,) + lane + (step,), sides[way])
            crossing[lane, step] = push(source, target, cross_sem, (1,) + lane + (step,), over)
            done.append(push(source, target, pair_sem, (1, 0) + lane + (step,), peer))
            if step == 0:
                keep.append(fetch(source, target, own_sem.at[(0,) + lane + (0,)]))
        if waiting:
            scatter(*waiting.pop(0))
        if step:
            hand_on(step - 1)
    hand_on(n - 1)
    while waiting:
        scatter(*waiting.pop(0))
    for copy in keep:
        copy.wait()
    for copy in done:
        copy.wait_recv()
    for copy in started:
        copy.wait_send()


def finish(blocks, rows_in, small, n, m, number):
    rows, cols = rows_in.shape
    each = rows // (4 * n)
    if m != 4 or rows % (4 * n * 32) or small.shape[0] > 4 * n * 16:
        return (
            ring_scatter(blocks, n, number, jnp.float32),
            *lax.psum((rows_in, small), ("seq", "exp")),
        )
    padded = jnp.pad(small, ((0, 4 * n * 16 - small.shape[0]), (0, 0)))
    arrays = [rows_in.reshape(2, 2, n, each, cols), padded.reshape(2, 2, n, 16, TILE)]
    few, many = len(blocks), len(arrays)
    halves = [(x.shape[-2] // 2, x.shape[-1], x.dtype) for x in blocks + arrays]
    ring_bufs = [pltpu.VMEM((2, n - 1, r, c), t) for r, c, t in halves[:few]]
    two = [pltpu.VMEM((2, 2, n, r, c), t) for r, c, t in halves[few:]]
    one = [pltpu.VMEM((2, n, r, c), t) for r, c, t in halves[few:]]
    dma = pltpu.SemaphoreType.DMA
    results = pl.pallas_call(
        functools.partial(finish_kernel, n, (few, many)),
        out_shape=[jax.ShapeDtypeStruct(x.shape[1:], jnp.float32) for x in blocks]
        + [jax.ShapeDtypeStruct(x.shape, x.dtype) for x in arrays],
        in_specs=[ANY] * (few + many),
        out_specs=[pl.BlockSpec(memory_space=pltpu.VMEM)] * few + [ANY] * many,
        scratch_shapes=ring_bufs * 2
        + two * 2
        + one * 2
        + [
            dma((few, 2, 2, n)),
            dma((2, few, 2, 2, n)),
            dma((2, many, 2, n)),
            dma((2, 2, 2, many, 2, n)),
            dma((2, 2, many, 2, n)),
            dma((2, 2, many, 2, n)),
        ],
        compiler_params=pltpu.CompilerParams(
            collective_id=number, has_side_effects=True, vmem_limit_bytes=58 << 20
        ),
        cost_estimate=cost(120),
        name="finish",
    )(*blocks, *arrays)
    return results[:few], results[few].reshape(rows, cols), results[-1].reshape(-1, TILE)


def dot_last(a, b):
    return lax.dot_general(a, b, (((1,), (1,)), ((), ())), preferred_element_type=jnp.float32)


def dot_first(a, b):
    return lax.dot_general(a, b, (((0,), (0,)), ((), ())), preferred_element_type=jnp.float32)


def dot_plain(a, b):
    return jnp.dot(a, b, preferred_element_type=jnp.float32)


def head_masks(dtype):
    low = lax.broadcasted_iota(jnp.int32, (1, TILE), 1) < HEAD_DIM
    first = jnp.where(low, 1.0, 0.0).astype(jnp.float32)
    return first.astype(dtype), (1.0 - first).astype(dtype)


def split_heads(pair):
    return jnp.concatenate([pair * mask for mask in head_masks(pair.dtype)], axis=0)


def own_bias(tiles, count):
    rows = []
    for r in range(count):
        row = []
        for c in range(count):
            if c == r:
                row.append(tiles[:, TILE:])
            elif c == r - 1:
                row.append(tiles[:, :TILE])
            else:
                row.append(jnp.full((TILE, TILE), 0.0 if c < r else masked_score, jnp.float32))
        rows.append(jnp.concatenate(row, axis=1))
    return jnp.concatenate(rows, axis=0)


def edge_bias(tiles, rows):
    edge = []
    for h in range(2):
        first = jnp.concatenate(
            [jnp.zeros((rows - TILE, TILE), jnp.float32), tiles[h][:, :TILE].T], axis=0
        )
        edge += [first, jnp.zeros((rows, rows - TILE), jnp.float32)]
    return jnp.concatenate(edge, axis=1)


def each_far(s, block, act, times=3):
    far = jnp.maximum(s - 1, 0)
    bundles = far // times

    def bundle(j, carry):
        act(pl.multiple_of(j * times * block, block), times)
        return carry

    def single(j, carry):
        act(pl.multiple_of(j * block, block), 1)
        return carry

    lax.fori_loop(0, bundles, bundle, 0)
    lax.fori_loop(bundles * times, far, single, 0)


def attend_kernel(causal, block, s_ref, q_ref, k_ref, v_ref, *refs):
    if causal:
        line_ref, low_ref, wide_ref, lse_ref, acc_ref, top_ref = refs
    else:
        low_ref, wide_ref, lse_ref, acc_ref, top_ref = refs
    rows = q_ref.shape[0]
    both = split_heads(q_ref[...])

    def visit(start, bias, first, times=1):
        ones = jnp.ones((16, times * block), v_ref.dtype)
        keys = k_ref[pl.ds(start, times * block), :]
        values = v_ref[pl.ds(start, times * block), :]
        t = dot_last(keys, both) * (scale_factor * log2e)
        if bias is not None:
            t = t + bias
        top = jnp.max(t, axis=0, keepdims=True)
        if not first:
            before = top_ref[...]
            top = jnp.maximum(before, top)
            fade = jnp.exp2(before - top)
        top_ref[...] = top
        p = jnp.exp2(t - top).astype(values.dtype)
        part = dot_plain(jnp.concatenate([values.T, ones], axis=0), p)
        if first:
            acc_ref[...] = part
        else:
            acc_ref[...] = acc_ref[...] * fade + part

    if causal:
        s = s_ref[0]
        count = rows // TILE
        tiles = [bias_tile(line_ref, h) for h in range(2)]
        visit(
            pl.multiple_of(s * block, block),
            jnp.concatenate([own_bias(tiles[h], count).T for h in range(2)], axis=1),
            True,
        )

        @pl.when(s > 0)
        def _():
            visit(pl.multiple_of((s - 1) * block, block), edge_bias(tiles, rows), False)

        each_far(s, block, lambda start, times: visit(start, None, False, times))
    else:
        for j in range(k_ref.shape[0] // block):
            visit(j * block, None, j == 0)
    sums = acc_ref[TILE : TILE + 1, :]
    wide = jnp.concatenate(
        [
            acc_ref[:HEAD_DIM, :rows] / sums[:, :rows],
            acc_ref[HEAD_DIM:TILE, rows:] / sums[:, rows:],
        ],
        axis=0,
    ).T
    wide_ref[...] = wide
    low_ref[...] = wide.astype(low_ref.dtype)
    lse = top_ref[...] + jnp.log2(sums)
    lse_ref[0] = jnp.concatenate([lse[:, :rows], lse[:, rows:]], axis=0)


def attend(seq_at, queries, keys, values, lines):
    rows, total = queries.shape[0], keys.shape[0]
    causal = lines is not None
    block = rows if causal else math.gcd(total, 1024)
    pair = pl.BlockSpec((rows, TILE), lambda g: (0, g))
    long = pl.BlockSpec((total, TILE), lambda g: (0, g))
    extra, specs = [], []
    if causal:
        extra, specs = [lines], [pl.BlockSpec((1,) + lines.shape[1:], lambda g: (g, 0, 0))]
    return pl.pallas_call(
        functools.partial(attend_kernel, causal, block),
        grid=(PAIRS,),
        out_shape=[
            jax.ShapeDtypeStruct((rows, D), jnp.bfloat16),
            jax.ShapeDtypeStruct((rows, D), jnp.float32),
            jax.ShapeDtypeStruct((PAIRS, 2, rows), jnp.float32),
        ],
        in_specs=[SMEM, pair, long, long] + specs,
        out_specs=[pair, pair, pl.BlockSpec((1, 2, rows), lambda g: (g, 0, 0))],
        scratch_shapes=[
            pltpu.VMEM((TILE + 16, 2 * rows), jnp.float32),
            pltpu.VMEM((1, 2 * rows), jnp.float32),
        ],
        compiler_params=pltpu.CompilerParams(vmem_limit_bytes=48 << 20),
        cost_estimate=cost(40 if causal else 10),
        name="attend_self" if causal else "attend_cross",
    )(seq_at, queries, keys, values, *extra)


def attend_back_kernel(causal, block, s_ref, q_ref, k_ref, v_ref, up_ref, wide_ref, lse_ref, *refs):
    if causal:
        line_ref, dq_ref, dk_ref, dv_ref, bias_ref, sum_ref, acc_ref, near_ref = refs
    else:
        dq_ref, dk_ref, dv_ref, acc_ref = refs
    rows = q_ref.shape[0]
    both = split_heads(q_ref[...])
    up = up_ref[...]
    up_both = split_heads(up)
    turned = (up.astype(jnp.float32) * wide_ref[...]).T
    delta = jnp.concatenate(
        [
            jnp.sum(turned[:HEAD_DIM], axis=0, keepdims=True),
            jnp.sum(turned[HEAD_DIM:], axis=0, keepdims=True),
        ],
        axis=1,
    )
    lse = jnp.concatenate([lse_ref[0, :1], lse_ref[0, 1:]], axis=1)

    def visit(start, bias, first, times=1):
        ones = jnp.ones((16, times * block), k_ref.dtype)
        keys = k_ref[pl.ds(start, times * block), :]
        values = v_ref[pl.ds(start, times * block), :]
        t = dot_last(keys, both) * (scale_factor * log2e)
        if bias is not None:
            t = t + bias
        p = jnp.exp2(t - lse)
        ds = (p * (dot_last(values, up_both) - delta)).astype(keys.dtype)
        dv_ref[pl.ds(start, times * block), :] = dot_plain(p.astype(keys.dtype), up_both).astype(
            dv_ref.dtype
        )
        dk_ref[pl.ds(start, times * block), :] = (dot_plain(ds, both) * scale_factor).astype(dk_ref.dtype)
        part = dot_plain(jnp.concatenate([keys.T, ones], axis=0), ds)
        if first:
            acc_ref[...] = part
        else:
            acc_ref[...] += part
        return ds

    if causal:
        s = s_ref[0]
        count = rows // TILE
        tiles = [bias_tile(line_ref, h) for h in range(2)]
        ds = visit(
            pl.multiple_of(s * block, block),
            jnp.concatenate([own_bias(tiles[h], count).T for h in range(2)], axis=1),
            True,
        )
        for h in range(2):
            same = before = jnp.zeros((TILE, TILE), jnp.float32)
            for r in range(count):
                columns = slice(h * rows + r * TILE, h * rows + (r + 1) * TILE)
                same = same + ds[r * TILE : (r + 1) * TILE, columns].astype(jnp.float32)
                if r:
                    before = before + ds[(r - 1) * TILE : r * TILE, columns].astype(jnp.float32)
            near_ref[h, :TILE] = before
            near_ref[h, TILE:] = same

        @pl.when(s > 0)
        def _():
            ds = visit(pl.multiple_of((s - 1) * block, block), edge_bias(tiles, rows), False)
            for h in range(2):
                near_ref[h, :TILE] += ds[rows - TILE :, h * rows : h * rows + TILE].astype(
                    jnp.float32
                )

        each_far(s, block, lambda start, times: visit(start, None, False, times))

        def beyond(j, carry):
            start = pl.multiple_of(j * block, block)
            dk_ref[pl.ds(start, block), :] = jnp.zeros((block, TILE), dk_ref.dtype)
            dv_ref[pl.ds(start, block), :] = jnp.zeros((block, TILE), dv_ref.dtype)
            return carry

        lax.fori_loop(s + 1, k_ref.shape[0] // block, beyond, 0)
        turn = (
            lax.broadcasted_iota(jnp.int32, (TILE, TILE), 0)
            + lax.broadcasted_iota(jnp.int32, (TILE, TILE), 1)
            == TILE - 1
        ).astype(jnp.float32)
        diagonals = []
        for h in range(2):
            near = jnp.dot(turn, near_ref[h].T, precision=highest, preferred_element_type=jnp.float32)
            near = jnp.concatenate([near, jnp.zeros((TILE, TILE), jnp.float32)], axis=1)
            near = pltpu.roll(near, 0, 1, stride=1, stride_axis=0)
            diagonals.append(jnp.sum(near, axis=0, keepdims=True))
        bias_ref[0] = jnp.concatenate(diagonals, axis=0)
        sum_ref[0] = jnp.concatenate(
            [acc_ref[TILE : TILE + 1, :rows], acc_ref[TILE : TILE + 1, rows:]], axis=0
        )
    else:
        for j in range(k_ref.shape[0] // block):
            visit(j * block, None, j == 0)
    dq = jnp.concatenate([acc_ref[:HEAD_DIM, :rows], acc_ref[HEAD_DIM:TILE, rows:]], axis=0)
    dq_ref[...] = (dq.T * scale_factor).astype(dq_ref.dtype)


def attend_back(seq_at, queries, keys, values, upstream, wide, lse, lines):
    rows, total = queries.shape[0], keys.shape[0]
    causal = lines is not None
    block = rows if causal else math.gcd(total, 1024)
    pair = pl.BlockSpec((rows, TILE), lambda g: (0, g))
    long = pl.BlockSpec((total, TILE), lambda g: (0, g))
    line = pl.BlockSpec((1, 2, rows), lambda g: (g, 0, 0))
    extra, specs, shapes, out_specs, scratch = [], [], [], [], []
    if causal:
        extra, specs = [lines], [pl.BlockSpec((1,) + lines.shape[1:], lambda g: (g, 0, 0))]
        shapes = [
            jax.ShapeDtypeStruct((PAIRS, 2, 3 * TILE), jnp.float32),
            jax.ShapeDtypeStruct((PAIRS, 2, rows), jnp.float32),
        ]
        out_specs = [pl.BlockSpec((1, 2, 3 * TILE), lambda g: (g, 0, 0)), line]
        scratch = [pltpu.VMEM((2, 2 * TILE, TILE), jnp.float32)]
    return pl.pallas_call(
        functools.partial(attend_back_kernel, causal, block),
        grid=(PAIRS,),
        out_shape=[
            jax.ShapeDtypeStruct((rows, D), jnp.bfloat16),
            jax.ShapeDtypeStruct((total, D), jnp.bfloat16),
            jax.ShapeDtypeStruct((total, D), jnp.bfloat16),
        ]
        + shapes,
        in_specs=[SMEM, pair, long, long, pair, pair, line] + specs,
        out_specs=[pair, long, long] + out_specs,
        scratch_shapes=[pltpu.VMEM((TILE + 16, 2 * rows), jnp.float32)] + scratch,
        compiler_params=pltpu.CompilerParams(vmem_limit_bytes=48 << 20),
        cost_estimate=cost(48 if causal else 15),
        name="attend_self_back" if causal else "attend_cross_back",
    )(seq_at, queries, keys, values, upstream, wide, lse, *extra)


def key_value_back(x_ref, dk_ref, dv_ref, wk_ref, wv_ref, dx_ref):
    x, both = x_ref[...], jnp.concatenate([dk_ref[...], dv_ref[...]], axis=1)
    dx = dot_last(both, jnp.concatenate([wk_ref[0], wv_ref[0]], axis=1))
    dx_ref[...] = dx.astype(dx_ref.dtype)
    gain = jnp.sum(dx * x.astype(jnp.float32), axis=0, keepdims=True)
    return gain, dot_first(x, both)


def add_up(step, last, made, total, outs):
    @pl.when(step == 0)
    def _():
        total[...] = made

    @pl.when(step > 0)
    def _():
        total[...] += made

    @pl.when(step == last)
    def _():
        for i, out in enumerate(outs):
            out[...] = total[:, i * D : (i + 1) * D].astype(out.dtype)


def memory_back_kernel(x_ref, dk_ref, dv_ref, wk_ref, wv_ref, dx_ref, grad_ref, acc_ref):
    _, made = key_value_back(x_ref, dk_ref, dv_ref, wk_ref, wv_ref, dx_ref)
    outs = [grad_ref.at[0], grad_ref.at[1]]
    add_up(pl.program_id(0), pl.num_programs(0) - 1, made, acc_ref, outs)


def token_back_kernel(*refs):
    x_ref, dk_ref, dv_ref, wk_ref, wv_ref, own_ref, dq_ref, wq_ref = refs[:8]
    terms, others, cross_ref = refs[8:14], refs[14:20], refs[20]
    (dx_ref, grad_ref, gain_ref, query_ref), sums = refs[21:25], refs[25:27]
    acc_ref = refs[27]
    step, last = pl.program_id(0), pl.num_programs(0) - 1
    for i, out in enumerate(sums):
        first, *rest = terms[3 * i : 3 * i + 3]
        total = first[...]
        for term in rest:
            total = total + term[...].astype(jnp.float32)
        out[...] = total
    gain, made = key_value_back(x_ref, dk_ref, dv_ref, wk_ref, wv_ref, dx_ref)
    add_up(step, last, made, acc_ref, [grad_ref.at[1], grad_ref.at[2]])

    @pl.when(step == 0)
    def _():
        own, dq = own_ref[...], dq_ref[...]
        back = dot_last(dq, wq_ref[0])
        query_ref[...] = back
        gain_ref[...] = gain + jnp.sum(back * own.astype(jnp.float32), axis=0, keepdims=True)
        grad_ref[0] = dot_first(own, dq).astype(grad_ref.dtype)
        grad_ref[4:6] = cross_ref[...]

    @pl.when(step > 0)
    def _():
        gain_ref[...] += gain

    for i, number in enumerate((3, 6, 7)):

        @pl.when(step == jnp.minimum(i + 1, last))
        def _(i=i, number=number):
            product = dot_first(others[2 * i][...], others[2 * i + 1][...])
            grad_ref[number] = product.astype(grad_ref.dtype)


def memory_back(tokens, grad_keys, grad_values, proj_in):
    total = tokens.shape[0]
    rows = math.gcd(total, 512)
    block = pl.BlockSpec((rows, D), lambda i: (i, 0))
    weight = lambda number: pl.BlockSpec((1, D, D), lambda i: (number, 0, 0))
    return pl.pallas_call(
        memory_back_kernel,
        grid=(total // rows,),
        out_shape=[
            jax.ShapeDtypeStruct(tokens.shape, tokens.dtype),
            jax.ShapeDtypeStruct((2, D, D), tokens.dtype),
        ],
        in_specs=[block] * 3 + [weight(4), weight(5)],
        out_specs=[block, pl.BlockSpec((2, D, D), lambda i: (0, 0, 0))],
        scratch_shapes=[pltpu.VMEM((D, 2 * D), jnp.float32)],
        compiler_params=pltpu.CompilerParams(vmem_limit_bytes=48 << 20),
        cost_estimate=cost(8),
        name="memory_back",
    )(tokens, grad_keys, grad_values, proj_in, proj_in)


def token_back(tokens, grad_keys, grad_values, own, grad_queries, proj_in, terms, others, grads_cross):
    steps = tokens.shape[0] // (2 * own.shape[0])
    block = pl.BlockSpec((2 * own.shape[0], D), lambda i: (i, 0))
    once = pl.Buffered(1)
    weight = lambda number: pl.BlockSpec((1, D, D), lambda i: (number, 0, 0), pipeline_mode=once)
    whole = pl.BlockSpec(own.shape, lambda i: (0, 0), pipeline_mode=once)
    pair = pl.BlockSpec((2, D, D), lambda i: (0, 0, 0), pipeline_mode=once)
    count, _, hidden = terms[0].shape
    expert = pl.BlockSpec((count, D // steps, hidden), lambda i: (0, i, 0))
    return pl.pallas_call(
        token_back_kernel,
        grid=(steps,),
        out_shape=[
            jax.ShapeDtypeStruct(tokens.shape, tokens.dtype),
            jax.ShapeDtypeStruct((8, D, D), tokens.dtype),
            jax.ShapeDtypeStruct((1, D), jnp.float32),
            jax.ShapeDtypeStruct(own.shape, jnp.float32),
        ]
        + [jax.ShapeDtypeStruct(terms[0].shape, jnp.float32)] * 2,
        in_specs=[block] * 3
        + [weight(1), weight(2), whole, whole, weight(0)]
        + [expert] * 6
        + [whole] * 6
        + [pair],
        out_specs=[
            block,
            pl.BlockSpec((8, D, D), lambda i: (0, 0, 0), pipeline_mode=once),
            pl.BlockSpec((1, D), lambda i: (0, 0)),
            pl.BlockSpec(own.shape, lambda i: (0, 0)),
            expert,
            expert,
        ],
        scratch_shapes=[pltpu.VMEM((D, 2 * D), jnp.float32)],
        compiler_params=pltpu.CompilerParams(vmem_limit_bytes=56 << 20),
        cost_estimate=cost(28),
        name="token_back",
    )(
        tokens,
        grad_keys,
        grad_values,
        proj_in,
        proj_in,
        own,
        grad_queries,
        proj_in,
        *terms,
        *others,
        grads_cross,
    )


def bias_lines(bias_table):
    at = jnp.arange(3 * TILE, dtype=jnp.int32)
    distance = jnp.where(at <= 2 * TILE, TILE - at, 4 * TILE - at)
    table = (bias_table - bias_table[NBUCKET - 1 :]) * log2e
    terms = jnp.broadcast_to(table[0][:, None], (HEADS, 3 * TILE))
    for number, threshold in enumerate(bucket_edges()):
        terms = jnp.where((distance >= threshold)[None], table[number + 1][:, None], terms)
    return jnp.where((distance >= 0)[None], terms, masked_score).reshape(PAIRS, 2, 3 * TILE)


def bias_tile(line_ref, h):
    line = jnp.broadcast_to(line_ref[0, h : h + 1, :], (TILE, 3 * TILE))
    return pltpu.roll(line, 0, 1, stride=1, stride_axis=0)[:, : 2 * TILE]


def bias_gradient(diagonals, sums):
    distance = 2 * TILE - 1 - jnp.arange(3 * TILE, dtype=jnp.int32)
    bucket = jnp.zeros(distance.shape, jnp.int32)
    for threshold in bucket_edges():
        bucket = bucket + (distance >= threshold).astype(jnp.int32)
    buckets = jnp.arange(NBUCKET, dtype=jnp.int32)[:, None]
    flat = diagonals.reshape(HEADS, -1)
    far = jnp.sum(sums, axis=-1).reshape(HEADS) - jnp.sum(flat, axis=-1)
    table = lax.dot_general(
        (bucket[None, :] == buckets).astype(jnp.float32),
        flat,
        (((1,), (1,)), ((), ())),
        precision=highest,
    )
    return table + jnp.where(buckets == NBUCKET - 1, far[None, :], 0.0)


def expert_kernel(n, m, slots, *refs):
    x_ref, maps, result_ref, grads = refs[0], refs[1:7], refs[7], refs[8:14]
    rows, parts, backs, up_all, down_all, act_all, du_all = refs[14:21]
    grad_bufs, far_bufs = refs[21:29], refs[29:31]
    map_sem, own_sem, grad_sem, go_sem, back_sem, term_sem, far_sem = refs[31:]
    seq, exp = lax.axis_index("seq"), lax.axis_index("exp")
    groups, count = n // QUAD, x_ref.shape[1] // slots
    batch = max(1, 128 // slots)
    far = [(g, k) for g in range(1, groups) for k in range(m)]
    moves = far + [(0, k) for k in range(1, m)]
    source_of = lambda k: lax.rem(exp + m - k, m)

    def push(source, target, sems, g, k, to_seq, to_exp):
        copy = pltpu.make_async_remote_copy(
            src_ref=source,
            dst_ref=target,
            send_sem=sems.at[0, g, k],
            recv_sem=sems.at[1, g, k],
            device_id={"seq": to_seq, "exp": to_exp},
            device_id_type=MESH,
        )
        copy.start()
        return copy

    def place(g, k):
        return lax.rem(seq + g * QUAD, n), lax.rem(exp + k, m)

    to_next, to_last = quad_moves(n)
    side = {"next": look_up(seq, [b for _, b in to_next]), "last": look_up(seq, [b for _, b in to_last])}
    greet(
        [dict(zip(("seq", "exp"), place(g, k))) for g, k in moves]
        + [{"seq": side["next"], "exp": exp}, {"seq": side["last"], "exp": exp}]
    )
    going = {}

    def go(some):
        for g, k in some:
            to_seq, to_exp = place(g, k)
            going[g, k] = push(x_ref.at[to_exp], rows.at[g, exp], go_sem, g, k, to_seq, to_exp)

    early = far[: len(far) // 2]
    go(early + moves[len(far) :])
    own = pltpu.make_async_copy(x_ref.at[exp], rows.at[0, exp], own_sem.at[0])
    own.start()
    fetched = []
    for j in range(1, QUAD):
        j = j % (QUAD - 1)
        for at, (source, target) in enumerate(((maps[2 * j], up_all), (maps[2 * j + 1], down_all))):
            copy = pltpu.make_async_copy(source, target.at[j], map_sem.at[at, j])
            copy.start()
            fetched.append(copy)
    for copy in fetched:
        copy.wait()
    far_maps = [
        push(up_all.at[1], up_all.at[3], far_sem, 0, 0, side["next"], exp),
        push(down_all.at[2], down_all.at[3], far_sem, 0, 1, side["last"], exp),
    ]
    own.wait()
    slope = math.sqrt(2.0 / math.pi)
    coming = {}

    def work(g, first, last):
        for k in range(first, last):
            if g or k:
                going[g, k].wait_recv()
        size = (last - first) * slots
        base = (g * m + first) * slots

        def one(e, carry):
            start = pl.multiple_of(e * slots, slots)
            piece = jnp.concatenate(
                [rows[g, source_of(k), pl.ds(start, slots), :] for k in range(first, last)], axis=0
            )
            tokens, upstream = piece[:, :D], piece[:, D:]
            result = back = None
            for j in range(QUAD):
                up_map, down_map = up_all[j, e], down_all[j, e]
                u = dot_plain(tokens, up_map)
                square = u * u
                bend = jnp.tanh(slope * (u + 0.044715 * (square * u)))
                half = 0.5 * (1.0 + bend)
                act = (u * half).astype(tokens.dtype)
                rise = half + 0.5 * u * (1.0 - bend * bend) * (
                    slope * (1.0 + 3 * 0.044715 * square)
                )
                du = (dot_plain(upstream, down_map) * rise).astype(tokens.dtype)
                act_all[e, j, base : base + size] = act
                du_all[e, j, base : base + size] = du
                y, dn = dot_last(act, down_map), dot_last(du, up_map)
                result = y if result is None else result + y
                back = dn if back is None else back + dn
            for i, k in enumerate(range(first, last)):
                span = slice(i * slots, (i + 1) * slots)
                where = (g, source_of(k), pl.ds(start, slots))
                parts[where + (slice(0, D),)] = result[span].astype(parts.dtype)
                parts[where + (slice(D, 2 * D),)] = back[span].astype(parts.dtype)
            return carry

        lax.fori_loop(0, count, one, 0)
        for k in range(first, last):
            if g or k:
                source = source_of(k)
                coming[g, k] = push(
                    parts.at[g, source],
                    backs.at[g, exp],
                    back_sem,
                    g,
                    k,
                    lax.rem(seq + n - g * QUAD, n),
                    source,
                )

    for move in early:
        going[move].wait_send()
    go(far[len(early) :])
    for copy in far_maps:
        copy.wait_recv()
    work(0, 0, m)
    for g in range(1, groups):
        for first in range(0, m, batch):
            work(g, first, min(m, first + batch))

    total = groups * m * slots

    def weigh(j):
        def one(e, carry):
            start = pl.multiple_of(e * slots, slots)
            piece = jnp.concatenate(
                [
                    rows[g, source_of(k), pl.ds(start, slots), :]
                    for g in range(groups)
                    for k in range(m)
                ],
                axis=0,
            )
            tokens, upstream = piece[:, :D], piece[:, D:]
            up_buf, down_buf = grad_bufs[2 * j], grad_bufs[2 * j + 1]
            up_buf[e] = dot_first(tokens, du_all[e, j, :total]).astype(up_buf.dtype)
            down_buf[e] = dot_first(upstream, act_all[e, j, :total]).astype(down_buf.dtype)
            return carry

        lax.fori_loop(0, count, one, 0)

    def term(source, target, number, to):
        return push(source, target, term_sem, 0, number, side[to], exp)

    def store(source, number):
        copy = pltpu.make_async_copy(source, grads[number], grad_sem.at[number])
        copy.start()
        return copy

    weigh(3)
    terms_out = [
        term(grad_bufs[6], far_bufs[0], 0, "next"),
        term(grad_bufs[7], far_bufs[1], 1, "last"),
    ]
    weigh(1)
    weigh(2)
    weigh(0)
    stored = [
        store(grad_bufs[i], number) for number, i in ((0, 0), (1, 1), (4, 2), (5, 5))
    ]
    for number, (buf, far_buf) in enumerate(((grad_bufs[4], far_bufs[0]), (grad_bufs[3], far_bufs[1]))):
        terms_out[number].wait_recv()
        buf[...] = (buf[...].astype(jnp.float32) + far_buf[...].astype(jnp.float32)).astype(buf.dtype)
        stored.append(store(buf, 2 + number))
    for k in range(m):
        where = source_of(k)
        terms = []
        for g in range(groups):
            back_k = (m - k) % m
            if g == 0 and k == 0:
                terms.append(parts[0, exp])
            else:
                coming[g, back_k].wait_recv()
                terms.append(backs[g, where])
        total_row = terms[0].astype(jnp.float32)
        for term in terms[1:]:
            total_row = total_row + term.astype(jnp.float32)
        result_ref[where] = total_row.astype(result_ref.dtype)
    for copy in stored:
        copy.wait()
    for copy in terms_out + far_maps:
        copy.wait_send()
    for move in moves[len(early) :]:
        going[move].wait_send()
    for copy in coming.values():
        copy.wait_send()


def run_experts(x, maps, n, m, slots, number):
    groups = n // QUAD
    count, _, hidden = maps[0].shape
    total = groups * m * slots
    big = pltpu.VMEM((groups,) + x.shape, x.dtype)
    stack = pltpu.VMEM((QUAD,) + maps[0].shape, x.dtype)
    kept = pltpu.VMEM((count, QUAD, total, hidden), x.dtype)
    grads = [(maps[0].shape, jnp.float32 if i < 2 else jnp.bfloat16) for i in range(2 * QUAD)]
    dma = pltpu.SemaphoreType.DMA
    return pl.pallas_call(
        functools.partial(expert_kernel, n, m, slots),
        out_shape=[jax.ShapeDtypeStruct(x.shape, x.dtype)]
        + [jax.ShapeDtypeStruct(shape, dtype) for shape, dtype in grads[:6]],
        in_specs=[ANY] * (1 + len(maps)),
        out_specs=[pl.BlockSpec(memory_space=pltpu.VMEM)] + [ANY] * 6,
        scratch_shapes=[big] * 3
        + [stack] * 2
        + [kept] * 2
        + [pltpu.VMEM(shape, dtype) for shape, dtype in grads + grads[6:]]
        + [
            dma((2, QUAD)),
            dma((1,)),
            dma((6,)),
            dma((2, groups, m)),
            dma((2, groups, m)),
            dma((2, 1, 2)),
            dma((2, 1, 2)),
        ],
        compiler_params=pltpu.CompilerParams(
            collective_id=number, has_side_effects=True, vmem_limit_bytes=60 << 20
        ),
        cost_estimate=cost(150),
        name="run_experts",
    )(x, *maps)


QUAD = 4


def quad_moves(n):
    ring = (0, 1, 3, 2)
    step = lambda i, by: i - i % QUAD + ring[(ring.index(i % QUAD) + by) % QUAD]
    return [(i, step(i, 1)) for i in range(n)], [(i, step(i, -1)) for i in range(n)]


def present_kernel(grad_ref, small_ref, in_ref, out_ref, gain_ref, table_ref, router_ref):
    step = pl.program_id(0)
    value = grad_ref[...].astype(jnp.float32)

    @pl.when(step < 6)
    def _():
        in_ref[...] = value

    @pl.when(step >= 6)
    def _():
        out_ref[...] = value

    @pl.when(step == 0)
    def _():
        experts = router_ref.shape[1]
        each = experts + 8
        pieces = D // TILE
        lines = jnp.concatenate(
            [small_ref[i * each : (i + 1) * each, :] for i in range(pieces)], axis=1
        )
        router_ref[...] = lines[:experts].T
        gain_ref[...] = lines[experts : experts + 3]
        table_ref[...] = small_ref[pieces * each : pieces * each + NBUCKET, :HEADS]


def present(grads, small, experts):
    whole = lambda shape: pl.BlockSpec(shape, lambda i: (0, 0))
    shapes = [(6, D, D), (2, D, D), (3, D), (NBUCKET, HEADS), (D, experts)]
    return pl.pallas_call(
        present_kernel,
        grid=(8,),
        out_shape=[jax.ShapeDtypeStruct(shape, jnp.float32) for shape in shapes],
        in_specs=[pl.BlockSpec((1, D, D), lambda i: (i, 0, 0)), whole(small.shape)],
        out_specs=[
            pl.BlockSpec((1, D, D), lambda i: (jnp.minimum(i, 5), 0, 0)),
            pl.BlockSpec((1, D, D), lambda i: (jnp.maximum(i - 6, 0), 0, 0)),
        ]
        + [whole(shape) for shape in shapes[2:]],
        compiler_params=pltpu.CompilerParams(vmem_limit_bytes=48 << 20),
        cost_estimate=cost(8),
        name="present",
    )(grads, small)


def project(source, matrix):
    return jnp.dot(source, matrix, preferred_element_type=jnp.float32).astype(jnp.bfloat16)


def input_grad(upstream, matrix):
    return jnp.einsum("te,de->td", upstream, matrix, preferred_element_type=jnp.float32)


def body(
    n,
    m,
    hidden_in,
    memory,
    proj_in,
    proj_out,
    norm_gains,
    rel_bias,
    router,
    expert_choice,
    expert_in,
    expert_out,
    cotangent,
):
    tokens = hidden_in[0].astype(jnp.float32)
    memory_rows = memory[0]
    memory_count = memory_rows.shape[0]
    gain_rows = norm_gains.astype(jnp.float32)
    token_count = tokens.shape[0]
    seq_at = lax.axis_index("seq").astype(jnp.int32).reshape(1)
    normed_self = rms_apply(tokens, gain_rows[0]).astype(jnp.bfloat16)
    lines = bias_lines(rel_bias)

    normed_all, memory_all, queries, key_all, value_all, memory_key_all, memory_value_all = (
        gather_projected(normed_self, memory_rows, proj_in, n, 1)
    )
    to_next, to_last = quad_moves(n)
    in_own, out_own, normed_all = lax.optimization_barrier((expert_in, expert_out, normed_all))
    in_last, out_last = (lax.ppermute(w, "seq", to_next) for w in (in_own, out_own))
    in_next, out_next = (lax.ppermute(w, "seq", to_last) for w in (in_own, out_own))
    normed_all = normed_all.reshape(n * token_count, D)
    memory_all = memory_all.reshape(n * memory_count, D)
    key_all, value_all = (x.reshape(n * token_count, D) for x in (key_all, value_all))
    memory_key_all, memory_value_all = (
        x.reshape(n * memory_count, D) for x in (memory_key_all, memory_value_all)
    )
    attended_self_low, attended_self, lse_self = attend(
        seq_at, queries, key_all, value_all, lines
    )
    after_self = tokens + jnp.dot(
        attended_self_low, proj_out[0], preferred_element_type=jnp.float32
    )

    normed_cross = rms_apply(after_self, gain_rows[1]).astype(jnp.bfloat16)
    cross_queries = project(normed_cross, proj_in[3])
    attended_cross_low, attended_cross, lse_cross = attend(
        seq_at, cross_queries, memory_key_all, memory_value_all, None
    )
    after_cross = after_self + jnp.dot(
        attended_cross_low, proj_out[1], preferred_element_type=jnp.float32
    )

    mixed_low = rms_apply(after_cross, gain_rows[2]).astype(jnp.bfloat16)
    softmax_probs = jax.nn.softmax(
        jnp.dot(mixed_low, router, preferred_element_type=jnp.float32), axis=-1
    )
    expert_count = router.shape[1]
    local_experts = expert_in.shape[0]
    capacity = max(2, 5 * token_count // (4 * expert_count))
    chosen = expert_choice[0, :, 0]
    onehot_int = (chosen[:, None] == jnp.arange(expert_count, dtype=jnp.int32)[None, :]).astype(
        jnp.int32
    )
    onehot = onehot_int.astype(jnp.float32)
    gate_prob = jnp.sum(softmax_probs * onehot, axis=-1)
    slot_index = jnp.sum(jnp.cumsum(onehot_int, axis=0) * onehot_int, axis=-1) - 1
    is_kept = slot_index < capacity
    slots = -(-capacity // 16) * 16
    place = jnp.where(is_kept, chosen * slots + slot_index, -1)
    dispatch = (
        place[:, None] == jnp.arange(expert_count * slots, dtype=jnp.int32)[None, :]
    ).astype(jnp.bfloat16)
    dispatched = jnp.sum(onehot_int * is_kept[:, None].astype(jnp.int32), axis=0)
    tally_counts = jnp.stack(
        [dispatched, jnp.sum(onehot_int, axis=0) - dispatched], axis=0
    ).reshape(1, 1, 2, expert_count)

    grad_top = cotangent[0].astype(jnp.float32)
    scaled = (gate_prob[:, None] * grad_top).astype(jnp.bfloat16)
    sent_rows = (
        jnp.einsum(
            "tx,td->xd",
            dispatch,
            jnp.concatenate([mixed_low, scaled], axis=1),
            preferred_element_type=jnp.float32,
        )
        .astype(jnp.bfloat16)
        .reshape(m, local_experts * slots, 2 * D)
    )
    maps = [in_own, out_own, in_last, out_last, in_next, out_next]
    returned, *terms = run_experts(sent_rows, maps, n, m, slots, 2)
    returned = returned.reshape(expert_count * slots, 2 * D)
    gin_own, gout_own, gin_next, gout_last, gin_last, gout_next = terms
    gout_next = lax.ppermute(gout_next, "seq", to_next)
    gin_last = lax.ppermute(gin_last, "seq", to_last)
    routed = jnp.dot(dispatch, returned, preferred_element_type=jnp.float32)
    combined, grad_mixed = routed[:, :D], routed[:, D:]
    output = (after_cross + gate_prob[:, None] * combined).astype(jnp.bfloat16)

    grad_gate = jnp.sum(grad_top * combined, axis=-1)
    grad_logits = softmax_probs * (onehot - gate_prob[:, None]) * grad_gate[:, None]
    grad_router = jnp.einsum(
        "td,te->de", mixed_low.astype(jnp.float32), grad_logits, precision=highest
    )
    grad_mixed = grad_mixed + jnp.einsum(
        "te,de->td", grad_logits, router.astype(jnp.float32), precision=highest
    )
    grad_cross_part, grad_gain_mix = rms_backward(after_cross, gain_rows[2], grad_mixed)
    grad_after_cross = grad_top + grad_cross_part

    grad_cross_low = grad_after_cross.astype(jnp.bfloat16)
    grad_attended_cross = input_grad(grad_cross_low, proj_out[1]).astype(jnp.bfloat16)
    grad_cross_query, grad_memory_keys, grad_memory_values = attend_back(
        seq_at,
        cross_queries,
        memory_key_all,
        memory_value_all,
        grad_attended_cross,
        attended_cross,
        lse_cross,
        None,
    )
    grad_cross_query, gin_last, gout_next, gin_next, gout_last = lax.optimization_barrier(
        (grad_cross_query, gin_last, gout_next, gin_next, gout_last)
    )
    gin_next = lax.ppermute(gin_next, "seq", to_next)
    gout_last = lax.ppermute(gout_last, "seq", to_last)
    grad_self_part, grad_gain_cross = rms_backward(
        after_self, gain_rows[1], input_grad(grad_cross_query, proj_in[3])
    )
    grad_after_self = grad_after_cross + grad_self_part
    grad_memory_part, grads_cross = memory_back(
        memory_all, grad_memory_keys, grad_memory_values, proj_in
    )

    grad_self_low = grad_after_self.astype(jnp.bfloat16)
    grad_attended_self = input_grad(grad_self_low, proj_out[0]).astype(jnp.bfloat16)
    grad_self_query, grad_keys, grad_values, near, sums = attend_back(
        seq_at,
        queries,
        key_all,
        value_all,
        grad_attended_self,
        attended_self,
        lse_self,
        lines,
    )
    grad_self_query, grad_keys, grad_values, near, sums, gout_last, gin_next = (
        lax.optimization_barrier(
            (grad_self_query, grad_keys, grad_values, near, sums, gout_last, gin_next)
        )
    )
    grad_table = bias_gradient(near, sums)
    (
        grad_normed_part,
        grads,
        grad_gain_part,
        grad_normed_query,
        grad_expert_in,
        grad_expert_out,
    ) = token_back(
        normed_all,
        grad_keys,
        grad_values,
        normed_self,
        grad_self_query,
        proj_in,
        [gin_own, gin_last, gin_next, gout_own, gout_last, gout_next],
        [
            normed_cross,
            grad_cross_query,
            attended_self_low,
            grad_self_low,
            attended_cross_low,
            grad_cross_low,
        ],
        grads_cross,
    )
    grad_gain_self = grad_gain_part[0] / gain_rows[0]

    grad_gains = jnp.stack([grad_gain_self, grad_gain_cross, grad_gain_mix])
    lines = jnp.concatenate(
        [grad_router.T, grad_gains, jnp.zeros((8 - grad_gains.shape[0], D), jnp.float32)]
    )
    small = [lines[:, i * TILE : (i + 1) * TILE] for i in range(D // TILE)]
    small.append(jnp.pad(grad_table, ((0, 0), (0, TILE - HEADS))))
    (grad_normed_own, grad_memory), grads, small = finish(
        [
            grad_normed_part.reshape(n, token_count, D),
            grad_memory_part.reshape(n, memory_count, D),
        ],
        grads.reshape(-1, D),
        jnp.concatenate(small),
        n,
        m,
        4,
    )
    wide = present(grads.reshape(8, D, D), small, expert_count)
    grad_token_part, _ = rms_backward(tokens, gain_rows[0], grad_normed_query + grad_normed_own)
    grad_in = (grad_after_self + grad_token_part).astype(jnp.bfloat16)
    return (
        output.reshape(1, token_count, D),
        grad_in.reshape(1, token_count, D),
        grad_memory.astype(jnp.bfloat16).reshape(1, memory_count, D),
        *wide,
        grad_expert_in,
        grad_expert_out,
        tally_counts,
    )


def solution(mesh):
    rows = P("exp", "seq", None)
    hidden = P("exp", None, "seq")
    return jax.shard_map(
        functools.partial(body, mesh.shape["seq"], mesh.shape["exp"]),
        mesh=mesh,
        in_specs=(rows, rows, P(), P(), P(), P(), P(), rows, hidden, hidden, rows),
        out_specs=(
            rows,
            rows,
            rows,
            P(),
            P(),
            P(),
            P(),
            P(),
            hidden,
            hidden,
            P("exp", "seq", None, None),
        ),
        check_vma=False,
    )
```
